32 devices in a mesh: seq: 2 (over core), blk: 16 (over z, y, x).
Axes of the slice: x: 2, y: 2, z: 4, core: 2. Of those that a mesh axis runs over, the one named last changes fastest.
Arguments:
- tokens: bfloat16 [2, 4096, 1024], P('seq', 'blk'), may hold values from -6 to 6
- segments: int32 [2, 4096], P('seq', 'blk'), may hold values from 0 to 6, as said below
- routes: int32 [2, 4096, 8], P('seq', 'blk'), may hold values from 0 to 15, all different within a row; in each aligned block of 256 rows (0 to 255, 256 to 511, ..., all dimensions but the last counted through in order) at most 256 rows name the same one
- route_weight: float32 [2, 4096, 8], P('seq', 'blk'), may hold values from 0.5 to 1.5
- norm1_gain: float32 [1024], replicated, may hold values from 0.5 to 1.5
- w_query: bfloat16 [1024, 1024], replicated, may hold values from -0.1875 to 0.1875
- w_key: bfloat16 [1024, 512], replicated, may hold values from -0.1875 to 0.1875
- w_value: bfloat16 [1024, 512], replicated, may hold values from -0.1875 to 0.1875
- w_out: bfloat16 [1024, 1024], replicated, may hold values from -4 to 4
- norm2_gain: float32 [1024], replicated, may hold values from 0.5 to 1.5
- w_router: bfloat16 [1024, 16], replicated, may hold values from -0.09375 to 0.09375
- w_gate: bfloat16 [16, 1024, 512], P('blk'), may hold values from -0.1875 to 0.1875
- w_up: bfloat16 [16, 1024, 512], P('blk'), may hold values from -0.1875 to 0.1875
- w_down: bfloat16 [16, 512, 1024], P('blk'), may hold values from -1 to 1
- cotangent: bfloat16 [2, 4096, 1024], P('seq', 'blk'), may hold values from -6 to 6
Outputs:
- output: bfloat16 [2, 4096, 1024], P('seq', 'blk')
- tokens_grad: float32 [2, 4096, 1024], P('seq', 'blk')
- norm1_gain_grad: float32 [1024], replicated
- w_query_grad: float32 [1024, 1024], replicated
- w_key_grad: float32 [1024, 512], replicated
- w_value_grad: float32 [1024, 512], replicated
- w_out_grad: float32 [1024, 1024], replicated
- norm2_gain_grad: float32 [1024], replicated
- w_router_grad: float32 [1024, 16], replicated
- w_gate_grad: float32 [16, 1024, 512], P('blk')
- w_up_grad: float32 [16, 1024, 512], P('blk')
- w_down_grad: float32 [16, 512, 1024], P('blk')
The draws below stay inside these ranges and needn't reach their ends.
Inputs may be any that keep to these rules, and one draw needn't show every extreme that they name: `segments`: segment numbers never fall along a sequence and begin at 0; each sequence has six document boundaries, some of which may coincide. In one of the 2 sequences, which one varies, the boundaries lie within its first 256 and its last 256 positions; in the others they may lie anywhere. `routes`: each token names 8 different experts; among the 256 tokens of one device no expert is named more than 256 times, a bound that some block reaches.
All inputs are finite; a program needn't handle non-finite values.
Results may differ from the reference program's by a relative error of at most 0.019.
Values may be sent and summed in bfloat16 or wider, within the bound.
A program may use at most 256 MiB of HBM per device.

```python
import math
import jax
import jax.numpy as jnp
import numpy as np
from jax import lax

D = 1024
H = 16
KV = 8
HD = 64
FF = 512
TOP = 8
TOK_DEV = 256
EXPERTS = 16
SEQS = 2
LEN = 4096
CAP = 256


def draw_segments(key, part):
    key = jax.random.fold_in(key, 11)
    first_key, second_key, third_key, fourth_key = jax.random.split(key, 4)
    early = jax.random.randint(first_key, (SEQS, 3), 1, TOK_DEV, dtype=jnp.int32)
    late = jax.random.randint(second_key, (SEQS, 3), LEN - TOK_DEV, LEN, dtype=jnp.int32)
    edges = jnp.concatenate([early, late], 1)
    spread = jax.random.randint(third_key, (SEQS, 6), 1, LEN, dtype=jnp.int32)
    spanning = jax.random.randint(fourth_key, (), 0, SEQS, dtype=jnp.int32)
    which = (jnp.arange(SEQS, dtype=jnp.int32) == spanning)[:, None]
    cuts = jnp.where(which, edges, spread)
    positions = jnp.arange(LEN, dtype=jnp.int32)
    return jnp.sum((positions[None, :, None] >= cuts[:, None, :]).astype(jnp.int32), -1)


def levels(key, shape, cuts, smallest, top_value):
    loudness = 1.0
    for position, shards_of in cuts:
        heights = jax.random.uniform(jax.random.fold_in(jax.random.fold_in(key, 6), position), (shards_of,), jnp.float32, smallest / len(cuts), top_value / len(cuts))
        loudness = loudness * jnp.repeat(jnp.exp(heights), shape[position] // shards_of).reshape((-1,) + (1,) * (len(shape) - 1 - position))
    return loudness


def shared_out(stream_key, own, number, rows, amount, top, reach, slope):
    order = jax.random.permutation(stream_key, amount)
    packed, ordinary = load_shares(amount, rows * top, reach, slope, True), load_shares(amount, rows * top, reach, slope, False)
    places = jnp.arange(amount)

    def named(lengths, turn):
        used = int((lengths > 0).sum())
        fixed = max(1, used // 4)
        moved = fixed + (places - fixed + turn * (used - fixed)) % max(1, amount - fixed)
        return jnp.zeros((amount,), jnp.int32).at[order[jnp.where(places < fixed, places, moved)]].set(jnp.asarray(lengths, jnp.int32))

    lengths = jnp.where(number % 4 == 0, named(packed, number // 4), named(ordinary, number - number // 4 - 1))
    mixed = jax.random.permutation(jax.random.fold_in(own, 3), amount)
    source_of, taker = mixed[0:amount // 2 * 2:2], mixed[1:amount // 2 * 2:2]
    room = jnp.minimum(lengths[source_of] - 1, reach - lengths[taker]) // 2
    room = jnp.where((source_of == order[0]) | (taker == order[0]) | (lengths[taker] == 0), 0, jnp.maximum(room, 0))
    moved = jax.random.randint(jax.random.fold_in(own, 4), (amount // 2,), 0, 1 << 20) % (room + 1)
    lengths = lengths.at[source_of].add(-moved).at[taker].add(moved)
    labels = jnp.searchsorted(jnp.cumsum(lengths), jnp.arange(rows * top), side="right").astype(jnp.int32)
    listing = labels.reshape(top, rows).T
    listing = listing[jax.random.permutation(jax.random.fold_in(own, 1), rows)]
    turn = jax.random.randint(jax.random.fold_in(own, 2), (rows, 1), 0, top)
    return jnp.take_along_axis(listing, (jnp.arange(top)[None, :] + turn) % top, axis=1)


def load_shares(number_of, total, most, lean, full):
    weights = [(1 << 20) // math.isqrt(rank ** lean) + 1 for rank in range(1, number_of + 1)]
    largest = most if full else min(most, max(-(-total // number_of), total * weights[0] // sum(weights)))
    least = 1 if total - largest >= number_of - 1 else 0
    counts, surplus = [largest] + [least] * (number_of - 1), total - largest - least * (number_of - 1)
    while surplus > 0:
        free = [i for i in range(1, number_of) if counts[i] < largest] or [i for i in range(1, number_of) if counts[i] < most]
        pool, budget = sum([weights[i] for i in free]), surplus
        for i in free:
            more = min(most - counts[i], max(1, budget * weights[i] // pool), surplus)
            counts[i] = counts[i] + more
            surplus = surplus - more
    return np.array(counts)


def normal_values(rng, extent, scale, reach, cuts=(), held_as=jnp.bfloat16):
    level = levels(rng, extent, cuts, -0.22, 0.18) if cuts else 1.0
    array = jax.random.normal(rng, extent, jnp.float32) * scale * level
    return jnp.minimum(jnp.maximum(array, -reach), reach).astype(held_as)


def setup_inputs(seed: int = 0) -> dict:
    keys = jax.random.split(jax.random.key(seed), 16)
    tokens = normal_values(keys[0], (SEQS, LEN, D), 1.0, 6.0, ((0, 2), (1, 16)))
    segments = draw_segments(jax.random.fold_in(keys[15], 71), 0)
    routes_keys = jax.random.split(jax.random.fold_in(keys[2], 1), SEQS * LEN // TOK_DEV)
    routes_turns = jax.random.permutation(jax.random.fold_in(keys[2], 3), SEQS * LEN // TOK_DEV)
    routes = jax.vmap(lambda own, number: shared_out(jax.random.fold_in(keys[2], 2), own, number, TOK_DEV, EXPERTS, TOP, CAP, 2))(routes_keys, routes_turns).reshape((SEQS, LEN, TOP))
    route_weight = jnp.clip(0.5 + 1.0 * jax.random.uniform(keys[3], (SEQS, LEN, TOP), jnp.float32) ** levels(keys[3], (SEQS, LEN, TOP), ((0, 2), (1, 16)), -0.2, 0.2), 0.5, 1.5)
    norm1_gain = jnp.clip(1.0 + 0.1 * jax.random.normal(keys[4], (D,), jnp.float32), 0.5, 1.5)
    w_query = normal_values(keys[5], (D, H * HD), D ** -0.5, 0.1875)
    w_key = normal_values(keys[6], (D, KV * HD), D ** -0.5, 0.1875)
    w_value = normal_values(keys[7], (D, KV * HD), D ** -0.5, 0.1875)
    w_out = normal_values(keys[8], (H * HD, D), (max(1, D * 8 // LEN)) ** -0.5, 4.0)
    norm2_gain = jnp.clip(1.0 + 0.1 * jax.random.normal(keys[9], (D,), jnp.float32), 0.5, 1.5)
    w_router = normal_values(keys[10], (D, EXPERTS), (4 * D) ** -0.5, 0.09375)
    w_gate = normal_values(keys[11], (EXPERTS, D, FF), D ** -0.5, 0.1875, ((0, 16),))
    w_up = normal_values(keys[12], (EXPERTS, D, FF), D ** -0.5, 0.1875, ((0, 16),))
    w_down = normal_values(keys[13], (EXPERTS, FF, D), (FF // 16) ** -0.5, 1.0, ((0, 16),))
    cotangent = normal_values(keys[14], (SEQS, LEN, D), 1.0, 6.0, ((0, 2), (1, 16)))
    return dict(tokens=tokens, segments=segments, routes=routes, route_weight=route_weight, norm1_gain=norm1_gain, w_query=w_query, w_key=w_key, w_value=w_value, w_out=w_out, norm2_gain=norm2_gain, w_router=w_router, w_gate=w_gate, w_up=w_up, w_down=w_down, cotangent=cotangent)


EPS = 1e-06
NEG = -1e+30
HIGH = lax.Precision.HIGHEST

@jax.custom_vjp
def low(v):
    return lax.optimization_barrier(v.astype(jnp.bfloat16)).astype(jnp.float32)

@jax.custom_vjp
def low_back(v):
    return v

def low_keep(v):
    return (low(v), None)

def low_pass(kept, grad):
    return (grad,)

def back_keep(v):
    return (v, None)

def back_low(kept, grad):
    return (low(grad),)
low.defvjp(low_keep, low_pass)
low_back.defvjp(back_keep, back_low)

def matmul(a, b):
    return jnp.dot(a, b, precision=HIGH, preferred_element_type=jnp.float32)

def rope_tables(positions):
    half = HD // 2
    freq = jnp.exp(-math.log(10000.0) * jnp.arange(half, dtype=jnp.float32) * 2.0 / HD)
    angle = positions.astype(jnp.float32)[:, None] * freq[None, :]
    cosine = jnp.concatenate([jnp.cos(angle), jnp.cos(angle)], -1)
    sine = jnp.concatenate([jnp.sin(angle), jnp.sin(angle)], -1)
    return (cosine, sine)

def rotate_half(v):
    half = v.shape[-1] // 2
    return jnp.concatenate([-v[..., half:], v[..., :half]], -1)

def rotary(v, cosine, sine):
    return v * cosine[:, None, :] + rotate_half(v) * sine[:, None, :]

def rms_scale(v):
    return lax.rsqrt(lax.optimization_barrier(jnp.mean(v * v, -1, keepdims=True)) + EPS)

def attention(q_rot, k_rot, value, seg):
    length = q_rot.shape[0]
    qblock = min(512, length)
    count = length // qblock
    group = H // KV
    keypos = jnp.arange(length, dtype=jnp.int32)
    values = value.reshape(length, KV, HD)
    scale = HD ** (-0.5)

    def block(args):
        qb, qseg, qstart = args
        score = low_back(jnp.einsum('qkgd,skd->kgqs', qb, k_rot, precision=HIGH) * scale)
        qpos = qstart + jnp.arange(qblock, dtype=jnp.int32)
        mask = ((qseg[:, None] == seg[None, :]) & (keypos[None, :] <= qpos[:, None]))[None, None]
        masked = jnp.where(mask, score, NEG)
        top = lax.optimization_barrier(jnp.max(masked, -1, keepdims=True))
        expo = jnp.where(mask, jnp.exp(masked - top), 0.0)
        total = lax.optimization_barrier(jnp.sum(expo, -1))
        acc = jnp.einsum('kgqs,skd->kgqd', low(expo), values, precision=HIGH)
        return (acc / total[..., None]).transpose(2, 0, 1, 3)
    starts = jnp.arange(count, dtype=jnp.int32) * qblock
    out = lax.map(jax.checkpoint(block), (q_rot.reshape(count, qblock, KV, group, HD), seg.reshape(count, qblock), starts))
    return out.reshape(length, H * HD)

def sequence_forward(xs, seg, route, rweight, g1, wq, wk, wv, wo, g2, wr, wg, wu, wd):
    length = xs.shape[0]
    group = H // KV
    positions = jnp.arange(length, dtype=jnp.int32)
    cosine, sine = rope_tables(positions)
    xa = low(xs * rms_scale(xs) * g1)
    query = low_back(matmul(xa, wq))
    key = low_back(matmul(xa, wk))
    value = low_back(low(matmul(xa, wv)))
    q_rot = low(rotary(query.reshape(length, H, HD), cosine, sine)).reshape(length, KV, group, HD)
    k_rot = low(rotary(key.reshape(length, KV, HD), cosine, sine))
    attended = attention(q_rot, k_rot, value, seg)
    att_low = low(low_back(attended))
    h1 = xs + low_back(matmul(att_low, wo))
    xl = low(h1 * rms_scale(h1) * g2)
    logits = low_back(matmul(xl, wr))
    experts = wr.shape[1]
    chooser = (route[:, :, None] == jnp.arange(experts, dtype=jnp.int32)[None, None, :]).astype(jnp.float32)
    chosen = jnp.einsum('tje,te->tj', chooser, logits, precision=HIGH)
    gates = jax.nn.softmax(chosen, -1)
    combine = low(rweight * gates)
    weights = jnp.einsum('tje,tj->et', chooser, combine, precision=HIGH)

    def expert(acc, args):
        gate_w, up_w, down_w, weight = args
        x_in = low_back(xl)
        gate_pre = low_back(matmul(x_in, gate_w))
        up_pre = low_back(matmul(x_in, up_w))
        hidden = low(jax.nn.silu(gate_pre) * up_pre)
        out = low_back(low(matmul(hidden, down_w)))
        return (acc + weight[:, None] * out, None)
    mixture, unused = lax.scan(jax.checkpoint(expert), jnp.zeros_like(xs), (wg, wu, wd, weights))
    return h1 + mixture

def reference(tokens, segments, routes, route_weight, norm1_gain, w_query, w_key, w_value, w_out, norm2_gain, w_router, w_gate, w_up, w_down, cotangent):
    floats = (tokens.astype(jnp.float32), norm1_gain.astype(jnp.float32), w_query.astype(jnp.float32), w_key.astype(jnp.float32), w_value.astype(jnp.float32), w_out.astype(jnp.float32), norm2_gain.astype(jnp.float32), w_router.astype(jnp.float32), w_gate.astype(jnp.float32), w_up.astype(jnp.float32), w_down.astype(jnp.float32))
    rweights = route_weight.astype(jnp.float32)

    def forward(x, g1, wq, wk, wv, wo, g2, wr, wg, wu, wd):

        def one(args):
            xs, seg, route, rweight = args
            return sequence_forward(xs, seg, route, rweight, g1, wq, wk, wv, wo, g2, wr, wg, wu, wd)
        return lax.map(one, (x, segments, routes, rweights))
    result, pull = jax.vjp(forward, *floats)
    grads = pull(cotangent.astype(jnp.float32))
    return (result.astype(jnp.bfloat16), grads[0], grads[1], grads[2], grads[3], grads[4], grads[5], grads[6], grads[7], grads[8], grads[9], grads[10])
```

```python
import functools
import math

import jax
import jax.numpy as jnp
import numpy as np
from jax import lax
from jax.experimental import pallas as pl
from jax.experimental.pallas import tpu as pltpu
from jax.sharding import PartitionSpec as P

H = 16
KV = 8
HD = 64
TOP = 8
EPS = 1e-06
NEG = -1e30
F32 = jnp.float32
BF16 = jnp.bfloat16
MESH = pl.DeviceIdType.MESH
VMEM_LIMIT = 60 * 2**20
NT = (((1,), (1,)), ((), ()))
TN = (((0,), (0,)), ((), ()))


def mm(a, b, dims=(((1,), (0,)), ((), ()))):
    return lax.dot_general(a, b, dims, preferred_element_type=F32)


def remote(src, dst, send, recv, seq, blk):
    return pltpu.make_async_remote_copy(
        src_ref=src,
        dst_ref=dst,
        send_sem=send,
        recv_sem=recv,
        device_id=(seq, blk),
        device_id_type=MESH,
    )


def greet_all(seqs, blocks, me_s, me_b):
    barrier = pltpu.get_barrier_semaphore()
    total = seqs * blocks

    def hello(n, carry):
        other = lax.rem(me_s * blocks + me_b + n, total)
        pl.semaphore_signal(
            barrier,
            inc=1,
            device_id=(other // blocks, lax.rem(other, blocks)),
            device_id_type=MESH,
        )
        return carry

    lax.fori_loop(1, total, hello, 0)
    pl.semaphore_wait(barrier, total - 1)


def rotate_pairs(u):
    lanes = u.shape[-1]
    half = HD // 2
    lane = lax.broadcasted_iota(jnp.int32, u.shape, u.ndim - 1)
    ahead = pltpu.roll(u, lanes - half, u.ndim - 1)
    behind = pltpu.roll(u, half, u.ndim - 1)
    return jnp.where(lane % HD < half, -ahead, behind)


def stacked_heads(wide):
    return jnp.concatenate([wide[:HD], wide[HD:]], axis=1)


def attention_forward_kernel(
    blocks,
    pay,
    o_ref,
    kv_ref,
    kvt_ref,
    q_ref,
    ot_ref,
    stat_ref,
    in_ref,
    other_ref,
    obuf,
    cnt,
    send_sem,
    recv_sem,
    fsend_sem,
    frecv_sem,
    osend_sem,
    orecv_sem,
):
    me_s = lax.axis_index("seq")
    me_b = lax.axis_index("blk")
    tok = q_ref.shape[1]
    steps = blocks // 2
    sigma = me_b // KV
    kappa = lax.rem(me_b, KV)
    greet_all(2, blocks, me_s, me_b)

    dest_core = lax.rem(me_b, 2)
    slot = me_b // 2

    def payload(n):
        k = lax.rem(me_b + n, KV)
        chip = me_s * KV + k
        mine = (dest_core == me_s) & (chip == me_b)
        return k, chip, mine

    def send_payload(n, carry):
        k, chip, mine = payload(n)

        @pl.when(mine)
        def _():
            pltpu.make_async_copy(pay.at[k], in_ref.at[slot], recv_sem.at[slot]).start()

        @pl.when(jnp.logical_not(mine))
        def _():
            remote(
                pay.at[k], in_ref.at[slot], send_sem.at[k], recv_sem.at[slot], dest_core, chip
            ).start()

        return carry

    lax.fori_loop(0, KV, send_payload, 0)

    def arrival(t):
        return pltpu.make_async_copy(pay.at[0], in_ref.at[t], recv_sem.at[t])

    def forward(t):
        return remote(
            in_ref.at[t, :, pl.ds(2 * HD, 2 * HD)],
            other_ref.at[t],
            fsend_sem.at[t],
            frecv_sem.at[t],
            1 - me_s,
            me_b,
        )

    arrival(0).wait()
    forward(0).start()
    cnt[...] = jnp.zeros_like(cnt)
    first_core = me_s == 0
    lane = lax.broadcasted_iota(jnp.int32, (1, 2 * tok), 1)
    qrow = jnp.where(lane < tok, lane, lane - tok)
    wide = 2 * tok

    def step(t, carry):
        @pl.when(t < steps - 1)
        def _():
            arrival(t + 1).wait()
            forward(t + 1).start()

        forward(t).wait_recv()
        mine = in_ref[t]
        kv_mine, seg_mine = mine[:tok, 2 * HD :], mine[tok:, 2 * HD :].astype(F32)
        other = other_ref[t]
        kv_other, seg_other = other[:tok], other[tok:].astype(F32)
        pair = jnp.where(
            first_core,
            jnp.concatenate([kv_mine, kv_other], 0).astype(F32),
            jnp.concatenate([kv_other, kv_mine], 0).astype(F32),
        )
        kv_ref[t] = pair.astype(BF16)
        kvt_ref[t] = jnp.transpose(pair).astype(BF16)
        number = lax.broadcasted_iota(jnp.int32, (8, tok), 0).astype(F32)
        seg_q = jnp.concatenate([seg_mine[0:1], seg_mine[1:2]], 1)
        seg_o = jnp.concatenate([seg_other[0:1], seg_other[1:2]], 1)
        below = (seg_q < number).astype(F32) + (seg_o < number).astype(F32)
        cnt[...] += jnp.sum(below, 1, keepdims=True)
        start_q = jnp.sum(jnp.where(seg_q == number, cnt[:, :1], 0.0), 0, keepdims=True)
        start = jnp.concatenate([start_q, start_q], 1).astype(jnp.int32)
        q_two = mine[:tok, : 2 * HD]
        q_ref[t] = q_two
        qt = stacked_heads(jnp.transpose(q_two.astype(F32)))
        qm = jnp.concatenate([qt, jnp.zeros_like(qt)], 0).astype(BF16)
        qpos = (2 * t + me_s) * tok + qrow

        def piece(u, state, last):
            running, total, acc = state
            score = mm(kv_ref[u], qm)
            kpos = u * wide + lax.broadcasted_iota(jnp.int32, score.shape, 0)
            mask = kpos >= start
            if last:
                mask &= kpos <= qpos
            score = jnp.where(mask, score, NEG)
            newmax = jnp.maximum(running, jnp.max(score, 0, keepdims=True))
            expo = jnp.exp(score - newmax)
            factor = jnp.exp(running - newmax)
            total = total * factor + jnp.sum(expo, 0, keepdims=True)
            acc = acc * factor + mm(kvt_ref[u, HD:, :], expo.astype(BF16))
            return newmax, total, acc

        state = (
            jnp.full((1, wide), NEG, F32),
            jnp.zeros((1, wide), F32),
            jnp.zeros((HD, wide), F32),
        )
        state = lax.fori_loop(0, t, lambda u, s: piece(u, s, False), state)
        running, total, acc = piece(t, state, True)
        out_t = acc / total
        ot_ref[t] = out_t
        rows = lax.broadcasted_iota(jnp.int32, (8, wide), 0)
        lse = running + jnp.log(total)
        stat_ref[t] = jnp.where(rows == 0, lse, start.astype(F32))
        upright = jnp.concatenate([out_t[:, :tok], out_t[:, tok:]], 0)
        obuf[t] = jnp.transpose(upright).astype(BF16)
        owner = 2 * t + me_s
        home = (sigma == me_s) & (owner == me_b)
        place = o_ref.at[:, pl.ds(pl.multiple_of(kappa * 2 * HD, 2 * HD), 2 * HD)]

        @pl.when(home)
        def _():
            pltpu.make_async_copy(obuf.at[t], place, orecv_sem.at[kappa]).start()

        @pl.when(jnp.logical_not(home))
        def _():
            remote(obuf.at[t], place, osend_sem.at[t], orecv_sem.at[kappa], sigma, owner).start()

        return carry

    lax.fori_loop(0, steps, step, 0)

    def finish(t, carry):
        k, chip, mine = payload(t)

        @pl.when(jnp.logical_not(mine))
        def _():
            remote(
                pay.at[k], in_ref.at[slot], send_sem.at[k], recv_sem.at[slot], dest_core, chip
            ).wait_send()

        return carry

    lax.fori_loop(0, KV, finish, 0)

    def finish_steps(t, carry):
        forward(t).wait_send()
        owner = 2 * t + me_s
        home = (sigma == me_s) & (owner == me_b)

        @pl.when(jnp.logical_not(home))
        def _():
            remote(
                obuf.at[t],
                o_ref.at[:, pl.ds(0, 2 * HD)],
                osend_sem.at[t],
                orecv_sem.at[0],
                sigma,
                owner,
            ).wait_send()

        return carry

    lax.fori_loop(0, steps, finish_steps, 0)

    def gather(k, carry):
        pltpu.make_async_copy(
            obuf.at[0],
            o_ref.at[:, pl.ds(pl.multiple_of(k * 2 * HD, 2 * HD), 2 * HD)],
            orecv_sem.at[k],
        ).wait()
        return carry

    lax.fori_loop(0, KV, gather, 0)


def attention_forward(blocks, pay):
    tok = pay.shape[2]
    steps = blocks // 2
    vm = pl.BlockSpec(memory_space=pltpu.VMEM)
    dma = pltpu.SemaphoreType.DMA
    return pl.pallas_call(
        functools.partial(attention_forward_kernel, blocks),
        out_shape=(
            jax.ShapeDtypeStruct((tok, H * HD), BF16),
            jax.ShapeDtypeStruct((steps, 2 * tok, 2 * HD), BF16),
            jax.ShapeDtypeStruct((steps, 2 * HD, 2 * tok), BF16),
            jax.ShapeDtypeStruct((steps, tok, 2 * HD), BF16),
            jax.ShapeDtypeStruct((steps, HD, 2 * tok), F32),
            jax.ShapeDtypeStruct((steps, 8, 2 * tok), F32),
        ),
        in_specs=[vm],
        out_specs=(vm,) * 6,
        scratch_shapes=[
            pltpu.VMEM((steps, tok + 16, 4 * HD), BF16),
            pltpu.VMEM((steps, tok + 16, 2 * HD), BF16),
            pltpu.VMEM((steps, tok, 2 * HD), BF16),
            pltpu.VMEM((8, 128), F32),
            dma((KV,)),
            dma((steps,)),
            dma((steps,)),
            dma((steps,)),
            dma((steps,)),
            dma((KV,)),
        ],
        compiler_params=pltpu.CompilerParams(
            collective_id=0, has_side_effects=True, vmem_limit_bytes=VMEM_LIMIT
        ),
        name="attention_forward",
    )(pay)


def attention_backward_kernel(
    blocks,
    do_ref,
    kv_ref,
    kvt_ref,
    q_ref,
    ot_ref,
    stat_ref,
    cos_ref,
    sin_ref,
    out_ref,
    in_ref,
    dkv,
    part,
    xch,
    done,
    send_sem,
    recv_sem,
    xsend_sem,
    xrecv_sem,
    osend_sem,
    orecv_sem,
):
    me_s = lax.axis_index("seq")
    me_b = lax.axis_index("blk")
    tok = q_ref.shape[1]
    steps = blocks // 2
    sigma = me_b // KV
    kappa = lax.rem(me_b, KV)
    greet_all(2, blocks, me_s, me_b)

    dest_core = lax.rem(me_b, 2)
    slot = me_b // 2

    def outgoing(n):
        k = lax.rem(me_b + n, KV)
        chip = me_s * KV + k
        mine = (dest_core == me_s) & (chip == me_b)
        src = do_ref.at[:, pl.ds(pl.multiple_of(k * 2 * HD, 2 * HD), 2 * HD)]
        return k, chip, mine, src

    def send_grad(n, carry):
        k, chip, mine, src = outgoing(n)

        @pl.when(mine)
        def _():
            pltpu.make_async_copy(src, in_ref.at[slot], recv_sem.at[slot]).start()

        @pl.when(jnp.logical_not(mine))
        def _():
            remote(src, in_ref.at[slot], send_sem.at[k], recv_sem.at[slot], dest_core, chip).start()

        return carry

    lax.fori_loop(0, KV, send_grad, 0)
    dkv[...] = jnp.zeros_like(dkv)
    wide = 2 * tok
    lane = lax.broadcasted_iota(jnp.int32, (1, wide), 1)
    qrow = jnp.where(lane < tok, lane, lane - tok)
    low = lax.broadcasted_iota(jnp.int32, (tok, 2 * HD), 1) < HD

    def swap(t):
        return remote(part.at[t], xch.at[t], xsend_sem.at[t], xrecv_sem.at[t], 1 - me_s, me_b)

    def deliver(t, act):
        owner = 2 * t + me_s
        home = (sigma == me_s) & (owner == me_b)
        src, dst = done.at[t], out_ref.at[kappa]

        @pl.when(home)
        def _():
            if act == "start":
                pltpu.make_async_copy(src, dst, orecv_sem.at[kappa]).start()

        @pl.when(jnp.logical_not(home))
        def _():
            copy = remote(src, dst, osend_sem.at[t], orecv_sem.at[kappa], sigma, owner)
            copy.start() if act == "start" else copy.wait_send()

    def finalize(t):
        swap(t).wait_recv()
        place = pl.ds(pl.multiple_of(me_s * tok, tok), tok)
        total = dkv[t, place, :] + xch[t]
        owner = 2 * t + me_s
        cosine = jnp.where(low, cos_ref[owner], 1.0)
        sine = jnp.where(low, sin_ref[owner], 0.0)
        back = total * cosine - rotate_pairs(total) * sine
        done[t, :, pl.ds(2 * HD, 2 * HD)] = back.astype(BF16)
        deliver(t, "start")

    def step(n, carry):
        t = steps - 1 - n
        pltpu.make_async_copy(do_ref.at[:, pl.ds(0, 2 * HD)], in_ref.at[t], recv_sem.at[t]).wait()
        d_two = in_ref[t].astype(F32)
        q_two = q_ref[t].astype(F32)
        dt = stacked_heads(jnp.transpose(d_two))
        qt = stacked_heads(jnp.transpose(q_two))
        zero = jnp.zeros_like(dt)
        dm = jnp.concatenate([zero, dt], 0).astype(BF16)
        qm = jnp.concatenate([qt, zero], 0).astype(BF16)
        delta = jnp.sum(ot_ref[t] * dt, 0, keepdims=True)
        right = jnp.concatenate(
            [
                jnp.where(low, q_two, 0.0),
                jnp.where(low, pltpu.roll(q_two, HD, 1), 0.0),
                jnp.where(low, 0.0, pltpu.roll(d_two, HD, 1)),
                jnp.where(low, 0.0, d_two),
            ],
            0,
        ).astype(BF16)
        stat = stat_ref[t]
        lse, start = stat[0:1], stat[1:2].astype(jnp.int32)
        qpos = (2 * t + me_s) * tok + qrow

        def piece(u, dq, last):
            keys = kv_ref[u]
            score = mm(keys, qm)
            kpos = u * wide + lax.broadcasted_iota(jnp.int32, score.shape, 0)
            mask = kpos >= start
            if last:
                mask &= kpos <= qpos
            prob = jnp.where(mask, jnp.exp(score - lse), 0.0)
            dprob = mm(keys, dm)
            dscore = (prob * (dprob - delta)).astype(BF16)
            both = jnp.concatenate([dscore, prob.astype(BF16)], 1)
            dkv[u] += mm(both, right)
            return dq + mm(kvt_ref[u, :HD, :], dscore)

        dq = jnp.zeros((HD, wide), F32)
        dq = lax.fori_loop(0, t, lambda u, s: piece(u, s, False), dq)
        dq = piece(t, dq, True) * HD ** (-0.5)
        upright = jnp.transpose(jnp.concatenate([dq[:, :tok], dq[:, tok:]], 0))
        owner = 2 * t + me_s
        back = upright * cos_ref[owner] - rotate_pairs(upright) * sin_ref[owner]
        done[t, :, pl.ds(0, 2 * HD)] = back.astype(BF16)
        part[t] = dkv[t, pl.ds(pl.multiple_of((1 - me_s) * tok, tok), tok), :]
        swap(t).start()

        @pl.when(n > 0)
        def _():
            finalize(t + 1)

        return carry

    lax.fori_loop(0, steps, step, 0)
    finalize(0)

    def finish(n, carry):
        k, chip, mine, src = outgoing(n)

        @pl.when(jnp.logical_not(mine))
        def _():
            remote(
                src, in_ref.at[slot], send_sem.at[k], recv_sem.at[slot], dest_core, chip
            ).wait_send()

        return carry

    lax.fori_loop(0, KV, finish, 0)

    def finish_steps(t, carry):
        swap(t).wait_send()
        deliver(t, "wait")
        return carry

    lax.fori_loop(0, steps, finish_steps, 0)

    def gather(k, carry):
        pltpu.make_async_copy(done.at[0], out_ref.at[k], orecv_sem.at[k]).wait()
        return carry

    lax.fori_loop(0, KV, gather, 0)


def attention_backward(blocks, d_o, kv, kvt, q_two, out_t, stat, cos_all, sin_all):
    tok = q_two.shape[1]
    steps = blocks // 2
    vm = pl.BlockSpec(memory_space=pltpu.VMEM)
    dma = pltpu.SemaphoreType.DMA
    return pl.pallas_call(
        functools.partial(attention_backward_kernel, blocks),
        out_shape=jax.ShapeDtypeStruct((KV, tok, 4 * HD), BF16),
        in_specs=[vm] * 8,
        out_specs=vm,
        scratch_shapes=[
            pltpu.VMEM((steps, tok, 2 * HD), BF16),
            pltpu.VMEM((steps, 2 * tok, 2 * HD), F32),
            pltpu.VMEM((steps, tok, 2 * HD), F32),
            pltpu.VMEM((steps, tok, 2 * HD), F32),
            pltpu.VMEM((steps, tok, 4 * HD), BF16),
            dma((KV,)),
            dma((steps,)),
            dma((steps,)),
            dma((steps,)),
            dma((steps,)),
            dma((KV,)),
        ],
        compiler_params=pltpu.CompilerParams(
            collective_id=1, has_side_effects=True, vmem_limit_bytes=VMEM_LIMIT
        ),
        name="attention_backward",
    )(d_o, kv, kvt, q_two, out_t, stat, cos_all, sin_all)


D = 1024
HIGH = lax.Precision.HIGHEST


def rope_tables(positions):
    half = HD // 2
    freq = jnp.exp(-math.log(10000.0) * jnp.arange(half, dtype=jnp.float32) * 2.0 / HD)
    angle = positions.astype(jnp.float32)[:, None] * freq[None, :]
    cosine = jnp.concatenate([jnp.cos(angle), jnp.cos(angle)], -1)
    sine = jnp.concatenate([jnp.sin(angle), jnp.sin(angle)], -1)
    return (cosine, sine)


def rotate_half(v):
    half = v.shape[-1] // 2
    return jnp.concatenate([-v[..., half:], v[..., :half]], -1)


def rotary(v, cosine, sine):
    return v * cosine[:, None, :] + rotate_half(v) * sine[:, None, :]


def unrotary(v, cosine, sine):
    return v * cosine[:, None, :] - rotate_half(v) * sine[:, None, :]


def rms_scale(v):
    return lax.rsqrt(jnp.mean(v * v, -1, keepdims=True) + EPS)


def rms_back(inputs, scale_rows, gain, grad):
    scaled = grad * gain
    d_inputs = scale_rows * scaled - inputs * scale_rows**3 * jnp.mean(
        scaled * inputs, -1, keepdims=True
    )
    return (d_inputs, jnp.sum(grad * inputs * scale_rows, 0))


def scores(queries, keys):
    return jnp.einsum("qkgd,skd->kgqs", queries, keys, preferred_element_type=jnp.float32) * HD ** (
        -0.5
    )


def per_device_plain(
    tokens,
    segments,
    routes,
    route_weight,
    norm1_gain,
    w_query,
    w_key,
    w_value,
    w_out,
    norm2_gain,
    w_router,
    w_gate,
    w_up,
    w_down,
    cotangent,
):
    f32 = jnp.float32
    bf16 = jnp.bfloat16
    scale = HD ** (-0.5)
    group = H // KV
    xs = tokens[0].astype(f32)
    tok = xs.shape[0]
    blocks = lax.axis_size("blk")
    length = tok * blocks
    first = lax.axis_index("blk") * tok
    last = first + tok - 1
    positions = first + jnp.arange(tok, dtype=jnp.int32)
    cosine, sine = rope_tables(positions)
    scale1 = rms_scale(xs)
    xa = (xs * scale1 * norm1_gain).astype(bf16)
    query = jnp.dot(xa, w_query, preferred_element_type=f32)
    key = jnp.dot(xa, w_key, preferred_element_type=f32)
    value = jnp.dot(xa, w_value, preferred_element_type=f32).astype(bf16)
    q_rot = rotary(query.reshape(tok, H, HD), cosine, sine).astype(bf16).reshape(tok, KV, group, HD)
    k_rot = rotary(key.reshape(tok, KV, HD), cosine, sine).astype(bf16).reshape(tok, KV * HD)
    seg_float = segments[0].astype(bf16)
    k_all, v_all, seg_all = (
        lax.all_gather(k_rot, "blk", axis=0, tiled=True),
        lax.all_gather(value, "blk", axis=0, tiled=True),
        lax.all_gather(seg_float, "blk", axis=0, tiled=True),
    )
    kblk = min(512, length)
    nblk = length // kblk
    k_blocks = k_all.reshape(nblk, kblk, KV, HD)
    v_blocks = v_all.reshape(nblk, kblk, KV, HD)
    s_blocks = seg_all.reshape(nblk, kblk)
    starts = jnp.arange(nblk, dtype=jnp.int32) * kblk

    def visible(kseg, kstart):
        kpos = kstart + jnp.arange(kblk, dtype=jnp.int32)
        return ((seg_float[:, None] == kseg[None, :]) & (kpos[None, :] <= positions[:, None]))[
            None, None
        ]

    def forward_step(carry, block):
        kb, vb, sb, start = block

        def forward_compute(state):
            running, total, acc = state
            mask = visible(sb, start)
            score = jnp.where(mask, scores(q_rot, kb), NEG)
            newmax = jnp.maximum(running, jnp.max(score, -1))
            expo = jnp.where(mask, jnp.exp(score - newmax[..., None]), 0.0)
            factor = jnp.exp(running - newmax)
            total = total * factor + jnp.sum(expo, -1)
            acc = acc * factor[..., None] + jnp.einsum(
                "kgqs,skd->kgqd", expo.astype(bf16), vb, preferred_element_type=f32
            )
            return (newmax, total, acc)

        return (lax.cond(start <= last, forward_compute, lambda state: state, carry), None)

    init = (
        jnp.full((KV, group, tok), NEG, f32),
        jnp.zeros((KV, group, tok), f32),
        jnp.zeros((KV, group, tok, HD), f32),
    )
    (running, total, acc), unused = lax.scan(
        forward_step, init, (k_blocks, v_blocks, s_blocks, starts)
    )
    lse = running + jnp.log(total)
    o_rows = (acc / total[..., None]).transpose(2, 0, 1, 3)
    att_low = o_rows.reshape(tok, H * HD).astype(bf16)
    h1 = xs + jnp.dot(att_low, w_out, preferred_element_type=f32)
    scale2 = rms_scale(h1)
    xl = (h1 * scale2 * norm2_gain).astype(bf16)
    logits = jnp.dot(xl, w_router, preferred_element_type=f32)
    experts = logits.shape[1]
    route = routes[0]
    rweight = route_weight[0]
    chooser = (route[:, :, None] == jnp.arange(experts, dtype=jnp.int32)[None, None, :]).astype(f32)
    chosen = jnp.sum(chooser * logits[:, None, :], -1)
    gates = jax.nn.softmax(chosen, -1)
    combine = (rweight * gates).astype(bf16)
    cap = min(tok, 2 * tok * TOP // experts)
    member = jnp.sum(chooser, 1)
    before = jnp.asarray(np.tril(np.ones((tok, tok), np.float32), -1))
    order = jnp.dot(before, member, precision=HIGH)
    rank = jnp.sum(chooser * order[:, None, :], -1).astype(jnp.int32)
    slots = route * cap + rank
    placed = jnp.any(
        slots[:, :, None] == jnp.arange(experts * cap, dtype=jnp.int32)[None, None, :], 1
    ).astype(bf16)
    outgoing = jnp.einsum("ts,td->sd", placed, xl, preferred_element_type=f32).astype(bf16)
    incoming = lax.all_to_all(
        outgoing.reshape(experts, cap, D), "blk", split_axis=0, concat_axis=0, tiled=True
    )
    local_exp = w_gate.shape[0]
    incoming = incoming.reshape(blocks, local_exp, cap, D)
    gate_pre = jnp.einsum("necd,edf->necf", incoming, w_gate, preferred_element_type=f32)
    up_pre = jnp.einsum("necd,edf->necf", incoming, w_up, preferred_element_type=f32)
    sigma = jax.nn.sigmoid(gate_pre)
    activated = gate_pre * sigma
    hidden = (activated * up_pre).astype(bf16)
    expert_out = jnp.einsum("necf,efd->necd", hidden, w_down, preferred_element_type=f32).astype(
        bf16
    )
    returned = lax.all_to_all(
        expert_out.reshape(experts, cap, D), "blk", split_axis=0, concat_axis=0, tiled=True
    )
    per_route = jnp.take(returned.reshape(experts * cap, D), slots.reshape(-1), axis=0).reshape(
        tok, TOP, D
    )
    mixture = jnp.einsum("tj,tjd->td", combine, per_route, preferred_element_type=f32)
    result = h1 + mixture
    grad_out = cotangent[0].astype(f32)
    grad_combine = jnp.einsum("td,tjd->tj", grad_out, per_route.astype(f32), precision=HIGH)
    route_grads = (combine.astype(f32)[:, :, None] * grad_out[:, None, :]).astype(bf16)
    grad_slots = (
        jnp.zeros((experts * cap, D), bf16)
        .at[slots.reshape(-1)]
        .set(route_grads.reshape(tok * TOP, D))
    )
    grad_incoming = lax.all_to_all(
        grad_slots.reshape(experts, cap, D), "blk", split_axis=0, concat_axis=0, tiled=True
    )
    grad_incoming = grad_incoming.reshape(blocks, local_exp, cap, D)
    grad_hidden = jnp.einsum("necd,efd->necf", grad_incoming, w_down, preferred_element_type=f32)
    grad_gate = (grad_hidden * up_pre * sigma * (1.0 + gate_pre * (1.0 - sigma))).astype(bf16)
    grad_up = (grad_hidden * activated).astype(bf16)
    d_down = jnp.einsum("necf,necd->efd", hidden, grad_incoming, preferred_element_type=f32)
    d_gate_w = jnp.einsum("necd,necf->edf", incoming, grad_gate, preferred_element_type=f32)
    d_up_w = jnp.einsum("necd,necf->edf", incoming, grad_up, preferred_element_type=f32)
    grad_in = (
        jnp.einsum("necf,edf->necd", grad_gate, w_gate, preferred_element_type=f32)
        + jnp.einsum("necf,edf->necd", grad_up, w_up, preferred_element_type=f32)
    ).astype(bf16)
    grad_back = lax.all_to_all(
        grad_in.reshape(experts, cap, D), "blk", split_axis=0, concat_axis=0, tiled=True
    )
    grad_xl = jnp.einsum(
        "ts,sd->td", placed, grad_back.reshape(experts * cap, D), preferred_element_type=f32
    )
    grad_gates = rweight * grad_combine
    grad_chosen = gates * (grad_gates - jnp.sum(gates * grad_gates, -1, keepdims=True))
    grad_logits = jnp.sum(chooser * grad_chosen[:, :, None], 1).astype(bf16)
    d_router = jnp.einsum("td,te->de", xl, grad_logits, preferred_element_type=f32)
    grad_xl = grad_xl + jnp.einsum("te,de->td", grad_logits, w_router, preferred_element_type=f32)
    grad_h1_norm, d_gain2 = rms_back(h1, scale2, norm2_gain, grad_xl)
    grad_h1 = grad_out + grad_h1_norm
    grad_att = grad_h1.astype(bf16)
    d_out_w = jnp.einsum("ti,td->id", att_low, grad_att, preferred_element_type=f32)
    grad_o = jnp.einsum("td,id->ti", grad_att, w_out, preferred_element_type=f32).astype(bf16)
    grad_o_rows = grad_o.reshape(tok, KV, group, HD)
    delta = jnp.einsum("qkgd,qkgd->kgq", grad_o_rows.astype(f32), o_rows)

    def query_terms(kb, vb, sb, start):
        mask = visible(sb, start)
        prob = jnp.where(mask, jnp.exp(scores(q_rot, kb) - lse[..., None]), 0.0)
        dprob = jnp.einsum("qkgd,skd->kgqs", grad_o_rows, vb, preferred_element_type=f32)
        dscore = (prob * (dprob - delta[..., None])).astype(bf16)
        dq_term = jnp.einsum("kgqs,skd->qkgd", dscore, kb, preferred_element_type=f32) * scale
        return (dq_term, dscore, prob)

    zero_q = jnp.zeros((tok, KV, group, HD), f32)

    def backward_step(grad_q, block):
        kb, vb, sb, start = block

        def backward_compute(acc_q):
            dq_term, dscore, prob = query_terms(kb, vb, sb, start)
            gk = jnp.einsum("kgqs,qkgd->skd", dscore, q_rot, preferred_element_type=f32) * scale
            gv = jnp.einsum(
                "kgqs,qkgd->skd", prob.astype(bf16), grad_o_rows, preferred_element_type=f32
            )
            return (acc_q + dq_term, (gk.reshape(kblk, KV * HD), gv.reshape(kblk, KV * HD)))

        def skip(acc_q):
            empty = jnp.zeros((kblk, KV * HD), f32)
            return (acc_q, (empty, empty))

        return lax.cond(start <= last, backward_compute, skip, grad_q)

    grad_q, (gk_blocks, gv_blocks) = lax.scan(
        backward_step, zero_q, (k_blocks, v_blocks, s_blocks, starts)
    )
    grad_k, grad_v = (
        lax.psum_scatter(
            gk_blocks.reshape(length, KV * HD).astype(jnp.bfloat16),
            "blk",
            scatter_dimension=0,
            tiled=True,
        ).astype(jnp.float32),
        lax.psum_scatter(
            gv_blocks.reshape(length, KV * HD).astype(jnp.bfloat16),
            "blk",
            scatter_dimension=0,
            tiled=True,
        ).astype(jnp.float32),
    )
    grad_qr = unrotary(grad_q.reshape(tok, H, HD), cosine, sine).reshape(tok, H * HD).astype(bf16)
    grad_kr = unrotary(grad_k.reshape(tok, KV, HD), cosine, sine).reshape(tok, KV * HD).astype(bf16)
    grad_vr = grad_v.astype(bf16)
    d_query = jnp.einsum("td,te->de", xa, grad_qr, preferred_element_type=f32)
    d_key = jnp.einsum("td,te->de", xa, grad_kr, preferred_element_type=f32)
    d_value = jnp.einsum("td,te->de", xa, grad_vr, preferred_element_type=f32)
    grad_xa = (
        jnp.einsum("te,de->td", grad_qr, w_query, preferred_element_type=f32)
        + jnp.einsum("te,de->td", grad_kr, w_key, preferred_element_type=f32)
        + jnp.einsum("te,de->td", grad_vr, w_value, preferred_element_type=f32)
    )
    grad_x_norm, d_gain1 = rms_back(xs, scale1, norm1_gain, grad_xa)
    grad_x = grad_h1 + grad_x_norm
    summed = lax.psum(
        (d_gain1, d_query, d_key, d_value, d_out_w, d_gain2, d_router), ("seq", "blk")
    )
    expert_summed = (
        lax.psum(d_gate_w.astype(jnp.bfloat16), "seq").astype(jnp.float32),
        lax.psum(d_up_w.astype(jnp.bfloat16), "seq").astype(jnp.float32),
        lax.psum(d_down.astype(jnp.bfloat16), "seq").astype(jnp.float32),
    )
    return (
        result.astype(bf16)[None],
        grad_x[None],
        summed[0],
        summed[1],
        summed[2],
        summed[3],
        summed[4],
        summed[5],
        summed[6],
        expert_summed[0],
        expert_summed[1],
        expert_summed[2],
    )


def by_head(w_query, w_key, w_value):
    d = w_query.shape[0]
    return jnp.concatenate(
        [w_query.reshape(d, KV, 2 * HD), w_key.reshape(d, KV, HD), w_value.reshape(d, KV, HD)], -1
    ).reshape(d, KV * 4 * HD)


def tables(length):
    half = HD // 2
    freq = np.exp(-math.log(10000.0) * np.arange(half, dtype=np.float32) * 2.0 / HD).astype(np.float32)
    angle = np.arange(length, dtype=np.float32)[:, None] * freq[None, :]
    return np.tile(np.cos(angle), (1, 4)), np.tile(np.sin(angle), (1, 4))


def per_device(
    tokens,
    segments,
    routes,
    route_weight,
    norm1_gain,
    w_query,
    w_key,
    w_value,
    w_out,
    norm2_gain,
    w_router,
    w_gate,
    w_up,
    w_down,
    cotangent,
):
    f32 = jnp.float32
    bf16 = jnp.bfloat16
    scale = HD ** (-0.5)
    xs = tokens[0].astype(f32)
    tok = xs.shape[0]
    blocks = lax.axis_size("blk")
    length = tok * blocks
    cos_np, sin_np = tables(length)
    cos_all = jnp.asarray(cos_np.reshape(blocks, tok, 2 * HD))
    sin_all = jnp.asarray(sin_np.reshape(blocks, tok, 2 * HD))
    me = lax.axis_index("blk")
    cosine = lax.dynamic_index_in_dim(cos_all, me, 0, keepdims=False)[:, None, :]
    sine = lax.dynamic_index_in_dim(sin_all, me, 0, keepdims=False)[:, None, :]
    scale1 = rms_scale(xs)
    xa = (xs * scale1 * norm1_gain).astype(bf16)
    w_all = by_head(w_query, w_key, w_value)
    qkv = jnp.dot(xa, w_all, preferred_element_type=f32).reshape(tok, KV, 4 * HD)

    def turned(u):
        parts = u.reshape(tok, KV, -1, HD)
        return (
            parts * cosine[:, :, None, :HD] + rotate_half(parts) * sine[:, :, None, :HD]
        ).reshape(u.shape)

    pay = jnp.concatenate(
        [turned(qkv[..., : 2 * HD]) * scale, turned(qkv[..., 2 * HD : 3 * HD]), qkv[..., 3 * HD :]], -1
    ).astype(bf16)
    seg = jnp.zeros((16, 4 * HD), bf16).at[:2, 2 * HD :].set(
        segments[0].astype(bf16).reshape(2, tok // 2)
    )
    pay = jnp.concatenate(
        [pay.transpose(1, 0, 2), jnp.broadcast_to(seg[None], (KV, 16, 4 * HD))], 1
    )
    att_low, *kept = attention_forward(blocks, pay)
    h1 = xs + jnp.dot(att_low, w_out, preferred_element_type=f32)
    scale2 = rms_scale(h1)
    xl = (h1 * scale2 * norm2_gain).astype(bf16)
    logits = jnp.dot(xl, w_router, preferred_element_type=f32)
    experts = logits.shape[1]
    route = routes[0]
    rweight = route_weight[0]
    chooser = (route[:, :, None] == jnp.arange(experts, dtype=jnp.int32)[None, None, :]).astype(f32)
    chosen = jnp.sum(chooser * logits[:, None, :], -1)
    gates = jax.nn.softmax(chosen, -1)
    combine = (rweight * gates).astype(bf16)
    cap = min(tok, 2 * tok * TOP // experts)
    member = jnp.sum(chooser, 1)
    before = jnp.asarray(np.tril(np.ones((tok, tok), np.float32), -1))
    order = jnp.dot(before, member, precision=HIGH)
    rank = jnp.sum(chooser * order[:, None, :], -1).astype(jnp.int32)
    slots = route * cap + rank
    placed = jnp.any(
        slots[:, :, None] == jnp.arange(experts * cap, dtype=jnp.int32)[None, None, :], 1
    ).astype(bf16)
    outgoing = jnp.einsum("ts,td->sd", placed, xl, preferred_element_type=f32).astype(bf16)
    incoming = lax.all_to_all(
        outgoing.reshape(experts, cap, D), "blk", split_axis=0, concat_axis=0, tiled=True
    )
    local_exp = w_gate.shape[0]
    incoming = incoming.reshape(blocks, local_exp, cap, D)
    gate_pre = jnp.einsum("necd,edf->necf", incoming, w_gate, preferred_element_type=f32)
    up_pre = jnp.einsum("necd,edf->necf", incoming, w_up, preferred_element_type=f32)
    sigma = jax.nn.sigmoid(gate_pre)
    activated = gate_pre * sigma
    hidden = (activated * up_pre).astype(bf16)
    expert_out = jnp.einsum("necf,efd->necd", hidden, w_down, preferred_element_type=f32).astype(
        bf16
    )
    returned = lax.all_to_all(
        expert_out.reshape(experts, cap, D), "blk", split_axis=0, concat_axis=0, tiled=True
    )
    per_route = jnp.take(returned.reshape(experts * cap, D), slots.reshape(-1), axis=0).reshape(
        tok, TOP, D
    )
    mixture = jnp.einsum("tj,tjd->td", combine, per_route, preferred_element_type=f32)
    result = h1 + mixture
    grad_out = cotangent[0].astype(f32)
    grad_combine = jnp.einsum("td,tjd->tj", grad_out, per_route.astype(f32), precision=HIGH)
    route_grads = (combine.astype(f32)[:, :, None] * grad_out[:, None, :]).astype(bf16)
    grad_slots = (
        jnp.zeros((experts * cap, D), bf16)
        .at[slots.reshape(-1)]
        .set(route_grads.reshape(tok * TOP, D))
    )
    grad_incoming = lax.all_to_all(
        grad_slots.reshape(experts, cap, D), "blk", split_axis=0, concat_axis=0, tiled=True
    )
    grad_incoming = grad_incoming.reshape(blocks, local_exp, cap, D)
    grad_hidden = jnp.einsum("necd,efd->necf", grad_incoming, w_down, preferred_element_type=f32)
    grad_gate = (grad_hidden * up_pre * sigma * (1.0 + gate_pre * (1.0 - sigma))).astype(bf16)
    grad_up = (grad_hidden * activated).astype(bf16)
    d_down = jnp.einsum("necf,necd->efd", hidden, grad_incoming, preferred_element_type=f32)
    d_gate_w = jnp.einsum("necd,necf->edf", incoming, grad_gate, preferred_element_type=f32)
    d_up_w = jnp.einsum("necd,necf->edf", incoming, grad_up, preferred_element_type=f32)
    grad_in = (
        jnp.einsum("necf,edf->necd", grad_gate, w_gate, preferred_element_type=f32)
        + jnp.einsum("necf,edf->necd", grad_up, w_up, preferred_element_type=f32)
    ).astype(bf16)
    grad_back = lax.all_to_all(
        grad_in.reshape(experts, cap, D), "blk", split_axis=0, concat_axis=0, tiled=True
    )
    grad_xl = jnp.einsum(
        "ts,sd->td", placed, grad_back.reshape(experts * cap, D), preferred_element_type=f32
    )
    grad_gates = rweight * grad_combine
    grad_chosen = gates * (grad_gates - jnp.sum(gates * grad_gates, -1, keepdims=True))
    grad_logits = jnp.sum(chooser * grad_chosen[:, :, None], 1).astype(bf16)
    d_router = jnp.einsum("td,te->de", xl, grad_logits, preferred_element_type=f32)
    grad_xl = grad_xl + jnp.einsum("te,de->td", grad_logits, w_router, preferred_element_type=f32)
    grad_h1_norm, d_gain2 = rms_back(h1, scale2, norm2_gain, grad_xl)
    grad_h1 = grad_out + grad_h1_norm
    grad_att = grad_h1.astype(bf16)
    d_out_w = jnp.einsum("ti,td->id", att_low, grad_att, preferred_element_type=f32)
    grad_o = jnp.einsum("td,id->ti", grad_att, w_out, preferred_element_type=f32).astype(bf16)
    got = attention_backward(blocks, grad_o, *kept, cos_all, sin_all)
    grad_all = got.transpose(1, 0, 2).reshape(tok, KV * 4 * HD)
    d_all = jnp.einsum("td,te->de", xa, grad_all, preferred_element_type=f32)
    grad_xa = jnp.einsum("te,de->td", grad_all, w_all, preferred_element_type=f32)
    d_model = d_all.shape[0]
    d_heads = d_all.reshape(d_model, KV, 4 * HD)
    d_query = d_heads[..., : 2 * HD].reshape(d_model, H * HD)
    d_key = d_heads[..., 2 * HD : 3 * HD].reshape(d_model, KV * HD)
    d_value = d_heads[..., 3 * HD :].reshape(d_model, KV * HD)
    grad_x_norm, d_gain1 = rms_back(xs, scale1, norm1_gain, grad_xa)
    grad_x = grad_h1 + grad_x_norm
    summed = lax.psum(
        (d_gain1, d_query, d_key, d_value, d_out_w, d_gain2, d_router), ("seq", "blk")
    )
    expert_summed = (
        lax.psum(d_gate_w.astype(jnp.bfloat16), "seq").astype(jnp.float32),
        lax.psum(d_up_w.astype(jnp.bfloat16), "seq").astype(jnp.float32),
        lax.psum(d_down.astype(jnp.bfloat16), "seq").astype(jnp.float32),
    )
    return (
        result.astype(bf16)[None],
        grad_x[None],
        summed[0],
        summed[1],
        summed[2],
        summed[3],
        summed[4],
        summed[5],
        summed[6],
        expert_summed[0],
        expert_summed[1],
        expert_summed[2],
    )


def solution(mesh):
    fused = dict(mesh.shape) == {"seq": 2, "blk": 2 * KV}
    return jax.shard_map(
        per_device if fused else per_device_plain,
        mesh=mesh,
        in_specs=(
            P("seq", "blk", None),
            P("seq", "blk"),
            P("seq", "blk", None),
            P("seq", "blk", None),
            P(),
            P(),
            P(),
            P(),
            P(),
            P(),
            P(),
            P("blk", None, None),
            P("blk", None, None),
            P("blk", None, None),
            P("seq", "blk", None),
        ),
        out_specs=(
            P("seq", "blk", None),
            P("seq", "blk", None),
            P(),
            P(),
            P(),
            P(),
            P(),
            P(),
            P(),
            P("blk", None, None),
            P("blk", None, None),
            P("blk", None, None),
        ),
        check_vma=False,
    )
```

```python
import functools
import math

import jax
import jax.numpy as jnp
import numpy as np
from jax import lax
from jax.experimental import pallas as pl
from jax.experimental.pallas import tpu as pltpu
from jax.sharding import PartitionSpec as P

H = 16
KV = 8
HD = 64
TOP = 8
EPS = 1e-06
NEG = -1e30
F32 = jnp.float32
BF16 = jnp.bfloat16
MESH = pl.DeviceIdType.MESH
VMEM_LIMIT = 60 * 2**20
NT = (((1,), (1,)), ((), ()))
TN = (((0,), (0,)), ((), ()))


def mm(a, b, dims=(((1,), (0,)), ((), ()))):
    return lax.dot_general(a, b, dims, preferred_element_type=F32)


def remote(src, dst, send, recv, seq, blk):
    return pltpu.make_async_remote_copy(
        src_ref=src,
        dst_ref=dst,
        send_sem=send,
        recv_sem=recv,
        device_id=(seq, blk),
        device_id_type=MESH,
    )


def greet_all(seqs, blocks, me_s, me_b):
    barrier = pltpu.get_barrier_semaphore()
    total = seqs * blocks

    def hello(n, carry):
        other = lax.rem(me_s * blocks + me_b + n, total)
        pl.semaphore_signal(
            barrier,
            inc=1,
            device_id=(other // blocks, lax.rem(other, blocks)),
            device_id_type=MESH,
        )
        return carry

    lax.fori_loop(1, total, hello, 0)
    pl.semaphore_wait(barrier, total - 1)


def flip(place, n):
    if n == 1:
        return place + 1 - 2 * lax.rem(place, 2)
    if n == 2:
        return place + 2 - 4 * (place // 2)
    return 3 - place


def rotate_pairs(u):
    lanes = u.shape[-1]
    half = HD // 2
    lane = lax.broadcasted_iota(jnp.int32, u.shape, u.ndim - 1)
    ahead = pltpu.roll(u, lanes - half, u.ndim - 1)
    behind = pltpu.roll(u, half, u.ndim - 1)
    return jnp.where(lane % HD < half, -ahead, behind)


def stacked_heads(wide):
    return jnp.concatenate([wide[:HD], wide[HD:]], axis=1)


def attention_forward_kernel(
    blocks,
    pay,
    g_ref,
    wg_ref,
    wu_ref,
    wd_ref,
    o_ref,
    kv_ref,
    kvt_ref,
    q_ref,
    ot_ref,
    stat_ref,
    g_all,
    wg_all,
    wu_all,
    wd_all,
    in_ref,
    other_ref,
    obuf,
    cnt,
    send_sem,
    recv_sem,
    fsend_sem,
    frecv_sem,
    osend_sem,
    orecv_sem,
    gsend_sem,
    grecv_sem,
    wsend_sem,
    wrecv_sem,
    hsend_sem,
    hrecv_sem,
):
    me_s = lax.axis_index("seq")
    me_b = lax.axis_index("blk")
    tok = q_ref.shape[1]
    steps = blocks // 2
    sigma = me_b // KV
    kappa = lax.rem(me_b, KV)
    greet_all(2, blocks, me_s, me_b)

    dest_core = lax.rem(me_b, 2)
    slot = me_b // 2
    line, plane = me_b // 4, lax.rem(me_b, 4)
    weights = ((wg_ref, wg_all), (wu_ref, wu_all), (wd_ref, wd_all))

    def share_grad(n):
        return remote(
            g_ref,
            g_all.at[line],
            gsend_sem.at[n - 1],
            grecv_sem.at[n - 1],
            me_s,
            flip(line, n) * 4 + plane,
        )

    def half(ref):
        rows = ref.shape[0] // 2
        return ref.at[pl.ds(pl.multiple_of(me_s * rows, rows), rows)]

    def share_weight(n, i):
        own, everyone = weights[i]
        return remote(
            half(own),
            half(everyone.at[plane]),
            wsend_sem.at[n - 1, i],
            wrecv_sem.at[n - 1, i],
            me_s,
            line * 4 + flip(plane, n),
        )

    def pass_weight(n, i):
        arrived = half(weights[i][1].at[flip(plane, n)])
        return remote(
            arrived, arrived, hsend_sem.at[n - 1, i], hrecv_sem.at[n - 1, i], 1 - me_s, me_b
        )

    def payload(n):
        k = lax.rem(me_b + n, KV)
        chip = me_s * KV + k
        mine = (dest_core == me_s) & (chip == me_b)
        return k, chip, mine

    def send_payload(n, carry):
        k, chip, mine = payload(n)

        @pl.when(mine)
        def _():
            pltpu.make_async_copy(pay.at[k], in_ref.at[slot], recv_sem.at[slot]).start()

        @pl.when(jnp.logical_not(mine))
        def _():
            remote(
                pay.at[k], in_ref.at[slot], send_sem.at[k], recv_sem.at[slot], dest_core, chip
            ).start()

        return carry

    lax.fori_loop(0, KV, send_payload, 0)
    for n in (1, 2, 3):
        share_grad(n).start()
        for i in range(3):
            share_weight(n, i).start()

    def arrival(t):
        return pltpu.make_async_copy(pay.at[0], in_ref.at[t], recv_sem.at[t])

    def forward(t):
        return remote(
            in_ref.at[t, :, pl.ds(2 * HD, 2 * HD)],
            other_ref.at[t],
            fsend_sem.at[t],
            frecv_sem.at[t],
            1 - me_s,
            me_b,
        )

    arrival(0).wait()
    forward(0).start()
    cnt[...] = jnp.zeros_like(cnt)
    first_core = me_s == 0
    lane = lax.broadcasted_iota(jnp.int32, (1, 2 * tok), 1)
    qrow = jnp.where(lane < tok, lane, lane - tok)
    wide = 2 * tok

    def step(t, carry):
        @pl.when(t < steps - 1)
        def _():
            arrival(t + 1).wait()
            forward(t + 1).start()

        forward(t).wait_recv()
        mine = in_ref[t]
        kv_mine, seg_mine = mine[:tok, 2 * HD :], mine[tok:, 2 * HD :].astype(F32)
        other = other_ref[t]
        kv_other, seg_other = other[:tok], other[tok:].astype(F32)
        pair = jnp.where(
            first_core,
            jnp.concatenate([kv_mine, kv_other], 0).astype(F32),
            jnp.concatenate([kv_other, kv_mine], 0).astype(F32),
        )
        kv_ref[t] = pair.astype(BF16)
        kvt_ref[t] = jnp.transpose(pair).astype(BF16)
        number = lax.broadcasted_iota(jnp.int32, (8, tok), 0).astype(F32)
        seg_q = jnp.concatenate([seg_mine[0:1], seg_mine[1:2]], 1)
        seg_o = jnp.concatenate([seg_other[0:1], seg_other[1:2]], 1)
        below = (seg_q < number).astype(F32) + (seg_o < number).astype(F32)
        cnt[...] += jnp.sum(below, 1, keepdims=True)
        start_q = jnp.sum(jnp.where(seg_q == number, cnt[:, :1], 0.0), 0, keepdims=True)
        start = jnp.concatenate([start_q, start_q], 1).astype(jnp.int32)
        q_two = mine[:tok, : 2 * HD]
        q_ref[t] = q_two
        qt = stacked_heads(jnp.transpose(q_two.astype(F32)))
        qm = jnp.concatenate([qt, jnp.zeros_like(qt)], 0).astype(BF16)
        qpos = (2 * t + me_s) * tok + qrow

        def piece(u, state, last):
            running, total, acc = state
            score = mm(kv_ref[u], qm)
            kpos = u * wide + lax.broadcasted_iota(jnp.int32, score.shape, 0)
            mask = kpos >= start
            if last:
                mask &= kpos <= qpos
            score = jnp.where(mask, score, NEG)
            newmax = jnp.maximum(running, jnp.max(score, 0, keepdims=True))
            expo = jnp.exp(score - newmax)
            factor = jnp.exp(running - newmax)
            total = total * factor + jnp.sum(expo, 0, keepdims=True)
            acc = acc * factor + mm(kvt_ref[u, HD:, :], expo.astype(BF16))
            return newmax, total, acc

        state = (
            jnp.full((1, wide), NEG, F32),
            jnp.zeros((1, wide), F32),
            jnp.zeros((HD, wide), F32),
        )
        state = lax.fori_loop(0, t, lambda u, s: piece(u, s, False), state)
        running, total, acc = piece(t, state, True)
        out_t = acc / total
        ot_ref[t] = out_t
        rows = lax.broadcasted_iota(jnp.int32, (8, wide), 0)
        lse = running + jnp.log(total)
        stat_ref[t] = jnp.where(rows == 0, lse, start.astype(F32))
        upright = jnp.concatenate([out_t[:, :tok], out_t[:, tok:]], 0)
        obuf[t] = jnp.transpose(upright).astype(BF16)
        owner = 2 * t + me_s
        home = (sigma == me_s) & (owner == me_b)
        place = o_ref.at[:, pl.ds(pl.multiple_of(kappa * 2 * HD, 2 * HD), 2 * HD)]

        @pl.when(home)
        def _():
            pltpu.make_async_copy(obuf.at[t], place, orecv_sem.at[kappa]).start()

        @pl.when(jnp.logical_not(home))
        def _():
            remote(obuf.at[t], place, osend_sem.at[t], orecv_sem.at[kappa], sigma, owner).start()

        return carry

    lax.fori_loop(0, steps, step, 0)
    for n in (1, 2, 3):
        for i in range(3):
            share_weight(n, i).wait_recv()
            pass_weight(n, i).start()

    def finish(t, carry):
        k, chip, mine = payload(t)

        @pl.when(jnp.logical_not(mine))
        def _():
            remote(
                pay.at[k], in_ref.at[slot], send_sem.at[k], recv_sem.at[slot], dest_core, chip
            ).wait_send()

        return carry

    lax.fori_loop(0, KV, finish, 0)

    def finish_steps(t, carry):
        forward(t).wait_send()
        owner = 2 * t + me_s
        home = (sigma == me_s) & (owner == me_b)

        @pl.when(jnp.logical_not(home))
        def _():
            remote(
                obuf.at[t],
                o_ref.at[:, pl.ds(0, 2 * HD)],
                osend_sem.at[t],
                orecv_sem.at[0],
                sigma,
                owner,
            ).wait_send()

        return carry

    lax.fori_loop(0, steps, finish_steps, 0)

    def gather(k, carry):
        pltpu.make_async_copy(
            obuf.at[0],
            o_ref.at[:, pl.ds(pl.multiple_of(k * 2 * HD, 2 * HD), 2 * HD)],
            orecv_sem.at[k],
        ).wait()
        return carry

    lax.fori_loop(0, KV, gather, 0)
    for n in (1, 2, 3):
        share_grad(n).wait()
        for i in range(3):
            share_weight(n, i).wait_send()
            pass_weight(n, i).wait()


def attention_forward(blocks, pay, g, w_gate, w_up, w_down):
    tok = pay.shape[2]
    steps = blocks // 2
    vm = pl.BlockSpec(memory_space=pltpu.VMEM)
    hbm = pl.BlockSpec(memory_space=pl.ANY)
    dma = pltpu.SemaphoreType.DMA
    return pl.pallas_call(
        functools.partial(attention_forward_kernel, blocks),
        out_shape=(
            jax.ShapeDtypeStruct((tok, H * HD), BF16),
            jax.ShapeDtypeStruct((steps, 2 * tok, 2 * HD), BF16),
            jax.ShapeDtypeStruct((steps, 2 * HD, 2 * tok), BF16),
            jax.ShapeDtypeStruct((steps, tok, 2 * HD), BF16),
            jax.ShapeDtypeStruct((steps, HD, 2 * tok), F32),
            jax.ShapeDtypeStruct((steps, 8, 2 * tok), F32),
            jax.ShapeDtypeStruct((4, *g.shape), BF16),
            jax.ShapeDtypeStruct((4, *w_gate.shape), BF16),
            jax.ShapeDtypeStruct((4, *w_up.shape), BF16),
            jax.ShapeDtypeStruct((4, *w_down.shape), BF16),
        ),
        in_specs=[vm] + [hbm] * 4,
        out_specs=(vm,) * 6 + (hbm,) * 4,
        scratch_shapes=[
            pltpu.VMEM((steps, tok + 16, 4 * HD), BF16),
            pltpu.VMEM((steps, tok + 16, 2 * HD), BF16),
            pltpu.VMEM((steps, tok, 2 * HD), BF16),
            pltpu.VMEM((8, 128), F32),
            dma((KV,)),
            dma((steps,)),
            dma((steps,)),
            dma((steps,)),
            dma((steps,)),
            dma((KV,)),
            dma((3,)),
            dma((3,)),
            dma((3, 3)),
            dma((3, 3)),
            dma((3, 3)),
            dma((3, 3)),
        ],
        compiler_params=pltpu.CompilerParams(
            collective_id=0, has_side_effects=True, vmem_limit_bytes=VMEM_LIMIT
        ),
        name="attention_forward",
    )(pay, g, w_gate, w_up, w_down)


def attention_backward_kernel(
    blocks,
    do_ref,
    kv_ref,
    kvt_ref,
    q_ref,
    ot_ref,
    stat_ref,
    cos_ref,
    sin_ref,
    mix_ref,
    dwg_ref,
    dwu_ref,
    dwd_ref,
    out_ref,
    mix_in,
    dwg_in,
    dwu_in,
    dwd_in,
    in_ref,
    dkv,
    part,
    xch,
    done,
    send_sem,
    recv_sem,
    xsend_sem,
    xrecv_sem,
    osend_sem,
    orecv_sem,
    msend_sem,
    mrecv_sem,
    wsend_sem,
    wrecv_sem,
):
    me_s = lax.axis_index("seq")
    me_b = lax.axis_index("blk")
    tok = q_ref.shape[1]
    steps = blocks // 2
    sigma = me_b // KV
    kappa = lax.rem(me_b, KV)
    greet_all(2, blocks, me_s, me_b)

    dest_core = lax.rem(me_b, 2)
    slot = me_b // 2
    line, plane = me_b // 4, lax.rem(me_b, 4)
    weights = ((dwg_ref, dwg_in), (dwu_ref, dwu_in), (dwd_ref, dwd_in))

    def give_mix(n):
        return remote(
            mix_ref.at[n - 1],
            mix_in.at[n - 1],
            msend_sem.at[n - 1],
            mrecv_sem.at[n - 1],
            me_s,
            flip(line, n) * 4 + plane,
        )

    def give_weight(n, i):
        src, dst = weights[i]
        return remote(
            src.at[flip(plane, n)],
            dst.at[n - 1],
            wsend_sem.at[n - 1, i],
            wrecv_sem.at[n - 1, i],
            me_s,
            line * 4 + flip(plane, n),
        )

    def outgoing(n):
        k = lax.rem(me_b + n, KV)
        chip = me_s * KV + k
        mine = (dest_core == me_s) & (chip == me_b)
        src = do_ref.at[:, pl.ds(pl.multiple_of(k * 2 * HD, 2 * HD), 2 * HD)]
        return k, chip, mine, src

    def send_grad(n, carry):
        k, chip, mine, src = outgoing(n)

        @pl.when(mine)
        def _():
            pltpu.make_async_copy(src, in_ref.at[slot], recv_sem.at[slot]).start()

        @pl.when(jnp.logical_not(mine))
        def _():
            remote(src, in_ref.at[slot], send_sem.at[k], recv_sem.at[slot], dest_core, chip).start()

        return carry

    lax.fori_loop(0, KV, send_grad, 0)
    for n in (1, 2, 3):
        give_mix(n).start()
        for i in range(3):
            give_weight(n, i).start()
    dkv[...] = jnp.zeros_like(dkv)
    wide = 2 * tok
    lane = lax.broadcasted_iota(jnp.int32, (1, wide), 1)
    qrow = jnp.where(lane < tok, lane, lane - tok)
    low = lax.broadcasted_iota(jnp.int32, (tok, 2 * HD), 1) < HD

    def swap(t):
        return remote(part.at[t], xch.at[t], xsend_sem.at[t], xrecv_sem.at[t], 1 - me_s, me_b)

    def deliver(t, act):
        owner = 2 * t + me_s
        home = (sigma == me_s) & (owner == me_b)
        src, dst = done.at[t], out_ref.at[kappa]

        @pl.when(home)
        def _():
            if act == "start":
                pltpu.make_async_copy(src, dst, orecv_sem.at[kappa]).start()

        @pl.when(jnp.logical_not(home))
        def _():
            copy = remote(src, dst, osend_sem.at[t], orecv_sem.at[kappa], sigma, owner)
            copy.start() if act == "start" else copy.wait_send()

    def finalize(t):
        swap(t).wait_recv()
        place = pl.ds(pl.multiple_of(me_s * tok, tok), tok)
        total = dkv[t, place, :] + xch[t]
        owner = 2 * t + me_s
        cosine = jnp.where(low, cos_ref[owner], 1.0)
        sine = jnp.where(low, sin_ref[owner], 0.0)
        back = total * cosine - rotate_pairs(total) * sine
        done[t, :, pl.ds(2 * HD, 2 * HD)] = back.astype(BF16)
        deliver(t, "start")

    def step(n, carry):
        t = steps - 1 - n
        pltpu.make_async_copy(do_ref.at[:, pl.ds(0, 2 * HD)], in_ref.at[t], recv_sem.at[t]).wait()
        d_two = in_ref[t].astype(F32)
        q_two = q_ref[t].astype(F32)
        dt = stacked_heads(jnp.transpose(d_two))
        qt = stacked_heads(jnp.transpose(q_two))
        zero = jnp.zeros_like(dt)
        dm = jnp.concatenate([zero, dt], 0).astype(BF16)
        qm = jnp.concatenate([qt, zero], 0).astype(BF16)
        delta = jnp.sum(ot_ref[t] * dt, 0, keepdims=True)
        right = jnp.concatenate(
            [
                jnp.where(low, q_two, 0.0),
                jnp.where(low, pltpu.roll(q_two, HD, 1), 0.0),
                jnp.where(low, 0.0, pltpu.roll(d_two, HD, 1)),
                jnp.where(low, 0.0, d_two),
            ],
            0,
        ).astype(BF16)
        stat = stat_ref[t]
        lse, start = stat[0:1], stat[1:2].astype(jnp.int32)
        qpos = (2 * t + me_s) * tok + qrow

        def piece(u, dq, last):
            keys = kv_ref[u]
            score = mm(keys, qm)
            kpos = u * wide + lax.broadcasted_iota(jnp.int32, score.shape, 0)
            mask = kpos >= start
            if last:
                mask &= kpos <= qpos
            prob = jnp.where(mask, jnp.exp(score - lse), 0.0)
            dprob = mm(keys, dm)
            dscore = (prob * (dprob - delta)).astype(BF16)
            both = jnp.concatenate([dscore, prob.astype(BF16)], 1)
            dkv[u] += mm(both, right)
            return dq + mm(kvt_ref[u, :HD, :], dscore)

        dq = jnp.zeros((HD, wide), F32)
        dq = lax.fori_loop(0, t, lambda u, s: piece(u, s, False), dq)
        dq = piece(t, dq, True) * HD ** (-0.5)
        upright = jnp.transpose(jnp.concatenate([dq[:, :tok], dq[:, tok:]], 0))
        owner = 2 * t + me_s
        back = upright * cos_ref[owner] - rotate_pairs(upright) * sin_ref[owner]
        done[t, :, pl.ds(0, 2 * HD)] = back.astype(BF16)
        part[t] = dkv[t, pl.ds(pl.multiple_of((1 - me_s) * tok, tok), tok), :]
        swap(t).start()

        @pl.when(n > 0)
        def _():
            finalize(t + 1)

        return carry

    lax.fori_loop(0, steps, step, 0)
    finalize(0)

    def finish(n, carry):
        k, chip, mine, src = outgoing(n)

        @pl.when(jnp.logical_not(mine))
        def _():
            remote(
                src, in_ref.at[slot], send_sem.at[k], recv_sem.at[slot], dest_core, chip
            ).wait_send()

        return carry

    lax.fori_loop(0, KV, finish, 0)

    def finish_steps(t, carry):
        swap(t).wait_send()
        deliver(t, "wait")
        return carry

    lax.fori_loop(0, steps, finish_steps, 0)

    def gather(k, carry):
        pltpu.make_async_copy(done.at[0], out_ref.at[k], orecv_sem.at[k]).wait()
        return carry

    lax.fori_loop(0, KV, gather, 0)
    for n in (1, 2, 3):
        give_mix(n).wait()
        for i in range(3):
            give_weight(n, i).wait()


def attention_backward(
    blocks, d_o, kv, kvt, q_two, out_t, stat, cos_all, sin_all, mix, dwg, dwu, dwd
):
    tok = q_two.shape[1]
    steps = blocks // 2
    vm = pl.BlockSpec(memory_space=pltpu.VMEM)
    hbm = pl.BlockSpec(memory_space=pl.ANY)
    dma = pltpu.SemaphoreType.DMA
    return pl.pallas_call(
        functools.partial(attention_backward_kernel, blocks),
        out_shape=(
            jax.ShapeDtypeStruct((KV, tok, 4 * HD), BF16),
            jax.ShapeDtypeStruct(mix.shape, BF16),
            jax.ShapeDtypeStruct((3, *dwg.shape[1:]), BF16),
            jax.ShapeDtypeStruct((3, *dwu.shape[1:]), BF16),
            jax.ShapeDtypeStruct((3, *dwd.shape[1:]), BF16),
        ),
        in_specs=[vm] * 8 + [hbm] * 4,
        out_specs=(vm,) + (hbm,) * 4,
        scratch_shapes=[
            pltpu.VMEM((steps, tok, 2 * HD), BF16),
            pltpu.VMEM((steps, 2 * tok, 2 * HD), F32),
            pltpu.VMEM((steps, tok, 2 * HD), F32),
            pltpu.VMEM((steps, tok, 2 * HD), F32),
            pltpu.VMEM((steps, tok, 4 * HD), BF16),
            dma((KV,)),
            dma((steps,)),
            dma((steps,)),
            dma((steps,)),
            dma((steps,)),
            dma((KV,)),
            dma((3,)),
            dma((3,)),
            dma((3, 3)),
            dma((3, 3)),
        ],
        compiler_params=pltpu.CompilerParams(
            collective_id=1, has_side_effects=True, vmem_limit_bytes=VMEM_LIMIT
        ),
        name="attention_backward",
    )(d_o, kv, kvt, q_two, out_t, stat, cos_all, sin_all, mix, dwg, dwu, dwd)


def mixture_kernel(
    x_ref,
    g_ref,
    wg_ref,
    wu_ref,
    wd_ref,
    g_all,
    wg_all,
    wu_all,
    wd_all,
    mix_own,
    mix_peer,
    d_in,
    dwg_out,
    dwu_out,
    dwd_out,
    x_in,
    x_t,
    g_in,
    wg,
    wu,
    wd,
    hc,
    dg,
    du,
    acc_o,
    acc_d,
    acc_c,
    d_send,
    d_recv,
    xg,
    xu,
    xd,
    load_sem,
    gload_sem,
    send_sem,
    recv_sem,
    bsend_sem,
    brecv_sem,
    psend_sem,
    precv_sem,
    store_sem,
):
    me_s = lax.axis_index("seq")
    me_b = lax.axis_index("blk")
    line, plane = me_b // 4, lax.rem(me_b, 4)
    tok, d = g_in.shape[1:]
    ff = wg.shape[2]
    barrier = pltpu.get_barrier_semaphore()
    places = [(me_s, flip(line, n) * 4 + plane) for n in (1, 2, 3)] + [(1 - me_s, me_b)]
    for place in places:
        pl.semaphore_signal(barrier, inc=1, device_id=place, device_id_type=MESH)

    owns = ((wg_ref, wg_all, wg), (wu_ref, wu_all, wu), (wd_ref, wd_all, wd))

    def load_own(i):
        return pltpu.make_async_copy(owns[i][0], owns[i][2].at[plane], load_sem.at[i, plane])

    def load_other(i, e):
        return pltpu.make_async_copy(owns[i][1].at[e], owns[i][2].at[e], load_sem.at[i, e])

    for i in range(3):
        load_own(i).start()
        for n in (1, 2, 3):
            load_other(i, flip(plane, n)).start()

    def load_grad(n):
        src = g_ref if n == 0 else g_all.at[flip(line, n)]
        return pltpu.make_async_copy(src, g_in.at[n], gload_sem.at[n])

    for n in range(4):
        load_grad(n).start()
    pl.semaphore_wait(barrier, 4)

    def spread(n):
        return remote(
            x_ref, x_in.at[n], send_sem.at[n - 1], recv_sem.at[n - 1], *places[n - 1]
        )

    for n in (1, 2, 3):
        spread(n).start()
    x_in[0] = x_ref[...]
    for n in range(4):
        load_grad(n).wait()

    def load_wait(e, carry):
        for i in range(3):
            load_other(i, e).wait()
        return carry

    lane = lax.broadcasted_iota(jnp.int32, (tok, 128), 1)

    def block(n, carry):
        @pl.when(n > 0)
        def _():
            pltpu.make_async_copy(x_ref, x_in.at[n], recv_sem.at[jnp.maximum(n - 1, 0)]).wait()

        acc_o[...] = jnp.zeros_like(acc_o)
        acc_d[...] = jnp.zeros_like(acc_d)
        acc_c[...] = jnp.zeros_like(acc_c)
        rows = pl.ds(pl.multiple_of(n * tok, tok), tok)

        def expert(e, carry):
            @pl.when(n == 0)
            def _():
                load_wait(e, 0)

            x = x_in[n, :, :d]
            here = lane == line * 4 + e
            share = jnp.sum(
                jnp.where(here, x_in[n, :, d:].astype(F32), 0.0), 1, keepdims=True
            )
            gate = mm(x, wg[e])
            up = mm(x, wu[e])
            dh = mm(g_in[n], wd[e], NT)
            sg = jax.nn.sigmoid(gate)
            act = gate * sg
            hidden = act * up
            acc_c[...] += jnp.where(here, jnp.sum(dh * hidden, 1, keepdims=True), 0.0)
            dh = dh * share
            hcb = (hidden * share).astype(BF16)
            dgb = (dh * up * sg * (1.0 + gate * (1.0 - sg))).astype(BF16)
            dub = (dh * act).astype(BF16)
            hc[e, rows, :] = hcb
            dg[e, rows, :] = dgb
            du[e, rows, :] = dub
            acc_o[...] += mm(hcb, wd[e])
            acc_d[...] += mm(dgb, wg[e], NT) + mm(dub, wu[e], NT)
            return carry

        lax.fori_loop(0, 4, expert, 0)

        @pl.when(n == 0)
        def _():
            mix_own[...] = acc_o[...]
            d_in[:, :d] = acc_d[...]
            d_in[:, d:] = acc_c[...]

        for m in (1, 2, 3):

            @pl.when(n == m)
            def _():
                mix_peer[m - 1] = acc_o[...].astype(BF16)
                d_send[m - 1, :, :d] = acc_d[...].astype(BF16)
                high = acc_c[...].astype(BF16).astype(F32)
                rest = acc_c[...] - high
                d_send[m - 1, :, d:] = (high + pltpu.roll(rest, 32, 1)).astype(BF16)
                give_back(m).start()

        x_t[:, rows] = jnp.transpose(x_in[n, :, :d].astype(F32)).astype(BF16)
        return carry

    def give_back(n):
        return remote(
            d_send.at[n - 1],
            d_recv.at[n - 1],
            bsend_sem.at[n - 1],
            brecv_sem.at[n - 1],
            *places[n - 1],
        )

    lax.fori_loop(0, 4, block, 0)

    half, dhalf = d // 2, ff // 2
    theirs = pl.multiple_of((1 - me_s) * half, half)
    dtheirs = pl.multiple_of((1 - me_s) * dhalf, dhalf)
    mine = pl.multiple_of(me_s * half, half)
    dmine = pl.multiple_of(me_s * dhalf, dhalf)
    g_rows = g_in.reshape(4 * tok, d)

    def swap(i, e):
        src = (wg.at[e, pl.ds(0, half)], wu.at[e, pl.ds(0, half)], wd.at[e, pl.ds(0, dhalf)])[i]
        dst = (xg, xu, xd)[i].at[e]
        return remote(src, dst, psend_sem.at[i, e], precv_sem.at[i, e], *places[3])

    def store(i, e):
        return pltpu.make_async_copy(
            (xg, xu, xd)[i].at[e], (dwg_out, dwu_out, dwd_out)[i].at[e], store_sem.at[i, e]
        )

    def give(e, carry):
        left = x_t[pl.ds(theirs, half), :]
        wg[e, :half, :] = mm(left, dg[e]).astype(BF16)
        swap(0, e).start()
        wu[e, :half, :] = mm(left, du[e]).astype(BF16)
        swap(1, e).start()
        wd[e, :dhalf, :] = mm(hc[e, :, pl.ds(dtheirs, dhalf)], g_rows[...], TN).astype(BF16)
        swap(2, e).start()
        return carry

    lax.fori_loop(0, 4, give, 0)

    def keep(e, carry):
        left = x_t[pl.ds(mine, half), :]
        own = mm(left, dg[e])
        swap(0, e).wait_recv()
        xg[e] = (own + xg[e].astype(F32)).astype(BF16)
        store(0, e).start()
        own = mm(left, du[e])
        swap(1, e).wait_recv()
        xu[e] = (own + xu[e].astype(F32)).astype(BF16)
        store(1, e).start()
        own = mm(hc[e, :, pl.ds(dmine, dhalf)], g_rows[...], TN)
        swap(2, e).wait_recv()
        xd[e] = (own + xd[e].astype(F32)).astype(BF16)
        store(2, e).start()
        return carry

    lax.fori_loop(0, 4, keep, 0)

    for n in (1, 2, 3):
        give_back(n).wait_recv()
        d_in[:, :d] += d_recv[n - 1, :, :d].astype(F32)
        tail = d_recv[n - 1, :, d:].astype(F32)
        both = tail + pltpu.roll(tail, 96, 1)
        d_in[:, d:] += jnp.where(lane < 32, both, 0.0)
    for n in (1, 2, 3):
        spread(n).wait_send()
        give_back(n).wait_send()

    def finish(e, carry):
        for i in range(3):
            swap(i, e).wait_send()
            store(i, e).wait()
        return carry

    lax.fori_loop(0, 4, finish, 0)


def mixture(x, g, w_gate, w_up, w_down, g_all, wg_all, wu_all, wd_all):
    tok, d = g.shape
    ff = w_gate.shape[1]
    vm = pl.BlockSpec(memory_space=pltpu.VMEM)
    hbm = pl.BlockSpec(memory_space=pl.ANY)
    dma = pltpu.SemaphoreType.DMA
    vmem = pltpu.VMEM
    return pl.pallas_call(
        mixture_kernel,
        out_shape=(
            jax.ShapeDtypeStruct((tok, d), F32),
            jax.ShapeDtypeStruct((3, tok, d), BF16),
            jax.ShapeDtypeStruct((tok, d + 128), F32),
            jax.ShapeDtypeStruct((4, d // 2, ff), BF16),
            jax.ShapeDtypeStruct((4, d // 2, ff), BF16),
            jax.ShapeDtypeStruct((4, ff // 2, d), BF16),
        ),
        in_specs=[vm] + [hbm] * 8,
        out_specs=(vm, vm, vm, hbm, hbm, hbm),
        scratch_shapes=[
            vmem((4, tok, d + 128), BF16),
            vmem((d, 4 * tok), BF16),
            vmem((4, tok, d), BF16),
            vmem((4, d, ff), BF16),
            vmem((4, d, ff), BF16),
            vmem((4, ff, d), BF16),
            vmem((4, 4 * tok, ff), BF16),
            vmem((4, 4 * tok, ff), BF16),
            vmem((4, 4 * tok, ff), BF16),
            vmem((tok, d), F32),
            vmem((tok, d), F32),
            vmem((tok, 128), F32),
            vmem((3, tok, d + 128), BF16),
            vmem((3, tok, d + 128), BF16),
            vmem((4, d // 2, ff), BF16),
            vmem((4, d // 2, ff), BF16),
            vmem((4, ff // 2, d), BF16),
            dma((3, 4)),
            dma((4,)),
            dma((3,)),
            dma((3,)),
            dma((3,)),
            dma((3,)),
            dma((3, 4)),
            dma((3, 4)),
            dma((3, 4)),
        ],
        compiler_params=pltpu.CompilerParams(
            collective_id=2, has_side_effects=True, vmem_limit_bytes=VMEM_LIMIT
        ),
        name="mixture",
    )(x, g, w_gate, w_up, w_down, g_all, wg_all, wu_all, wd_all)


D = 1024
HIGH = lax.Precision.HIGHEST


def rope_tables(positions):
    half = HD // 2
    freq = jnp.exp(-math.log(10000.0) * jnp.arange(half, dtype=jnp.float32) * 2.0 / HD)
    angle = positions.astype(jnp.float32)[:, None] * freq[None, :]
    cosine = jnp.concatenate([jnp.cos(angle), jnp.cos(angle)], -1)
    sine = jnp.concatenate([jnp.sin(angle), jnp.sin(angle)], -1)
    return (cosine, sine)


def rotate_half(v):
    half = v.shape[-1] // 2
    return jnp.concatenate([-v[..., half:], v[..., :half]], -1)


def rotary(v, cosine, sine):
    return v * cosine[:, None, :] + rotate_half(v) * sine[:, None, :]


def unrotary(v, cosine, sine):
    return v * cosine[:, None, :] - rotate_half(v) * sine[:, None, :]


def rms_scale(v):
    return lax.rsqrt(jnp.mean(v * v, -1, keepdims=True) + EPS)


def rms_back(inputs, scale_rows, gain, grad):
    scaled = grad * gain
    d_inputs = scale_rows * scaled - inputs * scale_rows**3 * jnp.mean(
        scaled * inputs, -1, keepdims=True
    )
    return (d_inputs, jnp.sum(grad * inputs * scale_rows, 0))


def scores(queries, keys):
    return jnp.einsum("qkgd,skd->kgqs", queries, keys, preferred_element_type=jnp.float32) * HD ** (
        -0.5
    )


def per_device_plain(
    tokens,
    segments,
    routes,
    route_weight,
    norm1_gain,
    w_query,
    w_key,
    w_value,
    w_out,
    norm2_gain,
    w_router,
    w_gate,
    w_up,
    w_down,
    cotangent,
):
    f32 = jnp.float32
    bf16 = jnp.bfloat16
    scale = HD ** (-0.5)
    group = H // KV
    xs = tokens[0].astype(f32)
    tok = xs.shape[0]
    blocks = lax.axis_size("blk")
    length = tok * blocks
    first = lax.axis_index("blk") * tok
    last = first + tok - 1
    positions = first + jnp.arange(tok, dtype=jnp.int32)
    cosine, sine = rope_tables(positions)
    scale1 = rms_scale(xs)
    xa = (xs * scale1 * norm1_gain).astype(bf16)
    query = jnp.dot(xa, w_query, preferred_element_type=f32)
    key = jnp.dot(xa, w_key, preferred_element_type=f32)
    value = jnp.dot(xa, w_value, preferred_element_type=f32).astype(bf16)
    q_rot = rotary(query.reshape(tok, H, HD), cosine, sine).astype(bf16).reshape(tok, KV, group, HD)
    k_rot = rotary(key.reshape(tok, KV, HD), cosine, sine).astype(bf16).reshape(tok, KV * HD)
    seg_float = segments[0].astype(bf16)
    k_all, v_all, seg_all = (
        lax.all_gather(k_rot, "blk", axis=0, tiled=True),
        lax.all_gather(value, "blk", axis=0, tiled=True),
        lax.all_gather(seg_float, "blk", axis=0, tiled=True),
    )
    kblk = min(512, length)
    nblk = length // kblk
    k_blocks = k_all.reshape(nblk, kblk, KV, HD)
    v_blocks = v_all.reshape(nblk, kblk, KV, HD)
    s_blocks = seg_all.reshape(nblk, kblk)
    starts = jnp.arange(nblk, dtype=jnp.int32) * kblk

    def visible(kseg, kstart):
        kpos = kstart + jnp.arange(kblk, dtype=jnp.int32)
        return ((seg_float[:, None] == kseg[None, :]) & (kpos[None, :] <= positions[:, None]))[
            None, None
        ]

    def forward_step(carry, block):
        kb, vb, sb, start = block

        def forward_compute(state):
            running, total, acc = state
            mask = visible(sb, start)
            score = jnp.where(mask, scores(q_rot, kb), NEG)
            newmax = jnp.maximum(running, jnp.max(score, -1))
            expo = jnp.where(mask, jnp.exp(score - newmax[..., None]), 0.0)
            factor = jnp.exp(running - newmax)
            total = total * factor + jnp.sum(expo, -1)
            acc = acc * factor[..., None] + jnp.einsum(
                "kgqs,skd->kgqd", expo.astype(bf16), vb, preferred_element_type=f32
            )
            return (newmax, total, acc)

        return (lax.cond(start <= last, forward_compute, lambda state: state, carry), None)

    init = (
        jnp.full((KV, group, tok), NEG, f32),
        jnp.zeros((KV, group, tok), f32),
        jnp.zeros((KV, group, tok, HD), f32),
    )
    (running, total, acc), unused = lax.scan(
        forward_step, init, (k_blocks, v_blocks, s_blocks, starts)
    )
    lse = running + jnp.log(total)
    o_rows = (acc / total[..., None]).transpose(2, 0, 1, 3)
    att_low = o_rows.reshape(tok, H * HD).astype(bf16)
    h1 = xs + jnp.dot(att_low, w_out, preferred_element_type=f32)
    scale2 = rms_scale(h1)
    xl = (h1 * scale2 * norm2_gain).astype(bf16)
    logits = jnp.dot(xl, w_router, preferred_element_type=f32)
    experts = logits.shape[1]
    route = routes[0]
    rweight = route_weight[0]
    chooser = (route[:, :, None] == jnp.arange(experts, dtype=jnp.int32)[None, None, :]).astype(f32)
    chosen = jnp.sum(chooser * logits[:, None, :], -1)
    gates = jax.nn.softmax(chosen, -1)
    combine = (rweight * gates).astype(bf16)
    cap = min(tok, 2 * tok * TOP // experts)
    member = jnp.sum(chooser, 1)
    before = jnp.asarray(np.tril(np.ones((tok, tok), np.float32), -1))
    order = jnp.dot(before, member, precision=HIGH)
    rank = jnp.sum(chooser * order[:, None, :], -1).astype(jnp.int32)
    slots = route * cap + rank
    placed = jnp.any(
        slots[:, :, None] == jnp.arange(experts * cap, dtype=jnp.int32)[None, None, :], 1
    ).astype(bf16)
    outgoing = jnp.einsum("ts,td->sd", placed, xl, preferred_element_type=f32).astype(bf16)
    incoming = lax.all_to_all(
        outgoing.reshape(experts, cap, D), "blk", split_axis=0, concat_axis=0, tiled=True
    )
    local_exp = w_gate.shape[0]
    incoming = incoming.reshape(blocks, local_exp, cap, D)
    gate_pre = jnp.einsum("necd,edf->necf", incoming, w_gate, preferred_element_type=f32)
    up_pre = jnp.einsum("necd,edf->necf", incoming, w_up, preferred_element_type=f32)
    sigma = jax.nn.sigmoid(gate_pre)
    activated = gate_pre * sigma
    hidden = (activated * up_pre).astype(bf16)
    expert_out = jnp.einsum("necf,efd->necd", hidden, w_down, preferred_element_type=f32).astype(
        bf16
    )
    returned = lax.all_to_all(
        expert_out.reshape(experts, cap, D), "blk", split_axis=0, concat_axis=0, tiled=True
    )
    per_route = jnp.take(returned.reshape(experts * cap, D), slots.reshape(-1), axis=0).reshape(
        tok, TOP, D
    )
    mixture = jnp.einsum("tj,tjd->td", combine, per_route, preferred_element_type=f32)
    result = h1 + mixture
    grad_out = cotangent[0].astype(f32)
    grad_combine = jnp.einsum("td,tjd->tj", grad_out, per_route.astype(f32), precision=HIGH)
    route_grads = (combine.astype(f32)[:, :, None] * grad_out[:, None, :]).astype(bf16)
    grad_slots = (
        jnp.zeros((experts * cap, D), bf16)
        .at[slots.reshape(-1)]
        .set(route_grads.reshape(tok * TOP, D))
    )
    grad_incoming = lax.all_to_all(
        grad_slots.reshape(experts, cap, D), "blk", split_axis=0, concat_axis=0, tiled=True
    )
    grad_incoming = grad_incoming.reshape(blocks, local_exp, cap, D)
    grad_hidden = jnp.einsum("necd,efd->necf", grad_incoming, w_down, preferred_element_type=f32)
    grad_gate = (grad_hidden * up_pre * sigma * (1.0 + gate_pre * (1.0 - sigma))).astype(bf16)
    grad_up = (grad_hidden * activated).astype(bf16)
    d_down = jnp.einsum("necf,necd->efd", hidden, grad_incoming, preferred_element_type=f32)
    d_gate_w = jnp.einsum("necd,necf->edf", incoming, grad_gate, preferred_element_type=f32)
    d_up_w = jnp.einsum("necd,necf->edf", incoming, grad_up, preferred_element_type=f32)
    grad_in = (
        jnp.einsum("necf,edf->necd", grad_gate, w_gate, preferred_element_type=f32)
        + jnp.einsum("necf,edf->necd", grad_up, w_up, preferred_element_type=f32)
    ).astype(bf16)
    grad_back = lax.all_to_all(
        grad_in.reshape(experts, cap, D), "blk", split_axis=0, concat_axis=0, tiled=True
    )
    grad_xl = jnp.einsum(
        "ts,sd->td", placed, grad_back.reshape(experts * cap, D), preferred_element_type=f32
    )
    grad_gates = rweight * grad_combine
    grad_chosen = gates * (grad_gates - jnp.sum(gates * grad_gates, -1, keepdims=True))
    grad_logits = jnp.sum(chooser * grad_chosen[:, :, None], 1).astype(bf16)
    d_router = jnp.einsum("td,te->de", xl, grad_logits, preferred_element_type=f32)
    grad_xl = grad_xl + jnp.einsum("te,de->td", grad_logits, w_router, preferred_element_type=f32)
    grad_h1_norm, d_gain2 = rms_back(h1, scale2, norm2_gain, grad_xl)
    grad_h1 = grad_out + grad_h1_norm
    grad_att = grad_h1.astype(bf16)
    d_out_w = jnp.einsum("ti,td->id", att_low, grad_att, preferred_element_type=f32)
    grad_o = jnp.einsum("td,id->ti", grad_att, w_out, preferred_element_type=f32).astype(bf16)
    grad_o_rows = grad_o.reshape(tok, KV, group, HD)
    delta = jnp.einsum("qkgd,qkgd->kgq", grad_o_rows.astype(f32), o_rows)

    def query_terms(kb, vb, sb, start):
        mask = visible(sb, start)
        prob = jnp.where(mask, jnp.exp(scores(q_rot, kb) - lse[..., None]), 0.0)
        dprob = jnp.einsum("qkgd,skd->kgqs", grad_o_rows, vb, preferred_element_type=f32)
        dscore = (prob * (dprob - delta[..., None])).astype(bf16)
        dq_term = jnp.einsum("kgqs,skd->qkgd", dscore, kb, preferred_element_type=f32) * scale
        return (dq_term, dscore, prob)

    zero_q = jnp.zeros((tok, KV, group, HD), f32)

    def backward_step(grad_q, block):
        kb, vb, sb, start = block

        def backward_compute(acc_q):
            dq_term, dscore, prob = query_terms(kb, vb, sb, start)
            gk = jnp.einsum("kgqs,qkgd->skd", dscore, q_rot, preferred_element_type=f32) * scale
            gv = jnp.einsum(
                "kgqs,qkgd->skd", prob.astype(bf16), grad_o_rows, preferred_element_type=f32
            )
            return (acc_q + dq_term, (gk.reshape(kblk, KV * HD), gv.reshape(kblk, KV * HD)))

        def skip(acc_q):
            empty = jnp.zeros((kblk, KV * HD), f32)
            return (acc_q, (empty, empty))

        return lax.cond(start <= last, backward_compute, skip, grad_q)

    grad_q, (gk_blocks, gv_blocks) = lax.scan(
        backward_step, zero_q, (k_blocks, v_blocks, s_blocks, starts)
    )
    grad_k, grad_v = (
        lax.psum_scatter(
            gk_blocks.reshape(length, KV * HD).astype(jnp.bfloat16),
            "blk",
            scatter_dimension=0,
            tiled=True,
        ).astype(jnp.float32),
        lax.psum_scatter(
            gv_blocks.reshape(length, KV * HD).astype(jnp.bfloat16),
            "blk",
            scatter_dimension=0,
            tiled=True,
        ).astype(jnp.float32),
    )
    grad_qr = unrotary(grad_q.reshape(tok, H, HD), cosine, sine).reshape(tok, H * HD).astype(bf16)
    grad_kr = unrotary(grad_k.reshape(tok, KV, HD), cosine, sine).reshape(tok, KV * HD).astype(bf16)
    grad_vr = grad_v.astype(bf16)
    d_query = jnp.einsum("td,te->de", xa, grad_qr, preferred_element_type=f32)
    d_key = jnp.einsum("td,te->de", xa, grad_kr, preferred_element_type=f32)
    d_value = jnp.einsum("td,te->de", xa, grad_vr, preferred_element_type=f32)
    grad_xa = (
        jnp.einsum("te,de->td", grad_qr, w_query, preferred_element_type=f32)
        + jnp.einsum("te,de->td", grad_kr, w_key, preferred_element_type=f32)
        + jnp.einsum("te,de->td", grad_vr, w_value, preferred_element_type=f32)
    )
    grad_x_norm, d_gain1 = rms_back(xs, scale1, norm1_gain, grad_xa)
    grad_x = grad_h1 + grad_x_norm
    summed = lax.psum(
        (d_gain1, d_query, d_key, d_value, d_out_w, d_gain2, d_router), ("seq", "blk")
    )
    expert_summed = (
        lax.psum(d_gate_w.astype(jnp.bfloat16), "seq").astype(jnp.float32),
        lax.psum(d_up_w.astype(jnp.bfloat16), "seq").astype(jnp.float32),
        lax.psum(d_down.astype(jnp.bfloat16), "seq").astype(jnp.float32),
    )
    return (
        result.astype(bf16)[None],
        grad_x[None],
        summed[0],
        summed[1],
        summed[2],
        summed[3],
        summed[4],
        summed[5],
        summed[6],
        expert_summed[0],
        expert_summed[1],
        expert_summed[2],
    )


def by_head(w_query, w_key, w_value):
    d = w_query.shape[0]
    return jnp.concatenate(
        [w_query.reshape(d, KV, 2 * HD), w_key.reshape(d, KV, HD), w_value.reshape(d, KV, HD)], -1
    ).reshape(d, KV * 4 * HD)


def tables(length):
    half = HD // 2
    freq = np.exp(-math.log(10000.0) * np.arange(half, dtype=np.float32) * 2.0 / HD).astype(np.float32)
    angle = np.arange(length, dtype=np.float32)[:, None] * freq[None, :]
    return np.tile(np.cos(angle), (1, 4)), np.tile(np.sin(angle), (1, 4))


def per_device(
    tokens,
    segments,
    routes,
    route_weight,
    norm1_gain,
    w_query,
    w_key,
    w_value,
    w_out,
    norm2_gain,
    w_router,
    w_gate,
    w_up,
    w_down,
    cotangent,
):
    scale = HD ** (-0.5)
    xs = tokens[0].astype(F32)
    tok, d = xs.shape
    blocks = lax.axis_size("blk")
    experts = w_router.shape[1]
    cos_np, sin_np = tables(tok * blocks)
    cos_all = jnp.asarray(cos_np.reshape(blocks, tok, 2 * HD))
    sin_all = jnp.asarray(sin_np.reshape(blocks, tok, 2 * HD))
    me = lax.axis_index("blk")
    me_s = lax.axis_index("seq")
    cosine = lax.dynamic_index_in_dim(cos_all, me, 0, keepdims=False)[:, None, :]
    sine = lax.dynamic_index_in_dim(sin_all, me, 0, keepdims=False)[:, None, :]
    scale1 = rms_scale(xs)
    xa = (xs * scale1 * norm1_gain).astype(BF16)
    w_all = by_head(w_query, w_key, w_value)
    qkv = mm(xa, w_all).reshape(tok, KV, 4 * HD)

    def turned(u):
        parts = u.reshape(tok, KV, -1, HD)
        return (
            parts * cosine[:, :, None, :HD] + rotate_half(parts) * sine[:, :, None, :HD]
        ).reshape(u.shape)

    pay = jnp.concatenate(
        [
            turned(qkv[..., : 2 * HD]) * scale,
            turned(qkv[..., 2 * HD : 3 * HD]),
            qkv[..., 3 * HD :],
        ],
        -1,
    ).astype(BF16)
    seg = (
        jnp.zeros((16, 4 * HD), BF16)
        .at[:2, 2 * HD :]
        .set(segments[0].astype(BF16).reshape(2, tok // 2))
    )
    pay = jnp.concatenate(
        [pay.transpose(1, 0, 2), jnp.broadcast_to(seg[None], (KV, 16, 4 * HD))], 1
    )
    g_low = cotangent[0]
    att_low, *kept = attention_forward(blocks, pay, g_low, w_gate[0], w_up[0], w_down[0])
    kept, shared = kept[:5], kept[5:]

    h1 = xs + mm(att_low, w_out)
    scale2 = rms_scale(h1)
    xl = (h1 * scale2 * norm2_gain).astype(BF16)
    logits = mm(xl, w_router)
    chooser = routes[0][:, :, None] == jnp.arange(experts, dtype=jnp.int32)[None, None, :]
    routed = jnp.any(chooser, 1)
    rweight = jnp.sum(jnp.where(chooser, route_weight[0][:, :, None], 0.0), 1)
    top = jnp.max(jnp.where(routed, logits, NEG), -1, keepdims=True)
    expo = jnp.where(routed, jnp.exp(logits - top), 0.0)
    gates = expo / jnp.sum(expo, -1, keepdims=True)
    combine = (rweight * gates).astype(BF16)
    sent = jnp.concatenate([xl, jnp.pad(combine, ((0, 0), (0, 128 - experts)))], 1)
    mix_own, mix_peer, d_in, dwg, dwu, dwd = mixture(
        sent, g_low, w_gate[0], w_up[0], w_down[0], *shared
    )

    grad_out = g_low.astype(F32)
    grad_gates = rweight * d_in[:, d : d + experts]
    grad_logits = (
        gates * (grad_gates - jnp.sum(gates * grad_gates, -1, keepdims=True))
    ).astype(BF16)
    d_router = mm(xl, grad_logits, TN)
    grad_xl = d_in[:, :d] + mm(grad_logits, w_router, NT)
    grad_h1_norm, d_gain2 = rms_back(h1, scale2, norm2_gain, grad_xl)
    grad_h1 = grad_out + grad_h1_norm
    grad_att = grad_h1.astype(BF16)
    d_out_w = mm(att_low, grad_att, TN)
    grad_o = mm(grad_att, w_out, NT).astype(BF16)
    got, mix_in, dwg_in, dwu_in, dwd_in = attention_backward(
        blocks, grad_o, *kept, cos_all, sin_all, mix_peer, dwg, dwu, dwd
    )
    result = h1 + mix_own + jnp.sum(mix_in.astype(F32), 0)
    plane = lax.rem(me, 4)

    def collect(own, arrived, axis):
        own = lax.dynamic_index_in_dim(own, plane, 0, keepdims=False).astype(F32)
        total = own + jnp.sum(arrived.astype(F32), 0)
        return lax.all_gather(total.astype(BF16), "seq", axis=axis, tiled=True).astype(F32)

    d_gate_w = collect(dwg, dwg_in, 0)[None]
    d_up_w = collect(dwu, dwu_in, 0)[None]
    d_down = collect(dwd, dwd_in, 0)[None]
    grad_all = got.transpose(1, 0, 2).reshape(tok, KV * 4 * HD)
    d_all = mm(xa, grad_all, TN)
    grad_xa = mm(grad_all, w_all, NT)
    d_heads = d_all.reshape(d, KV, 4 * HD)
    d_query = d_heads[..., : 2 * HD].reshape(d, H * HD)
    d_key = d_heads[..., 2 * HD : 3 * HD].reshape(d, KV * HD)
    d_value = d_heads[..., 3 * HD :].reshape(d, KV * HD)
    grad_x_norm, d_gain1 = rms_back(xs, scale1, norm1_gain, grad_xa)
    grad_x = grad_h1 + grad_x_norm
    summed = lax.psum(
        (d_gain1, d_query, d_key, d_value, d_out_w, d_gain2, d_router), ("seq", "blk")
    )
    return (result.astype(BF16)[None], grad_x[None], *summed, d_gate_w, d_up_w, d_down)


def solution(mesh):
    fused = dict(mesh.shape) == {"seq": 2, "blk": 2 * KV}
    return jax.shard_map(
        per_device if fused else per_device_plain,
        mesh=mesh,
        in_specs=(
            P("seq", "blk", None),
            P("seq", "blk"),
            P("seq", "blk", None),
            P("seq", "blk", None),
            P(),
            P(),
            P(),
            P(),
            P(),
            P(),
            P(),
            P("blk", None, None),
            P("blk", None, None),
            P("blk", None, None),
            P("seq", "blk", None),
        ),
        out_specs=(
            P("seq", "blk", None),
            P("seq", "blk", None),
            P(),
            P(),
            P(),
            P(),
            P(),
            P(),
            P(),
            P("blk", None, None),
            P("blk", None, None),
            P("blk", None, None),
        ),
        check_vma=False,
    )
```

```python
import functools
import math

import jax
import jax.numpy as jnp
import numpy as np
from jax import lax
from jax.experimental import pallas as pl
from jax.experimental.pallas import tpu as pltpu
from jax.sharding import PartitionSpec as P

H = 16
KV = 8
HD = 64
TOP = 8
EPS = 1e-06
NEG = -1e30
F32 = jnp.float32
BF16 = jnp.bfloat16
MESH = pl.DeviceIdType.MESH
VMEM_LIMIT = 60 * 2**20
NT = (((1,), (1,)), ((), ()))
TN = (((0,), (0,)), ((), ()))


def mm(a, b, dims=(((1,), (0,)), ((), ()))):
    return lax.dot_general(a, b, dims, preferred_element_type=F32)


def remote(src, dst, send, recv, seq, blk):
    return pltpu.make_async_remote_copy(
        src_ref=src,
        dst_ref=dst,
        send_sem=send,
        recv_sem=recv,
        device_id=(seq, blk),
        device_id_type=MESH,
    )


def greet_all(seqs, blocks, me_s, me_b):
    barrier = pltpu.get_barrier_semaphore()
    total = seqs * blocks

    def hello(n, carry):
        other = lax.rem(me_s * blocks + me_b + n, total)
        pl.semaphore_signal(
            barrier,
            inc=1,
            device_id=(other // blocks, lax.rem(other, blocks)),
            device_id_type=MESH,
        )
        return carry

    lax.fori_loop(1, total, hello, 0)
    pl.semaphore_wait(barrier, total - 1)


def flip(place, n):
    if n == 1:
        return place + 1 - 2 * lax.rem(place, 2)
    if n == 2:
        return place + 2 - 4 * (place // 2)
    return 3 - place


def rotate_pairs(u):
    lanes = u.shape[-1]
    half = HD // 2
    lane = lax.broadcasted_iota(jnp.int32, u.shape, u.ndim - 1)
    ahead = pltpu.roll(u, lanes - half, u.ndim - 1)
    behind = pltpu.roll(u, half, u.ndim - 1)
    return jnp.where(lane % HD < half, -ahead, behind)


def stacked_heads(wide):
    return jnp.concatenate([wide[:HD], wide[HD:]], axis=1)


def attention_forward_kernel(
    blocks,
    x_ref,
    gain_ref,
    wq_ref,
    wk_ref,
    wv_ref,
    seg_ref,
    cos_ref,
    sin_ref,
    g_ref,
    wg_ref,
    wu_ref,
    wd_ref,
    o_ref,
    xa_ref,
    kv_ref,
    kvt_ref,
    q_ref,
    ot_ref,
    stat_ref,
    g_all,
    wg_all,
    wu_all,
    wd_all,
    pay,
    turn,
    in_ref,
    other_ref,
    obuf,
    cnt,
    turn_sem,
    send_sem,
    recv_sem,
    fsend_sem,
    frecv_sem,
    osend_sem,
    orecv_sem,
    gsend_sem,
    grecv_sem,
    wsend_sem,
    wrecv_sem,
    hsend_sem,
    hrecv_sem,
):
    me_s = lax.axis_index("seq")
    me_b = lax.axis_index("blk")
    tok = q_ref.shape[1]
    steps = blocks // 2
    sigma = me_b // KV
    kappa = lax.rem(me_b, KV)
    tables_in = [
        pltpu.make_async_copy(src.at[me_b], turn.at[i], turn_sem.at[i])
        for i, src in enumerate((cos_ref, sin_ref))
    ]
    for copy in tables_in:
        copy.start()
    xs = x_ref[...].astype(F32)
    xa = (xs * rms_scale(xs) * gain_ref[...]).astype(BF16)
    xa_ref[...] = xa
    for copy in tables_in:
        copy.wait()
    cosine, sine = turn[0], turn[1]
    low = lax.broadcasted_iota(jnp.int32, (tok, 2 * HD), 1) < HD
    pay[:, tok:, : 2 * HD] = jnp.zeros((KV, 16, 2 * HD), BF16)
    for m in range(KV // 2):
        pair = slice(m * 2 * HD, (m + 1) * 2 * HD)
        keys = mm(xa, wk_ref[:, pair])
        keys = keys * cosine + rotate_pairs(keys) * sine
        values = mm(xa, wv_ref[:, pair])
        first = jnp.where(low, keys, pltpu.roll(values, HD, 1))
        second = jnp.where(low, pltpu.roll(keys, HD, 1), values)
        pay[2 * m, :tok, 2 * HD :] = first.astype(BF16)
        pay[2 * m + 1, :tok, 2 * HD :] = second.astype(BF16)
        for k in (2 * m, 2 * m + 1):
            query = mm(xa, wq_ref[:, k * 2 * HD : (k + 1) * 2 * HD])
            query = (query * cosine + rotate_pairs(query) * sine) * HD ** (-0.5)
            pay[k, :tok, : 2 * HD] = query.astype(BF16)
            pay[k, tok:, 2 * HD :] = seg_ref[...]
    greet_all(2, blocks, me_s, me_b)

    dest_core = lax.rem(me_b, 2)
    slot = me_b // 2
    line, plane = me_b // 4, lax.rem(me_b, 4)
    weights = ((wg_ref, wg_all), (wu_ref, wu_all), (wd_ref, wd_all))

    def share_grad(n):
        return remote(
            g_ref,
            g_all.at[line],
            gsend_sem.at[n - 1],
            grecv_sem.at[n - 1],
            me_s,
            flip(line, n) * 4 + plane,
        )

    def half(ref):
        rows = ref.shape[0] // 2
        return ref.at[pl.ds(pl.multiple_of(me_s * rows, rows), rows)]

    def share_weight(n, i):
        own, everyone = weights[i]
        return remote(
            half(own),
            half(everyone.at[plane]),
            wsend_sem.at[n - 1, i],
            wrecv_sem.at[n - 1, i],
            me_s,
            line * 4 + flip(plane, n),
        )

    def pass_weight(n, i):
        arrived = half(weights[i][1].at[flip(plane, n)])
        return remote(
            arrived, arrived, hsend_sem.at[n - 1, i], hrecv_sem.at[n - 1, i], 1 - me_s, me_b
        )

    def payload(n):
        k = lax.rem(me_b + n, KV)
        chip = me_s * KV + k
        mine = (dest_core == me_s) & (chip == me_b)
        return k, chip, mine

    def send_payload(n, carry):
        k, chip, mine = payload(n)

        @pl.when(mine)
        def _():
            pltpu.make_async_copy(pay.at[k], in_ref.at[slot], recv_sem.at[slot]).start()

        @pl.when(jnp.logical_not(mine))
        def _():
            remote(
                pay.at[k], in_ref.at[slot], send_sem.at[k], recv_sem.at[slot], dest_core, chip
            ).start()

        return carry

    lax.fori_loop(0, KV, send_payload, 0)
    for n in (1, 2, 3):
        share_grad(n).start()
        for i in range(3):
            share_weight(n, i).start()

    def arrival(t):
        return pltpu.make_async_copy(pay.at[0], in_ref.at[t], recv_sem.at[t])

    def forward(t):
        return remote(
            in_ref.at[t, :, pl.ds(2 * HD, 2 * HD)],
            other_ref.at[t],
            fsend_sem.at[t],
            frecv_sem.at[t],
            1 - me_s,
            me_b,
        )

    arrival(0).wait()
    forward(0).start()
    cnt[...] = jnp.zeros_like(cnt)
    first_core = me_s == 0
    lane = lax.broadcasted_iota(jnp.int32, (1, 2 * tok), 1)
    qrow = jnp.where(lane < tok, lane, lane - tok)
    wide = 2 * tok

    def step(t, carry):
        @pl.when(t < steps - 1)
        def _():
            arrival(t + 1).wait()
            forward(t + 1).start()

        forward(t).wait_recv()
        mine = in_ref[t]
        kv_mine, seg_mine = mine[:tok, 2 * HD :], mine[tok:, 2 * HD :].astype(F32)
        other = other_ref[t]
        kv_other, seg_other = other[:tok], other[tok:].astype(F32)
        pair = jnp.where(
            first_core,
            jnp.concatenate([kv_mine, kv_other], 0).astype(F32),
            jnp.concatenate([kv_other, kv_mine], 0).astype(F32),
        )
        kv_ref[t] = pair.astype(BF16)
        kvt_ref[t] = jnp.transpose(pair).astype(BF16)
        number = lax.broadcasted_iota(jnp.int32, (8, tok), 0).astype(F32)
        seg_q = jnp.concatenate([seg_mine[0:1], seg_mine[1:2]], 1)
        seg_o = jnp.concatenate([seg_other[0:1], seg_other[1:2]], 1)
        below = (seg_q < number).astype(F32) + (seg_o < number).astype(F32)
        cnt[...] += jnp.sum(below, 1, keepdims=True)
        start_q = jnp.sum(jnp.where(seg_q == number, cnt[:, :1], 0.0), 0, keepdims=True)
        start = jnp.concatenate([start_q, start_q], 1).astype(jnp.int32)
        q_two = mine[:tok, : 2 * HD]
        q_ref[t] = q_two
        qt = stacked_heads(jnp.transpose(q_two.astype(F32)))
        qm = jnp.concatenate([qt, jnp.zeros_like(qt)], 0).astype(BF16)
        qpos = (2 * t + me_s) * tok + qrow

        def piece(u, state, last):
            running, total, acc = state
            score = mm(kv_ref[u], qm)
            kpos = u * wide + lax.broadcasted_iota(jnp.int32, score.shape, 0)
            mask = kpos >= start
            if last:
                mask &= kpos <= qpos
            score = jnp.where(mask, score, NEG)
            newmax = jnp.maximum(running, jnp.max(score, 0, keepdims=True))
            expo = jnp.exp(score - newmax)
            factor = jnp.exp(running - newmax)
            total = total * factor + jnp.sum(expo, 0, keepdims=True)
            acc = acc * factor + mm(kvt_ref[u, HD:, :], expo.astype(BF16))
            return newmax, total, acc

        state = (
            jnp.full((1, wide), NEG, F32),
            jnp.zeros((1, wide), F32),
            jnp.zeros((HD, wide), F32),
        )
        state = lax.fori_loop(0, t, lambda u, s: piece(u, s, False), state)
        running, total, acc = piece(t, state, True)
        out_t = acc / total
        ot_ref[t] = out_t
        rows = lax.broadcasted_iota(jnp.int32, (8, wide), 0)
        lse = running + jnp.log(total)
        stat_ref[t] = jnp.where(rows == 0, lse, start.astype(F32))
        upright = jnp.concatenate([out_t[:, :tok], out_t[:, tok:]], 0)
        obuf[t] = jnp.transpose(upright).astype(BF16)
        owner = 2 * t + me_s
        home = (sigma == me_s) & (owner == me_b)
        place = o_ref.at[:, pl.ds(pl.multiple_of(kappa * 2 * HD, 2 * HD), 2 * HD)]

        @pl.when(home)
        def _():
            pltpu.make_async_copy(obuf.at[t], place, orecv_sem.at[kappa]).start()

        @pl.when(jnp.logical_not(home))
        def _():
            remote(obuf.at[t], place, osend_sem.at[t], orecv_sem.at[kappa], sigma, owner).start()

        return carry

    lax.fori_loop(0, steps, step, 0)
    for n in (1, 2, 3):
        for i in range(3):
            share_weight(n, i).wait_recv()
            pass_weight(n, i).start()

    def finish(t, carry):
        k, chip, mine = payload(t)

        @pl.when(jnp.logical_not(mine))
        def _():
            remote(
                pay.at[k], in_ref.at[slot], send_sem.at[k], recv_sem.at[slot], dest_core, chip
            ).wait_send()

        return carry

    lax.fori_loop(0, KV, finish, 0)

    def finish_steps(t, carry):
        forward(t).wait_send()
        owner = 2 * t + me_s
        home = (sigma == me_s) & (owner == me_b)

        @pl.when(jnp.logical_not(home))
        def _():
            remote(
                obuf.at[t],
                o_ref.at[:, pl.ds(0, 2 * HD)],
                osend_sem.at[t],
                orecv_sem.at[0],
                sigma,
                owner,
            ).wait_send()

        return carry

    lax.fori_loop(0, steps, finish_steps, 0)

    def gather(k, carry):
        pltpu.make_async_copy(
            obuf.at[0],
            o_ref.at[:, pl.ds(pl.multiple_of(k * 2 * HD, 2 * HD), 2 * HD)],
            orecv_sem.at[k],
        ).wait()
        return carry

    lax.fori_loop(0, KV, gather, 0)
    for n in (1, 2, 3):
        share_grad(n).wait()
        for i in range(3):
            share_weight(n, i).wait_send()
            pass_weight(n, i).wait()


def attention_forward(
    blocks, x, gain, w_query, w_key, w_value, seg, cos_all, sin_all, g, w_gate, w_up, w_down
):
    tok, d = x.shape
    steps = blocks // 2
    vm = pl.BlockSpec(memory_space=pltpu.VMEM)
    hbm = pl.BlockSpec(memory_space=pl.ANY)
    dma = pltpu.SemaphoreType.DMA
    return pl.pallas_call(
        functools.partial(attention_forward_kernel, blocks),
        out_shape=(
            jax.ShapeDtypeStruct((tok, H * HD), BF16),
            jax.ShapeDtypeStruct((tok, d), BF16),
            jax.ShapeDtypeStruct((steps, 2 * tok, 2 * HD), BF16),
            jax.ShapeDtypeStruct((steps, 2 * HD, 2 * tok), BF16),
            jax.ShapeDtypeStruct((steps, tok, 2 * HD), BF16),
            jax.ShapeDtypeStruct((steps, HD, 2 * tok), F32),
            jax.ShapeDtypeStruct((steps, 8, 2 * tok), F32),
            jax.ShapeDtypeStruct((4, *g.shape), BF16),
            jax.ShapeDtypeStruct((4, *w_gate.shape), BF16),
            jax.ShapeDtypeStruct((4, *w_up.shape), BF16),
            jax.ShapeDtypeStruct((4, *w_down.shape), BF16),
        ),
        in_specs=[vm] * 6 + [hbm] * 6,
        out_specs=(vm,) * 7 + (hbm,) * 4,
        scratch_shapes=[
            pltpu.VMEM((KV, tok + 16, 4 * HD), BF16),
            pltpu.VMEM((2, tok, 2 * HD), F32),
            pltpu.VMEM((steps, tok + 16, 4 * HD), BF16),
            pltpu.VMEM((steps, tok + 16, 2 * HD), BF16),
            pltpu.VMEM((steps, tok, 2 * HD), BF16),
            pltpu.VMEM((8, 128), F32),
            dma((2,)),
            dma((KV,)),
            dma((steps,)),
            dma((steps,)),
            dma((steps,)),
            dma((steps,)),
            dma((KV,)),
            dma((3,)),
            dma((3,)),
            dma((3, 3)),
            dma((3, 3)),
            dma((3, 3)),
            dma((3, 3)),
        ],
        compiler_params=pltpu.CompilerParams(
            collective_id=0, has_side_effects=True, vmem_limit_bytes=VMEM_LIMIT
        ),
        name="attention_forward",
    )(x, gain, w_query, w_key, w_value, seg, cos_all, sin_all, g, w_gate, w_up, w_down)


def attention_backward_kernel(
    blocks,
    do_ref,
    kv_ref,
    kvt_ref,
    q_ref,
    ot_ref,
    stat_ref,
    cos_ref,
    sin_ref,
    mix_ref,
    dwg_ref,
    dwu_ref,
    dwd_ref,
    out_ref,
    mix_in,
    dwg_in,
    dwu_in,
    dwd_in,
    in_ref,
    dkv,
    part,
    xch,
    done,
    send_sem,
    recv_sem,
    xsend_sem,
    xrecv_sem,
    osend_sem,
    orecv_sem,
    msend_sem,
    mrecv_sem,
    wsend_sem,
    wrecv_sem,
):
    me_s = lax.axis_index("seq")
    me_b = lax.axis_index("blk")
    tok = q_ref.shape[1]
    steps = blocks // 2
    sigma = me_b // KV
    kappa = lax.rem(me_b, KV)
    greet_all(2, blocks, me_s, me_b)

    dest_core = lax.rem(me_b, 2)
    slot = me_b // 2
    line, plane = me_b // 4, lax.rem(me_b, 4)
    weights = ((dwg_ref, dwg_in), (dwu_ref, dwu_in), (dwd_ref, dwd_in))

    def give_mix(n):
        return remote(
            mix_ref.at[n - 1],
            mix_in.at[n - 1],
            msend_sem.at[n - 1],
            mrecv_sem.at[n - 1],
            me_s,
            flip(line, n) * 4 + plane,
        )

    def give_weight(n, i):
        src, dst = weights[i]
        return remote(
            src.at[flip(plane, n)],
            dst.at[n - 1],
            wsend_sem.at[n - 1, i],
            wrecv_sem.at[n - 1, i],
            me_s,
            line * 4 + flip(plane, n),
        )

    def outgoing(n):
        k = lax.rem(me_b + n, KV)
        chip = me_s * KV + k
        mine = (dest_core == me_s) & (chip == me_b)
        src = do_ref.at[:, pl.ds(pl.multiple_of(k * 2 * HD, 2 * HD), 2 * HD)]
        return k, chip, mine, src

    def send_grad(n, carry):
        k, chip, mine, src = outgoing(n)

        @pl.when(mine)
        def _():
            pltpu.make_async_copy(src, in_ref.at[slot], recv_sem.at[slot]).start()

        @pl.when(jnp.logical_not(mine))
        def _():
            remote(src, in_ref.at[slot], send_sem.at[k], recv_sem.at[slot], dest_core, chip).start()

        return carry

    lax.fori_loop(0, KV, send_grad, 0)
    for n in (1, 2, 3):
        give_mix(n).start()
        for i in range(3):
            give_weight(n, i).start()
    dkv[...] = jnp.zeros_like(dkv)
    wide = 2 * tok
    lane = lax.broadcasted_iota(jnp.int32, (1, wide), 1)
    qrow = jnp.where(lane < tok, lane, lane - tok)
    low = lax.broadcasted_iota(jnp.int32, (tok, 2 * HD), 1) < HD

    def swap(t):
        return remote(part.at[t], xch.at[t], xsend_sem.at[t], xrecv_sem.at[t], 1 - me_s, me_b)

    def deliver(t, act):
        owner = 2 * t + me_s
        home = (sigma == me_s) & (owner == me_b)
        src, dst = done.at[t], out_ref.at[kappa]

        @pl.when(home)
        def _():
            if act == "start":
                pltpu.make_async_copy(src, dst, orecv_sem.at[kappa]).start()

        @pl.when(jnp.logical_not(home))
        def _():
            copy = remote(src, dst, osend_sem.at[t], orecv_sem.at[kappa], sigma, owner)
            copy.start() if act == "start" else copy.wait_send()

    def finalize(t):
        swap(t).wait_recv()
        place = pl.ds(pl.multiple_of(me_s * tok, tok), tok)
        total = dkv[t, place, :] + xch[t]
        owner = 2 * t + me_s
        cosine = jnp.where(low, cos_ref[owner], 1.0)
        sine = jnp.where(low, sin_ref[owner], 0.0)
        back = total * cosine - rotate_pairs(total) * sine
        done[t, :, pl.ds(2 * HD, 2 * HD)] = back.astype(BF16)
        deliver(t, "start")

    def step(n, carry):
        t = steps - 1 - n
        pltpu.make_async_copy(do_ref.at[:, pl.ds(0, 2 * HD)], in_ref.at[t], recv_sem.at[t]).wait()
        d_two = in_ref[t].astype(F32)
        q_two = q_ref[t].astype(F32)
        dt = stacked_heads(jnp.transpose(d_two))
        qt = stacked_heads(jnp.transpose(q_two))
        zero = jnp.zeros_like(dt)
        dm = jnp.concatenate([zero, dt], 0).astype(BF16)
        qm = jnp.concatenate([qt, zero], 0).astype(BF16)
        delta = jnp.sum(ot_ref[t] * dt, 0, keepdims=True)
        right = jnp.concatenate(
            [
                jnp.where(low, q_two, 0.0),
                jnp.where(low, pltpu.roll(q_two, HD, 1), 0.0),
                jnp.where(low, 0.0, pltpu.roll(d_two, HD, 1)),
                jnp.where(low, 0.0, d_two),
            ],
            0,
        ).astype(BF16)
        stat = stat_ref[t]
        lse, start = stat[0:1], stat[1:2].astype(jnp.int32)
        qpos = (2 * t + me_s) * tok + qrow

        def piece(u, dq, last):
            keys = kv_ref[u]
            score = mm(keys, qm)
            kpos = u * wide + lax.broadcasted_iota(jnp.int32, score.shape, 0)
            mask = kpos >= start
            if last:
                mask &= kpos <= qpos
            prob = jnp.where(mask, jnp.exp(score - lse), 0.0)
            dprob = mm(keys, dm)
            dscore = (prob * (dprob - delta)).astype(BF16)
            both = jnp.concatenate([dscore, prob.astype(BF16)], 1)
            dkv[u] += mm(both, right)
            return dq + mm(kvt_ref[u, :HD, :], dscore)

        dq = jnp.zeros((HD, wide), F32)
        dq = lax.fori_loop(0, t, lambda u, s: piece(u, s, False), dq)
        dq = piece(t, dq, True) * HD ** (-0.5)
        upright = jnp.transpose(jnp.concatenate([dq[:, :tok], dq[:, tok:]], 0))
        owner = 2 * t + me_s
        back = upright * cos_ref[owner] - rotate_pairs(upright) * sin_ref[owner]
        done[t, :, pl.ds(0, 2 * HD)] = back.astype(BF16)
        part[t] = dkv[t, pl.ds(pl.multiple_of((1 - me_s) * tok, tok), tok), :]
        swap(t).start()

        @pl.when(n > 0)
        def _():
            finalize(t + 1)

        return carry

    lax.fori_loop(0, steps, step, 0)
    finalize(0)

    def finish(n, carry):
        k, chip, mine, src = outgoing(n)

        @pl.when(jnp.logical_not(mine))
        def _():
            remote(
                src, in_ref.at[slot], send_sem.at[k], recv_sem.at[slot], dest_core, chip
            ).wait_send()

        return carry

    lax.fori_loop(0, KV, finish, 0)

    def finish_steps(t, carry):
        swap(t).wait_send()
        deliver(t, "wait")
        return carry

    lax.fori_loop(0, steps, finish_steps, 0)

    def gather(k, carry):
        pltpu.make_async_copy(done.at[0], out_ref.at[k], orecv_sem.at[k]).wait()
        return carry

    lax.fori_loop(0, KV, gather, 0)
    for n in (1, 2, 3):
        give_mix(n).wait()
        for i in range(3):
            give_weight(n, i).wait()


def attention_backward(
    blocks, d_o, kv, kvt, q_two, out_t, stat, cos_all, sin_all, mix, dwg, dwu, dwd
):
    tok = q_two.shape[1]
    steps = blocks // 2
    vm = pl.BlockSpec(memory_space=pltpu.VMEM)
    hbm = pl.BlockSpec(memory_space=pl.ANY)
    dma = pltpu.SemaphoreType.DMA
    return pl.pallas_call(
        functools.partial(attention_backward_kernel, blocks),
        out_shape=(
            jax.ShapeDtypeStruct((KV, tok, 4 * HD), BF16),
            jax.ShapeDtypeStruct(mix.shape, BF16),
            jax.ShapeDtypeStruct((3, *dwg.shape[1:]), BF16),
            jax.ShapeDtypeStruct((3, *dwu.shape[1:]), BF16),
            jax.ShapeDtypeStruct((3, *dwd.shape[1:]), BF16),
        ),
        in_specs=[vm] * 8 + [hbm] * 4,
        out_specs=(vm,) + (hbm,) * 4,
        scratch_shapes=[
            pltpu.VMEM((steps, tok, 2 * HD), BF16),
            pltpu.VMEM((steps, 2 * tok, 2 * HD), F32),
            pltpu.VMEM((steps, tok, 2 * HD), F32),
            pltpu.VMEM((steps, tok, 2 * HD), F32),
            pltpu.VMEM((steps, tok, 4 * HD), BF16),
            dma((KV,)),
            dma((steps,)),
            dma((steps,)),
            dma((steps,)),
            dma((steps,)),
            dma((KV,)),
            dma((3,)),
            dma((3,)),
            dma((3, 3)),
            dma((3, 3)),
        ],
        compiler_params=pltpu.CompilerParams(
            collective_id=1, has_side_effects=True, vmem_limit_bytes=VMEM_LIMIT
        ),
        name="attention_backward",
    )(d_o, kv, kvt, q_two, out_t, stat, cos_all, sin_all, mix, dwg, dwu, dwd)


def mixture_kernel(
    x_ref,
    g_ref,
    wg_ref,
    wu_ref,
    wd_ref,
    g_all,
    wg_all,
    wu_all,
    wd_all,
    mix_own,
    mix_peer,
    d_in,
    dwg_out,
    dwu_out,
    dwd_out,
    x_in,
    x_t,
    g_in,
    wg,
    wu,
    wd,
    hc,
    dg,
    du,
    acc_o,
    acc_d,
    acc_c,
    d_send,
    d_recv,
    xg,
    xu,
    xd,
    load_sem,
    gload_sem,
    send_sem,
    recv_sem,
    bsend_sem,
    brecv_sem,
    psend_sem,
    precv_sem,
    store_sem,
):
    me_s = lax.axis_index("seq")
    me_b = lax.axis_index("blk")
    line, plane = me_b // 4, lax.rem(me_b, 4)
    tok, d = g_in.shape[1:]
    ff = wg.shape[2]
    barrier = pltpu.get_barrier_semaphore()
    places = [(me_s, flip(line, n) * 4 + plane) for n in (1, 2, 3)] + [(1 - me_s, me_b)]
    for place in places:
        pl.semaphore_signal(barrier, inc=1, device_id=place, device_id_type=MESH)

    owns = ((wg_ref, wg_all, wg), (wu_ref, wu_all, wu), (wd_ref, wd_all, wd))

    def load_own(i):
        return pltpu.make_async_copy(owns[i][0], owns[i][2].at[plane], load_sem.at[i, plane])

    def load_other(i, e):
        return pltpu.make_async_copy(owns[i][1].at[e], owns[i][2].at[e], load_sem.at[i, e])

    for i in range(3):
        load_own(i).start()
        for n in (1, 2, 3):
            load_other(i, flip(plane, n)).start()

    def load_grad(n):
        src = g_ref if n == 0 else g_all.at[flip(line, n)]
        return pltpu.make_async_copy(src, g_in.at[n], gload_sem.at[n])

    for n in range(4):
        load_grad(n).start()
    pl.semaphore_wait(barrier, 4)

    def spread(n):
        return remote(
            x_ref, x_in.at[n], send_sem.at[n - 1], recv_sem.at[n - 1], *places[n - 1]
        )

    for n in (1, 2, 3):
        spread(n).start()
    x_in[0] = x_ref[...]
    for n in range(4):
        load_grad(n).wait()

    def load_wait(e, carry):
        for i in range(3):
            load_other(i, e).wait()
        return carry

    lane = lax.broadcasted_iota(jnp.int32, (tok, 128), 1)

    def block(n, carry):
        @pl.when(n > 0)
        def _():
            pltpu.make_async_copy(x_ref, x_in.at[n], recv_sem.at[jnp.maximum(n - 1, 0)]).wait()

        acc_o[...] = jnp.zeros_like(acc_o)
        acc_d[...] = jnp.zeros_like(acc_d)
        acc_c[...] = jnp.zeros_like(acc_c)
        rows = pl.ds(pl.multiple_of(n * tok, tok), tok)

        def expert(e, carry):
            @pl.when(n == 0)
            def _():
                load_wait(e, 0)

            x = x_in[n, :, :d]
            here = lane == line * 4 + e
            share = jnp.sum(
                jnp.where(here, x_in[n, :, d:].astype(F32), 0.0), 1, keepdims=True
            )
            gate = mm(x, wg[e])
            up = mm(x, wu[e])
            dh = mm(g_in[n], wd[e], NT)
            sg = jax.nn.sigmoid(gate)
            act = gate * sg
            hidden = act * up
            acc_c[...] += jnp.where(here, jnp.sum(dh * hidden, 1, keepdims=True), 0.0)
            dh = dh * share
            hcb = (hidden * share).astype(BF16)
            dgb = (dh * up * sg * (1.0 + gate * (1.0 - sg))).astype(BF16)
            dub = (dh * act).astype(BF16)
            hc[e, rows, :] = hcb
            dg[e, rows, :] = dgb
            du[e, rows, :] = dub
            acc_o[...] += mm(hcb, wd[e])
            acc_d[...] += mm(dgb, wg[e], NT) + mm(dub, wu[e], NT)
            return carry

        lax.fori_loop(0, 4, expert, 0)

        @pl.when(n == 0)
        def _():
            mix_own[...] = acc_o[...]
            d_in[:, :d] = acc_d[...]
            d_in[:, d:] = acc_c[...]

        for m in (1, 2, 3):

            @pl.when(n == m)
            def _():
                mix_peer[m - 1] = acc_o[...].astype(BF16)
                d_send[m - 1, :, :d] = acc_d[...].astype(BF16)
                high = acc_c[...].astype(BF16).astype(F32)
                rest = acc_c[...] - high
                d_send[m - 1, :, d:] = (high + pltpu.roll(rest, 32, 1)).astype(BF16)
                give_back(m).start()

        x_t[:, rows] = jnp.transpose(x_in[n, :, :d].astype(F32)).astype(BF16)
        return carry

    def give_back(n):
        return remote(
            d_send.at[n - 1],
            d_recv.at[n - 1],
            bsend_sem.at[n - 1],
            brecv_sem.at[n - 1],
            *places[n - 1],
        )

    lax.fori_loop(0, 4, block, 0)

    half, dhalf = d // 2, ff // 2
    theirs = pl.multiple_of((1 - me_s) * half, half)
    dtheirs = pl.multiple_of((1 - me_s) * dhalf, dhalf)
    mine = pl.multiple_of(me_s * half, half)
    dmine = pl.multiple_of(me_s * dhalf, dhalf)
    g_rows = g_in.reshape(4 * tok, d)

    def swap(i, e):
        src = (wg.at[e, pl.ds(0, half)], wu.at[e, pl.ds(0, half)], wd.at[e, pl.ds(0, dhalf)])[i]
        dst = (xg, xu, xd)[i].at[e]
        return remote(src, dst, psend_sem.at[i, e], precv_sem.at[i, e], *places[3])

    def store(i, e):
        return pltpu.make_async_copy(
            (xg, xu, xd)[i].at[e], (dwg_out, dwu_out, dwd_out)[i].at[e], store_sem.at[i, e]
        )

    def give(e, carry):
        left = x_t[pl.ds(theirs, half), :]
        wg[e, :half, :] = mm(left, dg[e]).astype(BF16)
        swap(0, e).start()
        wu[e, :half, :] = mm(left, du[e]).astype(BF16)
        swap(1, e).start()
        wd[e, :dhalf, :] = mm(hc[e, :, pl.ds(dtheirs, dhalf)], g_rows[...], TN).astype(BF16)
        swap(2, e).start()
        return carry

    lax.fori_loop(0, 4, give, 0)

    def keep(e, carry):
        left = x_t[pl.ds(mine, half), :]
        own = mm(left, dg[e])
        swap(0, e).wait_recv()
        xg[e] = (own + xg[e].astype(F32)).astype(BF16)
        store(0, e).start()
        own = mm(left, du[e])
        swap(1, e).wait_recv()
        xu[e] = (own + xu[e].astype(F32)).astype(BF16)
        store(1, e).start()
        own = mm(hc[e, :, pl.ds(dmine, dhalf)], g_rows[...], TN)
        swap(2, e).wait_recv()
        xd[e] = (own + xd[e].astype(F32)).astype(BF16)
        store(2, e).start()
        return carry

    lax.fori_loop(0, 4, keep, 0)

    for n in (1, 2, 3):
        give_back(n).wait_recv()
        d_in[:, :d] += d_recv[n - 1, :, :d].astype(F32)
        tail = d_recv[n - 1, :, d:].astype(F32)
        both = tail + pltpu.roll(tail, 96, 1)
        d_in[:, d:] += jnp.where(lane < 32, both, 0.0)
    for n in (1, 2, 3):
        spread(n).wait_send()
        give_back(n).wait_send()

    def finish(e, carry):
        for i in range(3):
            swap(i, e).wait_send()
            store(i, e).wait()
        return carry

    lax.fori_loop(0, 4, finish, 0)


def mixture(x, g, w_gate, w_up, w_down, g_all, wg_all, wu_all, wd_all):
    tok, d = g.shape
    ff = w_gate.shape[1]
    vm = pl.BlockSpec(memory_space=pltpu.VMEM)
    hbm = pl.BlockSpec(memory_space=pl.ANY)
    dma = pltpu.SemaphoreType.DMA
    vmem = pltpu.VMEM
    return pl.pallas_call(
        mixture_kernel,
        out_shape=(
            jax.ShapeDtypeStruct((tok, d), F32),
            jax.ShapeDtypeStruct((3, tok, d), BF16),
            jax.ShapeDtypeStruct((tok, d + 128), F32),
            jax.ShapeDtypeStruct((4, d // 2, ff), BF16),
            jax.ShapeDtypeStruct((4, d // 2, ff), BF16),
            jax.ShapeDtypeStruct((4, ff // 2, d), BF16),
        ),
        in_specs=[vm] + [hbm] * 8,
        out_specs=(vm, vm, vm, hbm, hbm, hbm),
        scratch_shapes=[
            vmem((4, tok, d + 128), BF16),
            vmem((d, 4 * tok), BF16),
            vmem((4, tok, d), BF16),
            vmem((4, d, ff), BF16),
            vmem((4, d, ff), BF16),
            vmem((4, ff, d), BF16),
            vmem((4, 4 * tok, ff), BF16),
            vmem((4, 4 * tok, ff), BF16),
            vmem((4, 4 * tok, ff), BF16),
            vmem((tok, d), F32),
            vmem((tok, d), F32),
            vmem((tok, 128), F32),
            vmem((3, tok, d + 128), BF16),
            vmem((3, tok, d + 128), BF16),
            vmem((4, d // 2, ff), BF16),
            vmem((4, d // 2, ff), BF16),
            vmem((4, ff // 2, d), BF16),
            dma((3, 4)),
            dma((4,)),
            dma((3,)),
            dma((3,)),
            dma((3,)),
            dma((3,)),
            dma((3, 4)),
            dma((3, 4)),
            dma((3, 4)),
        ],
        compiler_params=pltpu.CompilerParams(
            collective_id=2, has_side_effects=True, vmem_limit_bytes=VMEM_LIMIT
        ),
        name="mixture",
    )(x, g, w_gate, w_up, w_down, g_all, wg_all, wu_all, wd_all)


STAGES = 6


class Summed:
    def __init__(self, refs, send_sem, recv_sem, fin):
        self.out, self.arrived, self.acc, self.part, self.plane_in, self.line_in = refs
        self.send_sem, self.recv_sem, self.fin = send_sem, recv_sem, fin
        self.me_s = lax.axis_index("seq")
        me_b = lax.axis_index("blk")
        self.line, self.plane = me_b // 4, lax.rem(me_b, 4)
        self.sibling = [(1 - self.me_s, me_b)]
        self.planes = [(self.me_s, self.line * 4 + flip(self.plane, n)) for n in (1, 2, 3)]
        self.lines = [(self.me_s, flip(self.line, n) * 4 + self.plane) for n in (1, 2, 3)]
        rows = fin.shape[0]
        self.half, self.quarter, self.piece = rows // 2, rows // 8, rows // 32

    def rows(self, start, size):
        return pl.ds(pl.multiple_of(start, size), size)

    def halves(self):
        theirs = self.rows((1 - self.me_s) * self.half, self.half)
        return theirs, self.rows(self.me_s * self.half, self.half)

    def copy(self, stage, n):
        sems = self.send_sem.at[stage, n], self.recv_sem.at[stage, n]
        base = self.me_s * self.half
        if stage == 0:
            return remote(self.out, self.arrived, *sems, *self.sibling[n])
        if stage == 1:
            src = self.part.at[self.rows(flip(self.plane, n + 1) * self.quarter, self.quarter)]
            return remote(src, self.plane_in.at[n], *sems, *self.planes[n])
        if stage == 2:
            at = self.plane * self.quarter + flip(self.line, n + 1) * self.piece
            src = self.part.at[self.rows(at, self.piece)]
            return remote(src, self.line_in.at[n], *sems, *self.lines[n])
        if stage == 3:
            at = base + self.plane * self.quarter + self.line * self.piece
            part = self.fin.at[self.rows(at, self.piece)]
            return remote(part, part, *sems, *self.lines[n])
        if stage == 4:
            part = self.fin.at[self.rows(base + self.plane * self.quarter, self.quarter)]
            return remote(part, part, *sems, *self.planes[n])
        part = self.fin.at[self.rows(base, self.half)]
        return remote(part, part, *sems, *self.sibling[n])

    def start(self, stage):
        for n in range(1) if stage in (0, 5) else (2, 0, 1):
            self.copy(stage, n).start()

    def arrive(self, stage):
        for n in range(1 if stage in (0, 5) else 3):
            self.copy(stage, n).wait_recv()

    def pair(self):
        self.arrive(0)
        self.part[...] = (self.acc[...] + self.arrived[...].astype(F32)).astype(BF16)
        self.start(1)

    def over_plane(self):
        self.arrive(1)
        here = self.rows(self.plane * self.quarter, self.quarter)
        total = self.part[here, :].astype(F32)
        for n in range(3):
            total = total + self.plane_in[n].astype(F32)
        self.part[here, :] = total.astype(BF16)
        self.start(2)

    def over_line(self):
        self.arrive(2)
        at = self.plane * self.quarter + self.line * self.piece
        total = self.part[self.rows(at, self.piece), :].astype(F32)
        for n in range(3):
            total = total + self.line_in[n].astype(F32)
        self.fin[self.rows(self.me_s * self.half + at, self.piece), :] = total.astype(BF16)
        self.start(3)

    def back(self, stage):
        self.arrive(stage)
        self.start(stage + 1)

    def finish(self):
        self.arrive(5)
        for stage in range(STAGES):
            for n in range(1 if stage in (0, 5) else 3):
                self.copy(stage, n).wait_send()


def summed_scratch(rows, width):
    vmem, dma = pltpu.VMEM, pltpu.SemaphoreType.DMA
    return [
        vmem((rows // 2, width), BF16),
        vmem((rows // 2, width), BF16),
        vmem((rows // 2, width), F32),
        vmem((rows // 2, width), BF16),
        vmem((3, rows // 8, width), BF16),
        vmem((3, rows // 32, width), BF16),
        dma((STAGES, 3)),
        dma((STAGES, 3)),
    ]


def tail_kernel(
    got,
    xa_ref,
    x_ref,
    gain_ref,
    dh_ref,
    wq_ref,
    wk_ref,
    wv_ref,
    ao_ref,
    datt_ref,
    xl_ref,
    dlog_ref,
    dgain2_ref,
    eg_ref,
    eu_ref,
    ed_ref,
    eg_in,
    eu_in,
    ed_in,
    dx_ref,
    gsum_ref,
    fin_o,
    fin_q,
    fin_kv,
    eg_out,
    eu_out,
    ed_out,
    d_all,
    ev,
    edv,
    gbuf,
    grv,
    load_sem,
    esend,
    erecv,
    gsend,
    grecv,
    *summing,
):
    me_s = lax.axis_index("seq")
    me_b = lax.axis_index("blk")
    plane = lax.rem(me_b, 4)
    tok, d = xa_ref.shape
    sums = [
        Summed(summing[8 * i : 8 * i + 6], *summing[8 * i + 6 : 8 * i + 8], fin)
        for i, fin in enumerate((fin_o, fin_q, fin_kv))
    ]
    for_out, for_q, for_kv = sums
    [sibling], planes, lines = for_q.sibling, for_q.planes, for_q.lines
    barrier = pltpu.get_barrier_semaphore()
    for place in [sibling, *planes, *lines]:
        pl.semaphore_signal(barrier, inc=1, device_id=place, device_id_type=MESH)

    experts = ((eg_ref, eg_in, ev.at[0]), (eu_ref, eu_in, ev.at[1]), (ed_ref, ed_in, edv))

    def loads(i):
        own, arrived, dst = experts[i]
        return (
            pltpu.make_async_copy(own.at[plane], dst.at[0], load_sem.at[i, 0]),
            pltpu.make_async_copy(arrived, dst.at[pl.ds(1, 3)], load_sem.at[i, 1]),
        )

    for i in range(3):
        for copy in loads(i):
            copy.start()
    pl.semaphore_wait(barrier, 7)
    theirs, mine = for_q.halves()
    for_out.out[:, :d] = mm(ao_ref[:, theirs], datt_ref[...], TN).astype(BF16)
    for_out.out[:, d:] = mm(xl_ref[:, theirs], dlog_ref[...], TN).astype(BF16)
    for_out.start(0)

    low = lax.broadcasted_iota(jnp.int32, (tok, 2 * HD), 1) < HD
    for m in range(KV // 2):
        a, b = got[2 * m], got[2 * m + 1]
        d_all[:, 2 * m * 2 * HD : (2 * m + 1) * 2 * HD] = a[:, : 2 * HD]
        d_all[:, (2 * m + 1) * 2 * HD : (2 * m + 2) * 2 * HD] = b[:, : 2 * HD]
        ka, kb = a[:, 2 * HD :].astype(F32), b[:, 2 * HD :].astype(F32)
        at = H * HD + m * 2 * HD
        d_all[:, at : at + 2 * HD] = jnp.where(low, ka, pltpu.roll(kb, HD, 1)).astype(BF16)
        at += KV * HD
        d_all[:, at : at + 2 * HD] = jnp.where(low, pltpu.roll(ka, HD, 1), kb).astype(BF16)
    parts = ((for_q, slice(0, H * HD)), (for_kv, slice(H * HD, (H + 2 * KV) * HD)))
    for item, cols in parts:
        item.out[...] = mm(xa_ref[:, theirs], d_all[:, cols], TN).astype(BF16)
        item.start(0)
    for_out.acc[:, :d] = mm(ao_ref[:, mine], datt_ref[...], TN)
    for_out.acc[:, d:] = mm(xl_ref[:, mine], dlog_ref[...], TN)
    for_out.pair()
    for item, cols in parts:
        item.acc[...] = mm(xa_ref[:, mine], d_all[:, cols], TN)
        item.pair()

    grad = (
        mm(d_all[:, : H * HD], wq_ref[...], NT)
        + mm(d_all[:, H * HD : (H + KV) * HD], wk_ref[...], NT)
        + mm(d_all[:, (H + KV) * HD :], wv_ref[...], NT)
    )
    xs = x_ref[...].astype(F32)
    scale = rms_scale(xs)
    scaled = grad * gain_ref[...]
    inner = jnp.mean(scaled * xs, -1, keepdims=True)
    dx_ref[...] = dh_ref[...] + scale * scaled - xs * scale**3 * inner
    gbuf[0, :8, :] = jnp.sum((grad * xs * scale).reshape(tok // 8, 8, d), 0)
    gbuf[0, 8:, :] = dgain2_ref[...]

    stages = [[sibling], planes, lines]

    def gain_copy(s, n):
        at = (0, 1, 4)[s] + n
        return remote(gbuf.at[s], grv.at[at], gsend.at[at], grecv.at[at], *stages[s][n])

    def gain_stage(s):
        for n in range(len(stages[s])):
            gain_copy(s, n).start()

    def gain_total(s):
        total = gbuf[s]
        for n in range(len(stages[s])):
            gain_copy(s, n).wait_recv()
            total = total + grv[(0, 1, 4)[s] + n]
        return total

    gain_stage(0)
    for_out.over_plane()

    outs = (eg_out, eu_out, ed_out)

    def expert_swap(i):
        rows = outs[i].shape[0] // 2
        part = outs[i].at[pl.ds(pl.multiple_of(me_s * rows, rows), rows)]
        return remote(part, part, esend.at[i], erecv.at[i], *sibling)

    for i in range(3):
        for copy in loads(i):
            copy.wait()
        terms = experts[i][2]
        rows = outs[i].shape[0] // 2
        total = terms[0].astype(F32)
        for n in (1, 2, 3):
            total = total + terms[n].astype(F32)
        outs[i][pl.ds(pl.multiple_of(me_s * rows, rows), rows), :] = total.astype(BF16)
        expert_swap(i).start()
    gbuf[1] = gain_total(0)
    gain_stage(1)
    for_q.over_plane()
    for_out.over_line()
    for_kv.over_plane()
    gbuf[2] = gain_total(1)
    gain_stage(2)
    for_q.over_line()
    for_out.back(3)
    for_kv.over_line()
    for_q.back(3)
    for_kv.back(3)
    gsum_ref[...] = gain_total(2)
    for item in sums:
        item.back(4)
    for item in sums:
        item.finish()
    for i in range(3):
        expert_swap(i).wait()
    for s in range(3):
        for n in range(len(stages[s])):
            gain_copy(s, n).wait_send()


def tail(blocks_in, own, arrived):
    tok, d = blocks_in[1].shape
    ff = own[0].shape[2]
    widths = (d + 128, H * HD, 2 * KV * HD)
    vm = pl.BlockSpec(memory_space=pltpu.VMEM)
    hbm = pl.BlockSpec(memory_space=pl.ANY)
    dma = pltpu.SemaphoreType.DMA
    vmem = pltpu.VMEM
    return pl.pallas_call(
        tail_kernel,
        out_shape=(
            jax.ShapeDtypeStruct((tok, d), F32),
            jax.ShapeDtypeStruct((16, d), F32),
            *(jax.ShapeDtypeStruct((d, width), BF16) for width in widths),
            jax.ShapeDtypeStruct((d, ff), BF16),
            jax.ShapeDtypeStruct((d, ff), BF16),
            jax.ShapeDtypeStruct((ff, d), BF16),
        ),
        in_specs=[vm] * len(blocks_in) + [hbm] * 6,
        out_specs=(vm,) * 8,
        scratch_shapes=[
            vmem((tok, (H + 2 * KV) * HD), BF16),
            vmem((2, 4, d // 2, ff), BF16),
            vmem((4, ff // 2, d), BF16),
            vmem((3, 16, d), F32),
            vmem((7, 16, d), F32),
            dma((3, 2)),
            dma((3,)),
            dma((3,)),
            dma((7,)),
            dma((7,)),
            *(ref for width in widths for ref in summed_scratch(d, width)),
        ],
        compiler_params=pltpu.CompilerParams(
            collective_id=3, has_side_effects=True, vmem_limit_bytes=VMEM_LIMIT
        ),
        name="tail",
    )(*blocks_in, *own, *arrived)


D = 1024
HIGH = lax.Precision.HIGHEST


def rope_tables(positions):
    half = HD // 2
    freq = jnp.exp(-math.log(10000.0) * jnp.arange(half, dtype=jnp.float32) * 2.0 / HD)
    angle = positions.astype(jnp.float32)[:, None] * freq[None, :]
    cosine = jnp.concatenate([jnp.cos(angle), jnp.cos(angle)], -1)
    sine = jnp.concatenate([jnp.sin(angle), jnp.sin(angle)], -1)
    return (cosine, sine)


def rotate_half(v):
    half = v.shape[-1] // 2
    return jnp.concatenate([-v[..., half:], v[..., :half]], -1)


def rotary(v, cosine, sine):
    return v * cosine[:, None, :] + rotate_half(v) * sine[:, None, :]


def unrotary(v, cosine, sine):
    return v * cosine[:, None, :] - rotate_half(v) * sine[:, None, :]


def rms_scale(v):
    return lax.rsqrt(jnp.mean(v * v, -1, keepdims=True) + EPS)


def rms_back(inputs, scale_rows, gain, grad):
    scaled = grad * gain
    d_inputs = scale_rows * scaled - inputs * scale_rows**3 * jnp.mean(
        scaled * inputs, -1, keepdims=True
    )
    return (d_inputs, jnp.sum(grad * inputs * scale_rows, 0))


def scores(queries, keys):
    return jnp.einsum("qkgd,skd->kgqs", queries, keys, preferred_element_type=jnp.float32) * HD ** (
        -0.5
    )


def per_device_plain(
    tokens,
    segments,
    routes,
    route_weight,
    norm1_gain,
    w_query,
    w_key,
    w_value,
    w_out,
    norm2_gain,
    w_router,
    w_gate,
    w_up,
    w_down,
    cotangent,
):
    f32 = jnp.float32
    bf16 = jnp.bfloat16
    scale = HD ** (-0.5)
    group = H // KV
    xs = tokens[0].astype(f32)
    tok = xs.shape[0]
    blocks = lax.axis_size("blk")
    length = tok * blocks
    first = lax.axis_index("blk") * tok
    last = first + tok - 1
    positions = first + jnp.arange(tok, dtype=jnp.int32)
    cosine, sine = rope_tables(positions)
    scale1 = rms_scale(xs)
    xa = (xs * scale1 * norm1_gain).astype(bf16)
    query = jnp.dot(xa, w_query, preferred_element_type=f32)
    key = jnp.dot(xa, w_key, preferred_element_type=f32)
    value = jnp.dot(xa, w_value, preferred_element_type=f32).astype(bf16)
    q_rot = rotary(query.reshape(tok, H, HD), cosine, sine).astype(bf16).reshape(tok, KV, group, HD)
    k_rot = rotary(key.reshape(tok, KV, HD), cosine, sine).astype(bf16).reshape(tok, KV * HD)
    seg_float = segments[0].astype(bf16)
    k_all, v_all, seg_all = (
        lax.all_gather(k_rot, "blk", axis=0, tiled=True),
        lax.all_gather(value, "blk", axis=0, tiled=True),
        lax.all_gather(seg_float, "blk", axis=0, tiled=True),
    )
    kblk = min(512, length)
    nblk = length // kblk
    k_blocks = k_all.reshape(nblk, kblk, KV, HD)
    v_blocks = v_all.reshape(nblk, kblk, KV, HD)
    s_blocks = seg_all.reshape(nblk, kblk)
    starts = jnp.arange(nblk, dtype=jnp.int32) * kblk

    def visible(kseg, kstart):
        kpos = kstart + jnp.arange(kblk, dtype=jnp.int32)
        return ((seg_float[:, None] == kseg[None, :]) & (kpos[None, :] <= positions[:, None]))[
            None, None
        ]

    def forward_step(carry, block):
        kb, vb, sb, start = block

        def forward_compute(state):
            running, total, acc = state
            mask = visible(sb, start)
            score = jnp.where(mask, scores(q_rot, kb), NEG)
            newmax = jnp.maximum(running, jnp.max(score, -1))
            expo = jnp.where(mask, jnp.exp(score - newmax[..., None]), 0.0)
            factor = jnp.exp(running - newmax)
            total = total * factor + jnp.sum(expo, -1)
            acc = acc * factor[..., None] + jnp.einsum(
                "kgqs,skd->kgqd", expo.astype(bf16), vb, preferred_element_type=f32
            )
            return (newmax, total, acc)

        return (lax.cond(start <= last, forward_compute, lambda state: state, carry), None)

    init = (
        jnp.full((KV, group, tok), NEG, f32),
        jnp.zeros((KV, group, tok), f32),
        jnp.zeros((KV, group, tok, HD), f32),
    )
    (running, total, acc), unused = lax.scan(
        forward_step, init, (k_blocks, v_blocks, s_blocks, starts)
    )
    lse = running + jnp.log(total)
    o_rows = (acc / total[..., None]).transpose(2, 0, 1, 3)
    att_low = o_rows.reshape(tok, H * HD).astype(bf16)
    h1 = xs + jnp.dot(att_low, w_out, preferred_element_type=f32)
    scale2 = rms_scale(h1)
    xl = (h1 * scale2 * norm2_gain).astype(bf16)
    logits = jnp.dot(xl, w_router, preferred_element_type=f32)
    experts = logits.shape[1]
    route = routes[0]
    rweight = route_weight[0]
    chooser = (route[:, :, None] == jnp.arange(experts, dtype=jnp.int32)[None, None, :]).astype(f32)
    chosen = jnp.sum(chooser * logits[:, None, :], -1)
    gates = jax.nn.softmax(chosen, -1)
    combine = (rweight * gates).astype(bf16)
    cap = min(tok, 2 * tok * TOP // experts)
    member = jnp.sum(chooser, 1)
    before = jnp.asarray(np.tril(np.ones((tok, tok), np.float32), -1))
    order = jnp.dot(before, member, precision=HIGH)
    rank = jnp.sum(chooser * order[:, None, :], -1).astype(jnp.int32)
    slots = route * cap + rank
    placed = jnp.any(
        slots[:, :, None] == jnp.arange(experts * cap, dtype=jnp.int32)[None, None, :], 1
    ).astype(bf16)
    outgoing = jnp.einsum("ts,td->sd", placed, xl, preferred_element_type=f32).astype(bf16)
    incoming = lax.all_to_all(
        outgoing.reshape(experts, cap, D), "blk", split_axis=0, concat_axis=0, tiled=True
    )
    local_exp = w_gate.shape[0]
    incoming = incoming.reshape(blocks, local_exp, cap, D)
    gate_pre = jnp.einsum("necd,edf->necf", incoming, w_gate, preferred_element_type=f32)
    up_pre = jnp.einsum("necd,edf->necf", incoming, w_up, preferred_element_type=f32)
    sigma = jax.nn.sigmoid(gate_pre)
    activated = gate_pre * sigma
    hidden = (activated * up_pre).astype(bf16)
    expert_out = jnp.einsum("necf,efd->necd", hidden, w_down, preferred_element_type=f32).astype(
        bf16
    )
    returned = lax.all_to_all(
        expert_out.reshape(experts, cap, D), "blk", split_axis=0, concat_axis=0, tiled=True
    )
    per_route = jnp.take(returned.reshape(experts * cap, D), slots.reshape(-1), axis=0).reshape(
        tok, TOP, D
    )
    mixture = jnp.einsum("tj,tjd->td", combine, per_route, preferred_element_type=f32)
    result = h1 + mixture
    grad_out = cotangent[0].astype(f32)
    grad_combine = jnp.einsum("td,tjd->tj", grad_out, per_route.astype(f32), precision=HIGH)
    route_grads = (combine.astype(f32)[:, :, None] * grad_out[:, None, :]).astype(bf16)
    grad_slots = (
        jnp.zeros((experts * cap, D), bf16)
        .at[slots.reshape(-1)]
        .set(route_grads.reshape(tok * TOP, D))
    )
    grad_incoming = lax.all_to_all(
        grad_slots.reshape(experts, cap, D), "blk", split_axis=0, concat_axis=0, tiled=True
    )
    grad_incoming = grad_incoming.reshape(blocks, local_exp, cap, D)
    grad_hidden = jnp.einsum("necd,efd->necf", grad_incoming, w_down, preferred_element_type=f32)
    grad_gate = (grad_hidden * up_pre * sigma * (1.0 + gate_pre * (1.0 - sigma))).astype(bf16)
    grad_up = (grad_hidden * activated).astype(bf16)
    d_down = jnp.einsum("necf,necd->efd", hidden, grad_incoming, preferred_element_type=f32)
    d_gate_w = jnp.einsum("necd,necf->edf", incoming, grad_gate, preferred_element_type=f32)
    d_up_w = jnp.einsum("necd,necf->edf", incoming, grad_up, preferred_element_type=f32)
    grad_in = (
        jnp.einsum("necf,edf->necd", grad_gate, w_gate, preferred_element_type=f32)
        + jnp.einsum("necf,edf->necd", grad_up, w_up, preferred_element_type=f32)
    ).astype(bf16)
    grad_back = lax.all_to_all(
        grad_in.reshape(experts, cap, D), "blk", split_axis=0, concat_axis=0, tiled=True
    )
    grad_xl = jnp.einsum(
        "ts,sd->td", placed, grad_back.reshape(experts * cap, D), preferred_element_type=f32
    )
    grad_gates = rweight * grad_combine
    grad_chosen = gates * (grad_gates - jnp.sum(gates * grad_gates, -1, keepdims=True))
    grad_logits = jnp.sum(chooser * grad_chosen[:, :, None], 1).astype(bf16)
    d_router = jnp.einsum("td,te->de", xl, grad_logits, preferred_element_type=f32)
    grad_xl = grad_xl + jnp.einsum("te,de->td", grad_logits, w_router, preferred_element_type=f32)
    grad_h1_norm, d_gain2 = rms_back(h1, scale2, norm2_gain, grad_xl)
    grad_h1 = grad_out + grad_h1_norm
    grad_att = grad_h1.astype(bf16)
    d_out_w = jnp.einsum("ti,td->id", att_low, grad_att, preferred_element_type=f32)
    grad_o = jnp.einsum("td,id->ti", grad_att, w_out, preferred_element_type=f32).astype(bf16)
    grad_o_rows = grad_o.reshape(tok, KV, group, HD)
    delta = jnp.einsum("qkgd,qkgd->kgq", grad_o_rows.astype(f32), o_rows)

    def query_terms(kb, vb, sb, start):
        mask = visible(sb, start)
        prob = jnp.where(mask, jnp.exp(scores(q_rot, kb) - lse[..., None]), 0.0)
        dprob = jnp.einsum("qkgd,skd->kgqs", grad_o_rows, vb, preferred_element_type=f32)
        dscore = (prob * (dprob - delta[..., None])).astype(bf16)
        dq_term = jnp.einsum("kgqs,skd->qkgd", dscore, kb, preferred_element_type=f32) * scale
        return (dq_term, dscore, prob)

    zero_q = jnp.zeros((tok, KV, group, HD), f32)

    def backward_step(grad_q, block):
        kb, vb, sb, start = block

        def backward_compute(acc_q):
            dq_term, dscore, prob = query_terms(kb, vb, sb, start)
            gk = jnp.einsum("kgqs,qkgd->skd", dscore, q_rot, preferred_element_type=f32) * scale
            gv = jnp.einsum(
                "kgqs,qkgd->skd", prob.astype(bf16), grad_o_rows, preferred_element_type=f32
            )
            return (acc_q + dq_term, (gk.reshape(kblk, KV * HD), gv.reshape(kblk, KV * HD)))

        def skip(acc_q):
            empty = jnp.zeros((kblk, KV * HD), f32)
            return (acc_q, (empty, empty))

        return lax.cond(start <= last, backward_compute, skip, grad_q)

    grad_q, (gk_blocks, gv_blocks) = lax.scan(
        backward_step, zero_q, (k_blocks, v_blocks, s_blocks, starts)
    )
    grad_k, grad_v = (
        lax.psum_scatter(
            gk_blocks.reshape(length, KV * HD).astype(jnp.bfloat16),
            "blk",
            scatter_dimension=0,
            tiled=True,
        ).astype(jnp.float32),
        lax.psum_scatter(
            gv_blocks.reshape(length, KV * HD).astype(jnp.bfloat16),
            "blk",
            scatter_dimension=0,
            tiled=True,
        ).astype(jnp.float32),
    )
    grad_qr = unrotary(grad_q.reshape(tok, H, HD), cosine, sine).reshape(tok, H * HD).astype(bf16)
    grad_kr = unrotary(grad_k.reshape(tok, KV, HD), cosine, sine).reshape(tok, KV * HD).astype(bf16)
    grad_vr = grad_v.astype(bf16)
    d_query = jnp.einsum("td,te->de", xa, grad_qr, preferred_element_type=f32)
    d_key = jnp.einsum("td,te->de", xa, grad_kr, preferred_element_type=f32)
    d_value = jnp.einsum("td,te->de", xa, grad_vr, preferred_element_type=f32)
    grad_xa = (
        jnp.einsum("te,de->td", grad_qr, w_query, preferred_element_type=f32)
        + jnp.einsum("te,de->td", grad_kr, w_key, preferred_element_type=f32)
        + jnp.einsum("te,de->td", grad_vr, w_value, preferred_element_type=f32)
    )
    grad_x_norm, d_gain1 = rms_back(xs, scale1, norm1_gain, grad_xa)
    grad_x = grad_h1 + grad_x_norm
    summed = lax.psum(
        (d_gain1, d_query, d_key, d_value, d_out_w, d_gain2, d_router), ("seq", "blk")
    )
    expert_summed = (
        lax.psum(d_gate_w.astype(jnp.bfloat16), "seq").astype(jnp.float32),
        lax.psum(d_up_w.astype(jnp.bfloat16), "seq").astype(jnp.float32),
        lax.psum(d_down.astype(jnp.bfloat16), "seq").astype(jnp.float32),
    )
    return (
        result.astype(bf16)[None],
        grad_x[None],
        summed[0],
        summed[1],
        summed[2],
        summed[3],
        summed[4],
        summed[5],
        summed[6],
        expert_summed[0],
        expert_summed[1],
        expert_summed[2],
    )


def tables(length):
    half = HD // 2
    freq = np.exp(-math.log(10000.0) * np.arange(half, dtype=np.float32) * 2.0 / HD).astype(np.float32)
    angle = np.arange(length, dtype=np.float32)[:, None] * freq[None, :]
    return np.tile(np.cos(angle), (1, 4)), np.tile(np.sin(angle), (1, 4))


def per_device(
    tokens,
    segments,
    routes,
    route_weight,
    norm1_gain,
    w_query,
    w_key,
    w_value,
    w_out,
    norm2_gain,
    w_router,
    w_gate,
    w_up,
    w_down,
    cotangent,
):
    xs = tokens[0].astype(F32)
    tok, d = xs.shape
    blocks = lax.axis_size("blk")
    experts = w_router.shape[1]
    cos_np, sin_np = tables(tok * blocks)
    cos_all = jnp.asarray(cos_np.reshape(blocks, tok, 2 * HD))
    sin_all = jnp.asarray(sin_np.reshape(blocks, tok, 2 * HD))
    seg = jnp.pad(segments[0].astype(BF16).reshape(2, tok // 2), ((0, 14), (0, 0)))
    gain1 = norm1_gain[None]
    g_low = cotangent[0]
    att_low, xa, *kept = attention_forward(
        blocks,
        tokens[0],
        gain1,
        w_query,
        w_key,
        w_value,
        seg,
        cos_all,
        sin_all,
        g_low,
        w_gate[0],
        w_up[0],
        w_down[0],
    )
    kept, shared = kept[:5], kept[5:]

    h1 = xs + mm(att_low, w_out)
    scale2 = rms_scale(h1)
    xl = (h1 * scale2 * norm2_gain).astype(BF16)
    logits = mm(xl, w_router)
    chooser = routes[0][:, :, None] == jnp.arange(experts, dtype=jnp.int32)[None, None, :]
    routed = jnp.any(chooser, 1)
    rweight = jnp.sum(jnp.where(chooser, route_weight[0][:, :, None], 0.0), 1)
    top = jnp.max(jnp.where(routed, logits, NEG), -1, keepdims=True)
    expo = jnp.where(routed, jnp.exp(logits - top), 0.0)
    gates = expo / jnp.sum(expo, -1, keepdims=True)
    combine = (rweight * gates).astype(BF16)
    sent = jnp.concatenate([xl, jnp.pad(combine, ((0, 0), (0, 128 - experts)))], 1)
    mix_own, mix_peer, d_in, dwg, dwu, dwd = mixture(
        sent, g_low, w_gate[0], w_up[0], w_down[0], *shared
    )

    grad_out = g_low.astype(F32)
    grad_gates = rweight * d_in[:, d : d + experts]
    grad_logits = (
        gates * (grad_gates - jnp.sum(gates * grad_gates, -1, keepdims=True))
    ).astype(BF16)
    grad_xl = d_in[:, :d] + mm(grad_logits, w_router, NT)
    grad_h1_norm, unused = rms_back(h1, scale2, norm2_gain, grad_xl)
    gain2_terms = jnp.sum((grad_xl * h1 * scale2).reshape(tok // 8, 8, d), 0)
    grad_h1 = grad_out + grad_h1_norm
    grad_att = grad_h1.astype(BF16)
    grad_o = mm(grad_att, w_out, NT).astype(BF16)
    got, mix_in, *arrived = attention_backward(
        blocks, grad_o, *kept, cos_all, sin_all, mix_peer, dwg, dwu, dwd
    )
    result = h1 + mix_own + jnp.sum(mix_in.astype(F32), 0)
    blocks_in = (
        got,
        xa,
        tokens[0],
        gain1,
        grad_h1,
        w_query,
        w_key,
        w_value,
        att_low,
        grad_att,
        xl,
        jnp.pad(grad_logits, ((0, 0), (0, 128 - experts))),
        gain2_terms,
    )
    grad_x, gains, d_out, d_query, d_kv, d_gate_w, d_up_w, d_down = tail(
        blocks_in, (dwg, dwu, dwd), arrived
    )
    return (
        result.astype(BF16)[None],
        grad_x[None],
        jnp.sum(gains[:8], 0),
        d_query.astype(F32),
        d_kv[:, : KV * HD].astype(F32),
        d_kv[:, KV * HD :].astype(F32),
        d_out[:, :d].astype(F32),
        jnp.sum(gains[8:], 0),
        d_out[:, d : d + experts].astype(F32),
        d_gate_w[None].astype(F32),
        d_up_w[None].astype(F32),
        d_down[None].astype(F32),
    )


def solution(mesh):
    fused = dict(mesh.shape) == {"seq": 2, "blk": 2 * KV}
    return jax.shard_map(
        per_device if fused else per_device_plain,
        mesh=mesh,
        in_specs=(
            P("seq", "blk", None),
            P("seq", "blk"),
            P("seq", "blk", None),
            P("seq", "blk", None),
            P(),
            P(),
            P(),
            P(),
            P(),
            P(),
            P(),
            P("blk", None, None),
            P("blk", None, None),
            P("blk", None, None),
            P("seq", "blk", None),
        ),
        out_specs=(
            P("seq", "blk", None),
            P("seq", "blk", None),
            P(),
            P(),
            P(),
            P(),
            P(),
            P(),
            P(),
            P("blk", None, None),
            P("blk", None, None),
            P("blk", None, None),
        ),
        check_vma=False,
    )
```

```python
import functools
import math

import jax
import jax.numpy as jnp
import numpy as np
from jax import lax
from jax.experimental import pallas as pl
from jax.experimental.pallas import tpu as pltpu
from jax.sharding import PartitionSpec as P

H = 16
KV = 8
HD = 64
TOP = 8
EPS = 1e-06
NEG = -1e30
F32 = jnp.float32
BF16 = jnp.bfloat16
MESH = pl.DeviceIdType.MESH
VMEM_LIMIT = 60 * 2**20
GRAD_STEPS = (1, 4, 6)
HOP_STEP = 4
NT = (((1,), (1,)), ((), ()))
TN = (((0,), (0,)), ((), ()))


def mm(a, b, dims=(((1,), (0,)), ((), ()))):
    return lax.dot_general(a, b, dims, preferred_element_type=F32)


def remote(src, dst, send, recv, seq, blk):
    return pltpu.make_async_remote_copy(
        src_ref=src,
        dst_ref=dst,
        send_sem=send,
        recv_sem=recv,
        device_id=(seq, blk),
        device_id_type=MESH,
    )


def greet_all(seqs, blocks, me_s, me_b):
    barrier = pltpu.get_barrier_semaphore()
    total = seqs * blocks

    def hello(n, carry):
        other = lax.rem(me_s * blocks + me_b + n, total)
        pl.semaphore_signal(
            barrier,
            inc=1,
            device_id=(other // blocks, lax.rem(other, blocks)),
            device_id_type=MESH,
        )
        return carry

    lax.fori_loop(1, total, hello, 0)
    pl.semaphore_wait(barrier, total - 1)


def flip(place, n):
    if n == 1:
        return place + 1 - 2 * lax.rem(place, 2)
    if n == 2:
        return place + 2 - 4 * (place // 2)
    return 3 - place


def rotate_pairs(u):
    lanes = u.shape[-1]
    half = HD // 2
    lane = lax.broadcasted_iota(jnp.int32, u.shape, u.ndim - 1)
    ahead = pltpu.roll(u, lanes - half, u.ndim - 1)
    behind = pltpu.roll(u, half, u.ndim - 1)
    return jnp.where(lane % HD < half, -ahead, behind)


def stacked_heads(wide):
    return jnp.concatenate([wide[:HD], wide[HD:]], axis=1)


STAGES = 6


class Summed:
    def __init__(self, refs, send_sem, recv_sem, fin):
        self.out, self.arrived, self.acc, self.part, self.plane_in, self.line_in = refs
        self.send_sem, self.recv_sem, self.fin = send_sem, recv_sem, fin
        self.me_s = lax.axis_index("seq")
        me_b = lax.axis_index("blk")
        self.line, self.plane = me_b // 4, lax.rem(me_b, 4)
        self.sibling = [(1 - self.me_s, me_b)]
        self.planes = [(self.me_s, self.line * 4 + flip(self.plane, n)) for n in (1, 2, 3)]
        self.lines = [(self.me_s, flip(self.line, n) * 4 + self.plane) for n in (1, 2, 3)]
        rows = fin.shape[0]
        self.half, self.quarter, self.piece = rows // 2, rows // 8, rows // 32

    def rows(self, start, size):
        return pl.ds(pl.multiple_of(start, size), size)

    def halves(self):
        theirs = self.rows((1 - self.me_s) * self.half, self.half)
        return theirs, self.rows(self.me_s * self.half, self.half)

    def copy(self, stage, n):
        sems = self.send_sem.at[stage, n], self.recv_sem.at[stage, n]
        base = self.me_s * self.half
        if stage == 0:
            return remote(self.out, self.arrived, *sems, *self.sibling[n])
        if stage == 1:
            src = self.part.at[self.rows(flip(self.plane, n + 1) * self.quarter, self.quarter)]
            return remote(src, self.plane_in.at[n], *sems, *self.planes[n])
        if stage == 2:
            at = self.plane * self.quarter + flip(self.line, n + 1) * self.piece
            src = self.part.at[self.rows(at, self.piece)]
            return remote(src, self.line_in.at[n], *sems, *self.lines[n])
        if stage == 3:
            at = base + self.plane * self.quarter + self.line * self.piece
            part = self.fin.at[self.rows(at, self.piece)]
            return remote(part, part, *sems, *self.lines[n])
        if stage == 4:
            part = self.fin.at[self.rows(base + self.plane * self.quarter, self.quarter)]
            return remote(part, part, *sems, *self.planes[n])
        part = self.fin.at[self.rows(base, self.half)]
        return remote(part, part, *sems, *self.sibling[n])

    def start(self, stage):
        for n in range(1) if stage in (0, 5) else (2, 0, 1):
            self.copy(stage, n).start()

    def arrive(self, stage):
        for n in range(1 if stage in (0, 5) else 3):
            self.copy(stage, n).wait_recv()

    def pair(self):
        self.arrive(0)
        self.part[...] = (self.acc[...] + self.arrived[...].astype(F32)).astype(BF16)
        self.start(1)

    def over_plane(self):
        self.arrive(1)
        here = self.rows(self.plane * self.quarter, self.quarter)
        total = self.part[here, :].astype(F32)
        for n in range(3):
            total = total + self.plane_in[n].astype(F32)
        self.part[here, :] = total.astype(BF16)
        self.start(2)

    def over_line(self):
        self.arrive(2)
        at = self.plane * self.quarter + self.line * self.piece
        total = self.part[self.rows(at, self.piece), :].astype(F32)
        for n in range(3):
            total = total + self.line_in[n].astype(F32)
        self.fin[self.rows(self.me_s * self.half + at, self.piece), :] = total.astype(BF16)
        self.start(3)

    def back(self, stage):
        self.arrive(stage)
        self.start(stage + 1)

    def finish(self):
        self.arrive(5)
        for stage in range(STAGES):
            for n in range(1 if stage in (0, 5) else 3):
                self.copy(stage, n).wait_send()


def summed_scratch(rows, width):
    vmem, dma = pltpu.VMEM, pltpu.SemaphoreType.DMA
    return [
        vmem((rows // 2, width), BF16),
        vmem((rows // 2, width), BF16),
        vmem((rows // 2, width), F32),
        vmem((rows // 2, width), BF16),
        vmem((3, rows // 8, width), BF16),
        vmem((3, rows // 32, width), BF16),
        dma((STAGES, 3)),
        dma((STAGES, 3)),
    ]


def attention_forward_kernel(
    blocks,
    x_ref,
    gain_ref,
    wq_ref,
    wk_ref,
    wv_ref,
    seg_ref,
    cos_ref,
    sin_ref,
    g_ref,
    wg_ref,
    wu_ref,
    wd_ref,
    o_ref,
    xa_ref,
    kv_ref,
    kvt_ref,
    q_ref,
    ot_ref,
    stat_ref,
    g_all,
    wg_all,
    wu_all,
    wd_all,
    pay,
    turn,
    in_ref,
    other_ref,
    obuf,
    cnt,
    turn_sem,
    send_sem,
    recv_sem,
    fsend_sem,
    frecv_sem,
    osend_sem,
    orecv_sem,
    gsend_sem,
    grecv_sem,
    wsend_sem,
    wrecv_sem,
    hsend_sem,
    hrecv_sem,
    dsend_sem,
    drecv_sem,
):
    me_s = lax.axis_index("seq")
    me_b = lax.axis_index("blk")
    tok = q_ref.shape[1]
    steps = blocks // 2
    sigma = me_b // KV
    kappa = lax.rem(me_b, KV)
    greet_all(2, blocks, me_s, me_b)
    dest_core = lax.rem(me_b, 2)
    slot = me_b // 2
    line, plane = me_b // 4, lax.rem(me_b, 4)
    weights = ((wg_ref, wg_all), (wu_ref, wu_all), (wd_ref, wd_all))

    def along(k, step, own):
        at = 0 if step < 0 else 1
        return remote(
            g_ref if own else g_all.at[k],
            g_all.at[k],
            gsend_sem.at[at, k],
            grecv_sem.at[k],
            me_s,
            (line + step) * 4 + plane,
        )

    def pass_on(k, step, own=False):
        @pl.when((line + step >= 0) & (line + step < 4))
        def _():
            along(k, step, own).start()

    def pass_distance(j):
        for step in (-1, 1):
            k = line - step * j

            @pl.when((k >= 0) & (k < 4))
            def _():
                pltpu.make_async_copy(g_ref, g_all.at[k], grecv_sem.at[k]).wait()
                pass_on(k, step)

    def half(ref):
        rows = ref.shape[0] // 2
        return ref.at[pl.ds(pl.multiple_of(me_s * rows, rows), rows)]

    def share_weight(n, i):
        own, everyone = weights[i]
        return remote(
            half(own),
            half(everyone.at[plane]),
            wsend_sem.at[n - 1, i],
            wrecv_sem.at[n - 1, i],
            me_s,
            line * 4 + flip(plane, n),
        )

    def diagonal(n, i):
        place = weights[i][1].at[flip(plane, n)]
        rows = place.shape[0] // 2
        start, size = me_s * rows, rows
        if i == 2:
            size = rows // 2
            start = start + (n - 1) * size
        part = place.at[pl.ds(pl.multiple_of(start, size), size)]
        return remote(
            part,
            part,
            dsend_sem.at[n - 1, i],
            drecv_sem.at[n - 1, i],
            me_s,
            line * 4 + flip(plane, 3 - n),
        )

    def diagonal_in(n, i):
        place = weights[i][1].at[flip(plane, 3)]
        rows = place.shape[0] // 2
        start, size = me_s * rows, rows
        if i == 2:
            size = rows // 2
            start = start + (2 - n) * size
        part = place.at[pl.ds(pl.multiple_of(start, size), size)]
        return pltpu.make_async_copy(part, part, drecv_sem.at[2 - n, i])

    def pass_weight(n, i):
        arrived = half(weights[i][1].at[flip(plane, n)])
        return remote(
            arrived, arrived, hsend_sem.at[n - 1, i], hrecv_sem.at[n - 1, i], 1 - me_s, me_b
        )

    tables_in = [
        pltpu.make_async_copy(src.at[me_b], turn.at[i], turn_sem.at[i])
        for i, src in enumerate((cos_ref, sin_ref))
    ]
    for copy in tables_in:
        copy.start()
    xs = x_ref[...].astype(F32)
    xa = (xs * rms_scale(xs) * gain_ref[...]).astype(BF16)
    xa_ref[...] = xa
    for copy in tables_in:
        copy.wait()
    cosine, sine = turn[0], turn[1]
    low = lax.broadcasted_iota(jnp.int32, (tok, 2 * HD), 1) < HD
    pay[:, tok:, : 2 * HD] = jnp.zeros((KV, 16, 2 * HD), BF16)
    for m in range(KV // 2):
        pair = slice(m * 2 * HD, (m + 1) * 2 * HD)
        keys = mm(xa, wk_ref[:, pair])
        keys = keys * cosine + rotate_pairs(keys) * sine
        values = mm(xa, wv_ref[:, pair])
        first = jnp.where(low, keys, pltpu.roll(values, HD, 1))
        second = jnp.where(low, pltpu.roll(keys, HD, 1), values)
        pay[2 * m, :tok, 2 * HD :] = first.astype(BF16)
        pay[2 * m + 1, :tok, 2 * HD :] = second.astype(BF16)
        for k in (2 * m, 2 * m + 1):
            query = mm(xa, wq_ref[:, k * 2 * HD : (k + 1) * 2 * HD])
            query = (query * cosine + rotate_pairs(query) * sine) * HD ** (-0.5)
            pay[k, :tok, : 2 * HD] = query.astype(BF16)
            pay[k, tok:, 2 * HD :] = seg_ref[...]
    def payload(n):
        k = lax.rem(me_b + n, KV)
        chip = me_s * KV + k
        mine = (dest_core == me_s) & (chip == me_b)
        return k, chip, mine

    def send_payload(n, carry):
        k, chip, mine = payload(n)

        @pl.when(mine)
        def _():
            pltpu.make_async_copy(pay.at[k], in_ref.at[slot], recv_sem.at[slot]).start()

        @pl.when(jnp.logical_not(mine))
        def _():
            remote(
                pay.at[k], in_ref.at[slot], send_sem.at[k], recv_sem.at[slot], dest_core, chip
            ).start()

        return carry

    lax.fori_loop(0, KV, send_payload, 0)
    for i in range(3):
        share_weight(1, (0, 2, 1)[i]).start()
        share_weight(2, (1, 2, 0)[i]).start()

    def arrival(t):
        return pltpu.make_async_copy(pay.at[0], in_ref.at[t], recv_sem.at[t])

    def forward(t):
        return remote(
            in_ref.at[t, :, pl.ds(2 * HD, 2 * HD)],
            other_ref.at[t],
            fsend_sem.at[t],
            frecv_sem.at[t],
            1 - me_s,
            me_b,
        )

    arrival(0).wait()
    forward(0).start()
    cnt[...] = jnp.zeros_like(cnt)
    first_core = me_s == 0
    lane = lax.broadcasted_iota(jnp.int32, (1, 2 * tok), 1)
    qrow = jnp.where(lane < tok, lane, lane - tok)
    wide = 2 * tok

    def step(t, carry):
        @pl.when(t < steps - 1)
        def _():
            arrival(t + 1).wait()
            forward(t + 1).start()

        @pl.when(t == GRAD_STEPS[0])
        def _():
            for step in (-1, 1):
                pass_on(line, step, True)

        for j in (1, 2):

            @pl.when(t == GRAD_STEPS[j])
            def _():
                pass_distance(j)

        @pl.when(t == HOP_STEP)
        def _():
            for n, i in ((1, 0), (2, 1)):
                share_weight(n, i).wait_recv()
                diagonal(n, i).start()
                pass_weight(n, i).start()

        @pl.when(t == HOP_STEP + 1)
        def _():
            for n, i in ((1, 2), (2, 2)):
                share_weight(n, i).wait_recv()
                diagonal(n, i).start()
                pass_weight(n, i).start()

        @pl.when(t == HOP_STEP + 2)
        def _():
            for n, i in ((1, 1), (2, 0)):
                share_weight(n, i).wait_recv()
                pass_weight(n, i).start()

        forward(t).wait_recv()
        mine = in_ref[t]
        kv_mine, seg_mine = mine[:tok, 2 * HD :], mine[tok:, 2 * HD :].astype(F32)
        other = other_ref[t]
        kv_other, seg_other = other[:tok], other[tok:].astype(F32)
        pair = jnp.where(
            first_core,
            jnp.concatenate([kv_mine, kv_other], 0).astype(F32),
            jnp.concatenate([kv_other, kv_mine], 0).astype(F32),
        )
        kv_ref[t] = pair.astype(BF16)
        kvt_ref[t] = jnp.transpose(pair).astype(BF16)
        number = lax.broadcasted_iota(jnp.int32, (8, tok), 0).astype(F32)
        seg_q = jnp.concatenate([seg_mine[0:1], seg_mine[1:2]], 1)
        seg_o = jnp.concatenate([seg_other[0:1], seg_other[1:2]], 1)
        below = (seg_q < number).astype(F32) + (seg_o < number).astype(F32)
        cnt[...] += jnp.sum(below, 1, keepdims=True)
        start_q = jnp.sum(jnp.where(seg_q == number, cnt[:, :1], 0.0), 0, keepdims=True)
        start = jnp.concatenate([start_q, start_q], 1).astype(jnp.int32)
        q_two = mine[:tok, : 2 * HD]
        q_ref[t] = q_two
        qt = stacked_heads(jnp.transpose(q_two.astype(F32)))
        qm = jnp.concatenate([qt, jnp.zeros_like(qt)], 0).astype(BF16)
        qpos = (2 * t + me_s) * tok + qrow

        def piece(u, state, last):
            running, total, acc = state
            score = mm(kv_ref[u], qm)
            kpos = u * wide + lax.broadcasted_iota(jnp.int32, score.shape, 0)
            mask = kpos >= start
            if last:
                mask &= kpos <= qpos
            score = jnp.where(mask, score, NEG)
            newmax = jnp.maximum(running, jnp.max(score, 0, keepdims=True))
            expo = jnp.exp(score - newmax)
            factor = jnp.exp(running - newmax)
            total = total * factor + jnp.sum(expo, 0, keepdims=True)
            acc = acc * factor + mm(kvt_ref[u, HD:, :], expo.astype(BF16))
            return newmax, total, acc

        state = (
            jnp.full((1, wide), NEG, F32),
            jnp.zeros((1, wide), F32),
            jnp.zeros((HD, wide), F32),
        )
        state = lax.fori_loop(0, t, lambda u, s: piece(u, s, False), state)
        running, total, acc = piece(t, state, True)
        out_t = acc / total
        ot_ref[t] = out_t
        rows = lax.broadcasted_iota(jnp.int32, (8, wide), 0)
        lse = running + jnp.log(total)
        stat_ref[t] = jnp.where(rows == 0, lse, start.astype(F32))
        upright = jnp.concatenate([out_t[:, :tok], out_t[:, tok:]], 0)
        obuf[t] = jnp.transpose(upright).astype(BF16)
        owner = 2 * t + me_s
        home = (sigma == me_s) & (owner == me_b)
        place = o_ref.at[:, pl.ds(pl.multiple_of(kappa * 2 * HD, 2 * HD), 2 * HD)]

        @pl.when(home)
        def _():
            pltpu.make_async_copy(obuf.at[t], place, orecv_sem.at[kappa]).start()

        @pl.when(jnp.logical_not(home))
        def _():
            remote(obuf.at[t], place, osend_sem.at[t], orecv_sem.at[kappa], sigma, owner).start()

        return carry

    lax.fori_loop(0, steps, step, 0)
    diagonal_in(2, 0).wait()
    pass_weight(3, 0).start()
    diagonal_in(1, 1).wait()
    pass_weight(3, 1).start()
    diagonal_in(1, 2).wait()
    diagonal_in(2, 2).wait()
    pass_weight(3, 2).start()

    def finish(t, carry):
        k, chip, mine = payload(t)

        @pl.when(jnp.logical_not(mine))
        def _():
            remote(
                pay.at[k], in_ref.at[slot], send_sem.at[k], recv_sem.at[slot], dest_core, chip
            ).wait_send()

        return carry

    lax.fori_loop(0, KV, finish, 0)

    def finish_steps(t, carry):
        forward(t).wait_send()
        owner = 2 * t + me_s
        home = (sigma == me_s) & (owner == me_b)

        @pl.when(jnp.logical_not(home))
        def _():
            remote(
                obuf.at[t],
                o_ref.at[:, pl.ds(0, 2 * HD)],
                osend_sem.at[t],
                orecv_sem.at[0],
                sigma,
                owner,
            ).wait_send()

        return carry

    lax.fori_loop(0, steps, finish_steps, 0)

    def gather(k, carry):
        pltpu.make_async_copy(
            obuf.at[0],
            o_ref.at[:, pl.ds(pl.multiple_of(k * 2 * HD, 2 * HD), 2 * HD)],
            orecv_sem.at[k],
        ).wait()
        return carry

    lax.fori_loop(0, KV, gather, 0)
    pass_distance(3)
    for k in range(4):

        @pl.when((k <= line) & (line < 3))
        def _():
            along(k, 1, False).wait_send()

        @pl.when((k >= line) & (line > 0))
        def _():
            along(k, -1, False).wait_send()

    for n in (1, 2, 3):
        for i in range(3):
            pass_weight(n, i).wait()
    for n in (1, 2):
        for i in range(3):
            share_weight(n, i).wait_send()
        diagonal(n, n - 1).wait_send()
        diagonal(n, 2).wait_send()


def attention_forward(
    blocks, x, gain, w_query, w_key, w_value, seg, cos_all, sin_all, g, w_gate, w_up, w_down
):
    tok, d = x.shape
    steps = blocks // 2
    vm = pl.BlockSpec(memory_space=pltpu.VMEM)
    hbm = pl.BlockSpec(memory_space=pl.ANY)
    dma = pltpu.SemaphoreType.DMA
    return pl.pallas_call(
        functools.partial(attention_forward_kernel, blocks),
        out_shape=(
            jax.ShapeDtypeStruct((tok, H * HD), BF16),
            jax.ShapeDtypeStruct((tok, d), BF16),
            jax.ShapeDtypeStruct((steps, 2 * tok, 2 * HD), BF16),
            jax.ShapeDtypeStruct((steps, 2 * HD, 2 * tok), BF16),
            jax.ShapeDtypeStruct((steps, tok, 2 * HD), BF16),
            jax.ShapeDtypeStruct((steps, HD, 2 * tok), F32),
            jax.ShapeDtypeStruct((steps, 8, 2 * tok), F32),
            jax.ShapeDtypeStruct((4, *g.shape), BF16),
            jax.ShapeDtypeStruct((4, *w_gate.shape), BF16),
            jax.ShapeDtypeStruct((4, *w_up.shape), BF16),
            jax.ShapeDtypeStruct((4, *w_down.shape), BF16),
        ),
        in_specs=[vm] * 6 + [hbm] * 6,
        out_specs=(vm,) * 7 + (hbm,) * 4,
        scratch_shapes=[
            pltpu.VMEM((KV, tok + 16, 4 * HD), BF16),
            pltpu.VMEM((2, tok, 2 * HD), F32),
            pltpu.VMEM((steps, tok + 16, 4 * HD), BF16),
            pltpu.VMEM((steps, tok + 16, 2 * HD), BF16),
            pltpu.VMEM((steps, tok, 2 * HD), BF16),
            pltpu.VMEM((8, 128), F32),
            dma((2,)),
            dma((KV,)),
            dma((steps,)),
            dma((steps,)),
            dma((steps,)),
            dma((steps,)),
            dma((KV,)),
            dma((2, 4)),
            dma((4,)),
            dma((2, 3)),
            dma((2, 3)),
            dma((3, 3)),
            dma((3, 3)),
            dma((2, 3)),
            dma((2, 3)),
        ],
        compiler_params=pltpu.CompilerParams(
            collective_id=0, has_side_effects=True, vmem_limit_bytes=VMEM_LIMIT
        ),
        name="attention_forward",
    )(x, gain, w_query, w_key, w_value, seg, cos_all, sin_all, g, w_gate, w_up, w_down)


def attention_backward_kernel(
    blocks,
    do_ref,
    kv_ref,
    kvt_ref,
    q_ref,
    ot_ref,
    stat_ref,
    cos_ref,
    sin_ref,
    mix_ref,
    dwg_ref,
    dwu_ref,
    dwd_ref,
    out_ref,
    mix_in,
    dwg_in,
    dwu_in,
    dwd_in,
    in_ref,
    dkv,
    part,
    xch,
    done,
    send_sem,
    recv_sem,
    xsend_sem,
    xrecv_sem,
    osend_sem,
    orecv_sem,
    msend_sem,
    mrecv_sem,
    wsend_sem,
    wrecv_sem,
):
    me_s = lax.axis_index("seq")
    me_b = lax.axis_index("blk")
    tok = q_ref.shape[1]
    steps = blocks // 2
    sigma = me_b // KV
    kappa = lax.rem(me_b, KV)
    greet_all(2, blocks, me_s, me_b)

    dest_core = lax.rem(me_b, 2)
    slot = me_b // 2
    line, plane = me_b // 4, lax.rem(me_b, 4)
    weights = ((dwg_ref, dwg_in), (dwu_ref, dwu_in), (dwd_ref, dwd_in))

    def give_mix(n):
        return remote(
            mix_ref.at[flip(line, n)],
            mix_in.at[n - 1],
            msend_sem.at[n - 1],
            mrecv_sem.at[n - 1],
            me_s,
            flip(line, n) * 4 + plane,
        )

    def give_weight(n, i):
        src, dst = weights[i]
        return remote(
            src.at[flip(plane, n)],
            dst.at[n - 1],
            wsend_sem.at[n - 1, i],
            wrecv_sem.at[n - 1, i],
            me_s,
            line * 4 + flip(plane, n),
        )

    def outgoing(n):
        k = lax.rem(me_b + n, KV)
        chip = me_s * KV + k
        mine = (dest_core == me_s) & (chip == me_b)
        src = do_ref.at[:, pl.ds(pl.multiple_of(k * 2 * HD, 2 * HD), 2 * HD)]
        return k, chip, mine, src

    def send_grad(n, carry):
        k, chip, mine, src = outgoing(n)

        @pl.when(mine)
        def _():
            pltpu.make_async_copy(src, in_ref.at[slot], recv_sem.at[slot]).start()

        @pl.when(jnp.logical_not(mine))
        def _():
            remote(src, in_ref.at[slot], send_sem.at[k], recv_sem.at[slot], dest_core, chip).start()

        return carry

    lax.fori_loop(0, KV, send_grad, 0)
    for n in (2, 1):
        give_mix(n).start()
    for i in range(3):
        for n in (1, 2):
            give_weight(n, i).start()
    dkv[...] = jnp.zeros_like(dkv)
    wide = 2 * tok
    lane = lax.broadcasted_iota(jnp.int32, (1, wide), 1)
    qrow = jnp.where(lane < tok, lane, lane - tok)
    low = lax.broadcasted_iota(jnp.int32, (tok, 2 * HD), 1) < HD

    def swap(t):
        return remote(part.at[t], xch.at[t], xsend_sem.at[t], xrecv_sem.at[t], 1 - me_s, me_b)

    def deliver(t, act):
        owner = 2 * t + me_s
        home = (sigma == me_s) & (owner == me_b)
        src, dst = done.at[t], out_ref.at[kappa]

        @pl.when(home)
        def _():
            if act == "start":
                pltpu.make_async_copy(src, dst, orecv_sem.at[kappa]).start()

        @pl.when(jnp.logical_not(home))
        def _():
            copy = remote(src, dst, osend_sem.at[t], orecv_sem.at[kappa], sigma, owner)
            copy.start() if act == "start" else copy.wait_send()

    def finalize(t):
        swap(t).wait_recv()
        place = pl.ds(pl.multiple_of(me_s * tok, tok), tok)
        total = dkv[t, place, :] + xch[t]
        owner = 2 * t + me_s
        cosine = jnp.where(low, cos_ref[owner], 1.0)
        sine = jnp.where(low, sin_ref[owner], 0.0)
        back = total * cosine - rotate_pairs(total) * sine
        done[t, :, pl.ds(2 * HD, 2 * HD)] = back.astype(BF16)
        deliver(t, "start")

    def step(n, carry):
        t = steps - 1 - n
        pltpu.make_async_copy(do_ref.at[:, pl.ds(0, 2 * HD)], in_ref.at[t], recv_sem.at[t]).wait()
        d_two = in_ref[t].astype(F32)
        q_two = q_ref[t].astype(F32)
        dt = stacked_heads(jnp.transpose(d_two))
        qt = stacked_heads(jnp.transpose(q_two))
        zero = jnp.zeros_like(dt)
        dm = jnp.concatenate([zero, dt], 0).astype(BF16)
        qm = jnp.concatenate([qt, zero], 0).astype(BF16)
        delta = jnp.sum(ot_ref[t] * dt, 0, keepdims=True)
        right = jnp.concatenate(
            [
                jnp.where(low, q_two, 0.0),
                jnp.where(low, pltpu.roll(q_two, HD, 1), 0.0),
                jnp.where(low, 0.0, pltpu.roll(d_two, HD, 1)),
                jnp.where(low, 0.0, d_two),
            ],
            0,
        ).astype(BF16)
        stat = stat_ref[t]
        lse, start = stat[0:1], stat[1:2].astype(jnp.int32)
        qpos = (2 * t + me_s) * tok + qrow

        def piece(u, dq, last):
            keys = kv_ref[u]
            score = mm(keys, qm)
            kpos = u * wide + lax.broadcasted_iota(jnp.int32, score.shape, 0)
            mask = kpos >= start
            if last:
                mask &= kpos <= qpos
            prob = jnp.where(mask, jnp.exp(score - lse), 0.0)
            dprob = mm(keys, dm)
            dscore = (prob * (dprob - delta)).astype(BF16)
            both = jnp.concatenate([dscore, prob.astype(BF16)], 1)
            dkv[u] += mm(both, right)
            return dq + mm(kvt_ref[u, :HD, :], dscore)

        dq = jnp.zeros((HD, wide), F32)
        dq = lax.fori_loop(0, t, lambda u, s: piece(u, s, False), dq)
        dq = piece(t, dq, True) * HD ** (-0.5)
        upright = jnp.transpose(jnp.concatenate([dq[:, :tok], dq[:, tok:]], 0))
        owner = 2 * t + me_s
        back = upright * cos_ref[owner] - rotate_pairs(upright) * sin_ref[owner]
        done[t, :, pl.ds(0, 2 * HD)] = back.astype(BF16)
        part[t] = dkv[t, pl.ds(pl.multiple_of((1 - me_s) * tok, tok), tok), :]
        swap(t).start()

        @pl.when(n > 0)
        def _():
            finalize(t + 1)

        return carry

    lax.fori_loop(0, steps, step, 0)
    finalize(0)

    def finish(n, carry):
        k, chip, mine, src = outgoing(n)

        @pl.when(jnp.logical_not(mine))
        def _():
            remote(
                src, in_ref.at[slot], send_sem.at[k], recv_sem.at[slot], dest_core, chip
            ).wait_send()

        return carry

    lax.fori_loop(0, KV, finish, 0)

    def finish_steps(t, carry):
        swap(t).wait_send()
        deliver(t, "wait")
        return carry

    lax.fori_loop(0, steps, finish_steps, 0)

    def gather(k, carry):
        pltpu.make_async_copy(done.at[0], out_ref.at[k], orecv_sem.at[k]).wait()
        return carry

    lax.fori_loop(0, KV, gather, 0)
    for n in (1, 2):
        give_mix(n).wait()
        for i in range(3):
            give_weight(n, i).wait()


def attention_backward(
    blocks, vectors, mix, dwg, dwu, dwd
):
    tok = vectors[0].shape[0]
    steps = blocks // 2
    vm = pl.BlockSpec(memory_space=pltpu.VMEM)
    hbm = pl.BlockSpec(memory_space=pl.ANY)
    dma = pltpu.SemaphoreType.DMA
    return pl.pallas_call(
        functools.partial(attention_backward_kernel, blocks),
        out_shape=(
            jax.ShapeDtypeStruct((KV, tok, 4 * HD), BF16),
            jax.ShapeDtypeStruct((2, *mix.shape[1:]), BF16),
            jax.ShapeDtypeStruct((2, *dwg.shape[1:]), BF16),
            jax.ShapeDtypeStruct((2, *dwu.shape[1:]), BF16),
            jax.ShapeDtypeStruct((2, *dwd.shape[1:]), BF16),
        ),
        in_specs=[vm] * len(vectors) + [hbm] * 4,
        out_specs=(vm,) + (hbm,) * 4,
        scratch_shapes=[
            pltpu.VMEM((steps, tok, 2 * HD), BF16),
            pltpu.VMEM((steps, 2 * tok, 2 * HD), F32),
            pltpu.VMEM((steps, tok, 2 * HD), F32),
            pltpu.VMEM((steps, tok, 2 * HD), F32),
            pltpu.VMEM((steps, tok, 4 * HD), BF16),
            dma((KV,)),
            dma((steps,)),
            dma((steps,)),
            dma((steps,)),
            dma((steps,)),
            dma((KV,)),
            dma((2,)),
            dma((2,)),
            dma((2, 3)),
            dma((2, 3)),
        ],
        compiler_params=pltpu.CompilerParams(
            collective_id=1, has_side_effects=True, vmem_limit_bytes=VMEM_LIMIT
        ),
        name="attention_backward",
    )(*vectors, mix, dwg, dwu, dwd)


def mixture_kernel(
    x_ref,
    g_ref,
    wg_ref,
    wu_ref,
    wd_ref,
    g_all,
    wg_all,
    wu_all,
    wd_all,
    mix_own,
    mix_peer,
    d_in,
    dwg_out,
    dwu_out,
    dwd_out,
    dwg_in,
    dwu_in,
    dwd_in,
    x_in,
    x_t,
    g_in,
    wg,
    wu,
    wd,
    hc,
    dg,
    du,
    acc_o,
    acc_d,
    acc_c,
    d_send,
    d_recv,
    xg,
    xu,
    xd,
    load_sem,
    gload_sem,
    send_sem,
    recv_sem,
    bsend_sem,
    brecv_sem,
    psend_sem,
    precv_sem,
    store_sem,
    wsend_sem,
    wrecv_sem,
):
    me_s = lax.axis_index("seq")
    me_b = lax.axis_index("blk")
    line, plane = me_b // 4, lax.rem(me_b, 4)
    tok, d = g_in.shape[1:]
    ff = wg.shape[2]
    barrier = pltpu.get_barrier_semaphore()
    sibling = (1 - me_s, me_b)
    opposite = (me_s, line * 4 + flip(plane, 3))
    for place in [(me_s, flip(line, n) * 4 + plane) for n in (1, 2, 3)] + [sibling, opposite]:
        pl.semaphore_signal(barrier, inc=1, device_id=place, device_id_type=MESH)

    owns = ((wg_ref, wg_all, wg), (wu_ref, wu_all, wu), (wd_ref, wd_all, wd))

    def load_own(i):
        return pltpu.make_async_copy(owns[i][0], owns[i][2].at[plane], load_sem.at[i, plane])

    def load_other(i, e):
        return pltpu.make_async_copy(owns[i][1].at[e], owns[i][2].at[e], load_sem.at[i, e])

    for i in range(3):
        load_own(i).start()
        for n in (1, 2, 3):
            load_other(i, flip(plane, n)).start()

    def load_grad(k):
        return pltpu.make_async_copy(g_all.at[k], g_in.at[k], gload_sem.at[k])

    pltpu.make_async_copy(g_ref, g_in.at[line], gload_sem.at[line]).start()
    for n in (1, 2, 3):
        load_grad(flip(line, n)).start()
    x_in[line] = x_ref[...]
    pl.semaphore_wait(barrier, 5)

    def along(k, step):
        at = 0 if step < 0 else 1
        return remote(
            x_in.at[k],
            x_in.at[k],
            send_sem.at[at, k],
            recv_sem.at[k],
            me_s,
            (line + step) * 4 + plane,
        )

    def pass_on(k, step):
        @pl.when((line + step >= 0) & (line + step < 4))
        def _():
            along(k, step).start()

    for step in (-1, 1):
        pass_on(line, step)
    for k in range(4):
        load_grad(k).wait()

    def load_wait(e, carry):
        for i in range(3):
            load_other(i, e).wait()
        return carry

    lane = lax.broadcasted_iota(jnp.int32, (tok, 128), 1)

    def place_of(j):
        return jnp.where(line < 2, lax.rem(line + j, 4), lax.rem(line + 4 - j, 4))

    def block(j, carry):
        n = place_of(j)
        for step in (-1, 1):
            k = line - step * j

            @pl.when((j > 0) & (k >= 0) & (k < 4))
            def _():
                pltpu.make_async_copy(x_ref, x_in.at[k], recv_sem.at[k]).wait()
                pass_on(k, step)

        acc_o[...] = jnp.zeros_like(acc_o)
        acc_d[...] = jnp.zeros_like(acc_d)
        acc_c[...] = jnp.zeros_like(acc_c)
        rows = pl.ds(pl.multiple_of(n * tok, tok), tok)

        def expert(e, carry):
            @pl.when(j == 0)
            def _():
                load_wait(e, 0)

            x = x_in[n, :, :d]
            here = lane == line * 4 + e
            share = jnp.sum(
                jnp.where(here, x_in[n, :, d:].astype(F32), 0.0), 1, keepdims=True
            )
            gate = mm(x, wg[e])
            up = mm(x, wu[e])
            dh = mm(g_in[n], wd[e], NT)
            sg = jax.nn.sigmoid(gate)
            act = gate * sg
            hidden = act * up
            acc_c[...] += jnp.where(here, jnp.sum(dh * hidden, 1, keepdims=True), 0.0)
            dh = dh * share
            hcb = (hidden * share).astype(BF16)
            dgb = (dh * up * sg * (1.0 + gate * (1.0 - sg))).astype(BF16)
            dub = (dh * act).astype(BF16)
            hc[e, rows, :] = hcb
            dg[e, rows, :] = dgb
            du[e, rows, :] = dub
            acc_o[...] += mm(hcb, wd[e])
            acc_d[...] += mm(dgb, wg[e], NT) + mm(dub, wu[e], NT)
            return carry

        lax.fori_loop(0, 4, expert, 0)

        @pl.when(j == 0)
        def _():
            mix_own[...] = acc_o[...]
            d_in[:, :d] = acc_d[...]
            d_in[:, d:] = acc_c[...]

        @pl.when(j > 0)
        def _():
            mix_peer[n] = acc_o[...].astype(BF16)
            d_send[n, :, :d] = acc_d[...].astype(BF16)
            high = acc_c[...].astype(BF16).astype(F32)
            rest = acc_c[...] - high
            d_send[n, :, d:] = (high + pltpu.roll(rest, 32, 1)).astype(BF16)
            give_back(n).start()

        x_t[:, rows] = jnp.transpose(x_in[n, :, :d].astype(F32)).astype(BF16)
        return carry

    def give_back(n):
        return remote(
            d_send.at[n], d_recv.at[line], bsend_sem.at[n], brecv_sem.at[line], me_s, n * 4 + plane
        )

    lax.fori_loop(0, 4, block, 0)

    half, dhalf = d // 2, ff // 2
    theirs = pl.multiple_of((1 - me_s) * half, half)
    dtheirs = pl.multiple_of((1 - me_s) * dhalf, dhalf)
    mine = pl.multiple_of(me_s * half, half)
    dmine = pl.multiple_of(me_s * dhalf, dhalf)
    g_rows = g_in.reshape(4 * tok, d)

    def swap(i, e):
        src = (wg.at[e, pl.ds(0, half)], wu.at[e, pl.ds(0, half)], wd.at[e, pl.ds(0, dhalf)])[i]
        dst = (xg, xu, xd)[i].at[e]
        return remote(src, dst, psend_sem.at[i, e], precv_sem.at[i, e], *sibling)

    def store(i, e):
        return pltpu.make_async_copy(
            (xg, xu, xd)[i].at[e], (dwg_out, dwu_out, dwd_out)[i].at[e], store_sem.at[i, e]
        )

    def turn_of(n):
        return jnp.where(
            n == 0, flip(plane, 3), jnp.where(n == 1, flip(plane, 2), jnp.where(n == 2, flip(plane, 1), plane))
        )

    def opposed(i):
        return remote(
            (xg, xu, xd)[i].at[flip(plane, 3)],
            (dwg_in, dwu_in, dwd_in)[i],
            wsend_sem.at[i],
            wrecv_sem.at[i],
            *opposite,
        )

    def finished(i, n, e):
        @pl.when(n == 0)
        def _():
            opposed(i).start()

        @pl.when(n > 0)
        def _():
            store(i, e).start()

    def give(n, carry):
        e = turn_of(n)
        left = x_t[pl.ds(theirs, half), :]
        wg[e, :half, :] = mm(left, dg[e]).astype(BF16)
        swap(0, e).start()
        wu[e, :half, :] = mm(left, du[e]).astype(BF16)
        swap(1, e).start()
        wd[e, :dhalf, :] = mm(hc[e, :, pl.ds(dtheirs, dhalf)], g_rows[...], TN).astype(BF16)
        swap(2, e).start()
        return carry

    lax.fori_loop(0, 4, give, 0)

    def keep(n, carry):
        e = turn_of(n)

        left = x_t[pl.ds(mine, half), :]
        own = mm(left, dg[e])
        swap(0, e).wait_recv()
        xg[e] = (own + xg[e].astype(F32)).astype(BF16)
        finished(0, n, e)
        own = mm(left, du[e])
        swap(1, e).wait_recv()
        xu[e] = (own + xu[e].astype(F32)).astype(BF16)
        finished(1, n, e)
        own = mm(hc[e, :, pl.ds(dmine, dhalf)], g_rows[...], TN)
        swap(2, e).wait_recv()
        xd[e] = (own + xd[e].astype(F32)).astype(BF16)
        finished(2, n, e)
        return carry

    lax.fori_loop(0, 4, keep, 0)

    for n in (1, 2, 3):
        k = flip(line, n)
        pltpu.make_async_copy(d_send.at[k], d_recv.at[k], brecv_sem.at[k]).wait()
        d_in[:, :d] += d_recv[k, :, :d].astype(F32)
        tail = d_recv[k, :, d:].astype(F32)
        both = tail + pltpu.roll(tail, 96, 1)
        d_in[:, d:] += jnp.where(lane < 32, both, 0.0)
    for n in (1, 2, 3):
        give_back(flip(line, n)).wait_send()
    for k in range(4):

        @pl.when((k <= line) & (line < 3))
        def _():
            along(k, 1).wait_send()

        @pl.when((k >= line) & (line > 0))
        def _():
            along(k, -1).wait_send()

    def finish(n, carry):
        e = turn_of(n)
        for i in range(3):
            swap(i, e).wait_send()

            @pl.when(n > 0)
            def _():
                store(i, e).wait()

        return carry

    lax.fori_loop(0, 4, finish, 0)
    for i in range(3):
        opposed(i).wait()


def mixture(x, g, w_gate, w_up, w_down, g_all, wg_all, wu_all, wd_all):
    tok, d = g.shape
    ff = w_gate.shape[1]
    vm = pl.BlockSpec(memory_space=pltpu.VMEM)
    hbm = pl.BlockSpec(memory_space=pl.ANY)
    dma = pltpu.SemaphoreType.DMA
    vmem = pltpu.VMEM
    return pl.pallas_call(
        mixture_kernel,
        out_shape=(
            jax.ShapeDtypeStruct((tok, d), F32),
            jax.ShapeDtypeStruct((4, tok, d), BF16),
            jax.ShapeDtypeStruct((tok, d + 128), F32),
            jax.ShapeDtypeStruct((4, d // 2, ff), BF16),
            jax.ShapeDtypeStruct((4, d // 2, ff), BF16),
            jax.ShapeDtypeStruct((4, ff // 2, d), BF16),
            jax.ShapeDtypeStruct((d // 2, ff), BF16),
            jax.ShapeDtypeStruct((d // 2, ff), BF16),
            jax.ShapeDtypeStruct((ff // 2, d), BF16),
        ),
        in_specs=[vm] + [hbm] * 8,
        out_specs=(vm,) * 3 + (hbm,) * 6,
        scratch_shapes=[
            vmem((4, tok, d + 128), BF16),
            vmem((d, 4 * tok), BF16),
            vmem((4, tok, d), BF16),
            vmem((4, d, ff), BF16),
            vmem((4, d, ff), BF16),
            vmem((4, ff, d), BF16),
            vmem((4, 4 * tok, ff), BF16),
            vmem((4, 4 * tok, ff), BF16),
            vmem((4, 4 * tok, ff), BF16),
            vmem((tok, d), F32),
            vmem((tok, d), F32),
            vmem((tok, 128), F32),
            vmem((4, tok, d + 128), BF16),
            vmem((4, tok, d + 128), BF16),
            vmem((4, d // 2, ff), BF16),
            vmem((4, d // 2, ff), BF16),
            vmem((4, ff // 2, d), BF16),
            dma((3, 4)),
            dma((4,)),
            dma((2, 4)),
            dma((4,)),
            dma((4,)),
            dma((4,)),
            dma((3, 4)),
            dma((3, 4)),
            dma((3, 4)),
            dma((3,)),
            dma((3,)),
        ],
        compiler_params=pltpu.CompilerParams(
            collective_id=2, has_side_effects=True, vmem_limit_bytes=VMEM_LIMIT
        ),
        name="mixture",
    )(x, g, w_gate, w_up, w_down, g_all, wg_all, wu_all, wd_all)


def tail_kernel(
    got,
    xa_ref,
    x_ref,
    gain_ref,
    dh_ref,
    wq_ref,
    wk_ref,
    wv_ref,
    ao_ref,
    datt_ref,
    xl_ref,
    dlog_ref,
    dgain2_ref,
    h1_ref,
    mix_own,
    mix_ref,
    mix_near,
    eg_ref,
    eu_ref,
    ed_ref,
    eg_in,
    eu_in,
    ed_in,
    eg_far,
    eu_far,
    ed_far,
    res_ref,
    dx_ref,
    gsum_ref,
    fin_o,
    fin_q,
    fin_kv,
    eg_out,
    eu_out,
    ed_out,
    mix_in,
    d_all,
    ev,
    edv,
    gbuf,
    grv,
    load_sem,
    esend,
    erecv,
    gsend,
    grecv,
    msend,
    mrecv,
    *summing,
):
    me_s = lax.axis_index("seq")
    me_b = lax.axis_index("blk")
    plane = lax.rem(me_b, 4)
    tok, d = xa_ref.shape
    sums = [
        Summed(summing[8 * i : 8 * i + 6], *summing[8 * i + 6 : 8 * i + 8], fin)
        for i, fin in enumerate((fin_o, fin_q, fin_kv))
    ]
    for_out, for_q, for_kv = sums
    [sibling], planes, lines = for_q.sibling, for_q.planes, for_q.lines
    barrier = pltpu.get_barrier_semaphore()
    for place in [sibling, *planes, *lines]:
        pl.semaphore_signal(barrier, inc=1, device_id=place, device_id_type=MESH)

    experts = (
        (eg_ref, eg_in, eg_far, ev.at[0]),
        (eu_ref, eu_in, eu_far, ev.at[1]),
        (ed_ref, ed_in, ed_far, edv),
    )

    def loads(i):
        own, arrived, far, dst = experts[i]
        return (
            pltpu.make_async_copy(own.at[plane], dst.at[0], load_sem.at[i, 0]),
            pltpu.make_async_copy(arrived, dst.at[pl.ds(1, 2)], load_sem.at[i, 1]),
            pltpu.make_async_copy(far, dst.at[3], load_sem.at[i, 2]),
        )

    for i in range(3):
        for copy in loads(i):
            copy.start()
    pl.semaphore_wait(barrier, 7)
    line = me_b // 4

    far_mix = remote(mix_ref.at[flip(line, 3)], mix_in.at[2], msend, mrecv, *lines[2])
    near_mix = pltpu.make_async_copy(mix_near, mix_in.at[pl.ds(0, 2)], load_sem.at[3, 0])
    far_mix.start()
    near_mix.start()
    theirs, mine = for_q.halves()
    for_out.out[:, :d] = mm(ao_ref[:, theirs], datt_ref[...], TN).astype(BF16)
    for_out.out[:, d:] = mm(xl_ref[:, theirs], dlog_ref[...], TN).astype(BF16)
    for_out.start(0)

    low = lax.broadcasted_iota(jnp.int32, (tok, 2 * HD), 1) < HD
    for m in range(KV // 2):
        a, b = got[2 * m], got[2 * m + 1]
        d_all[:, 2 * m * 2 * HD : (2 * m + 1) * 2 * HD] = a[:, : 2 * HD]
        d_all[:, (2 * m + 1) * 2 * HD : (2 * m + 2) * 2 * HD] = b[:, : 2 * HD]
        ka, kb = a[:, 2 * HD :].astype(F32), b[:, 2 * HD :].astype(F32)
        at = H * HD + m * 2 * HD
        d_all[:, at : at + 2 * HD] = jnp.where(low, ka, pltpu.roll(kb, HD, 1)).astype(BF16)
        at += KV * HD
        d_all[:, at : at + 2 * HD] = jnp.where(low, pltpu.roll(ka, HD, 1), kb).astype(BF16)
    parts = ((for_q, slice(0, H * HD)), (for_kv, slice(H * HD, (H + 2 * KV) * HD)))
    for item, cols in parts:
        item.out[...] = mm(xa_ref[:, theirs], d_all[:, cols], TN).astype(BF16)
        item.start(0)
    for_out.acc[:, :d] = mm(ao_ref[:, mine], datt_ref[...], TN)
    for_out.acc[:, d:] = mm(xl_ref[:, mine], dlog_ref[...], TN)
    for_out.pair()
    for item, cols in parts:
        item.acc[...] = mm(xa_ref[:, mine], d_all[:, cols], TN)
        item.pair()

    grad = (
        mm(d_all[:, : H * HD], wq_ref[...], NT)
        + mm(d_all[:, H * HD : (H + KV) * HD], wk_ref[...], NT)
        + mm(d_all[:, (H + KV) * HD :], wv_ref[...], NT)
    )
    xs = x_ref[...].astype(F32)
    scale = rms_scale(xs)
    scaled = grad * gain_ref[...]
    inner = jnp.mean(scaled * xs, -1, keepdims=True)
    dx_ref[...] = dh_ref[...] + scale * scaled - xs * scale**3 * inner
    gbuf[0, :8, :] = jnp.sum((grad * xs * scale).reshape(tok // 8, 8, d), 0)
    gbuf[0, 8:, :] = dgain2_ref[...]

    stages = [[sibling], planes, lines]

    def gain_copy(s, n):
        at = (0, 1, 4)[s] + n
        return remote(gbuf.at[s], grv.at[at], gsend.at[at], grecv.at[at], *stages[s][n])

    def gain_stage(s):
        for n in range(len(stages[s])):
            gain_copy(s, n).start()

    def gain_total(s):
        total = gbuf[s]
        for n in range(len(stages[s])):
            gain_copy(s, n).wait_recv()
            total = total + grv[(0, 1, 4)[s] + n]
        return total

    gain_stage(0)
    for_out.over_plane()

    outs = (eg_out, eu_out, ed_out)

    def expert_swap(i):
        rows = outs[i].shape[0] // 2
        part = outs[i].at[pl.ds(pl.multiple_of(me_s * rows, rows), rows)]
        return remote(part, part, esend.at[i], erecv.at[i], *sibling)

    for i in range(3):
        for copy in loads(i):
            copy.wait()
        terms = experts[i][3]
        rows = outs[i].shape[0] // 2
        total = terms[0].astype(F32)
        for n in (1, 2, 3):
            total = total + terms[n].astype(F32)
        outs[i][pl.ds(pl.multiple_of(me_s * rows, rows), rows), :] = total.astype(BF16)
        expert_swap(i).start()
    gbuf[1] = gain_total(0)
    gain_stage(1)
    for_q.over_plane()
    for_out.over_line()
    for_kv.over_plane()
    gbuf[2] = gain_total(1)
    gain_stage(2)
    for_q.over_line()
    for_out.back(3)
    for_kv.over_line()
    for_q.back(3)
    for_kv.back(3)
    gsum_ref[...] = gain_total(2)
    for item in sums:
        item.back(4)
    result = h1_ref[...] + mix_own[...]
    near_mix.wait()
    far_mix.wait()
    for n in range(3):
        result = result + mix_in[n].astype(F32)
    res_ref[...] = result.astype(BF16)
    for item in sums:
        item.finish()
    for i in range(3):
        expert_swap(i).wait()
    for s in range(3):
        for n in range(len(stages[s])):
            gain_copy(s, n).wait_send()


def tail(blocks_in, mix_peer, mix_near, own, arrived, far):
    tok, d = blocks_in[1].shape
    ff = own[0].shape[2]
    widths = (d + 128, H * HD, 2 * KV * HD)
    vm = pl.BlockSpec(memory_space=pltpu.VMEM)
    hbm = pl.BlockSpec(memory_space=pl.ANY)
    dma = pltpu.SemaphoreType.DMA
    vmem = pltpu.VMEM
    return pl.pallas_call(
        tail_kernel,
        out_shape=(
            jax.ShapeDtypeStruct((tok, d), BF16),
            jax.ShapeDtypeStruct((tok, d), F32),
            jax.ShapeDtypeStruct((16, d), F32),
            *(jax.ShapeDtypeStruct((d, width), BF16) for width in widths),
            jax.ShapeDtypeStruct((d, ff), BF16),
            jax.ShapeDtypeStruct((d, ff), BF16),
            jax.ShapeDtypeStruct((ff, d), BF16),
        ),
        in_specs=[vm] * len(blocks_in) + [hbm] * 11,
        out_specs=(vm,) * 9,
        scratch_shapes=[
            vmem((3, tok, d), BF16),
            vmem((tok, (H + 2 * KV) * HD), BF16),
            vmem((2, 4, d // 2, ff), BF16),
            vmem((4, ff // 2, d), BF16),
            vmem((3, 16, d), F32),
            vmem((7, 16, d), F32),
            dma((4, 3)),
            dma((3,)),
            dma((3,)),
            dma((7,)),
            dma((7,)),
            dma,
            dma,
            *(ref for width in widths for ref in summed_scratch(d, width)),
        ],
        compiler_params=pltpu.CompilerParams(
            collective_id=3, has_side_effects=True, vmem_limit_bytes=VMEM_LIMIT
        ),
        name="tail",
    )(*blocks_in, mix_peer, mix_near, *own, *arrived, *far)


def widen_kernel(gains, o, q, kv, eg, eu, ed, n1, wq, wk, wv, wo, n2, wr, og, ou, od):
    d = wq.shape[1]
    half = wk.shape[1]
    wq[...] = q[...].astype(F32)
    wk[...] = kv[:, :half].astype(F32)
    wv[...] = kv[:, half:].astype(F32)
    wo[...] = o[:, :d].astype(F32)
    wr[...] = o[:, d : d + wr.shape[1]].astype(F32)
    og[0] = eg[...].astype(F32)
    ou[0] = eu[...].astype(F32)
    od[0] = ed[...].astype(F32)
    n1[...] = jnp.sum(gains[:8], 0, keepdims=True)
    n2[...] = jnp.sum(gains[8:], 0, keepdims=True)


def widen(gains, o, q, kv, eg, eu, ed, experts):
    d, ff = eg.shape
    parts = 8

    def block(shape):
        return pl.BlockSpec((shape[0] // parts, shape[1]), lambda i: (i, 0))

    def deep(shape):
        return pl.BlockSpec((1, shape[0] // parts, shape[1]), lambda i: (0, i, 0))

    flat = pl.BlockSpec((1, d), lambda i: (0, 0))
    shapes = [(d, H * HD), (d, KV * HD), (d, KV * HD), (H * HD, d)]
    return pl.pallas_call(
        widen_kernel,
        grid=(parts,),
        out_shape=(
            jax.ShapeDtypeStruct((1, d), F32),
            *(jax.ShapeDtypeStruct(shape, F32) for shape in shapes),
            jax.ShapeDtypeStruct((1, d), F32),
            jax.ShapeDtypeStruct((d, experts), F32),
            jax.ShapeDtypeStruct((1, d, ff), F32),
            jax.ShapeDtypeStruct((1, d, ff), F32),
            jax.ShapeDtypeStruct((1, ff, d), F32),
        ),
        in_specs=[pl.BlockSpec((16, d), lambda i: (0, 0))]
        + [block(a.shape) for a in (o, q, kv, eg, eu, ed)],
        out_specs=(
            flat,
            *(block(shape) for shape in shapes),
            flat,
            block((d, experts)),
            deep((d, ff)),
            deep((d, ff)),
            deep((ff, d)),
        ),
        compiler_params=pltpu.CompilerParams(vmem_limit_bytes=VMEM_LIMIT),
        name="widen",
    )(gains, o, q, kv, eg, eu, ed)


D = 1024
HIGH = lax.Precision.HIGHEST


def rope_tables(positions):
    half = HD // 2
    freq = jnp.exp(-math.log(10000.0) * jnp.arange(half, dtype=jnp.float32) * 2.0 / HD)
    angle = positions.astype(jnp.float32)[:, None] * freq[None, :]
    cosine = jnp.concatenate([jnp.cos(angle), jnp.cos(angle)], -1)
    sine = jnp.concatenate([jnp.sin(angle), jnp.sin(angle)], -1)
    return (cosine, sine)


def rotate_half(v):
    half = v.shape[-1] // 2
    return jnp.concatenate([-v[..., half:], v[..., :half]], -1)


def rotary(v, cosine, sine):
    return v * cosine[:, None, :] + rotate_half(v) * sine[:, None, :]


def unrotary(v, cosine, sine):
    return v * cosine[:, None, :] - rotate_half(v) * sine[:, None, :]


def rms_scale(v):
    return lax.rsqrt(jnp.mean(v * v, -1, keepdims=True) + EPS)


def rms_back(inputs, scale_rows, gain, grad):
    scaled = grad * gain
    d_inputs = scale_rows * scaled - inputs * scale_rows**3 * jnp.mean(
        scaled * inputs, -1, keepdims=True
    )
    return (d_inputs, jnp.sum(grad * inputs * scale_rows, 0))


def scores(queries, keys):
    return jnp.einsum("qkgd,skd->kgqs", queries, keys, preferred_element_type=jnp.float32) * HD ** (
        -0.5
    )


def per_device_plain(
    tokens,
    segments,
    routes,
    route_weight,
    norm1_gain,
    w_query,
    w_key,
    w_value,
    w_out,
    norm2_gain,
    w_router,
    w_gate,
    w_up,
    w_down,
    cotangent,
):
    f32 = jnp.float32
    bf16 = jnp.bfloat16
    scale = HD ** (-0.5)
    group = H // KV
    xs = tokens[0].astype(f32)
    tok = xs.shape[0]
    blocks = lax.axis_size("blk")
    length = tok * blocks
    first = lax.axis_index("blk") * tok
    last = first + tok - 1
    positions = first + jnp.arange(tok, dtype=jnp.int32)
    cosine, sine = rope_tables(positions)
    scale1 = rms_scale(xs)
    xa = (xs * scale1 * norm1_gain).astype(bf16)
    query = jnp.dot(xa, w_query, preferred_element_type=f32)
    key = jnp.dot(xa, w_key, preferred_element_type=f32)
    value = jnp.dot(xa, w_value, preferred_element_type=f32).astype(bf16)
    q_rot = rotary(query.reshape(tok, H, HD), cosine, sine).astype(bf16).reshape(tok, KV, group, HD)
    k_rot = rotary(key.reshape(tok, KV, HD), cosine, sine).astype(bf16).reshape(tok, KV * HD)
    seg_float = segments[0].astype(bf16)
    k_all, v_all, seg_all = (
        lax.all_gather(k_rot, "blk", axis=0, tiled=True),
        lax.all_gather(value, "blk", axis=0, tiled=True),
        lax.all_gather(seg_float, "blk", axis=0, tiled=True),
    )
    kblk = min(512, length)
    nblk = length // kblk
    k_blocks = k_all.reshape(nblk, kblk, KV, HD)
    v_blocks = v_all.reshape(nblk, kblk, KV, HD)
    s_blocks = seg_all.reshape(nblk, kblk)
    starts = jnp.arange(nblk, dtype=jnp.int32) * kblk

    def visible(kseg, kstart):
        kpos = kstart + jnp.arange(kblk, dtype=jnp.int32)
        return ((seg_float[:, None] == kseg[None, :]) & (kpos[None, :] <= positions[:, None]))[
            None, None
        ]

    def forward_step(carry, block):
        kb, vb, sb, start = block

        def forward_compute(state):
            running, total, acc = state
            mask = visible(sb, start)
            score = jnp.where(mask, scores(q_rot, kb), NEG)
            newmax = jnp.maximum(running, jnp.max(score, -1))
            expo = jnp.where(mask, jnp.exp(score - newmax[..., None]), 0.0)
            factor = jnp.exp(running - newmax)
            total = total * factor + jnp.sum(expo, -1)
            acc = acc * factor[..., None] + jnp.einsum(
                "kgqs,skd->kgqd", expo.astype(bf16), vb, preferred_element_type=f32
            )
            return (newmax, total, acc)

        return (lax.cond(start <= last, forward_compute, lambda state: state, carry), None)

    init = (
        jnp.full((KV, group, tok), NEG, f32),
        jnp.zeros((KV, group, tok), f32),
        jnp.zeros((KV, group, tok, HD), f32),
    )
    (running, total, acc), unused = lax.scan(
        forward_step, init, (k_blocks, v_blocks, s_blocks, starts)
    )
    lse = running + jnp.log(total)
    o_rows = (acc / total[..., None]).transpose(2, 0, 1, 3)
    att_low = o_rows.reshape(tok, H * HD).astype(bf16)
    h1 = xs + jnp.dot(att_low, w_out, preferred_element_type=f32)
    scale2 = rms_scale(h1)
    xl = (h1 * scale2 * norm2_gain).astype(bf16)
    logits = jnp.dot(xl, w_router, preferred_element_type=f32)
    experts = logits.shape[1]
    route = routes[0]
    rweight = route_weight[0]
    chooser = (route[:, :, None] == jnp.arange(experts, dtype=jnp.int32)[None, None, :]).astype(f32)
    chosen = jnp.sum(chooser * logits[:, None, :], -1)
    gates = jax.nn.softmax(chosen, -1)
    combine = (rweight * gates).astype(bf16)
    cap = min(tok, 2 * tok * TOP // experts)
    member = jnp.sum(chooser, 1)
    before = jnp.asarray(np.tril(np.ones((tok, tok), np.float32), -1))
    order = jnp.dot(before, member, precision=HIGH)
    rank = jnp.sum(chooser * order[:, None, :], -1).astype(jnp.int32)
    slots = route * cap + rank
    placed = jnp.any(
        slots[:, :, None] == jnp.arange(experts * cap, dtype=jnp.int32)[None, None, :], 1
    ).astype(bf16)
    outgoing = jnp.einsum("ts,td->sd", placed, xl, preferred_element_type=f32).astype(bf16)
    incoming = lax.all_to_all(
        outgoing.reshape(experts, cap, D), "blk", split_axis=0, concat_axis=0, tiled=True
    )
    local_exp = w_gate.shape[0]
    incoming = incoming.reshape(blocks, local_exp, cap, D)
    gate_pre = jnp.einsum("necd,edf->necf", incoming, w_gate, preferred_element_type=f32)
    up_pre = jnp.einsum("necd,edf->necf", incoming, w_up, preferred_element_type=f32)
    sigma = jax.nn.sigmoid(gate_pre)
    activated = gate_pre * sigma
    hidden = (activated * up_pre).astype(bf16)
    expert_out = jnp.einsum("necf,efd->necd", hidden, w_down, preferred_element_type=f32).astype(
        bf16
    )
    returned = lax.all_to_all(
        expert_out.reshape(experts, cap, D), "blk", split_axis=0, concat_axis=0, tiled=True
    )
    per_route = jnp.take(returned.reshape(experts * cap, D), slots.reshape(-1), axis=0).reshape(
        tok, TOP, D
    )
    mixture = jnp.einsum("tj,tjd->td", combine, per_route, preferred_element_type=f32)
    result = h1 + mixture
    grad_out = cotangent[0].astype(f32)
    grad_combine = jnp.einsum("td,tjd->tj", grad_out, per_route.astype(f32), precision=HIGH)
    route_grads = (combine.astype(f32)[:, :, None] * grad_out[:, None, :]).astype(bf16)
    grad_slots = (
        jnp.zeros((experts * cap, D), bf16)
        .at[slots.reshape(-1)]
        .set(route_grads.reshape(tok * TOP, D))
    )
    grad_incoming = lax.all_to_all(
        grad_slots.reshape(experts, cap, D), "blk", split_axis=0, concat_axis=0, tiled=True
    )
    grad_incoming = grad_incoming.reshape(blocks, local_exp, cap, D)
    grad_hidden = jnp.einsum("necd,efd->necf", grad_incoming, w_down, preferred_element_type=f32)
    grad_gate = (grad_hidden * up_pre * sigma * (1.0 + gate_pre * (1.0 - sigma))).astype(bf16)
    grad_up = (grad_hidden * activated).astype(bf16)
    d_down = jnp.einsum("necf,necd->efd", hidden, grad_incoming, preferred_element_type=f32)
    d_gate_w = jnp.einsum("necd,necf->edf", incoming, grad_gate, preferred_element_type=f32)
    d_up_w = jnp.einsum("necd,necf->edf", incoming, grad_up, preferred_element_type=f32)
    grad_in = (
        jnp.einsum("necf,edf->necd", grad_gate, w_gate, preferred_element_type=f32)
        + jnp.einsum("necf,edf->necd", grad_up, w_up, preferred_element_type=f32)
    ).astype(bf16)
    grad_back = lax.all_to_all(
        grad_in.reshape(experts, cap, D), "blk", split_axis=0, concat_axis=0, tiled=True
    )
    grad_xl = jnp.einsum(
        "ts,sd->td", placed, grad_back.reshape(experts * cap, D), preferred_element_type=f32
    )
    grad_gates = rweight * grad_combine
    grad_chosen = gates * (grad_gates - jnp.sum(gates * grad_gates, -1, keepdims=True))
    grad_logits = jnp.sum(chooser * grad_chosen[:, :, None], 1).astype(bf16)
    d_router = jnp.einsum("td,te->de", xl, grad_logits, preferred_element_type=f32)
    grad_xl = grad_xl + jnp.einsum("te,de->td", grad_logits, w_router, preferred_element_type=f32)
    grad_h1_norm, d_gain2 = rms_back(h1, scale2, norm2_gain, grad_xl)
    grad_h1 = grad_out + grad_h1_norm
    grad_att = grad_h1.astype(bf16)
    d_out_w = jnp.einsum("ti,td->id", att_low, grad_att, preferred_element_type=f32)
    grad_o = jnp.einsum("td,id->ti", grad_att, w_out, preferred_element_type=f32).astype(bf16)
    grad_o_rows = grad_o.reshape(tok, KV, group, HD)
    delta = jnp.einsum("qkgd,qkgd->kgq", grad_o_rows.astype(f32), o_rows)

    def query_terms(kb, vb, sb, start):
        mask = visible(sb, start)
        prob = jnp.where(mask, jnp.exp(scores(q_rot, kb) - lse[..., None]), 0.0)
        dprob = jnp.einsum("qkgd,skd->kgqs", grad_o_rows, vb, preferred_element_type=f32)
        dscore = (prob * (dprob - delta[..., None])).astype(bf16)
        dq_term = jnp.einsum("kgqs,skd->qkgd", dscore, kb, preferred_element_type=f32) * scale
        return (dq_term, dscore, prob)

    zero_q = jnp.zeros((tok, KV, group, HD), f32)

    def backward_step(grad_q, block):
        kb, vb, sb, start = block

        def backward_compute(acc_q):
            dq_term, dscore, prob = query_terms(kb, vb, sb, start)
            gk = jnp.einsum("kgqs,qkgd->skd", dscore, q_rot, preferred_element_type=f32) * scale
            gv = jnp.einsum(
                "kgqs,qkgd->skd", prob.astype(bf16), grad_o_rows, preferred_element_type=f32
            )
            return (acc_q + dq_term, (gk.reshape(kblk, KV * HD), gv.reshape(kblk, KV * HD)))

        def skip(acc_q):
            empty = jnp.zeros((kblk, KV * HD), f32)
            return (acc_q, (empty, empty))

        return lax.cond(start <= last, backward_compute, skip, grad_q)

    grad_q, (gk_blocks, gv_blocks) = lax.scan(
        backward_step, zero_q, (k_blocks, v_blocks, s_blocks, starts)
    )
    grad_k, grad_v = (
        lax.psum_scatter(
            gk_blocks.reshape(length, KV * HD).astype(jnp.bfloat16),
            "blk",
            scatter_dimension=0,
            tiled=True,
        ).astype(jnp.float32),
        lax.psum_scatter(
            gv_blocks.reshape(length, KV * HD).astype(jnp.bfloat16),
            "blk",
            scatter_dimension=0,
            tiled=True,
        ).astype(jnp.float32),
    )
    grad_qr = unrotary(grad_q.reshape(tok, H, HD), cosine, sine).reshape(tok, H * HD).astype(bf16)
    grad_kr = unrotary(grad_k.reshape(tok, KV, HD), cosine, sine).reshape(tok, KV * HD).astype(bf16)
    grad_vr = grad_v.astype(bf16)
    d_query = jnp.einsum("td,te->de", xa, grad_qr, preferred_element_type=f32)
    d_key = jnp.einsum("td,te->de", xa, grad_kr, preferred_element_type=f32)
    d_value = jnp.einsum("td,te->de", xa, grad_vr, preferred_element_type=f32)
    grad_xa = (
        jnp.einsum("te,de->td", grad_qr, w_query, preferred_element_type=f32)
        + jnp.einsum("te,de->td", grad_kr, w_key, preferred_element_type=f32)
        + jnp.einsum("te,de->td", grad_vr, w_value, preferred_element_type=f32)
    )
    grad_x_norm, d_gain1 = rms_back(xs, scale1, norm1_gain, grad_xa)
    grad_x = grad_h1 + grad_x_norm
    summed = lax.psum(
        (d_gain1, d_query, d_key, d_value, d_out_w, d_gain2, d_router), ("seq", "blk")
    )
    expert_summed = (
        lax.psum(d_gate_w.astype(jnp.bfloat16), "seq").astype(jnp.float32),
        lax.psum(d_up_w.astype(jnp.bfloat16), "seq").astype(jnp.float32),
        lax.psum(d_down.astype(jnp.bfloat16), "seq").astype(jnp.float32),
    )
    return (
        result.astype(bf16)[None],
        grad_x[None],
        summed[0],
        summed[1],
        summed[2],
        summed[3],
        summed[4],
        summed[5],
        summed[6],
        expert_summed[0],
        expert_summed[1],
        expert_summed[2],
    )


def tables(length):
    half = HD // 2
    freq = np.exp(-math.log(10000.0) * np.arange(half, dtype=np.float32) * 2.0 / HD).astype(np.float32)
    angle = np.arange(length, dtype=np.float32)[:, None] * freq[None, :]
    return np.tile(np.cos(angle), (1, 4)), np.tile(np.sin(angle), (1, 4))


def per_device(
    tokens,
    segments,
    routes,
    route_weight,
    norm1_gain,
    w_query,
    w_key,
    w_value,
    w_out,
    norm2_gain,
    w_router,
    w_gate,
    w_up,
    w_down,
    cotangent,
):
    xs = tokens[0].astype(F32)
    tok, d = xs.shape
    blocks = lax.axis_size("blk")
    experts = w_router.shape[1]
    cos_np, sin_np = tables(tok * blocks)
    cos_all = jnp.asarray(cos_np.reshape(blocks, tok, 2 * HD))
    sin_all = jnp.asarray(sin_np.reshape(blocks, tok, 2 * HD))
    seg = jnp.pad(segments[0].astype(BF16).reshape(2, tok // 2), ((0, 14), (0, 0)))
    gain1 = norm1_gain[None]
    g_low = cotangent[0]
    att_low, xa, *kept = attention_forward(
        blocks,
        tokens[0],
        gain1,
        w_query,
        w_key,
        w_value,
        seg,
        cos_all,
        sin_all,
        g_low,
        w_gate[0],
        w_up[0],
        w_down[0],
    )
    kept, shared = kept[:5], kept[5:]

    h1 = xs + mm(att_low, w_out)
    scale2 = rms_scale(h1)
    xl = (h1 * scale2 * norm2_gain).astype(BF16)
    logits = mm(xl, w_router)
    chooser = routes[0][:, :, None] == jnp.arange(experts, dtype=jnp.int32)[None, None, :]
    routed = jnp.any(chooser, 1)
    rweight = jnp.sum(jnp.where(chooser, route_weight[0][:, :, None], 0.0), 1)
    top = jnp.max(jnp.where(routed, logits, NEG), -1, keepdims=True)
    expo = jnp.where(routed, jnp.exp(logits - top), 0.0)
    gates = expo / jnp.sum(expo, -1, keepdims=True)
    combine = (rweight * gates).astype(BF16)
    sent = jnp.concatenate([xl, jnp.pad(combine, ((0, 0), (0, 128 - experts)))], 1)
    mix_own, mix_peer, d_in, dwg, dwu, dwd, *far = mixture(
        sent, g_low, w_gate[0], w_up[0], w_down[0], *shared
    )

    grad_out = g_low.astype(F32)
    grad_gates = rweight * d_in[:, d : d + experts]
    grad_logits = (
        gates * (grad_gates - jnp.sum(gates * grad_gates, -1, keepdims=True))
    ).astype(BF16)
    grad_xl = d_in[:, :d] + mm(grad_logits, w_router, NT)
    grad_h1_norm, unused = rms_back(h1, scale2, norm2_gain, grad_xl)
    gain2_terms = jnp.sum((grad_xl * h1 * scale2).reshape(tok // 8, 8, d), 0)
    grad_h1 = grad_out + grad_h1_norm
    grad_att = grad_h1.astype(BF16)
    grad_o = mm(grad_att, w_out, NT).astype(BF16)
    vectors = (
        grad_o,
        *kept,
        cos_all,
        sin_all,
    )
    got, mix_near, *arrived = attention_backward(
        blocks, vectors, mix_peer, dwg, dwu, dwd
    )
    blocks_in = (
        got,
        xa,
        tokens[0],
        gain1,
        grad_h1,
        w_query,
        w_key,
        w_value,
        att_low,
        grad_att,
        xl,
        jnp.pad(grad_logits, ((0, 0), (0, 128 - experts))),
        gain2_terms,
        h1,
        mix_own,
    )
    result, grad_x, gains, d_out, d_query, d_kv, d_gate_w, d_up_w, d_down = tail(
        blocks_in, mix_peer, mix_near, (dwg, dwu, dwd), arrived, far
    )
    wide = widen(gains, d_out, d_query, d_kv, d_gate_w, d_up_w, d_down, experts)
    d_gain1, d_query, d_key, d_value, d_out, d_gain2, *rest = wide
    return (
        result[None],
        grad_x[None],
        d_gain1[0],
        d_query,
        d_key,
        d_value,
        d_out,
        d_gain2[0],
        *rest,
    )


def solution(mesh):
    fused = dict(mesh.shape) == {"seq": 2, "blk": 2 * KV}
    return jax.shard_map(
        per_device if fused else per_device_plain,
        mesh=mesh,
        in_specs=(
            P("seq", "blk", None),
            P("seq", "blk"),
            P("seq", "blk", None),
            P("seq", "blk", None),
            P(),
            P(),
            P(),
            P(),
            P(),
            P(),
            P(),
            P("blk", None, None),
            P("blk", None, None),
            P("blk", None, None),
            P("seq", "blk", None),
        ),
        out_specs=(
            P("seq", "blk", None),
            P("seq", "blk", None),
            P(),
            P(),
            P(),
            P(),
            P(),
            P(),
            P(),
            P("blk", None, None),
            P("blk", None, None),
            P("blk", None, None),
        ),
        check_vma=False,
    )
```

```python
import functools
import math

import jax
import jax.numpy as jnp
import numpy as np
from jax import lax
from jax.experimental import pallas as pl
from jax.experimental.pallas import tpu as pltpu
from jax.sharding import PartitionSpec as P

H = 16
KV = 8
HD = 64
TOP = 8
EPS = 1e-06
NEG = -1e30
F32 = jnp.float32
BF16 = jnp.bfloat16
MESH = pl.DeviceIdType.MESH
VMEM_LIMIT = 60 * 2**20
GRAD_STEPS = (1, 4, 6)
HOP_STEP = 4
NT = (((1,), (1,)), ((), ()))
TN = (((0,), (0,)), ((), ()))


def mm(a, b, dims=(((1,), (0,)), ((), ()))):
    return lax.dot_general(a, b, dims, preferred_element_type=F32)


def remote(src, dst, send, recv, seq, blk):
    return pltpu.make_async_remote_copy(
        src_ref=src,
        dst_ref=dst,
        send_sem=send,
        recv_sem=recv,
        device_id=(seq, blk),
        device_id_type=MESH,
    )


def greet_all(seqs, blocks, me_s, me_b):
    barrier = pltpu.get_barrier_semaphore()
    total = seqs * blocks

    def hello(n, carry):
        other = lax.rem(me_s * blocks + me_b + n, total)
        pl.semaphore_signal(
            barrier,
            inc=1,
            device_id=(other // blocks, lax.rem(other, blocks)),
            device_id_type=MESH,
        )
        return carry

    lax.fori_loop(1, total, hello, 0)
    pl.semaphore_wait(barrier, total - 1)


def flip(place, n):
    if n == 1:
        return place + 1 - 2 * lax.rem(place, 2)
    if n == 2:
        return place + 2 - 4 * (place // 2)
    return 3 - place


def rotate_pairs(u):
    lanes = u.shape[-1]
    half = HD // 2
    lane = lax.broadcasted_iota(jnp.int32, u.shape, u.ndim - 1)
    ahead = pltpu.roll(u, lanes - half, u.ndim - 1)
    behind = pltpu.roll(u, half, u.ndim - 1)
    return jnp.where(lane % HD < half, -ahead, behind)


def stacked_heads(wide):
    return jnp.concatenate([wide[:HD], wide[HD:]], axis=1)


STAGES = 6


class Summed:
    def __init__(self, refs, send_sem, recv_sem, fin):
        self.out, self.arrived, self.acc, self.part, self.plane_in, self.line_in = refs
        self.send_sem, self.recv_sem, self.fin = send_sem, recv_sem, fin
        self.me_s = lax.axis_index("seq")
        me_b = lax.axis_index("blk")
        self.line, self.plane = me_b // 4, lax.rem(me_b, 4)
        self.sibling = [(1 - self.me_s, me_b)]
        self.planes = [(self.me_s, self.line * 4 + flip(self.plane, n)) for n in (1, 2, 3)]
        self.lines = [(self.me_s, flip(self.line, n) * 4 + self.plane) for n in (1, 2, 3)]
        rows = fin.shape[0]
        self.half, self.quarter, self.piece = rows // 2, rows // 8, rows // 32

    def rows(self, start, size):
        return pl.ds(pl.multiple_of(start, size), size)

    def halves(self):
        theirs = self.rows((1 - self.me_s) * self.half, self.half)
        return theirs, self.rows(self.me_s * self.half, self.half)

    def copy(self, stage, n):
        sems = self.send_sem.at[stage, n], self.recv_sem.at[stage, n]
        base = self.me_s * self.half
        if stage == 0:
            return remote(self.out, self.arrived, *sems, *self.sibling[n])
        if stage == 1:
            src = self.part.at[self.rows(flip(self.plane, n + 1) * self.quarter, self.quarter)]
            return remote(src, self.plane_in.at[n], *sems, *self.planes[n])
        if stage == 2:
            at = self.plane * self.quarter + flip(self.line, n + 1) * self.piece
            src = self.part.at[self.rows(at, self.piece)]
            return remote(src, self.line_in.at[n], *sems, *self.lines[n])
        if stage == 3:
            at = base + self.plane * self.quarter + self.line * self.piece
            part = self.fin.at[self.rows(at, self.piece)]
            return remote(part, part, *sems, *self.lines[n])
        if stage == 4:
            part = self.fin.at[self.rows(base + self.plane * self.quarter, self.quarter)]
            return remote(part, part, *sems, *self.planes[n])
        part = self.fin.at[self.rows(base, self.half)]
        return remote(part, part, *sems, *self.sibling[n])

    def start(self, stage):
        for n in range(1) if stage in (0, 5) else (2, 0, 1):
            self.copy(stage, n).start()

    def arrive(self, stage):
        for n in range(1 if stage in (0, 5) else 3):
            self.copy(stage, n).wait_recv()

    def pair(self):
        self.arrive(0)
        self.part[...] = (self.acc[...] + self.arrived[...].astype(F32)).astype(BF16)
        self.start(1)

    def over_plane(self):
        self.arrive(1)
        here = self.rows(self.plane * self.quarter, self.quarter)
        total = self.part[here, :].astype(F32)
        for n in range(3):
            total = total + self.plane_in[n].astype(F32)
        self.part[here, :] = total.astype(BF16)
        self.start(2)

    def over_line(self):
        self.arrive(2)
        at = self.plane * self.quarter + self.line * self.piece
        total = self.part[self.rows(at, self.piece), :].astype(F32)
        for n in range(3):
            total = total + self.line_in[n].astype(F32)
        self.fin[self.rows(self.me_s * self.half + at, self.piece), :] = total.astype(BF16)
        self.start(3)

    def back(self, stage):
        self.arrive(stage)
        self.start(stage + 1)

    def finish(self):
        self.arrive(5)
        for stage in range(STAGES):
            for n in range(1 if stage in (0, 5) else 3):
                self.copy(stage, n).wait_send()


def summed_scratch(rows, width):
    vmem, dma = pltpu.VMEM, pltpu.SemaphoreType.DMA
    return [
        vmem((rows // 2, width), BF16),
        vmem((rows // 2, width), BF16),
        vmem((rows // 2, width), F32),
        vmem((rows // 2, width), BF16),
        vmem((3, rows // 8, width), BF16),
        vmem((3, rows // 32, width), BF16),
        dma((STAGES, 3)),
        dma((STAGES, 3)),
    ]


def attention_forward_kernel(
    blocks,
    x_ref,
    gain_ref,
    wq_ref,
    wk_ref,
    wv_ref,
    seg_ref,
    cos_ref,
    sin_ref,
    g_ref,
    wg_ref,
    wu_ref,
    wd_ref,
    o_ref,
    xa_ref,
    kv_ref,
    kvt_ref,
    q_ref,
    ot_ref,
    stat_ref,
    g_all,
    wg_all,
    wu_all,
    wd_all,
    pay,
    turn,
    in_ref,
    other_ref,
    obuf,
    cnt,
    turn_sem,
    send_sem,
    recv_sem,
    fsend_sem,
    frecv_sem,
    osend_sem,
    orecv_sem,
    gsend_sem,
    grecv_sem,
    wsend_sem,
    wrecv_sem,
    hsend_sem,
    hrecv_sem,
    dsend_sem,
    drecv_sem,
):
    me_s = lax.axis_index("seq")
    me_b = lax.axis_index("blk")
    tok = q_ref.shape[1]
    steps = blocks // 2
    sigma = me_b // KV
    kappa = lax.rem(me_b, KV)
    greet_all(2, blocks, me_s, me_b)
    dest_core = lax.rem(me_b, 2)
    slot = me_b // 2
    line, plane = me_b // 4, lax.rem(me_b, 4)
    weights = ((wg_ref, wg_all), (wu_ref, wu_all), (wd_ref, wd_all))

    def along(k, step, own):
        at = 0 if step < 0 else 1
        return remote(
            g_ref if own else g_all.at[k],
            g_all.at[k],
            gsend_sem.at[at, k],
            grecv_sem.at[k],
            me_s,
            (line + step) * 4 + plane,
        )

    def pass_on(k, step, own=False):
        @pl.when((line + step >= 0) & (line + step < 4))
        def _():
            along(k, step, own).start()

    def pass_distance(j):
        for step in (-1, 1):
            k = line - step * j

            @pl.when((k >= 0) & (k < 4))
            def _():
                pltpu.make_async_copy(g_ref, g_all.at[k], grecv_sem.at[k]).wait()
                pass_on(k, step)

    def half(ref):
        rows = ref.shape[0] // 2
        return ref.at[pl.ds(pl.multiple_of(me_s * rows, rows), rows)]

    def share_weight(n, i):
        own, everyone = weights[i]
        return remote(
            half(own),
            half(everyone.at[plane]),
            wsend_sem.at[n - 1, i],
            wrecv_sem.at[n - 1, i],
            me_s,
            line * 4 + flip(plane, n),
        )

    def diagonal(n, i):
        place = weights[i][1].at[flip(plane, n)]
        rows = place.shape[0] // 2
        start, size = me_s * rows, rows
        if i == 2:
            size = rows // 2
            start = start + (n - 1) * size
        part = place.at[pl.ds(pl.multiple_of(start, size), size)]
        return remote(
            part,
            part,
            dsend_sem.at[n - 1, i],
            drecv_sem.at[n - 1, i],
            me_s,
            line * 4 + flip(plane, 3 - n),
        )

    def diagonal_in(n, i):
        place = weights[i][1].at[flip(plane, 3)]
        rows = place.shape[0] // 2
        start, size = me_s * rows, rows
        if i == 2:
            size = rows // 2
            start = start + (2 - n) * size
        part = place.at[pl.ds(pl.multiple_of(start, size), size)]
        return pltpu.make_async_copy(part, part, drecv_sem.at[2 - n, i])

    def pass_weight(n, i):
        arrived = half(weights[i][1].at[flip(plane, n)])
        return remote(
            arrived, arrived, hsend_sem.at[n - 1, i], hrecv_sem.at[n - 1, i], 1 - me_s, me_b
        )

    tables_in = [
        pltpu.make_async_copy(src.at[me_b], turn.at[i], turn_sem.at[i])
        for i, src in enumerate((cos_ref, sin_ref))
    ]
    for copy in tables_in:
        copy.start()
    xs = x_ref[...].astype(F32)
    xa = (xs * rms_scale(xs) * gain_ref[...]).astype(BF16)
    xa_ref[...] = xa
    for copy in tables_in:
        copy.wait()
    cosine, sine = turn[0], turn[1]
    low = lax.broadcasted_iota(jnp.int32, (tok, 2 * HD), 1) < HD
    pay[:, tok:, : 2 * HD] = jnp.zeros((KV, 16, 2 * HD), BF16)
    for m in range(KV // 2):
        pair = slice(m * 2 * HD, (m + 1) * 2 * HD)
        keys = mm(xa, wk_ref[:, pair])
        keys = keys * cosine + rotate_pairs(keys) * sine
        values = mm(xa, wv_ref[:, pair])
        first = jnp.where(low, keys, pltpu.roll(values, HD, 1))
        second = jnp.where(low, pltpu.roll(keys, HD, 1), values)
        pay[2 * m, :tok, 2 * HD :] = first.astype(BF16)
        pay[2 * m + 1, :tok, 2 * HD :] = second.astype(BF16)
        for k in (2 * m, 2 * m + 1):
            query = mm(xa, wq_ref[:, k * 2 * HD : (k + 1) * 2 * HD])
            query = (query * cosine + rotate_pairs(query) * sine) * HD ** (-0.5)
            pay[k, :tok, : 2 * HD] = query.astype(BF16)
            pay[k, tok:, 2 * HD :] = seg_ref[...]
    def payload(n):
        k = lax.rem(me_b + n, KV)
        chip = me_s * KV + k
        mine = (dest_core == me_s) & (chip == me_b)
        return k, chip, mine

    def send_payload(n, carry):
        k, chip, mine = payload(n)

        @pl.when(mine)
        def _():
            pltpu.make_async_copy(pay.at[k], in_ref.at[slot], recv_sem.at[slot]).start()

        @pl.when(jnp.logical_not(mine))
        def _():
            remote(
                pay.at[k], in_ref.at[slot], send_sem.at[k], recv_sem.at[slot], dest_core, chip
            ).start()

        return carry

    lax.fori_loop(0, KV, send_payload, 0)
    for i in range(3):
        share_weight(1, (0, 2, 1)[i]).start()
        share_weight(2, (1, 2, 0)[i]).start()

    def arrival(t):
        return pltpu.make_async_copy(pay.at[0], in_ref.at[t], recv_sem.at[t])

    def forward(t):
        return remote(
            in_ref.at[t, :, pl.ds(2 * HD, 2 * HD)],
            other_ref.at[t],
            fsend_sem.at[t],
            frecv_sem.at[t],
            1 - me_s,
            me_b,
        )

    arrival(0).wait()
    forward(0).start()
    cnt[...] = jnp.zeros_like(cnt)
    first_core = me_s == 0
    lane = lax.broadcasted_iota(jnp.int32, (1, 2 * tok), 1)
    qrow = jnp.where(lane < tok, lane, lane - tok)
    wide = 2 * tok

    def step(t, carry):
        @pl.when(t < steps - 1)
        def _():
            arrival(t + 1).wait()
            forward(t + 1).start()

        @pl.when(t == GRAD_STEPS[0])
        def _():
            for step in (-1, 1):
                pass_on(line, step, True)

        for j in (1, 2):

            @pl.when(t == GRAD_STEPS[j])
            def _():
                pass_distance(j)

        @pl.when(t == HOP_STEP)
        def _():
            for n, i in ((1, 0), (2, 1)):
                share_weight(n, i).wait_recv()
                diagonal(n, i).start()
                pass_weight(n, i).start()

        @pl.when(t == HOP_STEP + 1)
        def _():
            for n, i in ((1, 2), (2, 2)):
                share_weight(n, i).wait_recv()
                diagonal(n, i).start()
                pass_weight(n, i).start()

        @pl.when(t == HOP_STEP + 2)
        def _():
            for n, i in ((1, 1), (2, 0)):
                share_weight(n, i).wait_recv()
                pass_weight(n, i).start()

        forward(t).wait_recv()
        mine = in_ref[t]
        kv_mine, seg_mine = mine[:tok, 2 * HD :], mine[tok:, 2 * HD :].astype(F32)
        other = other_ref[t]
        kv_other, seg_other = other[:tok], other[tok:].astype(F32)
        pair = jnp.where(
            first_core,
            jnp.concatenate([kv_mine, kv_other], 0).astype(F32),
            jnp.concatenate([kv_other, kv_mine], 0).astype(F32),
        )
        kv_ref[t] = pair.astype(BF16)
        kvt_ref[t] = jnp.transpose(pair).astype(BF16)
        number = lax.broadcasted_iota(jnp.int32, (8, tok), 0).astype(F32)
        seg_q = jnp.concatenate([seg_mine[0:1], seg_mine[1:2]], 1)
        seg_o = jnp.concatenate([seg_other[0:1], seg_other[1:2]], 1)
        below = (seg_q < number).astype(F32) + (seg_o < number).astype(F32)
        cnt[...] += jnp.sum(below, 1, keepdims=True)
        start_q = jnp.sum(jnp.where(seg_q == number, cnt[:, :1], 0.0), 0, keepdims=True)
        start = jnp.concatenate([start_q, start_q], 1).astype(jnp.int32)
        q_two = mine[:tok, : 2 * HD]
        q_ref[t] = q_two
        qt = stacked_heads(jnp.transpose(q_two.astype(F32)))
        qm = jnp.concatenate([qt, jnp.zeros_like(qt)], 0).astype(BF16)
        qpos = (2 * t + me_s) * tok + qrow

        def piece(u, state, last):
            running, total, acc = state
            score = mm(kv_ref[u], qm)
            kpos = u * wide + lax.broadcasted_iota(jnp.int32, score.shape, 0)
            mask = kpos >= start
            if last:
                mask &= kpos <= qpos
            score = jnp.where(mask, score, NEG)
            newmax = jnp.maximum(running, jnp.max(score, 0, keepdims=True))
            expo = jnp.exp(score - newmax)
            factor = jnp.exp(running - newmax)
            total = total * factor + jnp.sum(expo, 0, keepdims=True)
            acc = acc * factor + mm(kvt_ref[u, HD:, :], expo.astype(BF16))
            return newmax, total, acc

        state = (
            jnp.full((1, wide), NEG, F32),
            jnp.zeros((1, wide), F32),
            jnp.zeros((HD, wide), F32),
        )
        state = lax.fori_loop(0, t, lambda u, s: piece(u, s, False), state)
        running, total, acc = piece(t, state, True)
        out_t = acc / total
        ot_ref[t] = out_t
        rows = lax.broadcasted_iota(jnp.int32, (8, wide), 0)
        lse = running + jnp.log(total)
        stat_ref[t] = jnp.where(rows == 0, lse, start.astype(F32))
        upright = jnp.concatenate([out_t[:, :tok], out_t[:, tok:]], 0)
        obuf[t] = jnp.transpose(upright).astype(BF16)
        owner = 2 * t + me_s
        home = (sigma == me_s) & (owner == me_b)
        place = o_ref.at[:, pl.ds(pl.multiple_of(kappa * 2 * HD, 2 * HD), 2 * HD)]

        @pl.when(home)
        def _():
            pltpu.make_async_copy(obuf.at[t], place, orecv_sem.at[kappa]).start()

        @pl.when(jnp.logical_not(home))
        def _():
            remote(obuf.at[t], place, osend_sem.at[t], orecv_sem.at[kappa], sigma, owner).start()

        return carry

    lax.fori_loop(0, steps, step, 0)
    diagonal_in(2, 0).wait()
    pass_weight(3, 0).start()
    diagonal_in(1, 1).wait()
    pass_weight(3, 1).start()
    diagonal_in(1, 2).wait()
    diagonal_in(2, 2).wait()
    pass_weight(3, 2).start()

    def finish(t, carry):
        k, chip, mine = payload(t)

        @pl.when(jnp.logical_not(mine))
        def _():
            remote(
                pay.at[k], in_ref.at[slot], send_sem.at[k], recv_sem.at[slot], dest_core, chip
            ).wait_send()

        return carry

    lax.fori_loop(0, KV, finish, 0)

    def finish_steps(t, carry):
        forward(t).wait_send()
        owner = 2 * t + me_s
        home = (sigma == me_s) & (owner == me_b)

        @pl.when(jnp.logical_not(home))
        def _():
            remote(
                obuf.at[t],
                o_ref.at[:, pl.ds(0, 2 * HD)],
                osend_sem.at[t],
                orecv_sem.at[0],
                sigma,
                owner,
            ).wait_send()

        return carry

    lax.fori_loop(0, steps, finish_steps, 0)

    def gather(k, carry):
        pltpu.make_async_copy(
            obuf.at[0],
            o_ref.at[:, pl.ds(pl.multiple_of(k * 2 * HD, 2 * HD), 2 * HD)],
            orecv_sem.at[k],
        ).wait()
        return carry

    lax.fori_loop(0, KV, gather, 0)
    pass_distance(3)
    for k in range(4):

        @pl.when((k <= line) & (line < 3))
        def _():
            along(k, 1, False).wait_send()

        @pl.when((k >= line) & (line > 0))
        def _():
            along(k, -1, False).wait_send()

    for n in (1, 2, 3):
        for i in range(3):
            pass_weight(n, i).wait()
    for n in (1, 2):
        for i in range(3):
            share_weight(n, i).wait_send()
        diagonal(n, n - 1).wait_send()
        diagonal(n, 2).wait_send()


def attention_forward(
    blocks, x, gain, w_query, w_key, w_value, seg, cos_all, sin_all, g, w_gate, w_up, w_down
):
    tok, d = x.shape
    steps = blocks // 2
    vm = pl.BlockSpec(memory_space=pltpu.VMEM)
    hbm = pl.BlockSpec(memory_space=pl.ANY)
    dma = pltpu.SemaphoreType.DMA
    return pl.pallas_call(
        functools.partial(attention_forward_kernel, blocks),
        out_shape=(
            jax.ShapeDtypeStruct((tok, H * HD), BF16),
            jax.ShapeDtypeStruct((tok, d), BF16),
            jax.ShapeDtypeStruct((steps, 2 * tok, 2 * HD), BF16),
            jax.ShapeDtypeStruct((steps, 2 * HD, 2 * tok), BF16),
            jax.ShapeDtypeStruct((steps, tok, 2 * HD), BF16),
            jax.ShapeDtypeStruct((steps, HD, 2 * tok), F32),
            jax.ShapeDtypeStruct((steps, 8, 2 * tok), F32),
            jax.ShapeDtypeStruct((4, *g.shape), BF16),
            jax.ShapeDtypeStruct((4, *w_gate.shape), BF16),
            jax.ShapeDtypeStruct((4, *w_up.shape), BF16),
            jax.ShapeDtypeStruct((4, *w_down.shape), BF16),
        ),
        in_specs=[vm] * 6 + [hbm] * 6,
        out_specs=(vm,) * 7 + (hbm,) * 4,
        scratch_shapes=[
            pltpu.VMEM((KV, tok + 16, 4 * HD), BF16),
            pltpu.VMEM((2, tok, 2 * HD), F32),
            pltpu.VMEM((steps, tok + 16, 4 * HD), BF16),
            pltpu.VMEM((steps, tok + 16, 2 * HD), BF16),
            pltpu.VMEM((steps, tok, 2 * HD), BF16),
            pltpu.VMEM((8, 128), F32),
            dma((2,)),
            dma((KV,)),
            dma((steps,)),
            dma((steps,)),
            dma((steps,)),
            dma((steps,)),
            dma((KV,)),
            dma((2, 4)),
            dma((4,)),
            dma((2, 3)),
            dma((2, 3)),
            dma((3, 3)),
            dma((3, 3)),
            dma((2, 3)),
            dma((2, 3)),
        ],
        compiler_params=pltpu.CompilerParams(
            collective_id=0, has_side_effects=True, vmem_limit_bytes=VMEM_LIMIT
        ),
        name="attention_forward",
    )(x, gain, w_query, w_key, w_value, seg, cos_all, sin_all, g, w_gate, w_up, w_down)


def attention_backward_kernel(
    blocks,
    do_ref,
    kv_ref,
    kvt_ref,
    q_ref,
    ot_ref,
    stat_ref,
    cos_ref,
    sin_ref,
    mix_ref,
    dwg_ref,
    dwu_ref,
    dwd_ref,
    out_ref,
    mix_in,
    dwg_in,
    dwu_in,
    dwd_in,
    turn,
    turn_sem,
    in_ref,
    dkv,
    part,
    xch,
    done,
    send_sem,
    recv_sem,
    xsend_sem,
    xrecv_sem,
    osend_sem,
    orecv_sem,
    msend_sem,
    mrecv_sem,
    wsend_sem,
    wrecv_sem,
):
    me_s = lax.axis_index("seq")
    me_b = lax.axis_index("blk")
    tok = q_ref.shape[1]
    steps = blocks // 2
    sigma = me_b // KV
    kappa = lax.rem(me_b, KV)
    tables_in = [
        pltpu.make_async_copy(src.at[2 * t + me_s], turn.at[i, t], turn_sem.at[i, t])
        for i, src in enumerate((cos_ref, sin_ref))
        for t in range(steps)
    ]
    for copy in tables_in:
        copy.start()
    greet_all(2, blocks, me_s, me_b)

    dest_core = lax.rem(me_b, 2)
    slot = me_b // 2
    line, plane = me_b // 4, lax.rem(me_b, 4)
    weights = ((dwg_ref, dwg_in), (dwu_ref, dwu_in), (dwd_ref, dwd_in))

    def give_mix(n):
        return remote(
            mix_ref.at[flip(line, n)],
            mix_in.at[n - 1],
            msend_sem.at[n - 1],
            mrecv_sem.at[n - 1],
            me_s,
            flip(line, n) * 4 + plane,
        )

    def give_weight(n, i):
        src, dst = weights[i]
        return remote(
            src.at[flip(plane, n)],
            dst.at[n - 1],
            wsend_sem.at[n - 1, i],
            wrecv_sem.at[n - 1, i],
            me_s,
            line * 4 + flip(plane, n),
        )

    def outgoing(n):
        k = lax.rem(me_b + n, KV)
        chip = me_s * KV + k
        mine = (dest_core == me_s) & (chip == me_b)
        src = do_ref.at[:, pl.ds(pl.multiple_of(k * 2 * HD, 2 * HD), 2 * HD)]
        return k, chip, mine, src

    def send_grad(n, carry):
        k, chip, mine, src = outgoing(n)

        @pl.when(mine)
        def _():
            pltpu.make_async_copy(src, in_ref.at[slot], recv_sem.at[slot]).start()

        @pl.when(jnp.logical_not(mine))
        def _():
            remote(src, in_ref.at[slot], send_sem.at[k], recv_sem.at[slot], dest_core, chip).start()

        return carry

    lax.fori_loop(0, KV, send_grad, 0)
    for copy in tables_in:
        copy.wait()
    for n in (2, 1):
        give_mix(n).start()
    for i in range(3):
        for n in (1, 2):
            give_weight(n, i).start()
    give_weight(3, 2).start()
    dkv[...] = jnp.zeros_like(dkv)
    wide = 2 * tok
    lane = lax.broadcasted_iota(jnp.int32, (1, wide), 1)
    qrow = jnp.where(lane < tok, lane, lane - tok)
    low = lax.broadcasted_iota(jnp.int32, (tok, 2 * HD), 1) < HD

    def swap(t):
        return remote(part.at[t], xch.at[t], xsend_sem.at[t], xrecv_sem.at[t], 1 - me_s, me_b)

    def deliver(t, act):
        owner = 2 * t + me_s
        home = (sigma == me_s) & (owner == me_b)
        src, dst = done.at[t], out_ref.at[kappa]

        @pl.when(home)
        def _():
            if act == "start":
                pltpu.make_async_copy(src, dst, orecv_sem.at[kappa]).start()

        @pl.when(jnp.logical_not(home))
        def _():
            copy = remote(src, dst, osend_sem.at[t], orecv_sem.at[kappa], sigma, owner)
            copy.start() if act == "start" else copy.wait_send()

    def finalize(t):
        swap(t).wait_recv()
        place = pl.ds(pl.multiple_of(me_s * tok, tok), tok)
        total = dkv[t, place, :] + xch[t]
        cosine = jnp.where(low, turn[0, t], 1.0)
        sine = jnp.where(low, turn[1, t], 0.0)
        back = total * cosine - rotate_pairs(total) * sine
        done[t, :, pl.ds(2 * HD, 2 * HD)] = back.astype(BF16)
        deliver(t, "start")

    def step(n, carry):
        t = steps - 1 - n
        pltpu.make_async_copy(do_ref.at[:, pl.ds(0, 2 * HD)], in_ref.at[t], recv_sem.at[t]).wait()
        d_two = in_ref[t].astype(F32)
        q_two = q_ref[t].astype(F32)
        dt = stacked_heads(jnp.transpose(d_two))
        qt = stacked_heads(jnp.transpose(q_two))
        zero = jnp.zeros_like(dt)
        dm = jnp.concatenate([zero, dt], 0).astype(BF16)
        qm = jnp.concatenate([qt, zero], 0).astype(BF16)
        delta = jnp.sum(ot_ref[t] * dt, 0, keepdims=True)
        right = jnp.concatenate(
            [
                jnp.where(low, q_two, 0.0),
                jnp.where(low, pltpu.roll(q_two, HD, 1), 0.0),
                jnp.where(low, 0.0, pltpu.roll(d_two, HD, 1)),
                jnp.where(low, 0.0, d_two),
            ],
            0,
        ).astype(BF16)
        stat = stat_ref[t]
        lse, start = stat[0:1], stat[1:2].astype(jnp.int32)
        qpos = (2 * t + me_s) * tok + qrow

        def piece(u, dq, last):
            keys = kv_ref[u]
            score = mm(keys, qm)
            kpos = u * wide + lax.broadcasted_iota(jnp.int32, score.shape, 0)
            mask = kpos >= start
            if last:
                mask &= kpos <= qpos
            prob = jnp.where(mask, jnp.exp(score - lse), 0.0)
            dprob = mm(keys, dm)
            dscore = (prob * (dprob - delta)).astype(BF16)
            both = jnp.concatenate([dscore, prob.astype(BF16)], 1)
            dkv[u] += mm(both, right)
            return dq + mm(kvt_ref[u, :HD, :], dscore)

        dq = jnp.zeros((HD, wide), F32)
        dq = lax.fori_loop(0, t, lambda u, s: piece(u, s, False), dq)
        dq = piece(t, dq, True) * HD ** (-0.5)
        upright = jnp.transpose(jnp.concatenate([dq[:, :tok], dq[:, tok:]], 0))
        back = upright * turn[0, t] - rotate_pairs(upright) * turn[1, t]
        done[t, :, pl.ds(0, 2 * HD)] = back.astype(BF16)
        part[t] = dkv[t, pl.ds(pl.multiple_of((1 - me_s) * tok, tok), tok), :]
        swap(t).start()

        @pl.when(n > 0)
        def _():
            finalize(t + 1)

        return carry

    lax.fori_loop(0, steps, step, 0)
    finalize(0)

    def finish(n, carry):
        k, chip, mine, src = outgoing(n)

        @pl.when(jnp.logical_not(mine))
        def _():
            remote(
                src, in_ref.at[slot], send_sem.at[k], recv_sem.at[slot], dest_core, chip
            ).wait_send()

        return carry

    lax.fori_loop(0, KV, finish, 0)

    def finish_steps(t, carry):
        swap(t).wait_send()
        deliver(t, "wait")
        return carry

    lax.fori_loop(0, steps, finish_steps, 0)

    def gather(k, carry):
        pltpu.make_async_copy(done.at[0], out_ref.at[k], orecv_sem.at[k]).wait()
        return carry

    lax.fori_loop(0, KV, gather, 0)
    for n in (1, 2):
        give_mix(n).wait()
        for i in range(3):
            give_weight(n, i).wait()
    give_weight(3, 2).wait()


def attention_backward(
    blocks, vectors, mix, dwg, dwu, dwd
):
    tok = vectors[0].shape[0]
    steps = blocks // 2
    vm = pl.BlockSpec(memory_space=pltpu.VMEM)
    hbm = pl.BlockSpec(memory_space=pl.ANY)
    dma = pltpu.SemaphoreType.DMA
    return pl.pallas_call(
        functools.partial(attention_backward_kernel, blocks),
        out_shape=(
            jax.ShapeDtypeStruct((KV, tok, 4 * HD), BF16),
            jax.ShapeDtypeStruct((2, *mix.shape[1:]), BF16),
            jax.ShapeDtypeStruct((2, *dwg.shape[1:]), BF16),
            jax.ShapeDtypeStruct((2, *dwu.shape[1:]), BF16),
            jax.ShapeDtypeStruct((3, *dwd.shape[1:]), BF16),
        ),
        in_specs=[vm] * (len(vectors) - 2) + [hbm] * 6,
        out_specs=(vm,) + (hbm,) * 4,
        scratch_shapes=[
            pltpu.VMEM((2, steps, tok, 2 * HD), F32),
            dma((2, steps)),
            pltpu.VMEM((steps, tok, 2 * HD), BF16),
            pltpu.VMEM((steps, 2 * tok, 2 * HD), F32),
            pltpu.VMEM((steps, tok, 2 * HD), F32),
            pltpu.VMEM((steps, tok, 2 * HD), F32),
            pltpu.VMEM((steps, tok, 4 * HD), BF16),
            dma((KV,)),
            dma((steps,)),
            dma((steps,)),
            dma((steps,)),
            dma((steps,)),
            dma((KV,)),
            dma((2,)),
            dma((2,)),
            dma((3, 3)),
            dma((3, 3)),
        ],
        compiler_params=pltpu.CompilerParams(
            collective_id=1, has_side_effects=True, vmem_limit_bytes=VMEM_LIMIT
        ),
        name="attention_backward",
    )(*vectors, mix, dwg, dwu, dwd)


def mixture_kernel(
    x_ref,
    ao_ref,
    gain_ref,
    router_ref,
    routes_ref,
    weight_ref,
    wo_ref,
    g_ref,
    wg_ref,
    wu_ref,
    wd_ref,
    g_all,
    wg_all,
    wu_all,
    wd_all,
    res_ref,
    mix_peer,
    xl_ref,
    dlog_ref,
    dh_ref,
    datt_ref,
    do_ref,
    dgain_ref,
    dwg_out,
    dwu_out,
    dwd_out,
    dwg_in,
    dwu_in,
    wr_ref,
    rw_ref,
    h1_ref,
    gate_ref,
    d_in,
    d_c,
    wo,
    x_in,
    x_t,
    g_in,
    wg,
    wu,
    wd,
    hc,
    dg,
    du,
    acc_o,
    acc_d,
    acc_c,
    d_send,
    d_recv,
    xg,
    xu,
    xd,
    load_sem,
    gload_sem,
    send_sem,
    recv_sem,
    bsend_sem,
    brecv_sem,
    psend_sem,
    precv_sem,
    store_sem,
    wsend_sem,
    wrecv_sem,
    wo_sem,
):
    me_s = lax.axis_index("seq")
    me_b = lax.axis_index("blk")
    line, plane = me_b // 4, lax.rem(me_b, 4)
    tok, d = g_in.shape[1:]
    ff = wg.shape[2]
    barrier = pltpu.get_barrier_semaphore()
    sibling = (1 - me_s, me_b)
    opposite = (me_s, line * 4 + flip(plane, 3))
    for place in [(me_s, flip(line, n) * 4 + plane) for n in (1, 2, 3)] + [sibling, opposite]:
        pl.semaphore_signal(barrier, inc=1, device_id=place, device_id_type=MESH)

    owns = ((wg_ref, wg_all, wg), (wu_ref, wu_all, wu), (wd_ref, wd_all, wd))

    def load_own(i):
        return pltpu.make_async_copy(owns[i][0], owns[i][2].at[plane], load_sem.at[i, plane])

    def load_other(i, e):
        return pltpu.make_async_copy(owns[i][1].at[e], owns[i][2].at[e], load_sem.at[i, e])

    load_out = pltpu.make_async_copy(wo_ref, wo, wo_sem)
    load_out.start()
    for i in (2, 0, 1):
        load_own(i).start()
        for n in (1, 2, 3):
            load_other(i, flip(plane, n)).start()

    def load_grad(k):
        return pltpu.make_async_copy(g_all.at[k], g_in.at[k], gload_sem.at[k])

    pltpu.make_async_copy(g_ref, g_in.at[line], gload_sem.at[line]).start()
    for n in (1, 2, 3):
        load_grad(flip(line, n)).start()
    lane = lax.broadcasted_iota(jnp.int32, (tok, 128), 1)
    rw = jnp.zeros((tok, 128), F32)
    for j in range(TOP):
        rw += jnp.where(routes_ref[:, j : j + 1] == lane, weight_ref[:, j : j + 1], 0.0)
    rw_ref[...] = rw
    shape = (router_ref.shape[1], 128)
    row, column = (lax.broadcasted_iota(jnp.int32, shape, i) for i in range(2))
    wr_ref[...] = mm(router_ref[...], (row == column).astype(BF16)).astype(BF16)
    load_out.wait()
    xs = x_ref[...].astype(F32)
    h1 = xs + mm(ao_ref[...], wo[...])
    h1_ref[...] = h1
    xl = (h1 * rms_scale(h1) * gain_ref[...]).astype(BF16)
    xl_ref[...] = xl
    logits = mm(xl, wr_ref[...])
    routed = rw > 0.0
    top = jnp.max(jnp.where(routed, logits, NEG), -1, keepdims=True)
    expo = jnp.where(routed, jnp.exp(logits - top), 0.0)
    gates = expo / jnp.sum(expo, -1, keepdims=True)
    gate_ref[...] = gates
    x_in[line, :, :d] = xl
    x_in[line, :, d:] = (rw * gates).astype(BF16)
    pl.semaphore_wait(barrier, 5)

    def along(k, step):
        at = 0 if step < 0 else 1
        return remote(
            x_in.at[k],
            x_in.at[k],
            send_sem.at[at, k],
            recv_sem.at[k],
            me_s,
            (line + step) * 4 + plane,
        )

    def pass_on(k, step):
        @pl.when((line + step >= 0) & (line + step < 4))
        def _():
            along(k, step).start()

    for step in (-1, 1):
        pass_on(line, step)
    for k in range(4):
        load_grad(k).wait()
    g_rows = g_in.reshape(4 * tok, d)

    def grad_hidden(e, carry):
        load_other(2, e).wait()
        for part in range(2):
            rows = slice(part * 2 * tok, (part + 1) * 2 * tok)
            dg[e, rows, :] = mm(g_rows[rows, :], wd[e], NT).astype(BF16)
        return carry

    lax.fori_loop(0, 4, grad_hidden, 0)

    def load_wait(e, carry):
        for i in range(2):
            load_other(i, e).wait()
        return carry

    def apart(k):
        return lax.rem(k - line + 3, 4)

    def place_of(j):
        return jnp.where(line < 2, lax.rem(line + j, 4), lax.rem(line + 4 - j, 4))

    def block(j, carry):
        n = place_of(j)
        acc_o[...] = jnp.zeros_like(acc_o)
        acc_d[...] = jnp.zeros_like(acc_d)
        acc_c[...] = jnp.zeros_like(acc_c)
        rows = pl.ds(pl.multiple_of(n * tok, tok), tok)

        def expert(e, carry):
            @pl.when(j == 0)
            def _():
                load_wait(e, 0)

            for step in (-1, 1):
                k = line - step * (j + 1)

                @pl.when((e == 3) & (j < 3) & (k >= 0) & (k < 4))
                def _():
                    pltpu.make_async_copy(x_in.at[line], x_in.at[k], recv_sem.at[k]).wait()
                    pass_on(k, step)

            x = x_in[n, :, :d]
            here = lane == line * 4 + e
            share = jnp.sum(
                jnp.where(here, x_in[n, :, d:].astype(F32), 0.0), 1, keepdims=True
            )
            gate = mm(x, wg[e])
            up = mm(x, wu[e])
            dh = dg[e, rows, :].astype(F32)
            sg = jax.nn.sigmoid(gate)
            act = gate * sg
            hidden = act * up
            acc_c[...] += jnp.where(here, jnp.sum(dh * hidden, 1, keepdims=True), 0.0)
            dh = dh * share
            hcb = (hidden * share).astype(BF16)
            dgb = (dh * up * sg * (1.0 + gate * (1.0 - sg))).astype(BF16)
            dub = (dh * act).astype(BF16)
            hc[e, rows, :] = hcb
            dg[e, rows, :] = dgb
            du[e, rows, :] = dub
            acc_o[...] += mm(hcb, wd[e])
            acc_d[...] += mm(dgb, wg[e], NT) + mm(dub, wu[e], NT)
            return carry

        lax.fori_loop(0, 4, expert, 0)

        @pl.when(j == 0)
        def _():
            res_ref[...] = h1_ref[...] + acc_o[...]
            d_in[...] = acc_d[...]
            d_c[...] = acc_c[...]

        @pl.when(j > 0)
        def _():
            mix_peer[n] = acc_o[...].astype(BF16)
            to = apart(n)
            d_send[to, :, :d] = acc_d[...].astype(BF16)
            high = acc_c[...].astype(BF16).astype(F32)
            rest = acc_c[...] - high
            d_send[to, :, d:] = (high + pltpu.roll(rest, 32, 1)).astype(BF16)
            give_back(n).start()

        x_t[:, rows] = jnp.transpose(x_in[n, :, :d].astype(F32)).astype(BF16)
        return carry

    def give_back(n):
        return remote(
            d_send.at[apart(n)], d_recv.at[lax.rem(line - n + 3, 4)], bsend_sem.at[n], brecv_sem.at[line], me_s, n * 4 + plane
        )

    lax.fori_loop(0, 4, block, 0)

    half, dhalf = d // 2, ff // 2
    theirs = pl.multiple_of((1 - me_s) * half, half)
    dtheirs = pl.multiple_of((1 - me_s) * dhalf, dhalf)
    mine = pl.multiple_of(me_s * half, half)
    dmine = pl.multiple_of(me_s * dhalf, dhalf)

    def swap(i, e):
        src = (wg.at[e, pl.ds(0, half)], wu.at[e, pl.ds(0, half)], wd.at[e, pl.ds(0, dhalf)])[i]
        dst = (xg, xu, xd)[i].at[e]
        return remote(src, dst, psend_sem.at[i, e], precv_sem.at[i, e], *sibling)

    def store(i, e):
        return pltpu.make_async_copy(
            (xg, xu, xd)[i].at[e], (dwg_out, dwu_out, dwd_out)[i].at[e], store_sem.at[i, e]
        )

    def turn_of(n):
        return jnp.where(
            n == 0, flip(plane, 3), jnp.where(n == 1, flip(plane, 2), jnp.where(n == 2, flip(plane, 1), plane))
        )

    def opposed(i):
        return remote(
            (xg, xu, xd)[i].at[flip(plane, 3)],
            (dwg_in, dwu_in)[i],
            wsend_sem.at[i],
            wrecv_sem.at[i],
            *opposite,
        )

    def finished(i, n, e):
        if i == 2:
            store(i, e).start()
            return

        @pl.when(n == 0)
        def _():
            opposed(i).start()

        @pl.when(n > 0)
        def _():
            store(i, e).start()

    def give(n, carry):
        e = turn_of(n)
        left = x_t[pl.ds(theirs, half), :]
        wg[e, :half, :] = mm(left, dg[e]).astype(BF16)
        swap(0, e).start()
        wu[e, :half, :] = mm(left, du[e]).astype(BF16)
        swap(1, e).start()
        wd[e, :dhalf, :] = mm(hc[e, :, pl.ds(dtheirs, dhalf)], g_rows[...], TN).astype(BF16)
        swap(2, e).start()
        return carry

    def keep(n, carry):
        e = turn_of(n)

        left = x_t[pl.ds(mine, half), :]
        own = mm(left, dg[e])
        swap(0, e).wait_recv()
        xg[e] = (own + xg[e].astype(F32)).astype(BF16)
        finished(0, n, e)
        own = mm(left, du[e])
        swap(1, e).wait_recv()
        xu[e] = (own + xu[e].astype(F32)).astype(BF16)
        finished(1, n, e)
        own = mm(hc[e, :, pl.ds(dmine, dhalf)], g_rows[...], TN)
        swap(2, e).wait_recv()
        xd[e] = (own + xd[e].astype(F32)).astype(BF16)
        finished(2, n, e)
        return carry

    give(0, 0)

    def both(n, carry):
        give(n, 0)
        keep(n - 1, 0)
        return carry

    lax.fori_loop(1, 4, both, 0)
    keep(3, 0)

    for n in (1, 2, 3):
        k = flip(line, n)
        at = apart(k)
        pltpu.make_async_copy(d_send.at[at], d_recv.at[at], brecv_sem.at[k]).wait()
        d_in[...] += d_recv[at, :, :d].astype(F32)
        rest = d_recv[at, :, d:].astype(F32)
        d_c[...] += jnp.where(lane < 32, rest + pltpu.roll(rest, 96, 1), 0.0)

    gates = gate_ref[...]
    d_gates = rw_ref[...] * d_c[...]
    dlog = (gates * (d_gates - jnp.sum(gates * d_gates, -1, keepdims=True))).astype(BF16)
    dlog_ref[...] = dlog
    d_xl = d_in[...] + mm(dlog, wr_ref[...], NT)
    h1 = h1_ref[...]
    scale = rms_scale(h1)
    scaled = d_xl * gain_ref[...]
    inner = jnp.mean(scaled * h1, -1, keepdims=True)
    d_h1 = g_in[line].astype(F32) + scale * scaled - h1 * scale**3 * inner
    dgain_ref[...] = jnp.sum((d_xl * h1 * scale).reshape(tok // 8, 8, d), 0)
    dh_ref[...] = d_h1
    d_att = d_h1.astype(BF16)
    datt_ref[...] = d_att
    do_ref[...] = mm(d_att, wo[...], NT).astype(BF16)
    for n in (1, 2, 3):
        give_back(flip(line, n)).wait_send()
    for k in range(4):

        @pl.when((k <= line) & (line < 3))
        def _():
            along(k, 1).wait_send()

        @pl.when((k >= line) & (line > 0))
        def _():
            along(k, -1).wait_send()

    def finish(n, carry):
        e = turn_of(n)
        for i in range(3):
            swap(i, e).wait_send()

            @pl.when((n > 0) | (i == 2))
            def _():
                store(i, e).wait()

        return carry

    lax.fori_loop(0, 4, finish, 0)
    for i in range(2):
        opposed(i).wait()


def mixture(vectors, w_out, g, w_gate, w_up, w_down, shared):
    tok, d = g.shape
    ff = w_gate.shape[1]
    vm = pl.BlockSpec(memory_space=pltpu.VMEM)
    hbm = pl.BlockSpec(memory_space=pl.ANY)
    dma = pltpu.SemaphoreType.DMA
    vmem = pltpu.VMEM
    return pl.pallas_call(
        mixture_kernel,
        out_shape=(
            jax.ShapeDtypeStruct((tok, d), F32),
            jax.ShapeDtypeStruct((4, tok, d), BF16),
            jax.ShapeDtypeStruct((tok, d), BF16),
            jax.ShapeDtypeStruct((tok, 128), BF16),
            jax.ShapeDtypeStruct((tok, d), F32),
            jax.ShapeDtypeStruct((tok, d), BF16),
            jax.ShapeDtypeStruct((tok, d), BF16),
            jax.ShapeDtypeStruct((8, d), F32),
            jax.ShapeDtypeStruct((4, d // 2, ff), BF16),
            jax.ShapeDtypeStruct((4, d // 2, ff), BF16),
            jax.ShapeDtypeStruct((4, ff // 2, d), BF16),
            jax.ShapeDtypeStruct((d // 2, ff), BF16),
            jax.ShapeDtypeStruct((d // 2, ff), BF16),
        ),
        in_specs=[vm] * 6 + [hbm] * 9,
        out_specs=(vm,) * 8 + (hbm,) * 5,
        scratch_shapes=[
            vmem((d, 128), BF16),
            vmem((tok, 128), F32),
            vmem((tok, d), F32),
            vmem((tok, 128), F32),
            vmem((tok, d), F32),
            vmem((tok, 128), F32),
            vmem((d, d), BF16),
            vmem((4, tok, d + 128), BF16),
            vmem((d, 4 * tok), BF16),
            vmem((4, tok, d), BF16),
            vmem((4, d, ff), BF16),
            vmem((4, d, ff), BF16),
            vmem((4, ff, d), BF16),
            vmem((4, 4 * tok, ff), BF16),
            vmem((4, 4 * tok, ff), BF16),
            vmem((4, 4 * tok, ff), BF16),
            vmem((tok, d), F32),
            vmem((tok, d), F32),
            vmem((tok, 128), F32),
            vmem((3, tok, d + 128), BF16),
            vmem((3, tok, d + 128), BF16),
            vmem((4, d // 2, ff), BF16),
            vmem((4, d // 2, ff), BF16),
            vmem((4, ff // 2, d), BF16),
            dma((3, 4)),
            dma((4,)),
            dma((2, 4)),
            dma((4,)),
            dma((4,)),
            dma((4,)),
            dma((3, 4)),
            dma((3, 4)),
            dma((3, 4)),
            dma((2,)),
            dma((2,)),
            dma,
        ],
        compiler_params=pltpu.CompilerParams(
            collective_id=2, has_side_effects=True, vmem_limit_bytes=VMEM_LIMIT
        ),
        name="mixture",
    )(*vectors, w_out, g, w_gate, w_up, w_down, *shared)


def tail_kernel(
    got,
    xa_ref,
    x_ref,
    gain_ref,
    dh_ref,
    ao_ref,
    datt_ref,
    xl_ref,
    dlog_ref,
    dgain2_ref,
    own_ref,
    wq_any,
    wk_any,
    wv_any,
    mix_ref,
    mix_near,
    eg_ref,
    eu_ref,
    ed_ref,
    eg_in,
    eu_in,
    ed_in,
    eg_far,
    eu_far,
    res_ref,
    dx_ref,
    gsum_ref,
    fin_o,
    fin_q,
    fin_kv,
    eg_out,
    eu_out,
    ed_out,
    mix_in,
    wq_ref,
    wk_ref,
    wv_ref,
    d_all,
    ev,
    edv,
    gbuf,
    grv,
    load_sem,
    esend,
    erecv,
    gsend,
    grecv,
    msend,
    mrecv,
    *summing,
):
    me_s = lax.axis_index("seq")
    me_b = lax.axis_index("blk")
    plane = lax.rem(me_b, 4)
    tok, d = xa_ref.shape
    sums = [
        Summed(summing[8 * i : 8 * i + 6], *summing[8 * i + 6 : 8 * i + 8], fin)
        for i, fin in enumerate((fin_o, fin_q, fin_kv))
    ]
    for_out, for_q, for_kv = sums
    [sibling], planes, lines = for_q.sibling, for_q.planes, for_q.lines
    barrier = pltpu.get_barrier_semaphore()
    for place in [sibling, *planes, *lines]:
        pl.semaphore_signal(barrier, inc=1, device_id=place, device_id_type=MESH)

    experts = (
        (eg_ref, eg_in, eg_far, ev.at[0]),
        (eu_ref, eu_in, eu_far, ev.at[1]),
        (ed_ref, ed_in, None, edv),
    )

    def loads(i):
        own, arrived, far, dst = experts[i]
        near = arrived.shape[0]
        copies = [
            pltpu.make_async_copy(own.at[plane], dst.at[0], load_sem.at[i, 0]),
            pltpu.make_async_copy(arrived, dst.at[pl.ds(1, near)], load_sem.at[i, 1]),
        ]
        if far is not None:
            copies.append(pltpu.make_async_copy(far, dst.at[3], load_sem.at[i, 2]))
        return copies

    projections = [
        pltpu.make_async_copy(src, dst, load_sem.at[3, i + 1])
        for i, (src, dst) in enumerate(((wq_any, wq_ref), (wk_any, wk_ref), (wv_any, wv_ref)))
    ]
    for copy in projections:
        copy.start()
    for i in range(3):
        for copy in loads(i):
            copy.start()
    pl.semaphore_wait(barrier, 7)
    line = me_b // 4

    far_mix = remote(mix_ref.at[flip(line, 3)], mix_in.at[2], msend, mrecv, *lines[2])
    near_mix = pltpu.make_async_copy(mix_near, mix_in.at[pl.ds(0, 2)], load_sem.at[3, 0])
    far_mix.start()
    near_mix.start()
    theirs, mine = for_q.halves()
    for_out.out[:, :d] = mm(ao_ref[:, theirs], datt_ref[...], TN).astype(BF16)
    for_out.out[:, d:] = mm(xl_ref[:, theirs], dlog_ref[...], TN).astype(BF16)
    for_out.start(0)

    low = lax.broadcasted_iota(jnp.int32, (tok, 2 * HD), 1) < HD
    for m in range(KV // 2):
        a, b = got[2 * m], got[2 * m + 1]
        d_all[:, 2 * m * 2 * HD : (2 * m + 1) * 2 * HD] = a[:, : 2 * HD]
        d_all[:, (2 * m + 1) * 2 * HD : (2 * m + 2) * 2 * HD] = b[:, : 2 * HD]
        ka, kb = a[:, 2 * HD :].astype(F32), b[:, 2 * HD :].astype(F32)
        at = H * HD + m * 2 * HD
        d_all[:, at : at + 2 * HD] = jnp.where(low, ka, pltpu.roll(kb, HD, 1)).astype(BF16)
        at += KV * HD
        d_all[:, at : at + 2 * HD] = jnp.where(low, pltpu.roll(ka, HD, 1), kb).astype(BF16)
    parts = ((for_q, slice(0, H * HD)), (for_kv, slice(H * HD, (H + 2 * KV) * HD)))
    for item, cols in parts:
        item.out[...] = mm(xa_ref[:, theirs], d_all[:, cols], TN).astype(BF16)
        item.start(0)
    for_out.acc[:, :d] = mm(ao_ref[:, mine], datt_ref[...], TN)
    for_out.acc[:, d:] = mm(xl_ref[:, mine], dlog_ref[...], TN)
    for_out.pair()
    for item, cols in parts:
        item.acc[...] = mm(xa_ref[:, mine], d_all[:, cols], TN)
        item.pair()

    for copy in projections:
        copy.wait()
    grad = (
        mm(d_all[:, : H * HD], wq_ref[...], NT)
        + mm(d_all[:, H * HD : (H + KV) * HD], wk_ref[...], NT)
        + mm(d_all[:, (H + KV) * HD :], wv_ref[...], NT)
    )
    xs = x_ref[...].astype(F32)
    scale = rms_scale(xs)
    scaled = grad * gain_ref[...]
    inner = jnp.mean(scaled * xs, -1, keepdims=True)
    dx_ref[...] = dh_ref[...] + scale * scaled - xs * scale**3 * inner
    gains = (
        jnp.sum(grad * xs * scale, 0, keepdims=True),
        jnp.sum(dgain2_ref[...], 0, keepdims=True),
    )
    part = d // 4
    gbuf[0] = jnp.concatenate(
        [gain[:, i * part : (i + 1) * part] for gain in gains for i in range(4)], 0
    )

    stages = [[sibling], planes, lines]

    def gain_copy(s, n):
        at = (0, 1, 4)[s] + n
        return remote(gbuf.at[s], grv.at[at], gsend.at[at], grecv.at[at], *stages[s][n])

    def gain_stage(s):
        for n in range(len(stages[s])):
            gain_copy(s, n).start()

    def gain_total(s):
        total = gbuf[s]
        for n in range(len(stages[s])):
            gain_copy(s, n).wait_recv()
            total = total + grv[(0, 1, 4)[s] + n]
        return total

    gain_stage(0)
    for_out.over_plane()

    outs = (eg_out, eu_out, ed_out)

    def expert_swap(i):
        rows = outs[i].shape[0] // 2
        part = outs[i].at[pl.ds(pl.multiple_of(me_s * rows, rows), rows)]
        return remote(part, part, esend.at[i], erecv.at[i], *sibling)

    for i in range(3):
        for copy in loads(i):
            copy.wait()
        terms = experts[i][3]
        rows = outs[i].shape[0] // 2
        total = terms[0].astype(F32)
        for n in (1, 2, 3):
            total = total + terms[n].astype(F32)
        outs[i][pl.ds(pl.multiple_of(me_s * rows, rows), rows), :] = total.astype(BF16)
        expert_swap(i).start()
    gbuf[1] = gain_total(0)
    gain_stage(1)
    for_q.over_plane()
    for_out.over_line()
    for_kv.over_plane()
    gbuf[2] = gain_total(1)
    gain_stage(2)
    for_q.over_line()
    for_out.back(3)
    for_kv.over_line()
    for_q.back(3)
    for_kv.back(3)
    gsum_ref[...] = gain_total(2)
    for item in sums:
        item.back(4)
    result = own_ref[...]
    near_mix.wait()
    far_mix.wait()
    for n in range(3):
        result = result + mix_in[n].astype(F32)
    res_ref[...] = result.astype(BF16)
    for item in sums:
        item.finish()
    for i in range(3):
        expert_swap(i).wait()
    for s in range(3):
        for n in range(len(stages[s])):
            gain_copy(s, n).wait_send()


def tail(blocks_in, mix_peer, mix_near, own, arrived, far):
    tok, d = blocks_in[1].shape
    ff = own[0].shape[2]
    widths = (d + 128, H * HD, 2 * KV * HD)
    vm = pl.BlockSpec(memory_space=pltpu.VMEM)
    hbm = pl.BlockSpec(memory_space=pl.ANY)
    dma = pltpu.SemaphoreType.DMA
    vmem = pltpu.VMEM
    return pl.pallas_call(
        tail_kernel,
        out_shape=(
            jax.ShapeDtypeStruct((tok, d), BF16),
            jax.ShapeDtypeStruct((tok, d), F32),
            jax.ShapeDtypeStruct((8, d // 4), F32),
            *(jax.ShapeDtypeStruct((d, width), BF16) for width in widths),
            jax.ShapeDtypeStruct((d, ff), BF16),
            jax.ShapeDtypeStruct((d, ff), BF16),
            jax.ShapeDtypeStruct((ff, d), BF16),
        ),
        in_specs=[vm] * (len(blocks_in) - 3) + [hbm] * 13,
        out_specs=(vm,) * 9,
        scratch_shapes=[
            vmem((3, tok, d), BF16),
            vmem((d, H * HD), BF16),
            vmem((d, KV * HD), BF16),
            vmem((d, KV * HD), BF16),
            vmem((tok, (H + 2 * KV) * HD), BF16),
            vmem((2, 4, d // 2, ff), BF16),
            vmem((4, ff // 2, d), BF16),
            vmem((3, 8, d // 4), F32),
            vmem((7, 8, d // 4), F32),
            dma((4, 4)),
            dma((3,)),
            dma((3,)),
            dma((7,)),
            dma((7,)),
            dma,
            dma,
            *(ref for width in widths for ref in summed_scratch(d, width)),
        ],
        compiler_params=pltpu.CompilerParams(
            collective_id=3, has_side_effects=True, vmem_limit_bytes=VMEM_LIMIT
        ),
        name="tail",
    )(*blocks_in, mix_peer, mix_near, *own, *arrived, *far)


def widen_kernel(
    gains, o, q, kv, eg, eu, ed, res, dx, n1, wq, wk, wv, wo, n2, wr, og, ou, od, res_out, dx_out
):
    d = wq.shape[1]
    half = wk.shape[1]
    wq[...] = q[...].astype(F32)
    wk[...] = kv[:, :half].astype(F32)
    wv[...] = kv[:, half:].astype(F32)
    wo[...] = o[:, :d].astype(F32)
    wr[...] = o[:, d : d + wr.shape[1]].astype(F32)
    og[0] = eg[...].astype(F32)
    ou[0] = eu[...].astype(F32)
    od[0] = ed[...].astype(F32)
    n1[...] = jnp.concatenate([gains[i : i + 1, :] for i in range(4)], 1)
    n2[...] = jnp.concatenate([gains[i : i + 1, :] for i in range(4, 8)], 1)
    res_out[0] = res[...]
    dx_out[0] = dx[...]


def widen(gains, o, q, kv, eg, eu, ed, res, dx, experts):
    d, ff = eg.shape
    tok = res.shape[0]
    parts = 8

    def block(shape):
        return pl.BlockSpec((shape[0] // parts, shape[1]), lambda i: (i, 0))

    def deep(shape):
        return pl.BlockSpec((1, shape[0] // parts, shape[1]), lambda i: (0, i, 0))

    flat = pl.BlockSpec((1, d), lambda i: (0, 0))
    shapes = [(d, H * HD), (d, KV * HD), (d, KV * HD), (H * HD, d)]
    return pl.pallas_call(
        widen_kernel,
        grid=(parts,),
        out_shape=(
            jax.ShapeDtypeStruct((1, d), F32),
            *(jax.ShapeDtypeStruct(shape, F32) for shape in shapes),
            jax.ShapeDtypeStruct((1, d), F32),
            jax.ShapeDtypeStruct((d, experts), F32),
            jax.ShapeDtypeStruct((1, d, ff), F32),
            jax.ShapeDtypeStruct((1, d, ff), F32),
            jax.ShapeDtypeStruct((1, ff, d), F32),
            jax.ShapeDtypeStruct((1, tok, d), BF16),
            jax.ShapeDtypeStruct((1, tok, d), F32),
        ),
        in_specs=[pl.BlockSpec((8, d // 4), lambda i: (0, 0))]
        + [block(a.shape) for a in (o, q, kv, eg, eu, ed, res, dx)],
        out_specs=(
            flat,
            *(block(shape) for shape in shapes),
            flat,
            block((d, experts)),
            deep((d, ff)),
            deep((d, ff)),
            deep((ff, d)),
            deep((tok, d)),
            deep((tok, d)),
        ),
        compiler_params=pltpu.CompilerParams(vmem_limit_bytes=VMEM_LIMIT),
        name="widen",
    )(gains, o, q, kv, eg, eu, ed, res, dx)


D = 1024
HIGH = lax.Precision.HIGHEST


def rope_tables(positions):
    half = HD // 2
    freq = jnp.exp(-math.log(10000.0) * jnp.arange(half, dtype=jnp.float32) * 2.0 / HD)
    angle = positions.astype(jnp.float32)[:, None] * freq[None, :]
    cosine = jnp.concatenate([jnp.cos(angle), jnp.cos(angle)], -1)
    sine = jnp.concatenate([jnp.sin(angle), jnp.sin(angle)], -1)
    return (cosine, sine)


def rotate_half(v):
    half = v.shape[-1] // 2
    return jnp.concatenate([-v[..., half:], v[..., :half]], -1)


def rotary(v, cosine, sine):
    return v * cosine[:, None, :] + rotate_half(v) * sine[:, None, :]


def unrotary(v, cosine, sine):
    return v * cosine[:, None, :] - rotate_half(v) * sine[:, None, :]


def rms_scale(v):
    return lax.rsqrt(jnp.mean(v * v, -1, keepdims=True) + EPS)


def rms_back(inputs, scale_rows, gain, grad):
    scaled = grad * gain
    d_inputs = scale_rows * scaled - inputs * scale_rows**3 * jnp.mean(
        scaled * inputs, -1, keepdims=True
    )
    return (d_inputs, jnp.sum(grad * inputs * scale_rows, 0))


def scores(queries, keys):
    return jnp.einsum("qkgd,skd->kgqs", queries, keys, preferred_element_type=jnp.float32) * HD ** (
        -0.5
    )


def per_device_plain(
    tokens,
    segments,
    routes,
    route_weight,
    norm1_gain,
    w_query,
    w_key,
    w_value,
    w_out,
    norm2_gain,
    w_router,
    w_gate,
    w_up,
    w_down,
    cotangent,
):
    f32 = jnp.float32
    bf16 = jnp.bfloat16
    scale = HD ** (-0.5)
    group = H // KV
    xs = tokens[0].astype(f32)
    tok = xs.shape[0]
    blocks = lax.axis_size("blk")
    length = tok * blocks
    first = lax.axis_index("blk") * tok
    last = first + tok - 1
    positions = first + jnp.arange(tok, dtype=jnp.int32)
    cosine, sine = rope_tables(positions)
    scale1 = rms_scale(xs)
    xa = (xs * scale1 * norm1_gain).astype(bf16)
    query = jnp.dot(xa, w_query, preferred_element_type=f32)
    key = jnp.dot(xa, w_key, preferred_element_type=f32)
    value = jnp.dot(xa, w_value, preferred_element_type=f32).astype(bf16)
    q_rot = rotary(query.reshape(tok, H, HD), cosine, sine).astype(bf16).reshape(tok, KV, group, HD)
    k_rot = rotary(key.reshape(tok, KV, HD), cosine, sine).astype(bf16).reshape(tok, KV * HD)
    seg_float = segments[0].astype(bf16)
    k_all, v_all, seg_all = (
        lax.all_gather(k_rot, "blk", axis=0, tiled=True),
        lax.all_gather(value, "blk", axis=0, tiled=True),
        lax.all_gather(seg_float, "blk", axis=0, tiled=True),
    )
    kblk = min(512, length)
    nblk = length // kblk
    k_blocks = k_all.reshape(nblk, kblk, KV, HD)
    v_blocks = v_all.reshape(nblk, kblk, KV, HD)
    s_blocks = seg_all.reshape(nblk, kblk)
    starts = jnp.arange(nblk, dtype=jnp.int32) * kblk

    def visible(kseg, kstart):
        kpos = kstart + jnp.arange(kblk, dtype=jnp.int32)
        return ((seg_float[:, None] == kseg[None, :]) & (kpos[None, :] <= positions[:, None]))[
            None, None
        ]

    def forward_step(carry, block):
        kb, vb, sb, start = block

        def forward_compute(state):
            running, total, acc = state
            mask = visible(sb, start)
            score = jnp.where(mask, scores(q_rot, kb), NEG)
            newmax = jnp.maximum(running, jnp.max(score, -1))
            expo = jnp.where(mask, jnp.exp(score - newmax[..., None]), 0.0)
            factor = jnp.exp(running - newmax)
            total = total * factor + jnp.sum(expo, -1)
            acc = acc * factor[..., None] + jnp.einsum(
                "kgqs,skd->kgqd", expo.astype(bf16), vb, preferred_element_type=f32
            )
            return (newmax, total, acc)

        return (lax.cond(start <= last, forward_compute, lambda state: state, carry), None)

    init = (
        jnp.full((KV, group, tok), NEG, f32),
        jnp.zeros((KV, group, tok), f32),
        jnp.zeros((KV, group, tok, HD), f32),
    )
    (running, total, acc), unused = lax.scan(
        forward_step, init, (k_blocks, v_blocks, s_blocks, starts)
    )
    lse = running + jnp.log(total)
    o_rows = (acc / total[..., None]).transpose(2, 0, 1, 3)
    att_low = o_rows.reshape(tok, H * HD).astype(bf16)
    h1 = xs + jnp.dot(att_low, w_out, preferred_element_type=f32)
    scale2 = rms_scale(h1)
    xl = (h1 * scale2 * norm2_gain).astype(bf16)
    logits = jnp.dot(xl, w_router, preferred_element_type=f32)
    experts = logits.shape[1]
    route = routes[0]
    rweight = route_weight[0]
    chooser = (route[:, :, None] == jnp.arange(experts, dtype=jnp.int32)[None, None, :]).astype(f32)
    chosen = jnp.sum(chooser * logits[:, None, :], -1)
    gates = jax.nn.softmax(chosen, -1)
    combine = (rweight * gates).astype(bf16)
    cap = min(tok, 2 * tok * TOP // experts)
    member = jnp.sum(chooser, 1)
    before = jnp.asarray(np.tril(np.ones((tok, tok), np.float32), -1))
    order = jnp.dot(before, member, precision=HIGH)
    rank = jnp.sum(chooser * order[:, None, :], -1).astype(jnp.int32)
    slots = route * cap + rank
    placed = jnp.any(
        slots[:, :, None] == jnp.arange(experts * cap, dtype=jnp.int32)[None, None, :], 1
    ).astype(bf16)
    outgoing = jnp.einsum("ts,td->sd", placed, xl, preferred_element_type=f32).astype(bf16)
    incoming = lax.all_to_all(
        outgoing.reshape(experts, cap, D), "blk", split_axis=0, concat_axis=0, tiled=True
    )
    local_exp = w_gate.shape[0]
    incoming = incoming.reshape(blocks, local_exp, cap, D)
    gate_pre = jnp.einsum("necd,edf->necf", incoming, w_gate, preferred_element_type=f32)
    up_pre = jnp.einsum("necd,edf->necf", incoming, w_up, preferred_element_type=f32)
    sigma = jax.nn.sigmoid(gate_pre)
    activated = gate_pre * sigma
    hidden = (activated * up_pre).astype(bf16)
    expert_out = jnp.einsum("necf,efd->necd", hidden, w_down, preferred_element_type=f32).astype(
        bf16
    )
    returned = lax.all_to_all(
        expert_out.reshape(experts, cap, D), "blk", split_axis=0, concat_axis=0, tiled=True
    )
    per_route = jnp.take(returned.reshape(experts * cap, D), slots.reshape(-1), axis=0).reshape(
        tok, TOP, D
    )
    mixture = jnp.einsum("tj,tjd->td", combine, per_route, preferred_element_type=f32)
    result = h1 + mixture
    grad_out = cotangent[0].astype(f32)
    grad_combine = jnp.einsum("td,tjd->tj", grad_out, per_route.astype(f32), precision=HIGH)
    route_grads = (combine.astype(f32)[:, :, None] * grad_out[:, None, :]).astype(bf16)
    grad_slots = (
        jnp.zeros((experts * cap, D), bf16)
        .at[slots.reshape(-1)]
        .set(route_grads.reshape(tok * TOP, D))
    )
    grad_incoming = lax.all_to_all(
        grad_slots.reshape(experts, cap, D), "blk", split_axis=0, concat_axis=0, tiled=True
    )
    grad_incoming = grad_incoming.reshape(blocks, local_exp, cap, D)
    grad_hidden = jnp.einsum("necd,efd->necf", grad_incoming, w_down, preferred_element_type=f32)
    grad_gate = (grad_hidden * up_pre * sigma * (1.0 + gate_pre * (1.0 - sigma))).astype(bf16)
    grad_up = (grad_hidden * activated).astype(bf16)
    d_down = jnp.einsum("necf,necd->efd", hidden, grad_incoming, preferred_element_type=f32)
    d_gate_w = jnp.einsum("necd,necf->edf", incoming, grad_gate, preferred_element_type=f32)
    d_up_w = jnp.einsum("necd,necf->edf", incoming, grad_up, preferred_element_type=f32)
    grad_in = (
        jnp.einsum("necf,edf->necd", grad_gate, w_gate, preferred_element_type=f32)
        + jnp.einsum("necf,edf->necd", grad_up, w_up, preferred_element_type=f32)
    ).astype(bf16)
    grad_back = lax.all_to_all(
        grad_in.reshape(experts, cap, D), "blk", split_axis=0, concat_axis=0, tiled=True
    )
    grad_xl = jnp.einsum(
        "ts,sd->td", placed, grad_back.reshape(experts * cap, D), preferred_element_type=f32
    )
    grad_gates = rweight * grad_combine
    grad_chosen = gates * (grad_gates - jnp.sum(gates * grad_gates, -1, keepdims=True))
    grad_logits = jnp.sum(chooser * grad_chosen[:, :, None], 1).astype(bf16)
    d_router = jnp.einsum("td,te->de", xl, grad_logits, preferred_element_type=f32)
    grad_xl = grad_xl + jnp.einsum("te,de->td", grad_logits, w_router, preferred_element_type=f32)
    grad_h1_norm, d_gain2 = rms_back(h1, scale2, norm2_gain, grad_xl)
    grad_h1 = grad_out + grad_h1_norm
    grad_att = grad_h1.astype(bf16)
    d_out_w = jnp.einsum("ti,td->id", att_low, grad_att, preferred_element_type=f32)
    grad_o = jnp.einsum("td,id->ti", grad_att, w_out, preferred_element_type=f32).astype(bf16)
    grad_o_rows = grad_o.reshape(tok, KV, group, HD)
    delta = jnp.einsum("qkgd,qkgd->kgq", grad_o_rows.astype(f32), o_rows)

    def query_terms(kb, vb, sb, start):
        mask = visible(sb, start)
        prob = jnp.where(mask, jnp.exp(scores(q_rot, kb) - lse[..., None]), 0.0)
        dprob = jnp.einsum("qkgd,skd->kgqs", grad_o_rows, vb, preferred_element_type=f32)
        dscore = (prob * (dprob - delta[..., None])).astype(bf16)
        dq_term = jnp.einsum("kgqs,skd->qkgd", dscore, kb, preferred_element_type=f32) * scale
        return (dq_term, dscore, prob)

    zero_q = jnp.zeros((tok, KV, group, HD), f32)

    def backward_step(grad_q, block):
        kb, vb, sb, start = block

        def backward_compute(acc_q):
            dq_term, dscore, prob = query_terms(kb, vb, sb, start)
            gk = jnp.einsum("kgqs,qkgd->skd", dscore, q_rot, preferred_element_type=f32) * scale
            gv = jnp.einsum(
                "kgqs,qkgd->skd", prob.astype(bf16), grad_o_rows, preferred_element_type=f32
            )
            return (acc_q + dq_term, (gk.reshape(kblk, KV * HD), gv.reshape(kblk, KV * HD)))

        def skip(acc_q):
            empty = jnp.zeros((kblk, KV * HD), f32)
            return (acc_q, (empty, empty))

        return lax.cond(start <= last, backward_compute, skip, grad_q)

    grad_q, (gk_blocks, gv_blocks) = lax.scan(
        backward_step, zero_q, (k_blocks, v_blocks, s_blocks, starts)
    )
    grad_k, grad_v = (
        lax.psum_scatter(
            gk_blocks.reshape(length, KV * HD).astype(jnp.bfloat16),
            "blk",
            scatter_dimension=0,
            tiled=True,
        ).astype(jnp.float32),
        lax.psum_scatter(
            gv_blocks.reshape(length, KV * HD).astype(jnp.bfloat16),
            "blk",
            scatter_dimension=0,
            tiled=True,
        ).astype(jnp.float32),
    )
    grad_qr = unrotary(grad_q.reshape(tok, H, HD), cosine, sine).reshape(tok, H * HD).astype(bf16)
    grad_kr = unrotary(grad_k.reshape(tok, KV, HD), cosine, sine).reshape(tok, KV * HD).astype(bf16)
    grad_vr = grad_v.astype(bf16)
    d_query = jnp.einsum("td,te->de", xa, grad_qr, preferred_element_type=f32)
    d_key = jnp.einsum("td,te->de", xa, grad_kr, preferred_element_type=f32)
    d_value = jnp.einsum("td,te->de", xa, grad_vr, preferred_element_type=f32)
    grad_xa = (
        jnp.einsum("te,de->td", grad_qr, w_query, preferred_element_type=f32)
        + jnp.einsum("te,de->td", grad_kr, w_key, preferred_element_type=f32)
        + jnp.einsum("te,de->td", grad_vr, w_value, preferred_element_type=f32)
    )
    grad_x_norm, d_gain1 = rms_back(xs, scale1, norm1_gain, grad_xa)
    grad_x = grad_h1 + grad_x_norm
    summed = lax.psum(
        (d_gain1, d_query, d_key, d_value, d_out_w, d_gain2, d_router), ("seq", "blk")
    )
    expert_summed = (
        lax.psum(d_gate_w.astype(jnp.bfloat16), "seq").astype(jnp.float32),
        lax.psum(d_up_w.astype(jnp.bfloat16), "seq").astype(jnp.float32),
        lax.psum(d_down.astype(jnp.bfloat16), "seq").astype(jnp.float32),
    )
    return (
        result.astype(bf16)[None],
        grad_x[None],
        summed[0],
        summed[1],
        summed[2],
        summed[3],
        summed[4],
        summed[5],
        summed[6],
        expert_summed[0],
        expert_summed[1],
        expert_summed[2],
    )


def tables(length):
    half = HD // 2
    freq = np.exp(-math.log(10000.0) * np.arange(half, dtype=np.float32) * 2.0 / HD).astype(np.float32)
    angle = np.arange(length, dtype=np.float32)[:, None] * freq[None, :]
    return np.tile(np.cos(angle), (1, 4)), np.tile(np.sin(angle), (1, 4))


def per_device(
    tokens,
    segments,
    routes,
    route_weight,
    norm1_gain,
    w_query,
    w_key,
    w_value,
    w_out,
    norm2_gain,
    w_router,
    w_gate,
    w_up,
    w_down,
    cotangent,
):
    tok, d = tokens[0].shape
    blocks = lax.axis_size("blk")
    experts = w_router.shape[1]
    cos_np, sin_np = tables(tok * blocks)
    cos_all = jnp.asarray(cos_np.reshape(blocks, tok, 2 * HD))
    sin_all = jnp.asarray(sin_np.reshape(blocks, tok, 2 * HD))
    seg = jnp.pad(segments[0].astype(BF16).reshape(2, tok // 2), ((0, 14), (0, 0)))
    gain1 = norm1_gain[None]
    g_low = cotangent[0]
    att_low, xa, *kept = attention_forward(
        blocks,
        tokens[0],
        gain1,
        w_query,
        w_key,
        w_value,
        seg,
        cos_all,
        sin_all,
        g_low,
        w_gate[0],
        w_up[0],
        w_down[0],
    )
    kept, shared = kept[:5], kept[5:]

    own, mix_peer, xl, grad_logits, grad_h1, grad_att, grad_o, gain2_terms, *rest = mixture(
        (tokens[0], att_low, norm2_gain[None], w_router, routes[0], route_weight[0]),
        w_out,
        g_low,
        w_gate[0],
        w_up[0],
        w_down[0],
        shared,
    )
    (dwg, dwu, dwd), far = rest[:3], rest[3:]
    vectors = (
        grad_o,
        *kept,
        cos_all,
        sin_all,
    )
    got, mix_near, *arrived = attention_backward(
        blocks, vectors, mix_peer, dwg, dwu, dwd
    )
    blocks_in = (
        got,
        xa,
        tokens[0],
        gain1,
        grad_h1,
        att_low,
        grad_att,
        xl,
        grad_logits,
        gain2_terms,
        own,
        w_query,
        w_key,
        w_value,
    )
    result, grad_x, gains, d_out, d_query, d_kv, d_gate_w, d_up_w, d_down = tail(
        blocks_in, mix_peer, mix_near, (dwg, dwu, dwd), arrived, far
    )
    wide = widen(gains, d_out, d_query, d_kv, d_gate_w, d_up_w, d_down, result, grad_x, experts)
    d_gain1, d_query, d_key, d_value, d_out, d_gain2, *rest, result, grad_x = wide
    return (
        result,
        grad_x,
        d_gain1[0],
        d_query,
        d_key,
        d_value,
        d_out,
        d_gain2[0],
        *rest,
    )


def solution(mesh):
    fused = dict(mesh.shape) == {"seq": 2, "blk": 2 * KV}
    return jax.shard_map(
        per_device if fused else per_device_plain,
        mesh=mesh,
        in_specs=(
            P("seq", "blk", None),
            P("seq", "blk"),
            P("seq", "blk", None),
            P("seq", "blk", None),
            P(),
            P(),
            P(),
            P(),
            P(),
            P(),
            P(),
            P("blk", None, None),
            P("blk", None, None),
            P("blk", None, None),
            P("seq", "blk", None),
        ),
        out_specs=(
            P("seq", "blk", None),
            P("seq", "blk", None),
            P(),
            P(),
            P(),
            P(),
            P(),
            P(),
            P(),
            P("blk", None, None),
            P("blk", None, None),
            P("blk", None, None),
        ),
        check_vma=False,
    )
```

```python
import functools
import math

import jax
import jax.numpy as jnp
import numpy as np
from jax import lax
from jax.experimental import pallas as pl
from jax.experimental.pallas import tpu as pltpu
from jax.sharding import PartitionSpec as P

H = 16
KV = 8
HD = 64
TOP = 8
EPS = 1e-06
NEG = -1e30
F32 = jnp.float32
BF16 = jnp.bfloat16
MESH = pl.DeviceIdType.MESH
VMEM_LIMIT = 60 * 2**20
GRAD_STEPS = (2, 5)
HOP_STEP = 4
NT = (((1,), (1,)), ((), ()))
TN = (((0,), (0,)), ((), ()))


def mm(a, b, dims=(((1,), (0,)), ((), ()))):
    return lax.dot_general(a, b, dims, preferred_element_type=F32)


def remote(src, dst, send, recv, seq, blk):
    return pltpu.make_async_remote_copy(
        src_ref=src,
        dst_ref=dst,
        send_sem=send,
        recv_sem=recv,
        device_id=(seq, blk),
        device_id_type=MESH,
    )


def greet_all(seqs, blocks, me_s, me_b):
    barrier = pltpu.get_barrier_semaphore()
    total = seqs * blocks

    def hello(n, carry):
        other = lax.rem(me_s * blocks + me_b + n, total)
        pl.semaphore_signal(
            barrier,
            inc=1,
            device_id=(other // blocks, lax.rem(other, blocks)),
            device_id_type=MESH,
        )
        return carry

    lax.fori_loop(1, total, hello, 0)
    pl.semaphore_wait(barrier, total - 1)


def flip(place, n):
    if n == 1:
        return place + 1 - 2 * lax.rem(place, 2)
    if n == 2:
        return place + 2 - 4 * (place // 2)
    return 3 - place


def rotate_pairs(u):
    lanes = u.shape[-1]
    half = HD // 2
    lane = lax.broadcasted_iota(jnp.int32, u.shape, u.ndim - 1)
    ahead = pltpu.roll(u, lanes - half, u.ndim - 1)
    behind = pltpu.roll(u, half, u.ndim - 1)
    return jnp.where(lane % HD < half, -ahead, behind)


def stacked_heads(wide):
    return jnp.concatenate([wide[:HD], wide[HD:]], axis=1)


STAGES = 6


class Summed:
    def __init__(self, refs, send_sem, recv_sem, fin):
        self.out, self.arrived, self.acc, self.part, self.plane_in, self.line_in = refs
        self.send_sem, self.recv_sem, self.fin = send_sem, recv_sem, fin
        self.me_s = lax.axis_index("seq")
        me_b = lax.axis_index("blk")
        self.line, self.plane = me_b // 4, lax.rem(me_b, 4)
        self.sibling = [(1 - self.me_s, me_b)]
        self.planes = [(self.me_s, self.line * 4 + flip(self.plane, n)) for n in (1, 2, 3)]
        self.lines = [(self.me_s, flip(self.line, n) * 4 + self.plane) for n in (1, 2, 3)]
        rows = fin.shape[0]
        self.half, self.quarter, self.piece = rows // 2, rows // 8, rows // 32

    def rows(self, start, size):
        return pl.ds(pl.multiple_of(start, size), size)

    def halves(self):
        theirs = self.rows((1 - self.me_s) * self.half, self.half)
        return theirs, self.rows(self.me_s * self.half, self.half)

    def copy(self, stage, n):
        sems = self.send_sem.at[stage, n], self.recv_sem.at[stage, n]
        base = self.me_s * self.half
        if stage == 0:
            return remote(self.out, self.arrived, *sems, *self.sibling[n])
        if stage == 1:
            src = self.part.at[self.rows(flip(self.plane, n + 1) * self.quarter, self.quarter)]
            return remote(src, self.plane_in.at[n], *sems, *self.planes[n])
        if stage == 2:
            at = self.plane * self.quarter + flip(self.line, n + 1) * self.piece
            src = self.part.at[self.rows(at, self.piece)]
            return remote(src, self.line_in.at[n], *sems, *self.lines[n])
        if stage == 3:
            at = base + self.plane * self.quarter + self.line * self.piece
            part = self.fin.at[self.rows(at, self.piece)]
            return remote(part, part, *sems, *self.lines[n])
        if stage == 4:
            part = self.fin.at[self.rows(base + self.plane * self.quarter, self.quarter)]
            return remote(part, part, *sems, *self.planes[n])
        part = self.fin.at[self.rows(base, self.half)]
        return remote(part, part, *sems, *self.sibling[n])

    def start(self, stage):
        for n in range(1) if stage in (0, 5) else (2, 0, 1):
            self.copy(stage, n).start()

    def arrive(self, stage):
        for n in range(1 if stage in (0, 5) else 3):
            self.copy(stage, n).wait_recv()

    def pair(self):
        self.arrive(0)
        self.part[...] = (self.acc[...] + self.arrived[...].astype(F32)).astype(BF16)
        self.start(1)

    def over_plane(self):
        self.arrive(1)
        here = self.rows(self.plane * self.quarter, self.quarter)
        total = self.part[here, :].astype(F32)
        for n in range(3):
            total = total + self.plane_in[n].astype(F32)
        self.part[here, :] = total.astype(BF16)
        self.start(2)

    def over_line(self):
        self.arrive(2)
        at = self.plane * self.quarter + self.line * self.piece
        total = self.part[self.rows(at, self.piece), :].astype(F32)
        for n in range(3):
            total = total + self.line_in[n].astype(F32)
        self.fin[self.rows(self.me_s * self.half + at, self.piece), :] = total.astype(BF16)
        self.start(3)

    def back(self, stage):
        self.arrive(stage)
        self.start(stage + 1)

    def finish(self):
        self.arrive(5)
        for stage in range(STAGES):
            for n in range(1 if stage in (0, 5) else 3):
                self.copy(stage, n).wait_send()


def summed_scratch(rows, width):
    vmem, dma = pltpu.VMEM, pltpu.SemaphoreType.DMA
    return [
        vmem((rows // 2, width), BF16),
        vmem((rows // 2, width), BF16),
        vmem((rows // 2, width), F32),
        vmem((rows // 2, width), BF16),
        vmem((3, rows // 8, width), BF16),
        vmem((3, rows // 32, width), BF16),
        dma((STAGES, 3)),
        dma((STAGES, 3)),
    ]


def attention_forward_kernel(
    blocks,
    x_ref,
    gain_ref,
    wq_ref,
    wk_ref,
    wv_ref,
    seg_ref,
    cos_ref,
    sin_ref,
    g_ref,
    wg_ref,
    wu_ref,
    wd_ref,
    o_ref,
    xa_ref,
    kv_ref,
    kvt_ref,
    q_ref,
    ot_ref,
    stat_ref,
    g_all,
    wg_all,
    wu_all,
    wd_all,
    pay,
    turn,
    in_ref,
    other_ref,
    obuf,
    cnt,
    turn_sem,
    send_sem,
    recv_sem,
    fsend_sem,
    frecv_sem,
    osend_sem,
    orecv_sem,
    gsend_sem,
    grecv_sem,
    wsend_sem,
    wrecv_sem,
    hsend_sem,
    hrecv_sem,
    dsend_sem,
    drecv_sem,
):
    me_s = lax.axis_index("seq")
    me_b = lax.axis_index("blk")
    tok = q_ref.shape[1]
    steps = blocks // 2
    sigma = me_b // KV
    kappa = lax.rem(me_b, KV)
    greet_all(2, blocks, me_s, me_b)
    dest_core = lax.rem(me_b, 2)
    slot = me_b // 2
    line, plane = me_b // 4, lax.rem(me_b, 4)
    weights = ((wg_ref, wg_all), (wu_ref, wu_all), (wd_ref, wd_all))

    def along(k, step, own):
        at = 0 if step < 0 else 1
        return remote(
            g_ref if own else g_all.at[k],
            g_all.at[k],
            gsend_sem.at[at, k],
            grecv_sem.at[k],
            me_s,
            (line + step) * 4 + plane,
        )

    def pass_on(k, step, own=False):
        @pl.when((line + step >= 0) & (line + step < 4))
        def _():
            along(k, step, own).start()

    def pass_distance(j):
        for step in (-1, 1):
            k = line - step * j

            @pl.when((k >= 0) & (k < 4))
            def _():
                pltpu.make_async_copy(g_ref, g_all.at[k], grecv_sem.at[k]).wait()
                pass_on(k, step)

    def half(ref):
        rows = ref.shape[0] // 2
        return ref.at[pl.ds(pl.multiple_of(me_s * rows, rows), rows)]

    def share_weight(n, i):
        own, everyone = weights[i]
        return remote(
            half(own),
            half(everyone.at[plane]),
            wsend_sem.at[n - 1, i],
            wrecv_sem.at[n - 1, i],
            me_s,
            line * 4 + flip(plane, n),
        )

    def diagonal(n, i):
        place = weights[i][1].at[flip(plane, n)]
        rows = place.shape[0] // 2
        start, size = me_s * rows, rows
        if i == 2:
            size = rows // 2
            start = start + (n - 1) * size
        part = place.at[pl.ds(pl.multiple_of(start, size), size)]
        return remote(
            part,
            part,
            dsend_sem.at[n - 1, i],
            drecv_sem.at[n - 1, i],
            me_s,
            line * 4 + flip(plane, 3 - n),
        )

    def diagonal_in(n, i):
        place = weights[i][1].at[flip(plane, 3)]
        rows = place.shape[0] // 2
        start, size = me_s * rows, rows
        if i == 2:
            size = rows // 2
            start = start + (2 - n) * size
        part = place.at[pl.ds(pl.multiple_of(start, size), size)]
        return pltpu.make_async_copy(part, part, drecv_sem.at[2 - n, i])

    def pass_weight(n, i):
        arrived = half(weights[i][1].at[flip(plane, n)])
        return remote(
            arrived, arrived, hsend_sem.at[n - 1, i], hrecv_sem.at[n - 1, i], 1 - me_s, me_b
        )

    share_weight(1, 0).start()
    share_weight(2, 1).start()
    for step in (-1, 1):
        pass_on(line, step, True)
    tables_in = [
        pltpu.make_async_copy(src.at[me_b], turn.at[i], turn_sem.at[i])
        for i, src in enumerate((cos_ref, sin_ref))
    ]
    for copy in tables_in:
        copy.start()
    xs = x_ref[...].astype(F32)
    xa = (xs * rms_scale(xs) * gain_ref[...]).astype(BF16)
    xa_ref[...] = xa
    for copy in tables_in:
        copy.wait()
    cosine, sine = turn[0], turn[1]
    low = lax.broadcasted_iota(jnp.int32, (tok, 2 * HD), 1) < HD
    pay[:, tok:, : 2 * HD] = jnp.zeros((KV, 16, 2 * HD), BF16)
    for m in range(KV // 2):
        pair = slice(m * 2 * HD, (m + 1) * 2 * HD)
        keys = mm(xa, wk_ref[:, pair])
        keys = keys * cosine + rotate_pairs(keys) * sine
        values = mm(xa, wv_ref[:, pair])
        first = jnp.where(low, keys, pltpu.roll(values, HD, 1))
        second = jnp.where(low, pltpu.roll(keys, HD, 1), values)
        pay[2 * m, :tok, 2 * HD :] = first.astype(BF16)
        pay[2 * m + 1, :tok, 2 * HD :] = second.astype(BF16)
        for k in (2 * m, 2 * m + 1):
            query = mm(xa, wq_ref[:, k * 2 * HD : (k + 1) * 2 * HD])
            query = (query * cosine + rotate_pairs(query) * sine) * HD ** (-0.5)
            pay[k, :tok, : 2 * HD] = query.astype(BF16)
            pay[k, tok:, 2 * HD :] = seg_ref[...]
    def payload(n):
        k = lax.rem(me_b + n, KV)
        chip = me_s * KV + k
        mine = (dest_core == me_s) & (chip == me_b)
        return k, chip, mine

    def send_payload(n, carry):
        k, chip, mine = payload(n)

        @pl.when(mine)
        def _():
            pltpu.make_async_copy(pay.at[k], in_ref.at[slot], recv_sem.at[slot]).start()

        @pl.when(jnp.logical_not(mine))
        def _():
            remote(
                pay.at[k], in_ref.at[slot], send_sem.at[k], recv_sem.at[slot], dest_core, chip
            ).start()

        return carry

    lax.fori_loop(0, KV, send_payload, 0)
    for i in (1, 2):
        share_weight(1, (0, 2, 1)[i]).start()
        share_weight(2, (1, 2, 0)[i]).start()

    def arrival(t):
        return pltpu.make_async_copy(pay.at[0], in_ref.at[t], recv_sem.at[t])

    def forward(t):
        return remote(
            in_ref.at[t, :, pl.ds(2 * HD, 2 * HD)],
            other_ref.at[t],
            fsend_sem.at[t],
            frecv_sem.at[t],
            1 - me_s,
            me_b,
        )

    arrival(0).wait()
    forward(0).start()
    cnt[...] = jnp.zeros_like(cnt)
    first_core = me_s == 0
    lane = lax.broadcasted_iota(jnp.int32, (1, 2 * tok), 1)
    qrow = jnp.where(lane < tok, lane, lane - tok)
    wide = 2 * tok

    def step(t, carry):
        @pl.when(t < steps - 1)
        def _():
            arrival(t + 1).wait()
            forward(t + 1).start()

        for j in (1, 2):

            @pl.when(t == GRAD_STEPS[j - 1])
            def _():
                pass_distance(j)

        @pl.when(t == HOP_STEP)
        def _():
            for n, i in ((1, 0), (2, 1)):
                share_weight(n, i).wait_recv()
                diagonal(n, i).start()
                pass_weight(n, i).start()

        @pl.when(t == HOP_STEP + 1)
        def _():
            for n, i in ((1, 2), (2, 2)):
                share_weight(n, i).wait_recv()
                diagonal(n, i).start()
                pass_weight(n, i).start()

        @pl.when(t == HOP_STEP + 2)
        def _():
            for n, i in ((1, 1), (2, 0)):
                share_weight(n, i).wait_recv()
                pass_weight(n, i).start()

        forward(t).wait_recv()
        mine = in_ref[t]
        kv_mine, seg_mine = mine[:tok, 2 * HD :], mine[tok:, 2 * HD :].astype(F32)
        other = other_ref[t]
        kv_other, seg_other = other[:tok], other[tok:].astype(F32)
        pair = jnp.where(
            first_core,
            jnp.concatenate([kv_mine, kv_other], 0).astype(F32),
            jnp.concatenate([kv_other, kv_mine], 0).astype(F32),
        )
        kv_ref[t] = pair.astype(BF16)
        kvt_ref[t] = jnp.transpose(pair).astype(BF16)
        number = lax.broadcasted_iota(jnp.int32, (8, tok), 0).astype(F32)
        seg_q = jnp.concatenate([seg_mine[0:1], seg_mine[1:2]], 1)
        seg_o = jnp.concatenate([seg_other[0:1], seg_other[1:2]], 1)
        below = (seg_q < number).astype(F32) + (seg_o < number).astype(F32)
        cnt[...] += jnp.sum(below, 1, keepdims=True)
        start_q = jnp.sum(jnp.where(seg_q == number, cnt[:, :1], 0.0), 0, keepdims=True)
        start = jnp.concatenate([start_q, start_q], 1).astype(jnp.int32)
        q_two = mine[:tok, : 2 * HD]
        q_ref[t] = q_two
        qt = stacked_heads(jnp.transpose(q_two.astype(F32)))
        qm = jnp.concatenate([qt, jnp.zeros_like(qt)], 0).astype(BF16)
        qpos = (2 * t + me_s) * tok + qrow

        def piece(u, state, last):
            running, total, acc = state
            score = mm(kv_ref[u], qm)
            kpos = u * wide + lax.broadcasted_iota(jnp.int32, score.shape, 0)
            mask = kpos >= start
            if last:
                mask &= kpos <= qpos
            score = jnp.where(mask, score, NEG)
            newmax = jnp.maximum(running, jnp.max(score, 0, keepdims=True))
            expo = jnp.exp(score - newmax)
            factor = jnp.exp(running - newmax)
            total = total * factor + jnp.sum(expo, 0, keepdims=True)
            acc = acc * factor + mm(kvt_ref[u, HD:, :], expo.astype(BF16))
            return newmax, total, acc

        state = (
            jnp.full((1, wide), NEG, F32),
            jnp.zeros((1, wide), F32),
            jnp.zeros((HD, wide), F32),
        )
        state = lax.fori_loop(0, t, lambda u, s: piece(u, s, False), state)
        running, total, acc = piece(t, state, True)
        out_t = acc / total
        ot_ref[t] = out_t
        rows = lax.broadcasted_iota(jnp.int32, (8, wide), 0)
        lse = running + jnp.log(total)
        stat_ref[t] = jnp.where(rows == 0, lse, start.astype(F32))
        upright = jnp.concatenate([out_t[:, :tok], out_t[:, tok:]], 0)
        obuf[t] = jnp.transpose(upright).astype(BF16)
        owner = 2 * t + me_s
        home = (sigma == me_s) & (owner == me_b)
        place = o_ref.at[:, pl.ds(pl.multiple_of(kappa * 2 * HD, 2 * HD), 2 * HD)]

        @pl.when(home)
        def _():
            pltpu.make_async_copy(obuf.at[t], place, orecv_sem.at[kappa]).start()

        @pl.when(jnp.logical_not(home))
        def _():
            remote(obuf.at[t], place, osend_sem.at[t], orecv_sem.at[kappa], sigma, owner).start()

        return carry

    lax.fori_loop(0, steps, step, 0)
    diagonal_in(2, 0).wait()
    pass_weight(3, 0).start()
    diagonal_in(1, 1).wait()
    pass_weight(3, 1).start()
    diagonal_in(1, 2).wait()
    diagonal_in(2, 2).wait()
    pass_weight(3, 2).start()

    def finish(t, carry):
        k, chip, mine = payload(t)

        @pl.when(jnp.logical_not(mine))
        def _():
            remote(
                pay.at[k], in_ref.at[slot], send_sem.at[k], recv_sem.at[slot], dest_core, chip
            ).wait_send()

        return carry

    lax.fori_loop(0, KV, finish, 0)

    def finish_steps(t, carry):
        forward(t).wait_send()
        owner = 2 * t + me_s
        home = (sigma == me_s) & (owner == me_b)

        @pl.when(jnp.logical_not(home))
        def _():
            remote(
                obuf.at[t],
                o_ref.at[:, pl.ds(0, 2 * HD)],
                osend_sem.at[t],
                orecv_sem.at[0],
                sigma,
                owner,
            ).wait_send()

        return carry

    lax.fori_loop(0, steps, finish_steps, 0)

    def gather(k, carry):
        pltpu.make_async_copy(
            obuf.at[0],
            o_ref.at[:, pl.ds(pl.multiple_of(k * 2 * HD, 2 * HD), 2 * HD)],
            orecv_sem.at[k],
        ).wait()
        return carry

    lax.fori_loop(0, KV, gather, 0)
    pass_distance(3)
    for k in range(4):

        @pl.when((k <= line) & (line < 3))
        def _():
            along(k, 1, False).wait_send()

        @pl.when((k >= line) & (line > 0))
        def _():
            along(k, -1, False).wait_send()

    for n in (1, 2, 3):
        for i in range(3):
            pass_weight(n, i).wait()
    for n in (1, 2):
        for i in range(3):
            share_weight(n, i).wait_send()
        diagonal(n, n - 1).wait_send()
        diagonal(n, 2).wait_send()


def attention_forward(
    blocks, x, gain, w_query, w_key, w_value, seg, cos_all, sin_all, g, w_gate, w_up, w_down
):
    tok, d = x.shape
    steps = blocks // 2
    vm = pl.BlockSpec(memory_space=pltpu.VMEM)
    hbm = pl.BlockSpec(memory_space=pl.ANY)
    dma = pltpu.SemaphoreType.DMA
    return pl.pallas_call(
        functools.partial(attention_forward_kernel, blocks),
        out_shape=(
            jax.ShapeDtypeStruct((tok, H * HD), BF16),
            jax.ShapeDtypeStruct((tok, d), BF16),
            jax.ShapeDtypeStruct((steps, 2 * tok, 2 * HD), BF16),
            jax.ShapeDtypeStruct((steps, 2 * HD, 2 * tok), BF16),
            jax.ShapeDtypeStruct((steps, tok, 2 * HD), BF16),
            jax.ShapeDtypeStruct((steps, HD, 2 * tok), F32),
            jax.ShapeDtypeStruct((steps, 8, 2 * tok), F32),
            jax.ShapeDtypeStruct((4, *g.shape), BF16),
            jax.ShapeDtypeStruct((4, *w_gate.shape), BF16),
            jax.ShapeDtypeStruct((4, *w_up.shape), BF16),
            jax.ShapeDtypeStruct((4, *w_down.shape), BF16),
        ),
        in_specs=[vm] * 6 + [hbm] * 6,
        out_specs=(vm,) * 7 + (hbm,) * 4,
        scratch_shapes=[
            pltpu.VMEM((KV, tok + 16, 4 * HD), BF16),
            pltpu.VMEM((2, tok, 2 * HD), F32),
            pltpu.VMEM((steps, tok + 16, 4 * HD), BF16),
            pltpu.VMEM((steps, tok + 16, 2 * HD), BF16),
            pltpu.VMEM((steps, tok, 2 * HD), BF16),
            pltpu.VMEM((8, 128), F32),
            dma((2,)),
            dma((KV,)),
            dma((steps,)),
            dma((steps,)),
            dma((steps,)),
            dma((steps,)),
            dma((KV,)),
            dma((2, 4)),
            dma((4,)),
            dma((2, 3)),
            dma((2, 3)),
            dma((3, 3)),
            dma((3, 3)),
            dma((2, 3)),
            dma((2, 3)),
        ],
        compiler_params=pltpu.CompilerParams(
            collective_id=0, has_side_effects=True, vmem_limit_bytes=VMEM_LIMIT
        ),
        name="attention_forward",
    )(x, gain, w_query, w_key, w_value, seg, cos_all, sin_all, g, w_gate, w_up, w_down)


def attention_backward_kernel(
    blocks,
    do_ref,
    kv_ref,
    kvt_ref,
    q_ref,
    ot_ref,
    stat_ref,
    cos_ref,
    sin_ref,
    mix_ref,
    dwg_ref,
    dwu_ref,
    dwd_ref,
    out_ref,
    mix_in,
    dwg_in,
    dwu_in,
    dwd_in,
    turn,
    turn_sem,
    in_ref,
    dkv,
    part,
    xch,
    done,
    send_sem,
    recv_sem,
    xsend_sem,
    xrecv_sem,
    osend_sem,
    orecv_sem,
    msend_sem,
    mrecv_sem,
    wsend_sem,
    wrecv_sem,
):
    me_s = lax.axis_index("seq")
    me_b = lax.axis_index("blk")
    tok = q_ref.shape[1]
    steps = blocks // 2
    sigma = me_b // KV
    kappa = lax.rem(me_b, KV)
    tables_in = [
        pltpu.make_async_copy(src.at[2 * t + me_s], turn.at[i, t], turn_sem.at[i, t])
        for i, src in enumerate((cos_ref, sin_ref))
        for t in range(steps)
    ]
    for copy in tables_in:
        copy.start()
    greet_all(2, blocks, me_s, me_b)

    dest_core = lax.rem(me_b, 2)
    slot = me_b // 2
    line, plane = me_b // 4, lax.rem(me_b, 4)
    weights = ((dwg_ref, dwg_in), (dwu_ref, dwu_in), (dwd_ref, dwd_in))

    def give_mix(n):
        return remote(
            mix_ref.at[flip(line, n)],
            mix_in.at[n - 1],
            msend_sem.at[n - 1],
            mrecv_sem.at[n - 1],
            me_s,
            flip(line, n) * 4 + plane,
        )

    def give_weight(n, i):
        src, dst = weights[i]
        return remote(
            src.at[flip(plane, n)],
            dst.at[n - 1],
            wsend_sem.at[n - 1, i],
            wrecv_sem.at[n - 1, i],
            me_s,
            line * 4 + flip(plane, n),
        )

    def outgoing(n):
        k = lax.rem(me_b + n, KV)
        chip = me_s * KV + k
        mine = (dest_core == me_s) & (chip == me_b)
        src = do_ref.at[:, pl.ds(pl.multiple_of(k * 2 * HD, 2 * HD), 2 * HD)]
        return k, chip, mine, src

    def send_grad(n, carry):
        k, chip, mine, src = outgoing(n)

        @pl.when(mine)
        def _():
            pltpu.make_async_copy(src, in_ref.at[slot], recv_sem.at[slot]).start()

        @pl.when(jnp.logical_not(mine))
        def _():
            remote(src, in_ref.at[slot], send_sem.at[k], recv_sem.at[slot], dest_core, chip).start()

        return carry

    lax.fori_loop(0, KV, send_grad, 0)
    for copy in tables_in:
        copy.wait()
    for n in (2, 1):
        give_mix(n).start()
    for i in range(3):
        for n in (1, 2):
            give_weight(n, i).start()
    give_weight(3, 2).start()
    dkv[...] = jnp.zeros_like(dkv)
    wide = 2 * tok
    lane = lax.broadcasted_iota(jnp.int32, (1, wide), 1)
    qrow = jnp.where(lane < tok, lane, lane - tok)
    low = lax.broadcasted_iota(jnp.int32, (tok, 2 * HD), 1) < HD

    def swap(t):
        return remote(part.at[t], xch.at[t], xsend_sem.at[t], xrecv_sem.at[t], 1 - me_s, me_b)

    def deliver(t, act):
        owner = 2 * t + me_s
        home = (sigma == me_s) & (owner == me_b)
        src, dst = done.at[t], out_ref.at[kappa]

        @pl.when(home)
        def _():
            if act == "start":
                pltpu.make_async_copy(src, dst, orecv_sem.at[kappa]).start()

        @pl.when(jnp.logical_not(home))
        def _():
            copy = remote(src, dst, osend_sem.at[t], orecv_sem.at[kappa], sigma, owner)
            copy.start() if act == "start" else copy.wait_send()

    def finalize(t):
        swap(t).wait_recv()
        place = pl.ds(pl.multiple_of(me_s * tok, tok), tok)
        total = dkv[t, place, :] + xch[t]
        cosine = jnp.where(low, turn[0, t], 1.0)
        sine = jnp.where(low, turn[1, t], 0.0)
        back = total * cosine - rotate_pairs(total) * sine
        done[t, :, pl.ds(2 * HD, 2 * HD)] = back.astype(BF16)
        deliver(t, "start")

    def step(n, carry):
        t = steps - 1 - n
        pltpu.make_async_copy(do_ref.at[:, pl.ds(0, 2 * HD)], in_ref.at[t], recv_sem.at[t]).wait()
        d_two = in_ref[t].astype(F32)
        q_two = q_ref[t].astype(F32)
        dt = stacked_heads(jnp.transpose(d_two))
        qt = stacked_heads(jnp.transpose(q_two))
        zero = jnp.zeros_like(dt)
        dm = jnp.concatenate([zero, dt], 0).astype(BF16)
        qm = jnp.concatenate([qt, zero], 0).astype(BF16)
        delta = jnp.sum(ot_ref[t] * dt, 0, keepdims=True)
        right = jnp.concatenate(
            [
                jnp.where(low, q_two, 0.0),
                jnp.where(low, pltpu.roll(q_two, HD, 1), 0.0),
                jnp.where(low, 0.0, pltpu.roll(d_two, HD, 1)),
                jnp.where(low, 0.0, d_two),
            ],
            0,
        ).astype(BF16)
        stat = stat_ref[t]
        lse, start = stat[0:1], stat[1:2].astype(jnp.int32)
        qpos = (2 * t + me_s) * tok + qrow

        def piece(u, dq, last):
            keys = kv_ref[u]
            score = mm(keys, qm)
            kpos = u * wide + lax.broadcasted_iota(jnp.int32, score.shape, 0)
            mask = kpos >= start
            if last:
                mask &= kpos <= qpos
            prob = jnp.where(mask, jnp.exp(score - lse), 0.0)
            dprob = mm(keys, dm)
            dscore = (prob * (dprob - delta)).astype(BF16)
            both = jnp.concatenate([dscore, prob.astype(BF16)], 1)
            dkv[u] += mm(both, right)
            return dq + mm(kvt_ref[u, :HD, :], dscore)

        dq = jnp.zeros((HD, wide), F32)
        dq = lax.fori_loop(0, t, lambda u, s: piece(u, s, False), dq)
        dq = piece(t, dq, True) * HD ** (-0.5)
        upright = jnp.transpose(jnp.concatenate([dq[:, :tok], dq[:, tok:]], 0))
        back = upright * turn[0, t] - rotate_pairs(upright) * turn[1, t]
        done[t, :, pl.ds(0, 2 * HD)] = back.astype(BF16)
        part[t] = dkv[t, pl.ds(pl.multiple_of((1 - me_s) * tok, tok), tok), :]
        swap(t).start()

        @pl.when(n > 0)
        def _():
            finalize(t + 1)

        return carry

    lax.fori_loop(0, steps, step, 0)
    finalize(0)

    def finish(n, carry):
        k, chip, mine, src = outgoing(n)

        @pl.when(jnp.logical_not(mine))
        def _():
            remote(
                src, in_ref.at[slot], send_sem.at[k], recv_sem.at[slot], dest_core, chip
            ).wait_send()

        return carry

    lax.fori_loop(0, KV, finish, 0)

    def finish_steps(t, carry):
        swap(t).wait_send()
        deliver(t, "wait")
        return carry

    lax.fori_loop(0, steps, finish_steps, 0)

    def gather(k, carry):
        pltpu.make_async_copy(done.at[0], out_ref.at[k], orecv_sem.at[k]).wait()
        return carry

    lax.fori_loop(0, KV, gather, 0)
    for n in (1, 2):
        give_mix(n).wait()
        for i in range(3):
            give_weight(n, i).wait()
    give_weight(3, 2).wait()


def attention_backward(
    blocks, vectors, mix, dwg, dwu, dwd
):
    tok = vectors[0].shape[0]
    steps = blocks // 2
    vm = pl.BlockSpec(memory_space=pltpu.VMEM)
    hbm = pl.BlockSpec(memory_space=pl.ANY)
    dma = pltpu.SemaphoreType.DMA
    return pl.pallas_call(
        functools.partial(attention_backward_kernel, blocks),
        out_shape=(
            jax.ShapeDtypeStruct((KV, tok, 4 * HD), BF16),
            jax.ShapeDtypeStruct((2, *mix.shape[1:]), BF16),
            jax.ShapeDtypeStruct((2, *dwg.shape[1:]), BF16),
            jax.ShapeDtypeStruct((2, *dwu.shape[1:]), BF16),
            jax.ShapeDtypeStruct((3, *dwd.shape[1:]), BF16),
        ),
        in_specs=[vm] * (len(vectors) - 2) + [hbm] * 6,
        out_specs=(vm,) + (hbm,) * 4,
        scratch_shapes=[
            pltpu.VMEM((2, steps, tok, 2 * HD), F32),
            dma((2, steps)),
            pltpu.VMEM((steps, tok, 2 * HD), BF16),
            pltpu.VMEM((steps, 2 * tok, 2 * HD), F32),
            pltpu.VMEM((steps, tok, 2 * HD), F32),
            pltpu.VMEM((steps, tok, 2 * HD), F32),
            pltpu.VMEM((steps, tok, 4 * HD), BF16),
            dma((KV,)),
            dma((steps,)),
            dma((steps,)),
            dma((steps,)),
            dma((steps,)),
            dma((KV,)),
            dma((2,)),
            dma((2,)),
            dma((3, 3)),
            dma((3, 3)),
        ],
        compiler_params=pltpu.CompilerParams(
            collective_id=1, has_side_effects=True, vmem_limit_bytes=VMEM_LIMIT
        ),
        name="attention_backward",
    )(*vectors, mix, dwg, dwu, dwd)


def mixture_kernel(
    x_ref,
    ao_ref,
    gain_ref,
    router_ref,
    routes_ref,
    weight_ref,
    wo_ref,
    g_ref,
    wg_ref,
    wu_ref,
    wd_ref,
    g_all,
    wg_all,
    wu_all,
    wd_all,
    res_ref,
    mix_peer,
    xl_ref,
    dlog_ref,
    dh_ref,
    datt_ref,
    do_ref,
    dgain_ref,
    dwg_out,
    dwu_out,
    dwd_out,
    dwg_in,
    dwu_in,
    wr_ref,
    rw_ref,
    h1_ref,
    gate_ref,
    d_in,
    d_c,
    wo,
    x_in,
    c_in,
    share_ref,
    x_t,
    g_in,
    wg,
    wu,
    wd,
    hc,
    dg,
    du,
    acc_o,
    acc_d,
    acc_c,
    d_send,
    d_recv,
    c_send,
    c_recv,
    xg,
    xu,
    xd,
    load_sem,
    gload_sem,
    send_sem,
    recv_sem,
    bsend_sem,
    brecv_sem,
    psend_sem,
    precv_sem,
    store_sem,
    wsend_sem,
    wrecv_sem,
    wo_sem,
    csend_sem,
    crecv_sem,
    ksend_sem,
    krecv_sem,
):
    me_s = lax.axis_index("seq")
    me_b = lax.axis_index("blk")
    line, plane = me_b // 4, lax.rem(me_b, 4)
    tok, d = g_in.shape[1:]
    ff = wg.shape[2]
    experts = router_ref.shape[0]
    barrier = pltpu.get_barrier_semaphore()
    sibling = (1 - me_s, me_b)
    opposite = (me_s, line * 4 + flip(plane, 3))
    for place in [(me_s, flip(line, n) * 4 + plane) for n in (1, 2, 3)] + [sibling, opposite]:
        pl.semaphore_signal(barrier, inc=1, device_id=place, device_id_type=MESH)

    owns = ((wg_ref, wg_all, wg), (wu_ref, wu_all, wu), (wd_ref, wd_all, wd))

    def load_own(i):
        return pltpu.make_async_copy(owns[i][0], owns[i][2].at[plane], load_sem.at[i, plane])

    def load_other(i, e):
        return pltpu.make_async_copy(owns[i][1].at[e], owns[i][2].at[e], load_sem.at[i, e])

    load_out = pltpu.make_async_copy(wo_ref, wo, wo_sem)
    load_out.start()
    for i in (2, 0, 1):
        load_own(i).start()
        for n in (1, 2, 3):
            load_other(i, flip(plane, n)).start()

    def load_grad(k):
        return pltpu.make_async_copy(g_all.at[k], g_in.at[k], gload_sem.at[k])

    pltpu.make_async_copy(g_ref, g_in.at[line], gload_sem.at[line]).start()
    for n in (1, 2, 3):
        load_grad(flip(line, n)).start()
    lane = lax.broadcasted_iota(jnp.int32, (tok, 128), 1)
    number = lax.broadcasted_iota(jnp.int32, (128, tok), 0)
    spread = jnp.zeros((128, tok), F32)
    for j in range(TOP):
        spread += jnp.where(routes_ref[j : j + 1, :] == number, weight_ref[j : j + 1, :], 0.0)
    rw = jnp.transpose(spread)
    rw_ref[...] = rw
    row, column = (lax.broadcasted_iota(jnp.int32, (experts, 128), i) for i in range(2))
    wr_ref[...] = mm(router_ref[...], (row == column).astype(BF16), TN).astype(BF16)
    load_out.wait()
    xs = x_ref[...].astype(F32)
    h1 = xs + mm(ao_ref[...], wo[...])
    h1_ref[...] = h1
    xl = (h1 * rms_scale(h1) * gain_ref[...]).astype(BF16)
    xl_ref[...] = xl
    logits = mm(xl, wr_ref[...])
    routed = rw > 0.0
    top = jnp.max(jnp.where(routed, logits, NEG), -1, keepdims=True)
    expo = jnp.where(routed, jnp.exp(logits - top), 0.0)
    gates = expo / jnp.sum(expo, -1, keepdims=True)
    gate_ref[...] = gates
    x_in[line] = xl
    c_in[line] = jnp.transpose(rw * gates)[:experts].astype(BF16)
    pl.semaphore_wait(barrier, 5)

    def along(k, step):
        at = 0 if step < 0 else 1
        return remote(
            x_in.at[k],
            x_in.at[k],
            send_sem.at[at, k],
            recv_sem.at[k],
            me_s,
            (line + step) * 4 + plane,
        )

    def along_too(k, step):
        at = 0 if step < 0 else 1
        return remote(
            c_in.at[k],
            c_in.at[k],
            csend_sem.at[at, k],
            crecv_sem.at[k],
            me_s,
            (line + step) * 4 + plane,
        )

    def pass_on(k, step):
        @pl.when((line + step >= 0) & (line + step < 4))
        def _():
            along_too(k, step).start()
            along(k, step).start()

    for step in (-1, 1):
        pass_on(line, step)
    for k in range(4):
        load_grad(k).wait()
    g_rows = g_in.reshape(4 * tok, d)

    def grad_hidden(e, carry):
        load_other(2, e).wait()
        for part in range(2):
            rows = slice(part * 2 * tok, (part + 1) * 2 * tok)
            dg[e, rows, :] = mm(g_rows[rows, :], wd[e], NT).astype(BF16)
        return carry

    lax.fori_loop(0, 4, grad_hidden, 0)

    def load_wait(e, carry):
        for i in range(2):
            load_other(i, e).wait()
        return carry

    def apart(k):
        return lax.rem(k - line + 3, 4)

    def place_of(j):
        return jnp.where(line < 2, lax.rem(line + j, 4), lax.rem(line + 4 - j, 4))

    def block(j, carry):
        n = place_of(j)
        filler = jnp.zeros((128 - experts, tok), F32)
        share_ref[...] = jnp.transpose(jnp.concatenate([c_in[n].astype(F32), filler], 0))
        acc_o[...] = jnp.zeros_like(acc_o)
        acc_d[...] = jnp.zeros_like(acc_d)
        acc_c[...] = jnp.zeros_like(acc_c)
        rows = pl.ds(pl.multiple_of(n * tok, tok), tok)

        def expert(e, carry):
            @pl.when(j == 0)
            def _():
                load_wait(e, 0)

            for step in (-1, 1):
                k = line - step * (j + 1)

                @pl.when((e == 3) & (j < 3) & (k >= 0) & (k < 4))
                def _():
                    pltpu.make_async_copy(c_in.at[line], c_in.at[k], crecv_sem.at[k]).wait()
                    pltpu.make_async_copy(x_in.at[line], x_in.at[k], recv_sem.at[k]).wait()
                    pass_on(k, step)

            x = x_in[n]
            here = lane == line * 4 + e
            share = jnp.sum(jnp.where(here, share_ref[...], 0.0), 1, keepdims=True)
            gate = mm(x, wg[e])
            up = mm(x, wu[e])
            dh = dg[e, rows, :].astype(F32)
            sg = jax.nn.sigmoid(gate)
            act = gate * sg
            hidden = act * up
            acc_c[...] += jnp.where(here, jnp.sum(dh * hidden, 1, keepdims=True), 0.0)
            dh = dh * share
            hcb = (hidden * share).astype(BF16)
            dgb = (dh * up * sg * (1.0 + gate * (1.0 - sg))).astype(BF16)
            dub = (dh * act).astype(BF16)
            hc[e, rows, :] = hcb
            dg[e, rows, :] = dgb
            du[e, rows, :] = dub
            acc_o[...] += mm(hcb, wd[e])
            acc_d[...] += mm(dgb, wg[e], NT) + mm(dub, wu[e], NT)
            return carry

        lax.fori_loop(0, 4, expert, 0)

        @pl.when(j == 0)
        def _():
            res_ref[...] = h1_ref[...] + acc_o[...]
            d_in[...] = acc_d[...]
            d_c[...] = acc_c[...]

        @pl.when(j > 0)
        def _():
            mix_peer[n] = acc_o[...].astype(BF16)
            to = apart(n)
            d_send[to] = acc_d[...].astype(BF16)
            turned = jnp.transpose(acc_c[...])[:experts]
            high = turned.astype(BF16)
            c_send[to, :experts, :] = high
            c_send[to, experts:, :] = (turned - high.astype(F32)).astype(BF16)
            give_back_too(n).start()
            give_back(n).start()

        x_t[:, rows] = jnp.transpose(x_in[n].astype(F32)).astype(BF16)
        return carry

    def give_back_too(n):
        return remote(
            c_send.at[apart(n)],
            c_recv.at[lax.rem(line - n + 3, 4)],
            ksend_sem.at[n],
            krecv_sem.at[line],
            me_s,
            n * 4 + plane,
        )

    def give_back(n):
        return remote(
            d_send.at[apart(n)], d_recv.at[lax.rem(line - n + 3, 4)], bsend_sem.at[n], brecv_sem.at[line], me_s, n * 4 + plane
        )

    lax.fori_loop(0, 4, block, 0)

    half, dhalf = d // 2, ff // 2
    theirs = pl.multiple_of((1 - me_s) * half, half)
    dtheirs = pl.multiple_of((1 - me_s) * dhalf, dhalf)
    mine = pl.multiple_of(me_s * half, half)
    dmine = pl.multiple_of(me_s * dhalf, dhalf)

    def swap(i, e):
        src = (wg.at[e, pl.ds(0, half)], wu.at[e, pl.ds(0, half)], wd.at[e, pl.ds(0, dhalf)])[i]
        dst = (xg, xu, xd)[i].at[e]
        return remote(src, dst, psend_sem.at[i, e], precv_sem.at[i, e], *sibling)

    def store(i, e):
        return pltpu.make_async_copy(
            (xg, xu, xd)[i].at[e], (dwg_out, dwu_out, dwd_out)[i].at[e], store_sem.at[i, e]
        )

    def turn_of(n):
        return jnp.where(
            n == 0, flip(plane, 3), jnp.where(n == 1, flip(plane, 2), jnp.where(n == 2, flip(plane, 1), plane))
        )

    def opposed(i):
        return remote(
            (xg, xu, xd)[i].at[flip(plane, 3)],
            (dwg_in, dwu_in)[i],
            wsend_sem.at[i],
            wrecv_sem.at[i],
            *opposite,
        )

    def finished(i, n, e):
        if i == 2:
            store(i, e).start()
            return

        @pl.when(n == 0)
        def _():
            opposed(i).start()

        @pl.when(n > 0)
        def _():
            store(i, e).start()

    def give(n, carry):
        e = turn_of(n)
        left = x_t[pl.ds(theirs, half), :]
        wg[e, :half, :] = mm(left, dg[e]).astype(BF16)
        swap(0, e).start()
        wu[e, :half, :] = mm(left, du[e]).astype(BF16)
        swap(1, e).start()
        wd[e, :dhalf, :] = mm(hc[e, :, pl.ds(dtheirs, dhalf)], g_rows[...], TN).astype(BF16)
        swap(2, e).start()
        return carry

    def keep(n, carry):
        e = turn_of(n)

        left = x_t[pl.ds(mine, half), :]
        own = mm(left, dg[e])
        swap(0, e).wait_recv()
        xg[e] = (own + xg[e].astype(F32)).astype(BF16)
        finished(0, n, e)
        own = mm(left, du[e])
        swap(1, e).wait_recv()
        xu[e] = (own + xu[e].astype(F32)).astype(BF16)
        finished(1, n, e)
        own = mm(hc[e, :, pl.ds(dmine, dhalf)], g_rows[...], TN)
        swap(2, e).wait_recv()
        xd[e] = (own + xd[e].astype(F32)).astype(BF16)
        finished(2, n, e)
        return carry

    give(0, 0)

    def both(n, carry):
        give(n, 0)
        keep(n - 1, 0)
        return carry

    lax.fori_loop(1, 4, both, 0)
    keep(3, 0)

    from_line = jnp.zeros((experts, tok), F32)
    for n in (1, 2, 3):
        k = flip(line, n)
        at = apart(k)
        pltpu.make_async_copy(c_send.at[at], c_recv.at[at], krecv_sem.at[k]).wait()
        from_line += c_recv[at, :experts, :].astype(F32) + c_recv[at, experts:, :].astype(F32)
        pltpu.make_async_copy(d_send.at[at], d_recv.at[at], brecv_sem.at[k]).wait()
        d_in[...] += d_recv[at].astype(F32)
    filler = jnp.zeros((128 - experts, tok), F32)
    d_c[...] += jnp.transpose(jnp.concatenate([from_line, filler], 0))

    gates = gate_ref[...]
    d_gates = rw_ref[...] * d_c[...]
    dlog = (gates * (d_gates - jnp.sum(gates * d_gates, -1, keepdims=True))).astype(BF16)
    dlog_ref[...] = dlog
    d_xl = d_in[...] + mm(dlog, wr_ref[...], NT)
    h1 = h1_ref[...]
    scale = rms_scale(h1)
    scaled = d_xl * gain_ref[...]
    inner = jnp.mean(scaled * h1, -1, keepdims=True)
    d_h1 = g_in[line].astype(F32) + scale * scaled - h1 * scale**3 * inner
    dgain_ref[...] = jnp.sum((d_xl * h1 * scale).reshape(tok // 8, 8, d), 0)
    dh_ref[...] = d_h1
    d_att = d_h1.astype(BF16)
    datt_ref[...] = d_att
    do_ref[...] = mm(d_att, wo[...], NT).astype(BF16)
    for n in (1, 2, 3):
        give_back(flip(line, n)).wait_send()
        give_back_too(flip(line, n)).wait_send()
    for k in range(4):

        @pl.when((k <= line) & (line < 3))
        def _():
            along(k, 1).wait_send()
            along_too(k, 1).wait_send()

        @pl.when((k >= line) & (line > 0))
        def _():
            along(k, -1).wait_send()
            along_too(k, -1).wait_send()

    def finish(n, carry):
        e = turn_of(n)
        for i in range(3):
            swap(i, e).wait_send()

            @pl.when((n > 0) | (i == 2))
            def _():
                store(i, e).wait()

        return carry

    lax.fori_loop(0, 4, finish, 0)
    for i in range(2):
        opposed(i).wait()


def mixture(vectors, w_out, g, w_gate, w_up, w_down, shared):
    tok, d = g.shape
    ff = w_gate.shape[1]
    experts = vectors[3].shape[0]
    vm = pl.BlockSpec(memory_space=pltpu.VMEM)
    hbm = pl.BlockSpec(memory_space=pl.ANY)
    dma = pltpu.SemaphoreType.DMA
    vmem = pltpu.VMEM
    return pl.pallas_call(
        mixture_kernel,
        out_shape=(
            jax.ShapeDtypeStruct((tok, d), F32),
            jax.ShapeDtypeStruct((4, tok, d), BF16),
            jax.ShapeDtypeStruct((tok, d), BF16),
            jax.ShapeDtypeStruct((tok, 128), BF16),
            jax.ShapeDtypeStruct((tok, d), F32),
            jax.ShapeDtypeStruct((tok, d), BF16),
            jax.ShapeDtypeStruct((tok, d), BF16),
            jax.ShapeDtypeStruct((8, d), F32),
            jax.ShapeDtypeStruct((4, d // 2, ff), BF16),
            jax.ShapeDtypeStruct((4, d // 2, ff), BF16),
            jax.ShapeDtypeStruct((4, ff // 2, d), BF16),
            jax.ShapeDtypeStruct((d // 2, ff), BF16),
            jax.ShapeDtypeStruct((d // 2, ff), BF16),
        ),
        in_specs=[vm] * 6 + [hbm] * 9,
        out_specs=(vm,) * 8 + (hbm,) * 5,
        scratch_shapes=[
            vmem((d, 128), BF16),
            vmem((tok, 128), F32),
            vmem((tok, d), F32),
            vmem((tok, 128), F32),
            vmem((tok, d), F32),
            vmem((tok, 128), F32),
            vmem((d, d), BF16),
            vmem((4, tok, d), BF16),
            vmem((4, experts, tok), BF16),
            vmem((tok, 128), F32),
            vmem((d, 4 * tok), BF16),
            vmem((4, tok, d), BF16),
            vmem((4, d, ff), BF16),
            vmem((4, d, ff), BF16),
            vmem((4, ff, d), BF16),
            vmem((4, 4 * tok, ff), BF16),
            vmem((4, 4 * tok, ff), BF16),
            vmem((4, 4 * tok, ff), BF16),
            vmem((tok, d), F32),
            vmem((tok, d), F32),
            vmem((tok, 128), F32),
            vmem((3, tok, d), BF16),
            vmem((3, tok, d), BF16),
            vmem((3, 2 * experts, tok), BF16),
            vmem((3, 2 * experts, tok), BF16),
            vmem((4, d // 2, ff), BF16),
            vmem((4, d // 2, ff), BF16),
            vmem((4, ff // 2, d), BF16),
            dma((3, 4)),
            dma((4,)),
            dma((2, 4)),
            dma((4,)),
            dma((4,)),
            dma((4,)),
            dma((3, 4)),
            dma((3, 4)),
            dma((3, 4)),
            dma((2,)),
            dma((2,)),
            dma,
            dma((2, 4)),
            dma((4,)),
            dma((4,)),
            dma((4,)),
        ],
        compiler_params=pltpu.CompilerParams(
            collective_id=2, has_side_effects=True, vmem_limit_bytes=VMEM_LIMIT
        ),
        name="mixture",
    )(*vectors, w_out, g, w_gate, w_up, w_down, *shared)


def tail_kernel(
    got,
    xa_ref,
    x_ref,
    gain_ref,
    dh_ref,
    ao_ref,
    datt_ref,
    xl_ref,
    dlog_ref,
    dgain2_ref,
    own_ref,
    wq_any,
    wk_any,
    wv_any,
    mix_ref,
    mix_near,
    eg_ref,
    eu_ref,
    ed_ref,
    eg_in,
    eu_in,
    ed_in,
    eg_far,
    eu_far,
    res_ref,
    dx_ref,
    gsum_ref,
    fin_o,
    fin_q,
    fin_kv,
    eg_out,
    eu_out,
    ed_out,
    mix_in,
    wq_ref,
    wk_ref,
    wv_ref,
    d_all,
    ev,
    edv,
    gbuf,
    grv,
    load_sem,
    esend,
    erecv,
    gsend,
    grecv,
    msend,
    mrecv,
    *summing,
):
    me_s = lax.axis_index("seq")
    me_b = lax.axis_index("blk")
    plane = lax.rem(me_b, 4)
    tok, d = xa_ref.shape
    sums = [
        Summed(summing[8 * i : 8 * i + 6], *summing[8 * i + 6 : 8 * i + 8], fin)
        for i, fin in enumerate((fin_o, fin_q, fin_kv))
    ]
    for_out, for_q, for_kv = sums
    [sibling], planes, lines = for_q.sibling, for_q.planes, for_q.lines
    barrier = pltpu.get_barrier_semaphore()
    for place in [sibling, *planes, *lines]:
        pl.semaphore_signal(barrier, inc=1, device_id=place, device_id_type=MESH)

    experts = (
        (eg_ref, eg_in, eg_far, ev.at[0]),
        (eu_ref, eu_in, eu_far, ev.at[1]),
        (ed_ref, ed_in, None, edv),
    )

    def loads(i):
        own, arrived, far, dst = experts[i]
        near = arrived.shape[0]
        copies = [
            pltpu.make_async_copy(own.at[plane], dst.at[0], load_sem.at[i, 0]),
            pltpu.make_async_copy(arrived, dst.at[pl.ds(1, near)], load_sem.at[i, 1]),
        ]
        if far is not None:
            copies.append(pltpu.make_async_copy(far, dst.at[3], load_sem.at[i, 2]))
        return copies

    projections = [
        pltpu.make_async_copy(src, dst, load_sem.at[3, i + 1])
        for i, (src, dst) in enumerate(((wq_any, wq_ref), (wk_any, wk_ref), (wv_any, wv_ref)))
    ]
    for copy in projections:
        copy.start()
    for i in range(3):
        for copy in loads(i):
            copy.start()
    pl.semaphore_wait(barrier, 7)
    line = me_b // 4

    far_mix = remote(mix_ref.at[flip(line, 3)], mix_in.at[2], msend, mrecv, *lines[2])
    near_mix = pltpu.make_async_copy(mix_near, mix_in.at[pl.ds(0, 2)], load_sem.at[3, 0])
    far_mix.start()
    near_mix.start()
    theirs, mine = for_q.halves()
    for_out.out[:, :d] = mm(ao_ref[:, theirs], datt_ref[...], TN).astype(BF16)
    for_out.out[:, d:] = mm(xl_ref[:, theirs], dlog_ref[...], TN).astype(BF16)
    for_out.start(0)

    low = lax.broadcasted_iota(jnp.int32, (tok, 2 * HD), 1) < HD
    for m in range(KV // 2):
        a, b = got[2 * m], got[2 * m + 1]
        d_all[:, 2 * m * 2 * HD : (2 * m + 1) * 2 * HD] = a[:, : 2 * HD]
        d_all[:, (2 * m + 1) * 2 * HD : (2 * m + 2) * 2 * HD] = b[:, : 2 * HD]
        ka, kb = a[:, 2 * HD :].astype(F32), b[:, 2 * HD :].astype(F32)
        at = H * HD + m * 2 * HD
        d_all[:, at : at + 2 * HD] = jnp.where(low, ka, pltpu.roll(kb, HD, 1)).astype(BF16)
        at += KV * HD
        d_all[:, at : at + 2 * HD] = jnp.where(low, pltpu.roll(ka, HD, 1), kb).astype(BF16)
    parts = ((for_q, slice(0, H * HD)), (for_kv, slice(H * HD, (H + 2 * KV) * HD)))
    for item, cols in parts:
        item.out[...] = mm(xa_ref[:, theirs], d_all[:, cols], TN).astype(BF16)
        item.start(0)
    for_out.acc[:, :d] = mm(ao_ref[:, mine], datt_ref[...], TN)
    for_out.acc[:, d:] = mm(xl_ref[:, mine], dlog_ref[...], TN)
    for_out.pair()
    for item, cols in parts:
        item.acc[...] = mm(xa_ref[:, mine], d_all[:, cols], TN)
        item.pair()

    for copy in projections:
        copy.wait()
    grad = (
        mm(d_all[:, : H * HD], wq_ref[...], NT)
        + mm(d_all[:, H * HD : (H + KV) * HD], wk_ref[...], NT)
        + mm(d_all[:, (H + KV) * HD :], wv_ref[...], NT)
    )
    xs = x_ref[...].astype(F32)
    scale = rms_scale(xs)
    scaled = grad * gain_ref[...]
    inner = jnp.mean(scaled * xs, -1, keepdims=True)
    dx_ref[...] = dh_ref[...] + scale * scaled - xs * scale**3 * inner
    gains = (
        jnp.sum(grad * xs * scale, 0, keepdims=True),
        jnp.sum(dgain2_ref[...], 0, keepdims=True),
    )
    part = d // 4
    gbuf[0] = jnp.concatenate(
        [gain[:, i * part : (i + 1) * part] for gain in gains for i in range(4)], 0
    )

    stages = [[sibling], planes, lines]

    def gain_copy(s, n):
        at = (0, 1, 4)[s] + n
        return remote(gbuf.at[s], grv.at[at], gsend.at[at], grecv.at[at], *stages[s][n])

    def gain_stage(s):
        for n in range(len(stages[s])):
            gain_copy(s, n).start()

    def gain_total(s):
        total = gbuf[s]
        for n in range(len(stages[s])):
            gain_copy(s, n).wait_recv()
            total = total + grv[(0, 1, 4)[s] + n]
        return total

    gain_stage(0)
    for_out.over_plane()

    outs = (eg_out, eu_out, ed_out)

    def expert_swap(i):
        rows = outs[i].shape[0] // 2
        part = outs[i].at[pl.ds(pl.multiple_of(me_s * rows, rows), rows)]
        return remote(part, part, esend.at[i], erecv.at[i], *sibling)

    for i in range(3):
        for copy in loads(i):
            copy.wait()
        terms = experts[i][3]
        rows = outs[i].shape[0] // 2
        total = terms[0].astype(F32)
        for n in (1, 2, 3):
            total = total + terms[n].astype(F32)
        outs[i][pl.ds(pl.multiple_of(me_s * rows, rows), rows), :] = total.astype(BF16)
        expert_swap(i).start()
    gbuf[1] = gain_total(0)
    gain_stage(1)
    for_q.over_plane()
    for_out.over_line()
    for_kv.over_plane()
    gbuf[2] = gain_total(1)
    gain_stage(2)
    for_q.over_line()
    for_out.back(3)
    for_kv.over_line()
    for_q.back(3)
    for_kv.back(3)
    gsum_ref[...] = gain_total(2)
    for item in sums:
        item.back(4)
    result = own_ref[...]
    near_mix.wait()
    far_mix.wait()
    for n in range(3):
        result = result + mix_in[n].astype(F32)
    res_ref[...] = result.astype(BF16)
    for item in sums:
        item.finish()
    for i in range(3):
        expert_swap(i).wait()
    for s in range(3):
        for n in range(len(stages[s])):
            gain_copy(s, n).wait_send()


def tail(blocks_in, mix_peer, mix_near, own, arrived, far):
    tok, d = blocks_in[1].shape
    ff = own[0].shape[2]
    widths = (d + 128, H * HD, 2 * KV * HD)
    vm = pl.BlockSpec(memory_space=pltpu.VMEM)
    hbm = pl.BlockSpec(memory_space=pl.ANY)
    dma = pltpu.SemaphoreType.DMA
    vmem = pltpu.VMEM
    return pl.pallas_call(
        tail_kernel,
        out_shape=(
            jax.ShapeDtypeStruct((tok, d), BF16),
            jax.ShapeDtypeStruct((tok, d), F32),
            jax.ShapeDtypeStruct((8, d // 4), F32),
            *(jax.ShapeDtypeStruct((d, width), BF16) for width in widths),
            jax.ShapeDtypeStruct((d, ff), BF16),
            jax.ShapeDtypeStruct((d, ff), BF16),
            jax.ShapeDtypeStruct((ff, d), BF16),
        ),
        in_specs=[vm] * (len(blocks_in) - 3) + [hbm] * 13,
        out_specs=(vm,) * 9,
        scratch_shapes=[
            vmem((3, tok, d), BF16),
            vmem((d, H * HD), BF16),
            vmem((d, KV * HD), BF16),
            vmem((d, KV * HD), BF16),
            vmem((tok, (H + 2 * KV) * HD), BF16),
            vmem((2, 4, d // 2, ff), BF16),
            vmem((4, ff // 2, d), BF16),
            vmem((3, 8, d // 4), F32),
            vmem((7, 8, d // 4), F32),
            dma((4, 4)),
            dma((3,)),
            dma((3,)),
            dma((7,)),
            dma((7,)),
            dma,
            dma,
            *(ref for width in widths for ref in summed_scratch(d, width)),
        ],
        compiler_params=pltpu.CompilerParams(
            collective_id=3, has_side_effects=True, vmem_limit_bytes=VMEM_LIMIT
        ),
        name="tail",
    )(*blocks_in, mix_peer, mix_near, *own, *arrived, *far)


def widen_kernel(
    gains, o, q, kv, eg, eu, ed, res, dx, n1, wq, wk, wv, wo, n2, wr, og, ou, od, res_out, dx_out
):
    d = wq.shape[1]
    half = wk.shape[1]
    wq[...] = q[...].astype(F32)
    wk[...] = kv[:, :half].astype(F32)
    wv[...] = kv[:, half:].astype(F32)
    wo[...] = o[:, :d].astype(F32)
    wr[...] = jnp.transpose(o[:, d:].astype(F32))[: wr.shape[0]]
    og[0] = eg[...].astype(F32)
    ou[0] = eu[...].astype(F32)
    od[0] = ed[...].astype(F32)
    n1[...] = jnp.concatenate([gains[i : i + 1, :] for i in range(4)], 1)
    n2[...] = jnp.concatenate([gains[i : i + 1, :] for i in range(4, 8)], 1)
    res_out[0] = res[...]
    dx_out[0] = dx[...]


def widen(gains, o, q, kv, eg, eu, ed, res, dx, experts):
    d, ff = eg.shape
    tok = res.shape[0]
    parts = 4

    def block(shape):
        return pl.BlockSpec((shape[0] // parts, shape[1]), lambda i: (i, 0))

    def deep(shape):
        return pl.BlockSpec((1, shape[0] // parts, shape[1]), lambda i: (0, i, 0))

    flat = pl.BlockSpec((1, d), lambda i: (0, 0))
    shapes = [(d, H * HD), (d, KV * HD), (d, KV * HD), (H * HD, d)]
    return pl.pallas_call(
        widen_kernel,
        grid=(parts,),
        out_shape=(
            jax.ShapeDtypeStruct((1, d), F32),
            *(jax.ShapeDtypeStruct(shape, F32) for shape in shapes),
            jax.ShapeDtypeStruct((1, d), F32),
            jax.ShapeDtypeStruct((experts, d), F32),
            jax.ShapeDtypeStruct((1, d, ff), F32),
            jax.ShapeDtypeStruct((1, d, ff), F32),
            jax.ShapeDtypeStruct((1, ff, d), F32),
            jax.ShapeDtypeStruct((1, tok, d), BF16),
            jax.ShapeDtypeStruct((1, tok, d), F32),
        ),
        in_specs=[pl.BlockSpec((8, d // 4), lambda i: (0, 0))]
        + [block(a.shape) for a in (o, q, kv, eg, eu, ed, res, dx)],
        out_specs=(
            flat,
            *(block(shape) for shape in shapes),
            flat,
            pl.BlockSpec((experts, d // parts), lambda i: (0, i)),
            deep((d, ff)),
            deep((d, ff)),
            deep((ff, d)),
            deep((tok, d)),
            deep((tok, d)),
        ),
        compiler_params=pltpu.CompilerParams(vmem_limit_bytes=VMEM_LIMIT),
        name="widen",
    )(gains, o, q, kv, eg, eu, ed, res, dx)


D = 1024
HIGH = lax.Precision.HIGHEST


def rope_tables(positions):
    half = HD // 2
    freq = jnp.exp(-math.log(10000.0) * jnp.arange(half, dtype=jnp.float32) * 2.0 / HD)
    angle = positions.astype(jnp.float32)[:, None] * freq[None, :]
    cosine = jnp.concatenate([jnp.cos(angle), jnp.cos(angle)], -1)
    sine = jnp.concatenate([jnp.sin(angle), jnp.sin(angle)], -1)
    return (cosine, sine)


def rotate_half(v):
    half = v.shape[-1] // 2
    return jnp.concatenate([-v[..., half:], v[..., :half]], -1)


def rotary(v, cosine, sine):
    return v * cosine[:, None, :] + rotate_half(v) * sine[:, None, :]


def unrotary(v, cosine, sine):
    return v * cosine[:, None, :] - rotate_half(v) * sine[:, None, :]


def rms_scale(v):
    return lax.rsqrt(jnp.mean(v * v, -1, keepdims=True) + EPS)


def rms_back(inputs, scale_rows, gain, grad):
    scaled = grad * gain
    d_inputs = scale_rows * scaled - inputs * scale_rows**3 * jnp.mean(
        scaled * inputs, -1, keepdims=True
    )
    return (d_inputs, jnp.sum(grad * inputs * scale_rows, 0))


def scores(queries, keys):
    return jnp.einsum("qkgd,skd->kgqs", queries, keys, preferred_element_type=jnp.float32) * HD ** (
        -0.5
    )


def per_device_plain(
    tokens,
    segments,
    routes,
    route_weight,
    norm1_gain,
    w_query,
    w_key,
    w_value,
    w_out,
    norm2_gain,
    w_router,
    w_gate,
    w_up,
    w_down,
    cotangent,
):
    f32 = jnp.float32
    bf16 = jnp.bfloat16
    scale = HD ** (-0.5)
    group = H // KV
    xs = tokens[0].astype(f32)
    tok = xs.shape[0]
    blocks = lax.axis_size("blk")
    length = tok * blocks
    first = lax.axis_index("blk") * tok
    last = first + tok - 1
    positions = first + jnp.arange(tok, dtype=jnp.int32)
    cosine, sine = rope_tables(positions)
    scale1 = rms_scale(xs)
    xa = (xs * scale1 * norm1_gain).astype(bf16)
    query = jnp.dot(xa, w_query, preferred_element_type=f32)
    key = jnp.dot(xa, w_key, preferred_element_type=f32)
    value = jnp.dot(xa, w_value, preferred_element_type=f32).astype(bf16)
    q_rot = rotary(query.reshape(tok, H, HD), cosine, sine).astype(bf16).reshape(tok, KV, group, HD)
    k_rot = rotary(key.reshape(tok, KV, HD), cosine, sine).astype(bf16).reshape(tok, KV * HD)
    seg_float = segments[0].astype(bf16)
    k_all, v_all, seg_all = (
        lax.all_gather(k_rot, "blk", axis=0, tiled=True),
        lax.all_gather(value, "blk", axis=0, tiled=True),
        lax.all_gather(seg_float, "blk", axis=0, tiled=True),
    )
    kblk = min(512, length)
    nblk = length // kblk
    k_blocks = k_all.reshape(nblk, kblk, KV, HD)
    v_blocks = v_all.reshape(nblk, kblk, KV, HD)
    s_blocks = seg_all.reshape(nblk, kblk)
    starts = jnp.arange(nblk, dtype=jnp.int32) * kblk

    def visible(kseg, kstart):
        kpos = kstart + jnp.arange(kblk, dtype=jnp.int32)
        return ((seg_float[:, None] == kseg[None, :]) & (kpos[None, :] <= positions[:, None]))[
            None, None
        ]

    def forward_step(carry, block):
        kb, vb, sb, start = block

        def forward_compute(state):
            running, total, acc = state
            mask = visible(sb, start)
            score = jnp.where(mask, scores(q_rot, kb), NEG)
            newmax = jnp.maximum(running, jnp.max(score, -1))
            expo = jnp.where(mask, jnp.exp(score - newmax[..., None]), 0.0)
            factor = jnp.exp(running - newmax)
            total = total * factor + jnp.sum(expo, -1)
            acc = acc * factor[..., None] + jnp.einsum(
                "kgqs,skd->kgqd", expo.astype(bf16), vb, preferred_element_type=f32
            )
            return (newmax, total, acc)

        return (lax.cond(start <= last, forward_compute, lambda state: state, carry), None)

    init = (
        jnp.full((KV, group, tok), NEG, f32),
        jnp.zeros((KV, group, tok), f32),
        jnp.zeros((KV, group, tok, HD), f32),
    )
    (running, total, acc), unused = lax.scan(
        forward_step, init, (k_blocks, v_blocks, s_blocks, starts)
    )
    lse = running + jnp.log(total)
    o_rows = (acc / total[..., None]).transpose(2, 0, 1, 3)
    att_low = o_rows.reshape(tok, H * HD).astype(bf16)
    h1 = xs + jnp.dot(att_low, w_out, preferred_element_type=f32)
    scale2 = rms_scale(h1)
    xl = (h1 * scale2 * norm2_gain).astype(bf16)
    logits = jnp.dot(xl, w_router, preferred_element_type=f32)
    experts = logits.shape[1]
    route = routes[0]
    rweight = route_weight[0]
    chooser = (route[:, :, None] == jnp.arange(experts, dtype=jnp.int32)[None, None, :]).astype(f32)
    chosen = jnp.sum(chooser * logits[:, None, :], -1)
    gates = jax.nn.softmax(chosen, -1)
    combine = (rweight * gates).astype(bf16)
    cap = min(tok, 2 * tok * TOP // experts)
    member = jnp.sum(chooser, 1)
    before = jnp.asarray(np.tril(np.ones((tok, tok), np.float32), -1))
    order = jnp.dot(before, member, precision=HIGH)
    rank = jnp.sum(chooser * order[:, None, :], -1).astype(jnp.int32)
    slots = route * cap + rank
    placed = jnp.any(
        slots[:, :, None] == jnp.arange(experts * cap, dtype=jnp.int32)[None, None, :], 1
    ).astype(bf16)
    outgoing = jnp.einsum("ts,td->sd", placed, xl, preferred_element_type=f32).astype(bf16)
    incoming = lax.all_to_all(
        outgoing.reshape(experts, cap, D), "blk", split_axis=0, concat_axis=0, tiled=True
    )
    local_exp = w_gate.shape[0]
    incoming = incoming.reshape(blocks, local_exp, cap, D)
    gate_pre = jnp.einsum("necd,edf->necf", incoming, w_gate, preferred_element_type=f32)
    up_pre = jnp.einsum("necd,edf->necf", incoming, w_up, preferred_element_type=f32)
    sigma = jax.nn.sigmoid(gate_pre)
    activated = gate_pre * sigma
    hidden = (activated * up_pre).astype(bf16)
    expert_out = jnp.einsum("necf,efd->necd", hidden, w_down, preferred_element_type=f32).astype(
        bf16
    )
    returned = lax.all_to_all(
        expert_out.reshape(experts, cap, D), "blk", split_axis=0, concat_axis=0, tiled=True
    )
    per_route = jnp.take(returned.reshape(experts * cap, D), slots.reshape(-1), axis=0).reshape(
        tok, TOP, D
    )
    mixture = jnp.einsum("tj,tjd->td", combine, per_route, preferred_element_type=f32)
    result = h1 + mixture
    grad_out = cotangent[0].astype(f32)
    grad_combine = jnp.einsum("td,tjd->tj", grad_out, per_route.astype(f32), precision=HIGH)
    route_grads = (combine.astype(f32)[:, :, None] * grad_out[:, None, :]).astype(bf16)
    grad_slots = (
        jnp.zeros((experts * cap, D), bf16)
        .at[slots.reshape(-1)]
        .set(route_grads.reshape(tok * TOP, D))
    )
    grad_incoming = lax.all_to_all(
        grad_slots.reshape(experts, cap, D), "blk", split_axis=0, concat_axis=0, tiled=True
    )
    grad_incoming = grad_incoming.reshape(blocks, local_exp, cap, D)
    grad_hidden = jnp.einsum("necd,efd->necf", grad_incoming, w_down, preferred_element_type=f32)
    grad_gate = (grad_hidden * up_pre * sigma * (1.0 + gate_pre * (1.0 - sigma))).astype(bf16)
    grad_up = (grad_hidden * activated).astype(bf16)
    d_down = jnp.einsum("necf,necd->efd", hidden, grad_incoming, preferred_element_type=f32)
    d_gate_w = jnp.einsum("necd,necf->edf", incoming, grad_gate, preferred_element_type=f32)
    d_up_w = jnp.einsum("necd,necf->edf", incoming, grad_up, preferred_element_type=f32)
    grad_in = (
        jnp.einsum("necf,edf->necd", grad_gate, w_gate, preferred_element_type=f32)
        + jnp.einsum("necf,edf->necd", grad_up, w_up, preferred_element_type=f32)
    ).astype(bf16)
    grad_back = lax.all_to_all(
        grad_in.reshape(experts, cap, D), "blk", split_axis=0, concat_axis=0, tiled=True
    )
    grad_xl = jnp.einsum(
        "ts,sd->td", placed, grad_back.reshape(experts * cap, D), preferred_element_type=f32
    )
    grad_gates = rweight * grad_combine
    grad_chosen = gates * (grad_gates - jnp.sum(gates * grad_gates, -1, keepdims=True))
    grad_logits = jnp.sum(chooser * grad_chosen[:, :, None], 1).astype(bf16)
    d_router = jnp.einsum("td,te->de", xl, grad_logits, preferred_element_type=f32)
    grad_xl = grad_xl + jnp.einsum("te,de->td", grad_logits, w_router, preferred_element_type=f32)
    grad_h1_norm, d_gain2 = rms_back(h1, scale2, norm2_gain, grad_xl)
    grad_h1 = grad_out + grad_h1_norm
    grad_att = grad_h1.astype(bf16)
    d_out_w = jnp.einsum("ti,td->id", att_low, grad_att, preferred_element_type=f32)
    grad_o = jnp.einsum("td,id->ti", grad_att, w_out, preferred_element_type=f32).astype(bf16)
    grad_o_rows = grad_o.reshape(tok, KV, group, HD)
    delta = jnp.einsum("qkgd,qkgd->kgq", grad_o_rows.astype(f32), o_rows)

    def query_terms(kb, vb, sb, start):
        mask = visible(sb, start)
        prob = jnp.where(mask, jnp.exp(scores(q_rot, kb) - lse[..., None]), 0.0)
        dprob = jnp.einsum("qkgd,skd->kgqs", grad_o_rows, vb, preferred_element_type=f32)
        dscore = (prob * (dprob - delta[..., None])).astype(bf16)
        dq_term = jnp.einsum("kgqs,skd->qkgd", dscore, kb, preferred_element_type=f32) * scale
        return (dq_term, dscore, prob)

    zero_q = jnp.zeros((tok, KV, group, HD), f32)

    def backward_step(grad_q, block):
        kb, vb, sb, start = block

        def backward_compute(acc_q):
            dq_term, dscore, prob = query_terms(kb, vb, sb, start)
            gk = jnp.einsum("kgqs,qkgd->skd", dscore, q_rot, preferred_element_type=f32) * scale
            gv = jnp.einsum(
                "kgqs,qkgd->skd", prob.astype(bf16), grad_o_rows, preferred_element_type=f32
            )
            return (acc_q + dq_term, (gk.reshape(kblk, KV * HD), gv.reshape(kblk, KV * HD)))

        def skip(acc_q):
            empty = jnp.zeros((kblk, KV * HD), f32)
            return (acc_q, (empty, empty))

        return lax.cond(start <= last, backward_compute, skip, grad_q)

    grad_q, (gk_blocks, gv_blocks) = lax.scan(
        backward_step, zero_q, (k_blocks, v_blocks, s_blocks, starts)
    )
    grad_k, grad_v = (
        lax.psum_scatter(
            gk_blocks.reshape(length, KV * HD).astype(jnp.bfloat16),
            "blk",
            scatter_dimension=0,
            tiled=True,
        ).astype(jnp.float32),
        lax.psum_scatter(
            gv_blocks.reshape(length, KV * HD).astype(jnp.bfloat16),
            "blk",
            scatter_dimension=0,
            tiled=True,
        ).astype(jnp.float32),
    )
    grad_qr = unrotary(grad_q.reshape(tok, H, HD), cosine, sine).reshape(tok, H * HD).astype(bf16)
    grad_kr = unrotary(grad_k.reshape(tok, KV, HD), cosine, sine).reshape(tok, KV * HD).astype(bf16)
    grad_vr = grad_v.astype(bf16)
    d_query = jnp.einsum("td,te->de", xa, grad_qr, preferred_element_type=f32)
    d_key = jnp.einsum("td,te->de", xa, grad_kr, preferred_element_type=f32)
    d_value = jnp.einsum("td,te->de", xa, grad_vr, preferred_element_type=f32)
    grad_xa = (
        jnp.einsum("te,de->td", grad_qr, w_query, preferred_element_type=f32)
        + jnp.einsum("te,de->td", grad_kr, w_key, preferred_element_type=f32)
        + jnp.einsum("te,de->td", grad_vr, w_value, preferred_element_type=f32)
    )
    grad_x_norm, d_gain1 = rms_back(xs, scale1, norm1_gain, grad_xa)
    grad_x = grad_h1 + grad_x_norm
    summed = lax.psum(
        (d_gain1, d_query, d_key, d_value, d_out_w, d_gain2, d_router), ("seq", "blk")
    )
    expert_summed = (
        lax.psum(d_gate_w.astype(jnp.bfloat16), "seq").astype(jnp.float32),
        lax.psum(d_up_w.astype(jnp.bfloat16), "seq").astype(jnp.float32),
        lax.psum(d_down.astype(jnp.bfloat16), "seq").astype(jnp.float32),
    )
    return (
        result.astype(bf16)[None],
        grad_x[None],
        summed[0],
        summed[1],
        summed[2],
        summed[3],
        summed[4],
        summed[5],
        summed[6],
        expert_summed[0],
        expert_summed[1],
        expert_summed[2],
    )


def tables(length):
    half = HD // 2
    freq = np.exp(-math.log(10000.0) * np.arange(half, dtype=np.float32) * 2.0 / HD).astype(np.float32)
    angle = np.arange(length, dtype=np.float32)[:, None] * freq[None, :]
    return np.tile(np.cos(angle), (1, 4)), np.tile(np.sin(angle), (1, 4))


def per_device(
    tokens,
    segments,
    routes,
    route_weight,
    norm1_gain,
    w_query,
    w_key,
    w_value,
    w_out,
    norm2_gain,
    w_router,
    w_gate,
    w_up,
    w_down,
    cotangent,
):
    tok, d = tokens[0].shape
    blocks = lax.axis_size("blk")
    experts = w_router.shape[1]
    cos_np, sin_np = tables(tok * blocks)
    cos_all = jnp.asarray(cos_np.reshape(blocks, tok, 2 * HD))
    sin_all = jnp.asarray(sin_np.reshape(blocks, tok, 2 * HD))
    seg = jnp.pad(segments[0].astype(BF16).reshape(2, tok // 2), ((0, 14), (0, 0)))
    gain1 = norm1_gain[None]
    g_low = cotangent[0]
    att_low, xa, *kept = attention_forward(
        blocks,
        tokens[0],
        gain1,
        w_query,
        w_key,
        w_value,
        seg,
        cos_all,
        sin_all,
        g_low,
        w_gate[0],
        w_up[0],
        w_down[0],
    )
    kept, shared = kept[:5], kept[5:]

    own, mix_peer, xl, grad_logits, grad_h1, grad_att, grad_o, gain2_terms, *rest = mixture(
        (tokens[0], att_low, norm2_gain[None], w_router.T, routes[0].T, route_weight[0].T),
        w_out,
        g_low,
        w_gate[0],
        w_up[0],
        w_down[0],
        shared,
    )
    (dwg, dwu, dwd), far = rest[:3], rest[3:]
    vectors = (
        grad_o,
        *kept,
        cos_all,
        sin_all,
    )
    got, mix_near, *arrived = attention_backward(
        blocks, vectors, mix_peer, dwg, dwu, dwd
    )
    blocks_in = (
        got,
        xa,
        tokens[0],
        gain1,
        grad_h1,
        att_low,
        grad_att,
        xl,
        grad_logits,
        gain2_terms,
        own,
        w_query,
        w_key,
        w_value,
    )
    result, grad_x, gains, d_out, d_query, d_kv, d_gate_w, d_up_w, d_down = tail(
        blocks_in, mix_peer, mix_near, (dwg, dwu, dwd), arrived, far
    )
    wide = widen(gains, d_out, d_query, d_kv, d_gate_w, d_up_w, d_down, result, grad_x, experts)
    d_gain1, d_query, d_key, d_value, d_out, d_gain2, d_router, *rest, result, grad_x = wide
    return (
        result,
        grad_x,
        d_gain1[0],
        d_query,
        d_key,
        d_value,
        d_out,
        d_gain2[0],
        d_router.T,
        *rest,
    )


def solution(mesh):
    fused = dict(mesh.shape) == {"seq": 2, "blk": 2 * KV}
    return jax.shard_map(
        per_device if fused else per_device_plain,
        mesh=mesh,
        in_specs=(
            P("seq", "blk", None),
            P("seq", "blk"),
            P("seq", "blk", None),
            P("seq", "blk", None),
            P(),
            P(),
            P(),
            P(),
            P(),
            P(),
            P(),
            P("blk", None, None),
            P("blk", None, None),
            P("blk", None, None),
            P("seq", "blk", None),
        ),
        out_specs=(
            P("seq", "blk", None),
            P("seq", "blk", None),
            P(),
            P(),
            P(),
            P(),
            P(),
            P(),
            P(),
            P("blk", None, None),
            P("blk", None, None),
            P("blk", None, None),
        ),
        check_vma=False,
    )
```

```python
import functools
import math

import jax
import jax.numpy as jnp
import numpy as np
from jax import lax
from jax.experimental import pallas as pl
from jax.experimental.pallas import tpu as pltpu
from jax.sharding import PartitionSpec as P

H = 16
KV = 8
HD = 64
TOP = 8
EPS = 1e-06
NEG = -1e30
F32 = jnp.float32
BF16 = jnp.bfloat16
MESH = pl.DeviceIdType.MESH
VMEM_LIMIT = 60 * 2**20
GRAD_STEPS = (2, 5)
HOP_STEP = 4
NT = (((1,), (1,)), ((), ()))
TN = (((0,), (0,)), ((), ()))


def mm(a, b, dims=(((1,), (0,)), ((), ()))):
    return lax.dot_general(a, b, dims, preferred_element_type=F32)


def remote(src, dst, send, recv, seq, blk):
    return pltpu.make_async_remote_copy(
        src_ref=src,
        dst_ref=dst,
        send_sem=send,
        recv_sem=recv,
        device_id=(seq, blk),
        device_id_type=MESH,
    )


def greet_all(seqs, blocks, me_s, me_b):
    barrier = pltpu.get_barrier_semaphore()
    total = seqs * blocks

    def hello(n, carry):
        other = lax.rem(me_s * blocks + me_b + n, total)
        pl.semaphore_signal(
            barrier,
            inc=1,
            device_id=(other // blocks, lax.rem(other, blocks)),
            device_id_type=MESH,
        )
        return carry

    lax.fori_loop(1, total, hello, 0)
    pl.semaphore_wait(barrier, total - 1)


def flip(place, n):
    if n == 1:
        return place + 1 - 2 * lax.rem(place, 2)
    if n == 2:
        return place + 2 - 4 * (place // 2)
    return 3 - place


def rotate_pairs(u):
    lanes = u.shape[-1]
    half = HD // 2
    lane = lax.broadcasted_iota(jnp.int32, u.shape, u.ndim - 1)
    ahead = pltpu.roll(u, lanes - half, u.ndim - 1)
    behind = pltpu.roll(u, half, u.ndim - 1)
    return jnp.where(lane % HD < half, -ahead, behind)


def stacked_heads(wide):
    return jnp.concatenate([wide[:HD], wide[HD:]], axis=1)


STAGES = 6


class Summed:
    def __init__(self, refs, send_sem, recv_sem, fin):
        self.out, self.arrived, self.acc, self.part, self.plane_in, self.line_in = refs
        self.send_sem, self.recv_sem, self.fin = send_sem, recv_sem, fin
        self.me_s = lax.axis_index("seq")
        me_b = lax.axis_index("blk")
        self.line, self.plane = me_b // 4, lax.rem(me_b, 4)
        self.sibling = [(1 - self.me_s, me_b)]
        self.planes = [(self.me_s, self.line * 4 + flip(self.plane, n)) for n in (1, 2, 3)]
        self.lines = [(self.me_s, flip(self.line, n) * 4 + self.plane) for n in (1, 2, 3)]
        rows = fin.shape[0]
        self.half, self.quarter, self.piece = rows // 2, rows // 8, rows // 32

    def rows(self, start, size):
        return pl.ds(pl.multiple_of(start, size), size)

    def halves(self):
        theirs = self.rows((1 - self.me_s) * self.half, self.half)
        return theirs, self.rows(self.me_s * self.half, self.half)

    def copy(self, stage, n):
        sems = self.send_sem.at[stage, n], self.recv_sem.at[stage, n]
        base = self.me_s * self.half
        if stage == 0:
            return remote(self.out, self.arrived, *sems, *self.sibling[n])
        if stage == 1:
            src = self.part.at[self.rows(flip(self.plane, n + 1) * self.quarter, self.quarter)]
            return remote(src, self.plane_in.at[n], *sems, *self.planes[n])
        if stage == 2:
            at = self.plane * self.quarter + flip(self.line, n + 1) * self.piece
            src = self.part.at[self.rows(at, self.piece)]
            return remote(src, self.line_in.at[n], *sems, *self.lines[n])
        if stage == 3:
            at = base + self.plane * self.quarter + self.line * self.piece
            part = self.fin.at[self.rows(at, self.piece)]
            return remote(part, part, *sems, *self.lines[n])
        if stage == 4:
            part = self.fin.at[self.rows(base + self.plane * self.quarter, self.quarter)]
            return remote(part, part, *sems, *self.planes[n])
        part = self.fin.at[self.rows(base, self.half)]
        return remote(part, part, *sems, *self.sibling[n])

    def start(self, stage):
        for n in range(1) if stage in (0, 5) else (2, 0, 1):
            self.copy(stage, n).start()

    def arrive(self, stage):
        for n in range(1 if stage in (0, 5) else 3):
            self.copy(stage, n).wait_recv()

    def pair(self):
        self.arrive(0)
        self.part[...] = (self.acc[...] + self.arrived[...].astype(F32)).astype(BF16)
        self.start(1)

    def over_plane(self):
        self.arrive(1)
        here = self.rows(self.plane * self.quarter, self.quarter)
        total = self.part[here, :].astype(F32)
        for n in range(3):
            total = total + self.plane_in[n].astype(F32)
        self.part[here, :] = total.astype(BF16)
        self.start(2)

    def over_line(self):
        self.arrive(2)
        at = self.plane * self.quarter + self.line * self.piece
        total = self.part[self.rows(at, self.piece), :].astype(F32)
        for n in range(3):
            total = total + self.line_in[n].astype(F32)
        self.fin[self.rows(self.me_s * self.half + at, self.piece), :] = total.astype(BF16)
        self.start(3)

    def back(self, stage):
        self.arrive(stage)
        self.start(stage + 1)

    def finish(self):
        self.arrive(5)
        for stage in range(STAGES):
            for n in range(1 if stage in (0, 5) else 3):
                self.copy(stage, n).wait_send()


def summed_scratch(rows, width):
    vmem, dma = pltpu.VMEM, pltpu.SemaphoreType.DMA
    return [
        vmem((rows // 2, width), BF16),
        vmem((rows // 2, width), BF16),
        vmem((rows // 2, width), F32),
        vmem((rows // 2, width), BF16),
        vmem((3, rows // 8, width), BF16),
        vmem((3, rows // 32, width), BF16),
        dma((STAGES, 3)),
        dma((STAGES, 3)),
    ]


def attention_forward_kernel(
    blocks,
    x_ref,
    gain_ref,
    wq_ref,
    wk_ref,
    wv_ref,
    seg_ref,
    cos_ref,
    sin_ref,
    g_ref,
    wg_ref,
    wu_ref,
    wd_ref,
    o_ref,
    xa_ref,
    kv_any,
    kvt_any,
    q_any,
    ot_any,
    stat_any,
    g_all,
    wg_all,
    wu_all,
    wd_all,
    kv_ref,
    kvt_ref,
    q_ref,
    ot_ref,
    stat_ref,
    kept_sem,
    pay,
    turn,
    in_ref,
    other_ref,
    obuf,
    cnt,
    turn_sem,
    send_sem,
    recv_sem,
    fsend_sem,
    frecv_sem,
    osend_sem,
    orecv_sem,
    gsend_sem,
    grecv_sem,
    wsend_sem,
    wrecv_sem,
    hsend_sem,
    hrecv_sem,
    dsend_sem,
    drecv_sem,
):
    me_s = lax.axis_index("seq")
    me_b = lax.axis_index("blk")
    tok = q_ref.shape[1]
    steps = blocks // 2
    sigma = me_b // KV
    kappa = lax.rem(me_b, KV)
    greet_all(2, blocks, me_s, me_b)
    dest_core = lax.rem(me_b, 2)
    slot = me_b // 2
    line, plane = me_b // 4, lax.rem(me_b, 4)
    weights = ((wg_ref, wg_all), (wu_ref, wu_all), (wd_ref, wd_all))

    def along(k, step, own):
        at = 0 if step < 0 else 1
        return remote(
            g_ref if own else g_all.at[k],
            g_all.at[k],
            gsend_sem.at[at, k],
            grecv_sem.at[k],
            me_s,
            (line + step) * 4 + plane,
        )

    def pass_on(k, step, own=False):
        @pl.when((line + step >= 0) & (line + step < 4))
        def _():
            along(k, step, own).start()

    def pass_distance(j):
        for step in (-1, 1):
            k = line - step * j

            @pl.when((k >= 0) & (k < 4))
            def _():
                pltpu.make_async_copy(g_ref, g_all.at[k], grecv_sem.at[k]).wait()
                pass_on(k, step)

    def half(ref):
        rows = ref.shape[0] // 2
        return ref.at[pl.ds(pl.multiple_of(me_s * rows, rows), rows)]

    def share_weight(n, i):
        own, everyone = weights[i]
        return remote(
            half(own),
            half(everyone.at[plane]),
            wsend_sem.at[n - 1, i],
            wrecv_sem.at[n - 1, i],
            me_s,
            line * 4 + flip(plane, n),
        )

    def diagonal(n, i):
        place = weights[i][1].at[flip(plane, n)]
        rows = place.shape[0] // 2
        start, size = me_s * rows, rows
        if i == 2:
            size = rows // 2
            start = start + (n - 1) * size
        part = place.at[pl.ds(pl.multiple_of(start, size), size)]
        return remote(
            part,
            part,
            dsend_sem.at[n - 1, i],
            drecv_sem.at[n - 1, i],
            me_s,
            line * 4 + flip(plane, 3 - n),
        )

    def diagonal_in(n, i):
        place = weights[i][1].at[flip(plane, 3)]
        rows = place.shape[0] // 2
        start, size = me_s * rows, rows
        if i == 2:
            size = rows // 2
            start = start + (2 - n) * size
        part = place.at[pl.ds(pl.multiple_of(start, size), size)]
        return pltpu.make_async_copy(part, part, drecv_sem.at[2 - n, i])

    def pass_weight(n, i):
        arrived = half(weights[i][1].at[flip(plane, n)])
        return remote(
            arrived, arrived, hsend_sem.at[n - 1, i], hrecv_sem.at[n - 1, i], 1 - me_s, me_b
        )

    share_weight(1, 0).start()
    share_weight(2, 1).start()
    for step in (-1, 1):
        pass_on(line, step, True)
    tables_in = [
        pltpu.make_async_copy(src.at[me_b], turn.at[i], turn_sem.at[i])
        for i, src in enumerate((cos_ref, sin_ref))
    ]
    for copy in tables_in:
        copy.start()
    xs = x_ref[...].astype(F32)
    xa = (xs * rms_scale(xs) * gain_ref[...]).astype(BF16)
    xa_ref[...] = xa
    for copy in tables_in:
        copy.wait()
    cosine, sine = turn[0], turn[1]
    low = lax.broadcasted_iota(jnp.int32, (tok, 2 * HD), 1) < HD
    pay[:, tok:, : 2 * HD] = jnp.zeros((KV, 16, 2 * HD), BF16)
    for m in range(KV // 2):
        pair = slice(m * 2 * HD, (m + 1) * 2 * HD)
        keys = mm(xa, wk_ref[:, pair])
        keys = keys * cosine + rotate_pairs(keys) * sine
        values = mm(xa, wv_ref[:, pair])
        first = jnp.where(low, keys, pltpu.roll(values, HD, 1))
        second = jnp.where(low, pltpu.roll(keys, HD, 1), values)
        pay[2 * m, :tok, 2 * HD :] = first.astype(BF16)
        pay[2 * m + 1, :tok, 2 * HD :] = second.astype(BF16)
        for k in (2 * m, 2 * m + 1):
            query = mm(xa, wq_ref[:, k * 2 * HD : (k + 1) * 2 * HD])
            query = (query * cosine + rotate_pairs(query) * sine) * HD ** (-0.5)
            pay[k, :tok, : 2 * HD] = query.astype(BF16)
            pay[k, tok:, 2 * HD :] = seg_ref[...]
    def payload(n):
        k = lax.rem(me_b + n, KV)
        chip = me_s * KV + k
        mine = (dest_core == me_s) & (chip == me_b)
        return k, chip, mine

    def send_payload(n, carry):
        k, chip, mine = payload(n)

        @pl.when(mine)
        def _():
            pltpu.make_async_copy(pay.at[k], in_ref.at[slot], recv_sem.at[slot]).start()

        @pl.when(jnp.logical_not(mine))
        def _():
            remote(
                pay.at[k], in_ref.at[slot], send_sem.at[k], recv_sem.at[slot], dest_core, chip
            ).start()

        return carry

    lax.fori_loop(0, KV, send_payload, 0)
    for i in (1, 2):
        share_weight(1, (0, 2, 1)[i]).start()
        share_weight(2, (1, 2, 0)[i]).start()

    kept = (
        (kv_ref, kv_any),
        (kvt_ref, kvt_any),
        (q_ref, q_any),
        (ot_ref, ot_any),
        (stat_ref, stat_any),
    )

    def keep(i, t):
        src, dst = kept[i]
        return pltpu.make_async_copy(src.at[t], dst.at[t], kept_sem.at[i, t])

    def arrival(t):
        return pltpu.make_async_copy(pay.at[0], in_ref.at[t], recv_sem.at[t])

    def forward(t):
        return remote(
            in_ref.at[t, :, pl.ds(2 * HD, 2 * HD)],
            other_ref.at[t],
            fsend_sem.at[t],
            frecv_sem.at[t],
            1 - me_s,
            me_b,
        )

    arrival(0).wait()
    forward(0).start()
    cnt[...] = jnp.zeros_like(cnt)
    first_core = me_s == 0
    lane = lax.broadcasted_iota(jnp.int32, (1, 2 * tok), 1)
    qrow = jnp.where(lane < tok, lane, lane - tok)
    wide = 2 * tok

    def step(t, carry):
        @pl.when(t < steps - 1)
        def _():
            arrival(t + 1).wait()
            forward(t + 1).start()

        for j in (1, 2):

            @pl.when(t == GRAD_STEPS[j - 1])
            def _():
                pass_distance(j)

        @pl.when(t == HOP_STEP)
        def _():
            for n, i in ((1, 0), (2, 1)):
                share_weight(n, i).wait_recv()
                diagonal(n, i).start()
                pass_weight(n, i).start()

        @pl.when(t == HOP_STEP + 1)
        def _():
            for n, i in ((1, 2), (2, 2)):
                share_weight(n, i).wait_recv()
                diagonal(n, i).start()
                pass_weight(n, i).start()

        @pl.when(t == HOP_STEP + 2)
        def _():
            for n, i in ((1, 1), (2, 0)):
                share_weight(n, i).wait_recv()
                pass_weight(n, i).start()

        forward(t).wait_recv()
        mine = in_ref[t]
        kv_mine, seg_mine = mine[:tok, 2 * HD :], mine[tok:, 2 * HD :].astype(F32)
        other = other_ref[t]
        kv_other, seg_other = other[:tok], other[tok:].astype(F32)
        pair = jnp.where(
            first_core,
            jnp.concatenate([kv_mine, kv_other], 0).astype(F32),
            jnp.concatenate([kv_other, kv_mine], 0).astype(F32),
        )
        kv_ref[t] = pair.astype(BF16)
        kvt_ref[t] = jnp.transpose(pair).astype(BF16)
        number = lax.broadcasted_iota(jnp.int32, (8, tok), 0).astype(F32)
        seg_q = jnp.concatenate([seg_mine[0:1], seg_mine[1:2]], 1)
        seg_o = jnp.concatenate([seg_other[0:1], seg_other[1:2]], 1)
        below = (seg_q < number).astype(F32) + (seg_o < number).astype(F32)
        cnt[...] += jnp.sum(below, 1, keepdims=True)
        start_q = jnp.sum(jnp.where(seg_q == number, cnt[:, :1], 0.0), 0, keepdims=True)
        start = jnp.concatenate([start_q, start_q], 1).astype(jnp.int32)
        q_two = mine[:tok, : 2 * HD]
        q_ref[t] = q_two
        qt = stacked_heads(jnp.transpose(q_two.astype(F32)))
        qm = jnp.concatenate([qt, jnp.zeros_like(qt)], 0).astype(BF16)
        qpos = (2 * t + me_s) * tok + qrow

        def piece(u, state, last):
            running, total, acc = state
            score = mm(kv_ref[u], qm)
            kpos = u * wide + lax.broadcasted_iota(jnp.int32, score.shape, 0)
            mask = kpos >= start
            if last:
                mask &= kpos <= qpos
            score = jnp.where(mask, score, NEG)
            newmax = jnp.maximum(running, jnp.max(score, 0, keepdims=True))
            expo = jnp.exp(score - newmax)
            factor = jnp.exp(running - newmax)
            total = total * factor + jnp.sum(expo, 0, keepdims=True)
            acc = acc * factor + mm(kvt_ref[u, HD:, :], expo.astype(BF16))
            return newmax, total, acc

        state = (
            jnp.full((1, wide), NEG, F32),
            jnp.zeros((1, wide), F32),
            jnp.zeros((HD, wide), F32),
        )
        state = lax.fori_loop(0, t, lambda u, s: piece(u, s, False), state)
        running, total, acc = piece(t, state, True)
        out_t = acc / total
        ot_ref[t] = out_t
        rows = lax.broadcasted_iota(jnp.int32, (8, wide), 0)
        lse = running + jnp.log(total)
        stat_ref[t] = jnp.where(rows == 0, lse, start.astype(F32))
        upright = jnp.concatenate([out_t[:, :tok], out_t[:, tok:]], 0)
        obuf[t] = jnp.transpose(upright).astype(BF16)
        for i in range(5):
            keep(i, t).start()
        owner = 2 * t + me_s
        home = (sigma == me_s) & (owner == me_b)
        place = o_ref.at[:, pl.ds(pl.multiple_of(kappa * 2 * HD, 2 * HD), 2 * HD)]

        @pl.when(home)
        def _():
            pltpu.make_async_copy(obuf.at[t], place, orecv_sem.at[kappa]).start()

        @pl.when(jnp.logical_not(home))
        def _():
            remote(obuf.at[t], place, osend_sem.at[t], orecv_sem.at[kappa], sigma, owner).start()

        return carry

    lax.fori_loop(0, steps, step, 0)
    diagonal_in(2, 0).wait()
    pass_weight(3, 0).start()
    diagonal_in(1, 1).wait()
    pass_weight(3, 1).start()
    diagonal_in(1, 2).wait()
    diagonal_in(2, 2).wait()
    pass_weight(3, 2).start()

    def finish(t, carry):
        k, chip, mine = payload(t)

        @pl.when(jnp.logical_not(mine))
        def _():
            remote(
                pay.at[k], in_ref.at[slot], send_sem.at[k], recv_sem.at[slot], dest_core, chip
            ).wait_send()

        return carry

    lax.fori_loop(0, KV, finish, 0)

    def finish_steps(t, carry):
        forward(t).wait_send()
        for i in range(5):
            keep(i, t).wait()
        owner = 2 * t + me_s
        home = (sigma == me_s) & (owner == me_b)

        @pl.when(jnp.logical_not(home))
        def _():
            remote(
                obuf.at[t],
                o_ref.at[:, pl.ds(0, 2 * HD)],
                osend_sem.at[t],
                orecv_sem.at[0],
                sigma,
                owner,
            ).wait_send()

        return carry

    lax.fori_loop(0, steps, finish_steps, 0)

    def gather(k, carry):
        pltpu.make_async_copy(
            obuf.at[0],
            o_ref.at[:, pl.ds(pl.multiple_of(k * 2 * HD, 2 * HD), 2 * HD)],
            orecv_sem.at[k],
        ).wait()
        return carry

    lax.fori_loop(0, KV, gather, 0)
    pass_distance(3)
    for k in range(4):

        @pl.when((k <= line) & (line < 3))
        def _():
            along(k, 1, False).wait_send()

        @pl.when((k >= line) & (line > 0))
        def _():
            along(k, -1, False).wait_send()

    for n in (1, 2, 3):
        for i in range(3):
            pass_weight(n, i).wait()
    for n in (1, 2):
        for i in range(3):
            share_weight(n, i).wait_send()
        diagonal(n, n - 1).wait_send()
        diagonal(n, 2).wait_send()


def attention_forward(
    blocks, x, gain, w_query, w_key, w_value, seg, cos_all, sin_all, g, w_gate, w_up, w_down
):
    tok, d = x.shape
    steps = blocks // 2
    vm = pl.BlockSpec(memory_space=pltpu.VMEM)
    hbm = pl.BlockSpec(memory_space=pl.ANY)
    dma = pltpu.SemaphoreType.DMA
    return pl.pallas_call(
        functools.partial(attention_forward_kernel, blocks),
        out_shape=(
            jax.ShapeDtypeStruct((tok, H * HD), BF16),
            jax.ShapeDtypeStruct((tok, d), BF16),
            jax.ShapeDtypeStruct((steps, 2 * tok, 2 * HD), BF16),
            jax.ShapeDtypeStruct((steps, 2 * HD, 2 * tok), BF16),
            jax.ShapeDtypeStruct((steps, tok, 2 * HD), BF16),
            jax.ShapeDtypeStruct((steps, HD, 2 * tok), F32),
            jax.ShapeDtypeStruct((steps, 8, 2 * tok), F32),
            jax.ShapeDtypeStruct((4, *g.shape), BF16),
            jax.ShapeDtypeStruct((4, *w_gate.shape), BF16),
            jax.ShapeDtypeStruct((4, *w_up.shape), BF16),
            jax.ShapeDtypeStruct((4, *w_down.shape), BF16),
        ),
        in_specs=[vm] * 6 + [hbm] * 6,
        out_specs=(vm,) * 2 + (hbm,) * 9,
        scratch_shapes=[
            pltpu.VMEM((steps, 2 * tok, 2 * HD), BF16),
            pltpu.VMEM((steps, 2 * HD, 2 * tok), BF16),
            pltpu.VMEM((steps, tok, 2 * HD), BF16),
            pltpu.VMEM((steps, HD, 2 * tok), F32),
            pltpu.VMEM((steps, 8, 2 * tok), F32),
            dma((5, steps)),
            pltpu.VMEM((KV, tok + 16, 4 * HD), BF16),
            pltpu.VMEM((2, tok, 2 * HD), F32),
            pltpu.VMEM((steps, tok + 16, 4 * HD), BF16),
            pltpu.VMEM((steps, tok + 16, 2 * HD), BF16),
            pltpu.VMEM((steps, tok, 2 * HD), BF16),
            pltpu.VMEM((8, 128), F32),
            dma((2,)),
            dma((KV,)),
            dma((steps,)),
            dma((steps,)),
            dma((steps,)),
            dma((steps,)),
            dma((KV,)),
            dma((2, 4)),
            dma((4,)),
            dma((2, 3)),
            dma((2, 3)),
            dma((3, 3)),
            dma((3, 3)),
            dma((2, 3)),
            dma((2, 3)),
        ],
        compiler_params=pltpu.CompilerParams(
            collective_id=0, has_side_effects=True, vmem_limit_bytes=VMEM_LIMIT
        ),
        name="attention_forward",
    )(x, gain, w_query, w_key, w_value, seg, cos_all, sin_all, g, w_gate, w_up, w_down)


def attention_backward_kernel(
    blocks,
    do_ref,
    kv_any,
    kvt_any,
    q_any,
    ot_any,
    stat_any,
    cos_ref,
    sin_ref,
    mix_ref,
    dwg_ref,
    dwu_ref,
    dwd_ref,
    out_ref,
    mix_in,
    dwg_in,
    dwu_in,
    dwd_in,
    kv_ref,
    kvt_ref,
    q_ref,
    ot_ref,
    stat_ref,
    kept_sem,
    turn,
    turn_sem,
    in_ref,
    dkv,
    part,
    xch,
    done,
    send_sem,
    recv_sem,
    xsend_sem,
    xrecv_sem,
    osend_sem,
    orecv_sem,
    msend_sem,
    mrecv_sem,
    wsend_sem,
    wrecv_sem,
):
    me_s = lax.axis_index("seq")
    me_b = lax.axis_index("blk")
    tok = q_ref.shape[1]
    steps = blocks // 2
    sigma = me_b // KV
    kappa = lax.rem(me_b, KV)
    tables_in = [
        pltpu.make_async_copy(src.at[2 * t + me_s], turn.at[i, t], turn_sem.at[i, t])
        for i, src in enumerate((cos_ref, sin_ref))
        for t in range(steps)
    ]
    kept = ((q_any, q_ref), (kv_any, kv_ref), (kvt_any, kvt_ref), (ot_any, ot_ref), (stat_any, stat_ref))
    tables_in += [
        pltpu.make_async_copy(src, dst, kept_sem.at[i]) for i, (src, dst) in enumerate(kept)
    ]
    for copy in tables_in:
        copy.start()
    greet_all(2, blocks, me_s, me_b)

    dest_core = lax.rem(me_b, 2)
    slot = me_b // 2
    line, plane = me_b // 4, lax.rem(me_b, 4)
    weights = ((dwg_ref, dwg_in), (dwu_ref, dwu_in), (dwd_ref, dwd_in))

    def give_mix(n):
        return remote(
            mix_ref.at[flip(line, n)],
            mix_in.at[n - 1],
            msend_sem.at[n - 1],
            mrecv_sem.at[n - 1],
            me_s,
            flip(line, n) * 4 + plane,
        )

    def give_weight(n, i):
        src, dst = weights[i]
        return remote(
            src.at[flip(plane, n)],
            dst.at[n - 1],
            wsend_sem.at[n - 1, i],
            wrecv_sem.at[n - 1, i],
            me_s,
            line * 4 + flip(plane, n),
        )

    def outgoing(n):
        k = lax.rem(me_b + n, KV)
        chip = me_s * KV + k
        mine = (dest_core == me_s) & (chip == me_b)
        src = do_ref.at[:, pl.ds(pl.multiple_of(k * 2 * HD, 2 * HD), 2 * HD)]
        return k, chip, mine, src

    def send_grad(n, carry):
        k, chip, mine, src = outgoing(n)

        @pl.when(mine)
        def _():
            pltpu.make_async_copy(src, in_ref.at[slot], recv_sem.at[slot]).start()

        @pl.when(jnp.logical_not(mine))
        def _():
            remote(src, in_ref.at[slot], send_sem.at[k], recv_sem.at[slot], dest_core, chip).start()

        return carry

    lax.fori_loop(0, KV, send_grad, 0)
    for copy in tables_in:
        copy.wait()
    for n in (2, 1):
        give_mix(n).start()
    for i in range(3):
        for n in (1, 2):
            give_weight(n, i).start()
    give_weight(3, 2).start()
    dkv[...] = jnp.zeros_like(dkv)
    wide = 2 * tok
    lane = lax.broadcasted_iota(jnp.int32, (1, wide), 1)
    qrow = jnp.where(lane < tok, lane, lane - tok)
    low = lax.broadcasted_iota(jnp.int32, (tok, 2 * HD), 1) < HD

    def swap(t):
        return remote(part.at[t], xch.at[t], xsend_sem.at[t], xrecv_sem.at[t], 1 - me_s, me_b)

    def deliver(t, act):
        owner = 2 * t + me_s
        home = (sigma == me_s) & (owner == me_b)
        src, dst = done.at[t], out_ref.at[kappa]

        @pl.when(home)
        def _():
            if act == "start":
                pltpu.make_async_copy(src, dst, orecv_sem.at[kappa]).start()

        @pl.when(jnp.logical_not(home))
        def _():
            copy = remote(src, dst, osend_sem.at[t], orecv_sem.at[kappa], sigma, owner)
            copy.start() if act == "start" else copy.wait_send()

    def finalize(t):
        swap(t).wait_recv()
        place = pl.ds(pl.multiple_of(me_s * tok, tok), tok)
        total = dkv[t, place, :] + xch[t]
        cosine = jnp.where(low, turn[0, t], 1.0)
        sine = jnp.where(low, turn[1, t], 0.0)
        back = total * cosine - rotate_pairs(total) * sine
        done[t, :, pl.ds(2 * HD, 2 * HD)] = back.astype(BF16)
        deliver(t, "start")

    def step(n, carry):
        t = steps - 1 - n
        pltpu.make_async_copy(do_ref.at[:, pl.ds(0, 2 * HD)], in_ref.at[t], recv_sem.at[t]).wait()
        d_two = in_ref[t].astype(F32)
        q_two = q_ref[t].astype(F32)
        dt = stacked_heads(jnp.transpose(d_two))
        qt = stacked_heads(jnp.transpose(q_two))
        zero = jnp.zeros_like(dt)
        dm = jnp.concatenate([zero, dt], 0).astype(BF16)
        qm = jnp.concatenate([qt, zero], 0).astype(BF16)
        delta = jnp.sum(ot_ref[t] * dt, 0, keepdims=True)
        right = jnp.concatenate(
            [
                jnp.where(low, q_two, 0.0),
                jnp.where(low, pltpu.roll(q_two, HD, 1), 0.0),
                jnp.where(low, 0.0, pltpu.roll(d_two, HD, 1)),
                jnp.where(low, 0.0, d_two),
            ],
            0,
        ).astype(BF16)
        stat = stat_ref[t]
        lse, start = stat[0:1], stat[1:2].astype(jnp.int32)
        qpos = (2 * t + me_s) * tok + qrow

        def piece(u, dq, last):
            keys = kv_ref[u]
            score = mm(keys, qm)
            kpos = u * wide + lax.broadcasted_iota(jnp.int32, score.shape, 0)
            mask = kpos >= start
            if last:
                mask &= kpos <= qpos
            prob = jnp.where(mask, jnp.exp(score - lse), 0.0)
            dprob = mm(keys, dm)
            dscore = (prob * (dprob - delta)).astype(BF16)
            both = jnp.concatenate([dscore, prob.astype(BF16)], 1)
            dkv[u] += mm(both, right)
            return dq + mm(kvt_ref[u, :HD, :], dscore)

        dq = jnp.zeros((HD, wide), F32)
        dq = lax.fori_loop(0, t, lambda u, s: piece(u, s, False), dq)
        dq = piece(t, dq, True) * HD ** (-0.5)
        upright = jnp.transpose(jnp.concatenate([dq[:, :tok], dq[:, tok:]], 0))
        back = upright * turn[0, t] - rotate_pairs(upright) * turn[1, t]
        done[t, :, pl.ds(0, 2 * HD)] = back.astype(BF16)
        part[t] = dkv[t, pl.ds(pl.multiple_of((1 - me_s) * tok, tok), tok), :]
        swap(t).start()

        @pl.when(n > 0)
        def _():
            finalize(t + 1)

        return carry

    lax.fori_loop(0, steps, step, 0)
    finalize(0)

    def finish(n, carry):
        k, chip, mine, src = outgoing(n)

        @pl.when(jnp.logical_not(mine))
        def _():
            remote(
                src, in_ref.at[slot], send_sem.at[k], recv_sem.at[slot], dest_core, chip
            ).wait_send()

        return carry

    lax.fori_loop(0, KV, finish, 0)

    def finish_steps(t, carry):
        swap(t).wait_send()
        deliver(t, "wait")
        return carry

    lax.fori_loop(0, steps, finish_steps, 0)

    def gather(k, carry):
        pltpu.make_async_copy(done.at[0], out_ref.at[k], orecv_sem.at[k]).wait()
        return carry

    lax.fori_loop(0, KV, gather, 0)
    for n in (1, 2):
        give_mix(n).wait()
        for i in range(3):
            give_weight(n, i).wait()
    give_weight(3, 2).wait()


def attention_backward(
    blocks, vectors, mix, dwg, dwu, dwd
):
    tok = vectors[0].shape[0]
    steps = blocks // 2
    vm = pl.BlockSpec(memory_space=pltpu.VMEM)
    hbm = pl.BlockSpec(memory_space=pl.ANY)
    dma = pltpu.SemaphoreType.DMA
    return pl.pallas_call(
        functools.partial(attention_backward_kernel, blocks),
        out_shape=(
            jax.ShapeDtypeStruct((KV, tok, 4 * HD), BF16),
            jax.ShapeDtypeStruct((2, *mix.shape[1:]), BF16),
            jax.ShapeDtypeStruct((2, *dwg.shape[1:]), BF16),
            jax.ShapeDtypeStruct((2, *dwu.shape[1:]), BF16),
            jax.ShapeDtypeStruct((3, *dwd.shape[1:]), BF16),
        ),
        in_specs=[vm] + [hbm] * (len(vectors) + 3),
        out_specs=(vm,) + (hbm,) * 4,
        scratch_shapes=[
            *(pltpu.VMEM(a.shape, a.dtype) for a in vectors[1:6]),
            dma((5,)),
            pltpu.VMEM((2, steps, tok, 2 * HD), F32),
            dma((2, steps)),
            pltpu.VMEM((steps, tok, 2 * HD), BF16),
            pltpu.VMEM((steps, 2 * tok, 2 * HD), F32),
            pltpu.VMEM((steps, tok, 2 * HD), F32),
            pltpu.VMEM((steps, tok, 2 * HD), F32),
            pltpu.VMEM((steps, tok, 4 * HD), BF16),
            dma((KV,)),
            dma((steps,)),
            dma((steps,)),
            dma((steps,)),
            dma((steps,)),
            dma((KV,)),
            dma((2,)),
            dma((2,)),
            dma((3, 3)),
            dma((3, 3)),
        ],
        compiler_params=pltpu.CompilerParams(
            collective_id=1, has_side_effects=True, vmem_limit_bytes=VMEM_LIMIT
        ),
        name="attention_backward",
    )(*vectors, mix, dwg, dwu, dwd)


def mixture_kernel(
    x_ref,
    ao_ref,
    gain_ref,
    router_ref,
    routes_ref,
    weight_ref,
    wo_ref,
    g_ref,
    wg_ref,
    wu_ref,
    wd_ref,
    g_all,
    wg_all,
    wu_all,
    wd_all,
    res_any,
    mix_any,
    xl_any,
    dlog_ref,
    dh_ref,
    datt_ref,
    do_ref,
    dgain_ref,
    dwg_out,
    dwu_out,
    dwd_out,
    dwg_in,
    dwu_in,
    res_ref,
    mix_peer,
    xl_ref,
    out_sem,
    wr_ref,
    rw_ref,
    h1_ref,
    gate_ref,
    d_in,
    d_c,
    wo,
    x_in,
    c_in,
    share_ref,
    x_t,
    g_in,
    wg,
    wu,
    wd,
    hc,
    dg,
    du,
    acc_o,
    acc_d,
    acc_c,
    d_send,
    d_recv,
    c_send,
    c_recv,
    xg,
    xu,
    xd,
    load_sem,
    gload_sem,
    send_sem,
    recv_sem,
    bsend_sem,
    brecv_sem,
    psend_sem,
    precv_sem,
    store_sem,
    wsend_sem,
    wrecv_sem,
    wo_sem,
    csend_sem,
    crecv_sem,
    ksend_sem,
    krecv_sem,
):
    me_s = lax.axis_index("seq")
    me_b = lax.axis_index("blk")
    line, plane = me_b // 4, lax.rem(me_b, 4)
    tok, d = g_in.shape[1:]
    ff = wg.shape[2]
    experts = router_ref.shape[0]
    barrier = pltpu.get_barrier_semaphore()
    sibling = (1 - me_s, me_b)
    opposite = (me_s, line * 4 + flip(plane, 3))
    for place in [(me_s, flip(line, n) * 4 + plane) for n in (1, 2, 3)] + [sibling, opposite]:
        pl.semaphore_signal(barrier, inc=1, device_id=place, device_id_type=MESH)

    owns = ((wg_ref, wg_all, wg), (wu_ref, wu_all, wu), (wd_ref, wd_all, wd))

    def load_own(i):
        return pltpu.make_async_copy(owns[i][0], owns[i][2].at[plane], load_sem.at[i, plane])

    def load_other(i, e):
        return pltpu.make_async_copy(owns[i][1].at[e], owns[i][2].at[e], load_sem.at[i, e])

    load_out = pltpu.make_async_copy(wo_ref, wo, wo_sem)
    load_out.start()
    for i in (2, 0, 1):
        load_own(i).start()
        for n in (1, 2, 3):
            load_other(i, flip(plane, n)).start()

    def load_grad(k):
        return pltpu.make_async_copy(g_all.at[k], g_in.at[k], gload_sem.at[k])

    pltpu.make_async_copy(g_ref, g_in.at[line], gload_sem.at[line]).start()
    for n in (1, 2, 3):
        load_grad(flip(line, n)).start()
    lane = lax.broadcasted_iota(jnp.int32, (tok, 128), 1)
    number = lax.broadcasted_iota(jnp.int32, (128, tok), 0)
    spread = jnp.zeros((128, tok), F32)
    for j in range(TOP):
        spread += jnp.where(routes_ref[j : j + 1, :] == number, weight_ref[j : j + 1, :], 0.0)
    rw = jnp.transpose(spread)
    rw_ref[...] = rw
    row, column = (lax.broadcasted_iota(jnp.int32, (experts, 128), i) for i in range(2))
    wr_ref[...] = mm(router_ref[...], (row == column).astype(BF16), TN).astype(BF16)
    load_out.wait()
    xs = x_ref[...].astype(F32)
    h1 = xs + mm(ao_ref[...], wo[...])
    h1_ref[...] = h1
    xl = (h1 * rms_scale(h1) * gain_ref[...]).astype(BF16)
    xl_ref[...] = xl
    store_xl = pltpu.make_async_copy(xl_ref, xl_any, out_sem.at[3])
    store_xl.start()
    store_res = pltpu.make_async_copy(res_ref, res_any, out_sem.at[4])
    logits = mm(xl, wr_ref[...])
    routed = rw > 0.0
    top = jnp.max(jnp.where(routed, logits, NEG), -1, keepdims=True)
    expo = jnp.where(routed, jnp.exp(logits - top), 0.0)
    gates = expo / jnp.sum(expo, -1, keepdims=True)
    gate_ref[...] = gates
    x_in[line] = xl
    c_in[line] = jnp.transpose(rw * gates)[:experts].astype(BF16)
    pl.semaphore_wait(barrier, 5)

    def along(k, step):
        at = 0 if step < 0 else 1
        return remote(
            x_in.at[k],
            x_in.at[k],
            send_sem.at[at, k],
            recv_sem.at[k],
            me_s,
            (line + step) * 4 + plane,
        )

    def along_too(k, step):
        at = 0 if step < 0 else 1
        return remote(
            c_in.at[k],
            c_in.at[k],
            csend_sem.at[at, k],
            crecv_sem.at[k],
            me_s,
            (line + step) * 4 + plane,
        )

    def pass_on(k, step):
        @pl.when((line + step >= 0) & (line + step < 4))
        def _():
            along_too(k, step).start()
            along(k, step).start()

    for step in (-1, 1):
        pass_on(line, step)
    for k in range(4):
        load_grad(k).wait()
    g_rows = g_in.reshape(4 * tok, d)

    def grad_hidden(e, carry):
        load_other(2, e).wait()
        for part in range(2):
            rows = slice(part * 2 * tok, (part + 1) * 2 * tok)
            dg[e, rows, :] = mm(g_rows[rows, :], wd[e], NT).astype(BF16)
        return carry

    lax.fori_loop(0, 4, grad_hidden, 0)

    def load_wait(e, carry):
        for i in range(2):
            load_other(i, e).wait()
        return carry

    def apart(k):
        return lax.rem(k - line + 3, 4)

    def store_mix(n):
        return pltpu.make_async_copy(mix_peer.at[apart(n)], mix_any.at[n], out_sem.at[apart(n)])

    def place_of(j):
        return jnp.where(line < 2, lax.rem(line + j, 4), lax.rem(line + 4 - j, 4))

    def block(j, carry):
        n = place_of(j)
        filler = jnp.zeros((128 - experts, tok), F32)
        share_ref[...] = jnp.transpose(jnp.concatenate([c_in[n].astype(F32), filler], 0))
        acc_o[...] = jnp.zeros_like(acc_o)
        acc_d[...] = jnp.zeros_like(acc_d)
        acc_c[...] = jnp.zeros_like(acc_c)
        rows = pl.ds(pl.multiple_of(n * tok, tok), tok)

        def expert(e, carry):
            @pl.when(j == 0)
            def _():
                load_wait(e, 0)

            for step in (-1, 1):
                k = line - step * (j + 1)

                @pl.when((e == 3) & (j < 3) & (k >= 0) & (k < 4))
                def _():
                    pltpu.make_async_copy(c_in.at[line], c_in.at[k], crecv_sem.at[k]).wait()
                    pltpu.make_async_copy(x_in.at[line], x_in.at[k], recv_sem.at[k]).wait()
                    pass_on(k, step)

            x = x_in[n]
            here = lane == line * 4 + e
            share = jnp.sum(jnp.where(here, share_ref[...], 0.0), 1, keepdims=True)
            gate = mm(x, wg[e])
            up = mm(x, wu[e])
            dh = dg[e, rows, :].astype(F32)
            sg = jax.nn.sigmoid(gate)
            act = gate * sg
            hidden = act * up
            acc_c[...] += jnp.where(here, jnp.sum(dh * hidden, 1, keepdims=True), 0.0)
            dh = dh * share
            hcb = (hidden * share).astype(BF16)
            dgb = (dh * up * sg * (1.0 + gate * (1.0 - sg))).astype(BF16)
            dub = (dh * act).astype(BF16)
            hc[e, rows, :] = hcb
            dg[e, rows, :] = dgb
            du[e, rows, :] = dub
            acc_o[...] += mm(hcb, wd[e])
            acc_d[...] += mm(dgb, wg[e], NT) + mm(dub, wu[e], NT)
            return carry

        lax.fori_loop(0, 4, expert, 0)

        @pl.when(j == 0)
        def _():
            res_ref[...] = h1_ref[...] + acc_o[...]
            store_res.start()
            d_in[...] = acc_d[...]
            d_c[...] = acc_c[...]

        @pl.when(j > 0)
        def _():
            to = apart(n)
            mix_peer[to] = acc_o[...].astype(BF16)
            store_mix(n).start()
            d_send[to] = acc_d[...].astype(BF16)
            turned = jnp.transpose(acc_c[...])[:experts]
            high = turned.astype(BF16)
            c_send[to, :experts, :] = high
            c_send[to, experts:, :] = (turned - high.astype(F32)).astype(BF16)
            give_back_too(n).start()
            give_back(n).start()

        x_t[:, rows] = jnp.transpose(x_in[n].astype(F32)).astype(BF16)
        return carry

    def give_back_too(n):
        return remote(
            c_send.at[apart(n)],
            c_recv.at[lax.rem(line - n + 3, 4)],
            ksend_sem.at[n],
            krecv_sem.at[line],
            me_s,
            n * 4 + plane,
        )

    def give_back(n):
        return remote(
            d_send.at[apart(n)], d_recv.at[lax.rem(line - n + 3, 4)], bsend_sem.at[n], brecv_sem.at[line], me_s, n * 4 + plane
        )

    lax.fori_loop(0, 4, block, 0)

    half, dhalf = d // 2, ff // 2
    theirs = pl.multiple_of((1 - me_s) * half, half)
    dtheirs = pl.multiple_of((1 - me_s) * dhalf, dhalf)
    mine = pl.multiple_of(me_s * half, half)
    dmine = pl.multiple_of(me_s * dhalf, dhalf)

    def swap(i, e):
        src = (wg.at[e, pl.ds(0, half)], wu.at[e, pl.ds(0, half)], wd.at[e, pl.ds(0, dhalf)])[i]
        dst = (xg, xu, xd)[i].at[e]
        return remote(src, dst, psend_sem.at[i, e], precv_sem.at[i, e], *sibling)

    def store(i, e):
        return pltpu.make_async_copy(
            (xg, xu, xd)[i].at[e], (dwg_out, dwu_out, dwd_out)[i].at[e], store_sem.at[i, e]
        )

    def turn_of(n):
        return jnp.where(
            n == 0, flip(plane, 3), jnp.where(n == 1, flip(plane, 2), jnp.where(n == 2, flip(plane, 1), plane))
        )

    def opposed(i):
        return remote(
            (xg, xu, xd)[i].at[flip(plane, 3)],
            (dwg_in, dwu_in)[i],
            wsend_sem.at[i],
            wrecv_sem.at[i],
            *opposite,
        )

    def finished(i, n, e):
        if i == 2:
            store(i, e).start()
            return

        @pl.when(n == 0)
        def _():
            opposed(i).start()

        @pl.when(n > 0)
        def _():
            store(i, e).start()

    def give(n, carry):
        e = turn_of(n)
        left = x_t[pl.ds(theirs, half), :]
        wg[e, :half, :] = mm(left, dg[e]).astype(BF16)
        swap(0, e).start()
        wu[e, :half, :] = mm(left, du[e]).astype(BF16)
        swap(1, e).start()
        wd[e, :dhalf, :] = mm(hc[e, :, pl.ds(dtheirs, dhalf)], g_rows[...], TN).astype(BF16)
        swap(2, e).start()
        return carry

    def keep(n, carry):
        e = turn_of(n)

        left = x_t[pl.ds(mine, half), :]
        own = mm(left, dg[e])
        swap(0, e).wait_recv()
        xg[e] = (own + xg[e].astype(F32)).astype(BF16)
        finished(0, n, e)
        own = mm(left, du[e])
        swap(1, e).wait_recv()
        xu[e] = (own + xu[e].astype(F32)).astype(BF16)
        finished(1, n, e)
        own = mm(hc[e, :, pl.ds(dmine, dhalf)], g_rows[...], TN)
        swap(2, e).wait_recv()
        xd[e] = (own + xd[e].astype(F32)).astype(BF16)
        finished(2, n, e)
        return carry

    give(0, 0)

    def both(n, carry):
        give(n, 0)
        keep(n - 1, 0)
        return carry

    lax.fori_loop(1, 4, both, 0)
    keep(3, 0)

    from_line = jnp.zeros((experts, tok), F32)
    for n in (1, 2, 3):
        k = flip(line, n)
        at = apart(k)
        pltpu.make_async_copy(c_send.at[at], c_recv.at[at], krecv_sem.at[k]).wait()
        from_line += c_recv[at, :experts, :].astype(F32) + c_recv[at, experts:, :].astype(F32)
        pltpu.make_async_copy(d_send.at[at], d_recv.at[at], brecv_sem.at[k]).wait()
        d_in[...] += d_recv[at].astype(F32)
    filler = jnp.zeros((128 - experts, tok), F32)
    d_c[...] += jnp.transpose(jnp.concatenate([from_line, filler], 0))

    gates = gate_ref[...]
    d_gates = rw_ref[...] * d_c[...]
    dlog = (gates * (d_gates - jnp.sum(gates * d_gates, -1, keepdims=True))).astype(BF16)
    dlog_ref[...] = dlog
    d_xl = d_in[...] + mm(dlog, wr_ref[...], NT)
    h1 = h1_ref[...]
    scale = rms_scale(h1)
    scaled = d_xl * gain_ref[...]
    inner = jnp.mean(scaled * h1, -1, keepdims=True)
    d_h1 = g_in[line].astype(F32) + scale * scaled - h1 * scale**3 * inner
    dgain_ref[...] = jnp.sum((d_xl * h1 * scale).reshape(tok // 8, 8, d), 0)
    dh_ref[...] = d_h1
    d_att = d_h1.astype(BF16)
    datt_ref[...] = d_att
    do_ref[...] = mm(d_att, wo[...], NT).astype(BF16)
    for n in (1, 2, 3):
        give_back(flip(line, n)).wait_send()
        give_back_too(flip(line, n)).wait_send()
        store_mix(flip(line, n)).wait()
    store_xl.wait()
    store_res.wait()
    for k in range(4):

        @pl.when((k <= line) & (line < 3))
        def _():
            along(k, 1).wait_send()
            along_too(k, 1).wait_send()

        @pl.when((k >= line) & (line > 0))
        def _():
            along(k, -1).wait_send()
            along_too(k, -1).wait_send()

    def finish(n, carry):
        e = turn_of(n)
        for i in range(3):
            swap(i, e).wait_send()

            @pl.when((n > 0) | (i == 2))
            def _():
                store(i, e).wait()

        return carry

    lax.fori_loop(0, 4, finish, 0)
    for i in range(2):
        opposed(i).wait()


def mixture(vectors, w_out, g, w_gate, w_up, w_down, shared):
    tok, d = g.shape
    ff = w_gate.shape[1]
    experts = vectors[3].shape[0]
    vm = pl.BlockSpec(memory_space=pltpu.VMEM)
    hbm = pl.BlockSpec(memory_space=pl.ANY)
    dma = pltpu.SemaphoreType.DMA
    vmem = pltpu.VMEM
    return pl.pallas_call(
        mixture_kernel,
        out_shape=(
            jax.ShapeDtypeStruct((tok, d), F32),
            jax.ShapeDtypeStruct((4, tok, d), BF16),
            jax.ShapeDtypeStruct((tok, d), BF16),
            jax.ShapeDtypeStruct((tok, 128), BF16),
            jax.ShapeDtypeStruct((tok, d), F32),
            jax.ShapeDtypeStruct((tok, d), BF16),
            jax.ShapeDtypeStruct((tok, d), BF16),
            jax.ShapeDtypeStruct((8, d), F32),
            jax.ShapeDtypeStruct((4, d // 2, ff), BF16),
            jax.ShapeDtypeStruct((4, d // 2, ff), BF16),
            jax.ShapeDtypeStruct((4, ff // 2, d), BF16),
            jax.ShapeDtypeStruct((d // 2, ff), BF16),
            jax.ShapeDtypeStruct((d // 2, ff), BF16),
        ),
        in_specs=[vm] * 6 + [hbm] * 9,
        out_specs=(hbm,) * 3 + (vm,) * 5 + (hbm,) * 5,
        scratch_shapes=[
            vmem((tok, d), F32),
            vmem((3, tok, d), BF16),
            vmem((tok, d), BF16),
            dma((5,)),
            vmem((d, 128), BF16),
            vmem((tok, 128), F32),
            vmem((tok, d), F32),
            vmem((tok, 128), F32),
            vmem((tok, d), F32),
            vmem((tok, 128), F32),
            vmem((d, d), BF16),
            vmem((4, tok, d), BF16),
            vmem((4, experts, tok), BF16),
            vmem((tok, 128), F32),
            vmem((d, 4 * tok), BF16),
            vmem((4, tok, d), BF16),
            vmem((4, d, ff), BF16),
            vmem((4, d, ff), BF16),
            vmem((4, ff, d), BF16),
            vmem((4, 4 * tok, ff), BF16),
            vmem((4, 4 * tok, ff), BF16),
            vmem((4, 4 * tok, ff), BF16),
            vmem((tok, d), F32),
            vmem((tok, d), F32),
            vmem((tok, 128), F32),
            vmem((3, tok, d), BF16),
            vmem((3, tok, d), BF16),
            vmem((3, 2 * experts, tok), BF16),
            vmem((3, 2 * experts, tok), BF16),
            vmem((4, d // 2, ff), BF16),
            vmem((4, d // 2, ff), BF16),
            vmem((4, ff // 2, d), BF16),
            dma((3, 4)),
            dma((4,)),
            dma((2, 4)),
            dma((4,)),
            dma((4,)),
            dma((4,)),
            dma((3, 4)),
            dma((3, 4)),
            dma((3, 4)),
            dma((2,)),
            dma((2,)),
            dma,
            dma((2, 4)),
            dma((4,)),
            dma((4,)),
            dma((4,)),
        ],
        compiler_params=pltpu.CompilerParams(
            collective_id=2, has_side_effects=True, vmem_limit_bytes=VMEM_LIMIT
        ),
        name="mixture",
    )(*vectors, w_out, g, w_gate, w_up, w_down, *shared)


def tail_kernel(
    got,
    xa_ref,
    gain_ref,
    ao_ref,
    datt_ref,
    xl_ref,
    dlog_ref,
    dgain2_ref,
    x_any,
    dh_any,
    own_any,
    wq_any,
    wk_any,
    wv_any,
    mix_ref,
    mix_near,
    eg_ref,
    eu_ref,
    ed_ref,
    eg_in,
    eu_in,
    ed_in,
    eg_far,
    eu_far,
    res_ref,
    dx_ref,
    gsum_ref,
    o_any,
    q_any,
    kv_any,
    eg_any,
    eu_any,
    ed_any,
    fin_o,
    fin_q,
    fin_kv,
    eg_out,
    eu_out,
    ed_out,
    store_sem,
    x_ref,
    dh_ref,
    own_ref,
    late_sem,
    mix_in,
    wq_ref,
    wk_ref,
    wv_ref,
    d_all,
    ev,
    edv,
    gbuf,
    grv,
    load_sem,
    esend,
    erecv,
    gsend,
    grecv,
    msend,
    mrecv,
    *summing,
):
    me_s = lax.axis_index("seq")
    me_b = lax.axis_index("blk")
    plane = lax.rem(me_b, 4)
    tok, d = xa_ref.shape
    sums = [
        Summed(summing[8 * i : 8 * i + 6], *summing[8 * i + 6 : 8 * i + 8], fin)
        for i, fin in enumerate((fin_o, fin_q, fin_kv))
    ]
    for_out, for_q, for_kv = sums
    [sibling], planes, lines = for_q.sibling, for_q.planes, for_q.lines
    barrier = pltpu.get_barrier_semaphore()
    for place in [sibling, *planes, *lines]:
        pl.semaphore_signal(barrier, inc=1, device_id=place, device_id_type=MESH)

    experts = (
        (eg_ref, eg_in, eg_far, ev.at[0]),
        (eu_ref, eu_in, eu_far, ev.at[1]),
        (ed_ref, ed_in, None, edv),
    )

    def loads(i):
        own, arrived, far, dst = experts[i]
        near = arrived.shape[0]
        copies = [
            pltpu.make_async_copy(own.at[plane], dst.at[0], load_sem.at[i, 0]),
            pltpu.make_async_copy(arrived, dst.at[pl.ds(1, near)], load_sem.at[i, 1]),
        ]
        if far is not None:
            copies.append(pltpu.make_async_copy(far, dst.at[3], load_sem.at[i, 2]))
        return copies

    projections = [
        pltpu.make_async_copy(src, dst, load_sem.at[3, i + 1])
        for i, (src, dst) in enumerate(((wq_any, wq_ref), (wk_any, wk_ref), (wv_any, wv_ref)))
    ]
    projections += [
        pltpu.make_async_copy(src, dst, late_sem.at[i])
        for i, (src, dst) in enumerate(((x_any, x_ref), (dh_any, dh_ref), (own_any, own_ref)))
    ]
    stores = [
        pltpu.make_async_copy(src, dst, store_sem.at[i])
        for i, (src, dst) in enumerate(
            (
                (fin_o, o_any),
                (fin_q, q_any),
                (fin_kv, kv_any),
                (eg_out, eg_any),
                (eu_out, eu_any),
                (ed_out, ed_any),
            )
        )
    ]
    for copy in projections:
        copy.start()
    for i in range(3):
        for copy in loads(i):
            copy.start()
    pl.semaphore_wait(barrier, 7)
    line = me_b // 4

    far_mix = remote(mix_ref.at[flip(line, 3)], mix_in.at[2], msend, mrecv, *lines[2])
    near_mix = pltpu.make_async_copy(mix_near, mix_in.at[pl.ds(0, 2)], load_sem.at[3, 0])
    far_mix.start()
    near_mix.start()
    theirs, mine = for_q.halves()
    for_out.out[:, :d] = mm(ao_ref[:, theirs], datt_ref[...], TN).astype(BF16)
    for_out.out[:, d:] = mm(xl_ref[:, theirs], dlog_ref[...], TN).astype(BF16)
    for_out.start(0)

    low = lax.broadcasted_iota(jnp.int32, (tok, 2 * HD), 1) < HD
    for m in range(KV // 2):
        a, b = got[2 * m], got[2 * m + 1]
        d_all[:, 2 * m * 2 * HD : (2 * m + 1) * 2 * HD] = a[:, : 2 * HD]
        d_all[:, (2 * m + 1) * 2 * HD : (2 * m + 2) * 2 * HD] = b[:, : 2 * HD]
        ka, kb = a[:, 2 * HD :].astype(F32), b[:, 2 * HD :].astype(F32)
        at = H * HD + m * 2 * HD
        d_all[:, at : at + 2 * HD] = jnp.where(low, ka, pltpu.roll(kb, HD, 1)).astype(BF16)
        at += KV * HD
        d_all[:, at : at + 2 * HD] = jnp.where(low, pltpu.roll(ka, HD, 1), kb).astype(BF16)
    parts = ((for_q, slice(0, H * HD)), (for_kv, slice(H * HD, (H + 2 * KV) * HD)))
    for item, cols in parts:
        item.out[...] = mm(xa_ref[:, theirs], d_all[:, cols], TN).astype(BF16)
        item.start(0)
    for_out.acc[:, :d] = mm(ao_ref[:, mine], datt_ref[...], TN)
    for_out.acc[:, d:] = mm(xl_ref[:, mine], dlog_ref[...], TN)
    for_out.pair()
    for item, cols in parts:
        item.acc[...] = mm(xa_ref[:, mine], d_all[:, cols], TN)
        item.pair()

    for copy in projections:
        copy.wait()
    grad = (
        mm(d_all[:, : H * HD], wq_ref[...], NT)
        + mm(d_all[:, H * HD : (H + KV) * HD], wk_ref[...], NT)
        + mm(d_all[:, (H + KV) * HD :], wv_ref[...], NT)
    )
    xs = x_ref[...].astype(F32)
    scale = rms_scale(xs)
    scaled = grad * gain_ref[...]
    inner = jnp.mean(scaled * xs, -1, keepdims=True)
    dx_ref[...] = dh_ref[...] + scale * scaled - xs * scale**3 * inner
    gains = (
        jnp.sum(grad * xs * scale, 0, keepdims=True),
        jnp.sum(dgain2_ref[...], 0, keepdims=True),
    )
    part = d // 4
    gbuf[0] = jnp.concatenate(
        [gain[:, i * part : (i + 1) * part] for gain in gains for i in range(4)], 0
    )

    stages = [[sibling], planes, lines]

    def gain_copy(s, n):
        at = (0, 1, 4)[s] + n
        return remote(gbuf.at[s], grv.at[at], gsend.at[at], grecv.at[at], *stages[s][n])

    def gain_stage(s):
        for n in range(len(stages[s])):
            gain_copy(s, n).start()

    def gain_total(s):
        total = gbuf[s]
        for n in range(len(stages[s])):
            gain_copy(s, n).wait_recv()
            total = total + grv[(0, 1, 4)[s] + n]
        return total

    gain_stage(0)
    for_out.over_plane()

    outs = (eg_out, eu_out, ed_out)

    def expert_swap(i):
        rows = outs[i].shape[0] // 2
        part = outs[i].at[pl.ds(pl.multiple_of(me_s * rows, rows), rows)]
        return remote(part, part, esend.at[i], erecv.at[i], *sibling)

    for i in range(3):
        for copy in loads(i):
            copy.wait()
        terms = experts[i][3]
        rows = outs[i].shape[0] // 2
        total = terms[0].astype(F32)
        for n in (1, 2, 3):
            total = total + terms[n].astype(F32)
        outs[i][pl.ds(pl.multiple_of(me_s * rows, rows), rows), :] = total.astype(BF16)
        expert_swap(i).start()
    gbuf[1] = gain_total(0)
    gain_stage(1)
    for_q.over_plane()
    for_out.over_line()
    for_kv.over_plane()
    gbuf[2] = gain_total(1)
    gain_stage(2)
    for_q.over_line()
    for_out.back(3)
    for_kv.over_line()
    for_q.back(3)
    for_kv.back(3)
    gsum_ref[...] = gain_total(2)
    for i in range(3):
        expert_swap(i).wait()
        stores[3 + i].start()
    for item in sums:
        item.back(4)
    result = own_ref[...]
    near_mix.wait()
    far_mix.wait()
    for n in range(3):
        result = result + mix_in[n].astype(F32)
    res_ref[...] = result.astype(BF16)
    for item, store in zip(sums, stores):
        item.finish()
        store.start()
    for store in stores:
        store.wait()
    for s in range(3):
        for n in range(len(stages[s])):
            gain_copy(s, n).wait_send()


def tail(blocks_in, mix_peer, mix_near, own, arrived, far):
    tok, d = blocks_in[1].shape
    ff = own[0].shape[2]
    widths = (d + 128, H * HD, 2 * KV * HD)
    vm = pl.BlockSpec(memory_space=pltpu.VMEM)
    hbm = pl.BlockSpec(memory_space=pl.ANY)
    dma = pltpu.SemaphoreType.DMA
    vmem = pltpu.VMEM
    return pl.pallas_call(
        tail_kernel,
        out_shape=(
            jax.ShapeDtypeStruct((tok, d), BF16),
            jax.ShapeDtypeStruct((tok, d), F32),
            jax.ShapeDtypeStruct((8, d // 4), F32),
            *(jax.ShapeDtypeStruct((d, width), BF16) for width in widths),
            jax.ShapeDtypeStruct((d, ff), BF16),
            jax.ShapeDtypeStruct((d, ff), BF16),
            jax.ShapeDtypeStruct((ff, d), BF16),
        ),
        in_specs=[vm] * (len(blocks_in) - 6) + [hbm] * 16,
        out_specs=(vm,) * 3 + (hbm,) * 6,
        scratch_shapes=[
            *(vmem((d, width), BF16) for width in widths),
            vmem((d, ff), BF16),
            vmem((d, ff), BF16),
            vmem((ff, d), BF16),
            dma((6,)),
            vmem((tok, d), BF16),
            vmem((tok, d), F32),
            vmem((tok, d), F32),
            dma((3,)),
            vmem((3, tok, d), BF16),
            vmem((d, H * HD), BF16),
            vmem((d, KV * HD), BF16),
            vmem((d, KV * HD), BF16),
            vmem((tok, (H + 2 * KV) * HD), BF16),
            vmem((2, 4, d // 2, ff), BF16),
            vmem((4, ff // 2, d), BF16),
            vmem((3, 8, d // 4), F32),
            vmem((7, 8, d // 4), F32),
            dma((4, 4)),
            dma((3,)),
            dma((3,)),
            dma((7,)),
            dma((7,)),
            dma,
            dma,
            *(ref for width in widths for ref in summed_scratch(d, width)),
        ],
        compiler_params=pltpu.CompilerParams(
            collective_id=3, has_side_effects=True, vmem_limit_bytes=VMEM_LIMIT
        ),
        name="tail",
    )(*blocks_in, mix_peer, mix_near, *own, *arrived, *far)


def widen_kernel(
    gains, o, q, kv, eg, eu, ed, res, dx, n1, wq, wk, wv, wo, n2, wr, og, ou, od, res_out, dx_out
):
    d = wq.shape[1]
    half = wk.shape[1]
    wq[...] = q[...].astype(F32)
    wk[...] = kv[:, :half].astype(F32)
    wv[...] = kv[:, half:].astype(F32)
    wo[...] = o[:, :d].astype(F32)
    wr[...] = jnp.transpose(o[:, d:].astype(F32))[: wr.shape[0]]
    og[0] = eg[...].astype(F32)
    ou[0] = eu[...].astype(F32)
    od[0] = ed[...].astype(F32)
    n1[...] = jnp.concatenate([gains[i : i + 1, :] for i in range(4)], 1)
    n2[...] = jnp.concatenate([gains[i : i + 1, :] for i in range(4, 8)], 1)
    res_out[0] = res[...]
    dx_out[0] = dx[...]


def widen(gains, o, q, kv, eg, eu, ed, res, dx, experts):
    d, ff = eg.shape
    tok = res.shape[0]
    parts = 4

    def block(shape):
        return pl.BlockSpec((shape[0] // parts, shape[1]), lambda i: (i, 0))

    def deep(shape):
        return pl.BlockSpec((1, shape[0] // parts, shape[1]), lambda i: (0, i, 0))

    flat = pl.BlockSpec((1, d), lambda i: (0, 0))
    shapes = [(d, H * HD), (d, KV * HD), (d, KV * HD), (H * HD, d)]
    return pl.pallas_call(
        widen_kernel,
        grid=(parts,),
        out_shape=(
            jax.ShapeDtypeStruct((1, d), F32),
            *(jax.ShapeDtypeStruct(shape, F32) for shape in shapes),
            jax.ShapeDtypeStruct((1, d), F32),
            jax.ShapeDtypeStruct((experts, d), F32),
            jax.ShapeDtypeStruct((1, d, ff), F32),
            jax.ShapeDtypeStruct((1, d, ff), F32),
            jax.ShapeDtypeStruct((1, ff, d), F32),
            jax.ShapeDtypeStruct((1, tok, d), BF16),
            jax.ShapeDtypeStruct((1, tok, d), F32),
        ),
        in_specs=[pl.BlockSpec((8, d // 4), lambda i: (0, 0))]
        + [block(a.shape) for a in (o, q, kv, eg, eu, ed, res, dx)],
        out_specs=(
            flat,
            *(block(shape) for shape in shapes),
            flat,
            pl.BlockSpec((experts, d // parts), lambda i: (0, i)),
            deep((d, ff)),
            deep((d, ff)),
            deep((ff, d)),
            deep((tok, d)),
            deep((tok, d)),
        ),
        compiler_params=pltpu.CompilerParams(vmem_limit_bytes=VMEM_LIMIT),
        name="widen",
    )(gains, o, q, kv, eg, eu, ed, res, dx)


D = 1024
HIGH = lax.Precision.HIGHEST


def rope_tables(positions):
    half = HD // 2
    freq = jnp.exp(-math.log(10000.0) * jnp.arange(half, dtype=jnp.float32) * 2.0 / HD)
    angle = positions.astype(jnp.float32)[:, None] * freq[None, :]
    cosine = jnp.concatenate([jnp.cos(angle), jnp.cos(angle)], -1)
    sine = jnp.concatenate([jnp.sin(angle), jnp.sin(angle)], -1)
    return (cosine, sine)


def rotate_half(v):
    half = v.shape[-1] // 2
    return jnp.concatenate([-v[..., half:], v[..., :half]], -1)


def rotary(v, cosine, sine):
    return v * cosine[:, None, :] + rotate_half(v) * sine[:, None, :]


def unrotary(v, cosine, sine):
    return v * cosine[:, None, :] - rotate_half(v) * sine[:, None, :]


def rms_scale(v):
    return lax.rsqrt(jnp.mean(v * v, -1, keepdims=True) + EPS)


def rms_back(inputs, scale_rows, gain, grad):
    scaled = grad * gain
    d_inputs = scale_rows * scaled - inputs * scale_rows**3 * jnp.mean(
        scaled * inputs, -1, keepdims=True
    )
    return (d_inputs, jnp.sum(grad * inputs * scale_rows, 0))


def scores(queries, keys):
    return jnp.einsum("qkgd,skd->kgqs", queries, keys, preferred_element_type=jnp.float32) * HD ** (
        -0.5
    )


def per_device_plain(
    tokens,
    segments,
    routes,
    route_weight,
    norm1_gain,
    w_query,
    w_key,
    w_value,
    w_out,
    norm2_gain,
    w_router,
    w_gate,
    w_up,
    w_down,
    cotangent,
):
    f32 = jnp.float32
    bf16 = jnp.bfloat16
    scale = HD ** (-0.5)
    group = H // KV
    xs = tokens[0].astype(f32)
    tok = xs.shape[0]
    blocks = lax.axis_size("blk")
    length = tok * blocks
    first = lax.axis_index("blk") * tok
    last = first + tok - 1
    positions = first + jnp.arange(tok, dtype=jnp.int32)
    cosine, sine = rope_tables(positions)
    scale1 = rms_scale(xs)
    xa = (xs * scale1 * norm1_gain).astype(bf16)
    query = jnp.dot(xa, w_query, preferred_element_type=f32)
    key = jnp.dot(xa, w_key, preferred_element_type=f32)
    value = jnp.dot(xa, w_value, preferred_element_type=f32).astype(bf16)
    q_rot = rotary(query.reshape(tok, H, HD), cosine, sine).astype(bf16).reshape(tok, KV, group, HD)
    k_rot = rotary(key.reshape(tok, KV, HD), cosine, sine).astype(bf16).reshape(tok, KV * HD)
    seg_float = segments[0].astype(bf16)
    k_all, v_all, seg_all = (
        lax.all_gather(k_rot, "blk", axis=0, tiled=True),
        lax.all_gather(value, "blk", axis=0, tiled=True),
        lax.all_gather(seg_float, "blk", axis=0, tiled=True),
    )
    kblk = min(512, length)
    nblk = length // kblk
    k_blocks = k_all.reshape(nblk, kblk, KV, HD)
    v_blocks = v_all.reshape(nblk, kblk, KV, HD)
    s_blocks = seg_all.reshape(nblk, kblk)
    starts = jnp.arange(nblk, dtype=jnp.int32) * kblk

    def visible(kseg, kstart):
        kpos = kstart + jnp.arange(kblk, dtype=jnp.int32)
        return ((seg_float[:, None] == kseg[None, :]) & (kpos[None, :] <= positions[:, None]))[
            None, None
        ]

    def forward_step(carry, block):
        kb, vb, sb, start = block

        def forward_compute(state):
            running, total, acc = state
            mask = visible(sb, start)
            score = jnp.where(mask, scores(q_rot, kb), NEG)
            newmax = jnp.maximum(running, jnp.max(score, -1))
            expo = jnp.where(mask, jnp.exp(score - newmax[..., None]), 0.0)
            factor = jnp.exp(running - newmax)
            total = total * factor + jnp.sum(expo, -1)
            acc = acc * factor[..., None] + jnp.einsum(
                "kgqs,skd->kgqd", expo.astype(bf16), vb, preferred_element_type=f32
            )
            return (newmax, total, acc)

        return (lax.cond(start <= last, forward_compute, lambda state: state, carry), None)

    init = (
        jnp.full((KV, group, tok), NEG, f32),
        jnp.zeros((KV, group, tok), f32),
        jnp.zeros((KV, group, tok, HD), f32),
    )
    (running, total, acc), unused = lax.scan(
        forward_step, init, (k_blocks, v_blocks, s_blocks, starts)
    )
    lse = running + jnp.log(total)
    o_rows = (acc / total[..., None]).transpose(2, 0, 1, 3)
    att_low = o_rows.reshape(tok, H * HD).astype(bf16)
    h1 = xs + jnp.dot(att_low, w_out, preferred_element_type=f32)
    scale2 = rms_scale(h1)
    xl = (h1 * scale2 * norm2_gain).astype(bf16)
    logits = jnp.dot(xl, w_router, preferred_element_type=f32)
    experts = logits.shape[1]
    route = routes[0]
    rweight = route_weight[0]
    chooser = (route[:, :, None] == jnp.arange(experts, dtype=jnp.int32)[None, None, :]).astype(f32)
    chosen = jnp.sum(chooser * logits[:, None, :], -1)
    gates = jax.nn.softmax(chosen, -1)
    combine = (rweight * gates).astype(bf16)
    cap = min(tok, 2 * tok * TOP // experts)
    member = jnp.sum(chooser, 1)
    before = jnp.asarray(np.tril(np.ones((tok, tok), np.float32), -1))
    order = jnp.dot(before, member, precision=HIGH)
    rank = jnp.sum(chooser * order[:, None, :], -1).astype(jnp.int32)
    slots = route * cap + rank
    placed = jnp.any(
        slots[:, :, None] == jnp.arange(experts * cap, dtype=jnp.int32)[None, None, :], 1
    ).astype(bf16)
    outgoing = jnp.einsum("ts,td->sd", placed, xl, preferred_element_type=f32).astype(bf16)
    incoming = lax.all_to_all(
        outgoing.reshape(experts, cap, D), "blk", split_axis=0, concat_axis=0, tiled=True
    )
    local_exp = w_gate.shape[0]
    incoming = incoming.reshape(blocks, local_exp, cap, D)
    gate_pre = jnp.einsum("necd,edf->necf", incoming, w_gate, preferred_element_type=f32)
    up_pre = jnp.einsum("necd,edf->necf", incoming, w_up, preferred_element_type=f32)
    sigma = jax.nn.sigmoid(gate_pre)
    activated = gate_pre * sigma
    hidden = (activated * up_pre).astype(bf16)
    expert_out = jnp.einsum("necf,efd->necd", hidden, w_down, preferred_element_type=f32).astype(
        bf16
    )
    returned = lax.all_to_all(
        expert_out.reshape(experts, cap, D), "blk", split_axis=0, concat_axis=0, tiled=True
    )
    per_route = jnp.take(returned.reshape(experts * cap, D), slots.reshape(-1), axis=0).reshape(
        tok, TOP, D
    )
    mixture = jnp.einsum("tj,tjd->td", combine, per_route, preferred_element_type=f32)
    result = h1 + mixture
    grad_out = cotangent[0].astype(f32)
    grad_combine = jnp.einsum("td,tjd->tj", grad_out, per_route.astype(f32), precision=HIGH)
    route_grads = (combine.astype(f32)[:, :, None] * grad_out[:, None, :]).astype(bf16)
    grad_slots = (
        jnp.zeros((experts * cap, D), bf16)
        .at[slots.reshape(-1)]
        .set(route_grads.reshape(tok * TOP, D))
    )
    grad_incoming = lax.all_to_all(
        grad_slots.reshape(experts, cap, D), "blk", split_axis=0, concat_axis=0, tiled=True
    )
    grad_incoming = grad_incoming.reshape(blocks, local_exp, cap, D)
    grad_hidden = jnp.einsum("necd,efd->necf", grad_incoming, w_down, preferred_element_type=f32)
    grad_gate = (grad_hidden * up_pre * sigma * (1.0 + gate_pre * (1.0 - sigma))).astype(bf16)
    grad_up = (grad_hidden * activated).astype(bf16)
    d_down = jnp.einsum("necf,necd->efd", hidden, grad_incoming, preferred_element_type=f32)
    d_gate_w = jnp.einsum("necd,necf->edf", incoming, grad_gate, preferred_element_type=f32)
    d_up_w = jnp.einsum("necd,necf->edf", incoming, grad_up, preferred_element_type=f32)
    grad_in = (
        jnp.einsum("necf,edf->necd", grad_gate, w_gate, preferred_element_type=f32)
        + jnp.einsum("necf,edf->necd", grad_up, w_up, preferred_element_type=f32)
    ).astype(bf16)
    grad_back = lax.all_to_all(
        grad_in.reshape(experts, cap, D), "blk", split_axis=0, concat_axis=0, tiled=True
    )
    grad_xl = jnp.einsum(
        "ts,sd->td", placed, grad_back.reshape(experts * cap, D), preferred_element_type=f32
    )
    grad_gates = rweight * grad_combine
    grad_chosen = gates * (grad_gates - jnp.sum(gates * grad_gates, -1, keepdims=True))
    grad_logits = jnp.sum(chooser * grad_chosen[:, :, None], 1).astype(bf16)
    d_router = jnp.einsum("td,te->de", xl, grad_logits, preferred_element_type=f32)
    grad_xl = grad_xl + jnp.einsum("te,de->td", grad_logits, w_router, preferred_element_type=f32)
    grad_h1_norm, d_gain2 = rms_back(h1, scale2, norm2_gain, grad_xl)
    grad_h1 = grad_out + grad_h1_norm
    grad_att = grad_h1.astype(bf16)
    d_out_w = jnp.einsum("ti,td->id", att_low, grad_att, preferred_element_type=f32)
    grad_o = jnp.einsum("td,id->ti", grad_att, w_out, preferred_element_type=f32).astype(bf16)
    grad_o_rows = grad_o.reshape(tok, KV, group, HD)
    delta = jnp.einsum("qkgd,qkgd->kgq", grad_o_rows.astype(f32), o_rows)

    def query_terms(kb, vb, sb, start):
        mask = visible(sb, start)
        prob = jnp.where(mask, jnp.exp(scores(q_rot, kb) - lse[..., None]), 0.0)
        dprob = jnp.einsum("qkgd,skd->kgqs", grad_o_rows, vb, preferred_element_type=f32)
        dscore = (prob * (dprob - delta[..., None])).astype(bf16)
        dq_term = jnp.einsum("kgqs,skd->qkgd", dscore, kb, preferred_element_type=f32) * scale
        return (dq_term, dscore, prob)

    zero_q = jnp.zeros((tok, KV, group, HD), f32)

    def backward_step(grad_q, block):
        kb, vb, sb, start = block

        def backward_compute(acc_q):
            dq_term, dscore, prob = query_terms(kb, vb, sb, start)
            gk = jnp.einsum("kgqs,qkgd->skd", dscore, q_rot, preferred_element_type=f32) * scale
            gv = jnp.einsum(
                "kgqs,qkgd->skd", prob.astype(bf16), grad_o_rows, preferred_element_type=f32
            )
            return (acc_q + dq_term, (gk.reshape(kblk, KV * HD), gv.reshape(kblk, KV * HD)))

        def skip(acc_q):
            empty = jnp.zeros((kblk, KV * HD), f32)
            return (acc_q, (empty, empty))

        return lax.cond(start <= last, backward_compute, skip, grad_q)

    grad_q, (gk_blocks, gv_blocks) = lax.scan(
        backward_step, zero_q, (k_blocks, v_blocks, s_blocks, starts)
    )
    grad_k, grad_v = (
        lax.psum_scatter(
            gk_blocks.reshape(length, KV * HD).astype(jnp.bfloat16),
            "blk",
            scatter_dimension=0,
            tiled=True,
        ).astype(jnp.float32),
        lax.psum_scatter(
            gv_blocks.reshape(length, KV * HD).astype(jnp.bfloat16),
            "blk",
            scatter_dimension=0,
            tiled=True,
        ).astype(jnp.float32),
    )
    grad_qr = unrotary(grad_q.reshape(tok, H, HD), cosine, sine).reshape(tok, H * HD).astype(bf16)
    grad_kr = unrotary(grad_k.reshape(tok, KV, HD), cosine, sine).reshape(tok, KV * HD).astype(bf16)
    grad_vr = grad_v.astype(bf16)
    d_query = jnp.einsum("td,te->de", xa, grad_qr, preferred_element_type=f32)
    d_key = jnp.einsum("td,te->de", xa, grad_kr, preferred_element_type=f32)
    d_value = jnp.einsum("td,te->de", xa, grad_vr, preferred_element_type=f32)
    grad_xa = (
        jnp.einsum("te,de->td", grad_qr, w_query, preferred_element_type=f32)
        + jnp.einsum("te,de->td", grad_kr, w_key, preferred_element_type=f32)
        + jnp.einsum("te,de->td", grad_vr, w_value, preferred_element_type=f32)
    )
    grad_x_norm, d_gain1 = rms_back(xs, scale1, norm1_gain, grad_xa)
    grad_x = grad_h1 + grad_x_norm
    summed = lax.psum(
        (d_gain1, d_query, d_key, d_value, d_out_w, d_gain2, d_router), ("seq", "blk")
    )
    expert_summed = (
        lax.psum(d_gate_w.astype(jnp.bfloat16), "seq").astype(jnp.float32),
        lax.psum(d_up_w.astype(jnp.bfloat16), "seq").astype(jnp.float32),
        lax.psum(d_down.astype(jnp.bfloat16), "seq").astype(jnp.float32),
    )
    return (
        result.astype(bf16)[None],
        grad_x[None],
        summed[0],
        summed[1],
        summed[2],
        summed[3],
        summed[4],
        summed[5],
        summed[6],
        expert_summed[0],
        expert_summed[1],
        expert_summed[2],
    )


def tables(length):
    half = HD // 2
    freq = np.exp(-math.log(10000.0) * np.arange(half, dtype=np.float32) * 2.0 / HD).astype(np.float32)
    angle = np.arange(length, dtype=np.float32)[:, None] * freq[None, :]
    return np.tile(np.cos(angle), (1, 4)), np.tile(np.sin(angle), (1, 4))


def per_device(
    tokens,
    segments,
    routes,
    route_weight,
    norm1_gain,
    w_query,
    w_key,
    w_value,
    w_out,
    norm2_gain,
    w_router,
    w_gate,
    w_up,
    w_down,
    cotangent,
):
    tok, d = tokens[0].shape
    blocks = lax.axis_size("blk")
    experts = w_router.shape[1]
    cos_np, sin_np = tables(tok * blocks)
    cos_all = jnp.asarray(cos_np.reshape(blocks, tok, 2 * HD))
    sin_all = jnp.asarray(sin_np.reshape(blocks, tok, 2 * HD))
    seg = jnp.pad(segments[0].astype(BF16).reshape(2, tok // 2), ((0, 14), (0, 0)))
    gain1 = norm1_gain[None]
    g_low = cotangent[0]
    att_low, xa, *kept = attention_forward(
        blocks,
        tokens[0],
        gain1,
        w_query,
        w_key,
        w_value,
        seg,
        cos_all,
        sin_all,
        g_low,
        w_gate[0],
        w_up[0],
        w_down[0],
    )
    kept, shared = kept[:5], kept[5:]

    own, mix_peer, xl, grad_logits, grad_h1, grad_att, grad_o, gain2_terms, *rest = mixture(
        (tokens[0], att_low, norm2_gain[None], w_router.T, routes[0].T, route_weight[0].T),
        w_out,
        g_low,
        w_gate[0],
        w_up[0],
        w_down[0],
        shared,
    )
    (dwg, dwu, dwd), far = rest[:3], rest[3:]
    vectors = (
        grad_o,
        *kept,
        cos_all,
        sin_all,
    )
    got, mix_near, *arrived = attention_backward(
        blocks, vectors, mix_peer, dwg, dwu, dwd
    )
    blocks_in = (
        got,
        xa,
        gain1,
        att_low,
        grad_att,
        xl,
        grad_logits,
        gain2_terms,
        tokens[0],
        grad_h1,
        own,
        w_query,
        w_key,
        w_value,
    )
    result, grad_x, gains, d_out, d_query, d_kv, d_gate_w, d_up_w, d_down = tail(
        blocks_in, mix_peer, mix_near, (dwg, dwu, dwd), arrived, far
    )
    wide = widen(gains, d_out, d_query, d_kv, d_gate_w, d_up_w, d_down, result, grad_x, experts)
    d_gain1, d_query, d_key, d_value, d_out, d_gain2, d_router, *rest, result, grad_x = wide
    return (
        result,
        grad_x,
        d_gain1[0],
        d_query,
        d_key,
        d_value,
        d_out,
        d_gain2[0],
        d_router.T,
        *rest,
    )


def solution(mesh):
    fused = dict(mesh.shape) == {"seq": 2, "blk": 2 * KV}
    return jax.shard_map(
        per_device if fused else per_device_plain,
        mesh=mesh,
        in_specs=(
            P("seq", "blk", None),
            P("seq", "blk"),
            P("seq", "blk", None),
            P("seq", "blk", None),
            P(),
            P(),
            P(),
            P(),
            P(),
            P(),
            P(),
            P("blk", None, None),
            P("blk", None, None),
            P("blk", None, None),
            P("seq", "blk", None),
        ),
        out_specs=(
            P("seq", "blk", None),
            P("seq", "blk", None),
            P(),
            P(),
            P(),
            P(),
            P(),
            P(),
            P(),
            P("blk", None, None),
            P("blk", None, None),
            P("blk", None, None),
        ),
        check_vma=False,
    )
```

```python
import functools
import math

import jax
import jax.numpy as jnp
import numpy as np
from jax import lax
from jax.experimental import pallas as pl
from jax.experimental.pallas import tpu as pltpu
from jax.sharding import PartitionSpec as P

H = 16
KV = 8
HD = 64
TOP = 8
EPS = 1e-06
NEG = -1e30
F32 = jnp.float32
BF16 = jnp.bfloat16
MESH = pl.DeviceIdType.MESH
VMEM_LIMIT = 60 * 2**20
GRAD_STEPS = (2, 5)
HOP_STEP = 4
NT = (((1,), (1,)), ((), ()))
TN = (((0,), (0,)), ((), ()))


def mm(a, b, dims=(((1,), (0,)), ((), ()))):
    return lax.dot_general(a, b, dims, preferred_element_type=F32)


def remote(src, dst, send, recv, seq, blk):
    return pltpu.make_async_remote_copy(
        src_ref=src,
        dst_ref=dst,
        send_sem=send,
        recv_sem=recv,
        device_id=(seq, blk),
        device_id_type=MESH,
    )


def greet_all(seqs, blocks, me_s, me_b):
    barrier = pltpu.get_barrier_semaphore()
    total = seqs * blocks

    def hello(n, carry):
        other = lax.rem(me_s * blocks + me_b + n, total)
        pl.semaphore_signal(
            barrier,
            inc=1,
            device_id=(other // blocks, lax.rem(other, blocks)),
            device_id_type=MESH,
        )
        return carry

    lax.fori_loop(1, total, hello, 0)
    pl.semaphore_wait(barrier, total - 1)


def flip(place, n):
    if n == 1:
        return place + 1 - 2 * lax.rem(place, 2)
    if n == 2:
        return place + 2 - 4 * (place // 2)
    return 3 - place


def rotate_pairs(u):
    lanes = u.shape[-1]
    half = HD // 2
    lane = lax.broadcasted_iota(jnp.int32, u.shape, u.ndim - 1)
    ahead = pltpu.roll(u, lanes - half, u.ndim - 1)
    behind = pltpu.roll(u, half, u.ndim - 1)
    return jnp.where(lane % HD < half, -ahead, behind)


def stacked_heads(wide):
    return jnp.concatenate([wide[:HD], wide[HD:]], axis=1)


STAGES = 6


class Summed:
    def __init__(self, refs, send_sem, recv_sem, fin):
        self.out, self.arrived, self.acc, self.part, self.plane_in, self.line_in = refs
        self.send_sem, self.recv_sem, self.fin = send_sem, recv_sem, fin
        self.me_s = lax.axis_index("seq")
        me_b = lax.axis_index("blk")
        self.line, self.plane = me_b // 4, lax.rem(me_b, 4)
        self.sibling = [(1 - self.me_s, me_b)]
        self.planes = [(self.me_s, self.line * 4 + flip(self.plane, n)) for n in (1, 2, 3)]
        self.lines = [(self.me_s, flip(self.line, n) * 4 + self.plane) for n in (1, 2, 3)]
        rows = fin.shape[0]
        self.half, self.quarter, self.piece = rows // 2, rows // 8, rows // 32

    def rows(self, start, size):
        return pl.ds(pl.multiple_of(start, size), size)

    def halves(self):
        theirs = self.rows((1 - self.me_s) * self.half, self.half)
        return theirs, self.rows(self.me_s * self.half, self.half)

    def copy(self, stage, n):
        sems = self.send_sem.at[stage, n], self.recv_sem.at[stage, n]
        base = self.me_s * self.half
        if stage == 0:
            return remote(self.out, self.arrived, *sems, *self.sibling[n])
        if stage == 1:
            src = self.part.at[self.rows(flip(self.plane, n + 1) * self.quarter, self.quarter)]
            return remote(src, self.plane_in.at[n], *sems, *self.planes[n])
        if stage == 2:
            at = self.plane * self.quarter + flip(self.line, n + 1) * self.piece
            src = self.part.at[self.rows(at, self.piece)]
            return remote(src, self.line_in.at[n], *sems, *self.lines[n])
        if stage == 3:
            at = base + self.plane * self.quarter + self.line * self.piece
            part = self.fin.at[self.rows(at, self.piece)]
            return remote(part, part, *sems, *self.lines[n])
        if stage == 4:
            part = self.fin.at[self.rows(base + self.plane * self.quarter, self.quarter)]
            return remote(part, part, *sems, *self.planes[n])
        part = self.fin.at[self.rows(base, self.half)]
        return remote(part, part, *sems, *self.sibling[n])

    def start(self, stage):
        for n in range(1) if stage in (0, 5) else (2, 0, 1):
            self.copy(stage, n).start()

    def arrive(self, stage):
        for n in range(1 if stage in (0, 5) else 3):
            self.copy(stage, n).wait_recv()

    def pair(self):
        self.arrive(0)
        self.part[...] = (self.acc[...] + self.arrived[...].astype(F32)).astype(BF16)
        self.start(1)

    def over_plane(self):
        self.arrive(1)
        here = self.rows(self.plane * self.quarter, self.quarter)
        total = self.part[here, :].astype(F32)
        for n in range(3):
            total = total + self.plane_in[n].astype(F32)
        self.part[here, :] = total.astype(BF16)
        self.start(2)

    def over_line(self):
        self.arrive(2)
        at = self.plane * self.quarter + self.line * self.piece
        total = self.part[self.rows(at, self.piece), :].astype(F32)
        for n in range(3):
            total = total + self.line_in[n].astype(F32)
        self.fin[self.rows(self.me_s * self.half + at, self.piece), :] = total.astype(BF16)
        self.start(3)

    def back(self, stage):
        self.arrive(stage)
        self.start(stage + 1)

    def finish(self):
        self.arrive(5)
        for stage in range(STAGES):
            for n in range(1 if stage in (0, 5) else 3):
                self.copy(stage, n).wait_send()


def summed_scratch(rows, width):
    vmem, dma = pltpu.VMEM, pltpu.SemaphoreType.DMA
    return [
        vmem((rows // 2, width), BF16),
        vmem((rows // 2, width), BF16),
        vmem((rows // 2, width), F32),
        vmem((rows // 2, width), BF16),
        vmem((3, rows // 8, width), BF16),
        vmem((3, rows // 32, width), BF16),
        dma((STAGES, 3)),
        dma((STAGES, 3)),
    ]


def attention_forward_kernel(
    blocks,
    x_ref,
    gain_ref,
    wq_ref,
    wk_ref,
    wv_ref,
    seg_ref,
    cos_ref,
    sin_ref,
    g_ref,
    wg_ref,
    wu_ref,
    wd_ref,
    o_ref,
    xa_ref,
    kv_any,
    kvt_any,
    q_any,
    ot_any,
    stat_any,
    g_all,
    wg_all,
    wu_all,
    wd_all,
    kv_ref,
    kvt_ref,
    q_ref,
    ot_ref,
    stat_ref,
    kept_sem,
    pay,
    turn,
    in_ref,
    other_ref,
    obuf,
    cnt,
    turn_sem,
    send_sem,
    recv_sem,
    fsend_sem,
    frecv_sem,
    osend_sem,
    orecv_sem,
    gsend_sem,
    grecv_sem,
    wsend_sem,
    wrecv_sem,
    hsend_sem,
    hrecv_sem,
    dsend_sem,
    drecv_sem,
):
    me_s = lax.axis_index("seq")
    me_b = lax.axis_index("blk")
    tok = q_ref.shape[1]
    steps = blocks // 2
    sigma = me_b // KV
    kappa = lax.rem(me_b, KV)
    greet_all(2, blocks, me_s, me_b)
    dest_core = lax.rem(me_b, 2)
    slot = me_b // 2
    line, plane = me_b // 4, lax.rem(me_b, 4)
    weights = ((wg_ref, wg_all), (wu_ref, wu_all), (wd_ref, wd_all))

    def along(k, step, own):
        at = 0 if step < 0 else 1
        return remote(
            g_ref if own else g_all.at[k],
            g_all.at[k],
            gsend_sem.at[at, k],
            grecv_sem.at[k],
            me_s,
            (line + step) * 4 + plane,
        )

    def pass_on(k, step, own=False):
        @pl.when((line + step >= 0) & (line + step < 4))
        def _():
            along(k, step, own).start()

    def pass_distance(j):
        for step in (-1, 1):
            k = line - step * j

            @pl.when((k >= 0) & (k < 4))
            def _():
                pltpu.make_async_copy(g_ref, g_all.at[k], grecv_sem.at[k]).wait()
                pass_on(k, step)

    def half(ref):
        rows = ref.shape[0] // 2
        return ref.at[pl.ds(pl.multiple_of(me_s * rows, rows), rows)]

    def share_weight(n, i):
        own, everyone = weights[i]
        return remote(
            half(own),
            half(everyone.at[plane]),
            wsend_sem.at[n - 1, i],
            wrecv_sem.at[n - 1, i],
            me_s,
            line * 4 + flip(plane, n),
        )

    def diagonal(n, i):
        place = weights[i][1].at[flip(plane, n)]
        rows = place.shape[0] // 2
        start, size = me_s * rows, rows
        if i == 2:
            size = rows // 2
            start = start + (n - 1) * size
        part = place.at[pl.ds(pl.multiple_of(start, size), size)]
        return remote(
            part,
            part,
            dsend_sem.at[n - 1, i],
            drecv_sem.at[n - 1, i],
            me_s,
            line * 4 + flip(plane, 3 - n),
        )

    def diagonal_in(n, i):
        place = weights[i][1].at[flip(plane, 3)]
        rows = place.shape[0] // 2
        start, size = me_s * rows, rows
        if i == 2:
            size = rows // 2
            start = start + (2 - n) * size
        part = place.at[pl.ds(pl.multiple_of(start, size), size)]
        return pltpu.make_async_copy(part, part, drecv_sem.at[2 - n, i])

    def pass_weight(n, i):
        arrived = half(weights[i][1].at[flip(plane, n)])
        return remote(
            arrived, arrived, hsend_sem.at[n - 1, i], hrecv_sem.at[n - 1, i], 1 - me_s, me_b
        )

    share_weight(1, 0).start()
    share_weight(2, 1).start()
    for step in (-1, 1):
        pass_on(line, step, True)
    tables_in = [
        pltpu.make_async_copy(src.at[me_b], turn.at[i], turn_sem.at[i])
        for i, src in enumerate((cos_ref, sin_ref))
    ]
    for copy in tables_in:
        copy.start()
    xs = x_ref[...].astype(F32)
    xa = (xs * rms_scale(xs) * gain_ref[...]).astype(BF16)
    xa_ref[...] = xa
    for copy in tables_in:
        copy.wait()
    cosine, sine = turn[0], turn[1]
    low = lax.broadcasted_iota(jnp.int32, (tok, 2 * HD), 1) < HD
    pay[:, tok:, : 2 * HD] = jnp.zeros((KV, 16, 2 * HD), BF16)
    for m in range(KV // 2):
        pair = slice(m * 2 * HD, (m + 1) * 2 * HD)
        keys = mm(xa, wk_ref[:, pair])
        keys = keys * cosine + rotate_pairs(keys) * sine
        values = mm(xa, wv_ref[:, pair])
        first = jnp.where(low, keys, pltpu.roll(values, HD, 1))
        second = jnp.where(low, pltpu.roll(keys, HD, 1), values)
        pay[2 * m, :tok, 2 * HD :] = first.astype(BF16)
        pay[2 * m + 1, :tok, 2 * HD :] = second.astype(BF16)
        for k in (2 * m, 2 * m + 1):
            query = mm(xa, wq_ref[:, k * 2 * HD : (k + 1) * 2 * HD])
            query = (query * cosine + rotate_pairs(query) * sine) * HD ** (-0.5)
            pay[k, :tok, : 2 * HD] = query.astype(BF16)
            pay[k, tok:, 2 * HD :] = seg_ref[...]
    def payload(n):
        k = lax.rem(me_b + n, KV)
        chip = me_s * KV + k
        mine = (dest_core == me_s) & (chip == me_b)
        return k, chip, mine

    def send_payload(n, carry):
        k, chip, mine = payload(n)

        @pl.when(mine)
        def _():
            pltpu.make_async_copy(pay.at[k], in_ref.at[slot], recv_sem.at[slot]).start()

        @pl.when(jnp.logical_not(mine))
        def _():
            remote(
                pay.at[k], in_ref.at[slot], send_sem.at[k], recv_sem.at[slot], dest_core, chip
            ).start()

        return carry

    lax.fori_loop(0, KV, send_payload, 0)
    for i in (1, 2):
        share_weight(1, (0, 2, 1)[i]).start()
        share_weight(2, (1, 2, 0)[i]).start()

    kept = (
        (kv_ref, kv_any),
        (kvt_ref, kvt_any),
        (q_ref, q_any),
        (ot_ref, ot_any),
        (stat_ref, stat_any),
    )

    def keep(i, t):
        src, dst = kept[i]
        return pltpu.make_async_copy(src.at[t], dst.at[t], kept_sem.at[i, t])

    def arrival(t):
        return pltpu.make_async_copy(pay.at[0], in_ref.at[t], recv_sem.at[t])

    def forward(t):
        return remote(
            in_ref.at[t, :, pl.ds(2 * HD, 2 * HD)],
            other_ref.at[t],
            fsend_sem.at[t],
            frecv_sem.at[t],
            1 - me_s,
            me_b,
        )

    arrival(0).wait()
    forward(0).start()
    cnt[...] = jnp.zeros_like(cnt)
    first_core = me_s == 0
    lane = lax.broadcasted_iota(jnp.int32, (1, 2 * tok), 1)
    qrow = jnp.where(lane < tok, lane, lane - tok)
    wide = 2 * tok

    def step(t, carry):
        @pl.when(t < steps - 1)
        def _():
            arrival(t + 1).wait()
            forward(t + 1).start()

        for j in (1, 2):

            @pl.when(t == GRAD_STEPS[j - 1])
            def _():
                pass_distance(j)

        @pl.when(t == HOP_STEP)
        def _():
            for n, i in ((1, 0), (2, 1)):
                share_weight(n, i).wait_recv()
                diagonal(n, i).start()
                pass_weight(n, i).start()

        @pl.when(t == HOP_STEP + 1)
        def _():
            for n, i in ((1, 2), (2, 2)):
                share_weight(n, i).wait_recv()
                diagonal(n, i).start()
                pass_weight(n, i).start()

        @pl.when(t == HOP_STEP + 2)
        def _():
            for n, i in ((1, 1), (2, 0)):
                share_weight(n, i).wait_recv()
                pass_weight(n, i).start()

        forward(t).wait_recv()
        mine = in_ref[t]
        kv_mine, seg_mine = mine[:tok, 2 * HD :], mine[tok:, 2 * HD :].astype(F32)
        other = other_ref[t]
        kv_other, seg_other = other[:tok], other[tok:].astype(F32)
        pair = jnp.where(
            first_core,
            jnp.concatenate([kv_mine, kv_other], 0).astype(F32),
            jnp.concatenate([kv_other, kv_mine], 0).astype(F32),
        )
        kv_ref[t] = pair.astype(BF16)
        kvt_ref[t] = jnp.transpose(pair).astype(BF16)
        number = lax.broadcasted_iota(jnp.int32, (8, tok), 0).astype(F32)
        seg_q = jnp.concatenate([seg_mine[0:1], seg_mine[1:2]], 1)
        seg_o = jnp.concatenate([seg_other[0:1], seg_other[1:2]], 1)
        below = (seg_q < number).astype(F32) + (seg_o < number).astype(F32)
        cnt[...] += jnp.sum(below, 1, keepdims=True)
        start_q = jnp.sum(jnp.where(seg_q == number, cnt[:, :1], 0.0), 0, keepdims=True)
        start = jnp.concatenate([start_q, start_q], 1).astype(jnp.int32)
        q_two = mine[:tok, : 2 * HD]
        q_ref[t] = q_two
        qt = stacked_heads(jnp.transpose(q_two.astype(F32)))
        qm = jnp.concatenate([qt, jnp.zeros_like(qt)], 0).astype(BF16)
        qpos = (2 * t + me_s) * tok + qrow

        def piece(u, state, last):
            running, total, acc = state
            score = mm(kv_ref[u], qm)
            kpos = u * wide + lax.broadcasted_iota(jnp.int32, score.shape, 0)
            mask = kpos >= start
            if last:
                mask &= kpos <= qpos
            score = jnp.where(mask, score, NEG)
            newmax = jnp.maximum(running, jnp.max(score, 0, keepdims=True))
            expo = jnp.exp(score - newmax)
            factor = jnp.exp(running - newmax)
            total = total * factor + jnp.sum(expo, 0, keepdims=True)
            acc = acc * factor + mm(kvt_ref[u, HD:, :], expo.astype(BF16))
            return newmax, total, acc

        state = (
            jnp.full((1, wide), NEG, F32),
            jnp.zeros((1, wide), F32),
            jnp.zeros((HD, wide), F32),
        )
        state = lax.fori_loop(0, t, lambda u, s: piece(u, s, False), state)
        running, total, acc = piece(t, state, True)
        out_t = acc / total
        ot_ref[t] = out_t
        rows = lax.broadcasted_iota(jnp.int32, (8, wide), 0)
        lse = running + jnp.log(total)
        stat_ref[t] = jnp.where(rows == 0, lse, start.astype(F32))
        upright = jnp.concatenate([out_t[:, :tok], out_t[:, tok:]], 0)
        obuf[t] = jnp.transpose(upright).astype(BF16)
        for i in range(5):
            keep(i, t).start()
        owner = 2 * t + me_s
        home = (sigma == me_s) & (owner == me_b)
        place = o_ref.at[:, pl.ds(pl.multiple_of(kappa * 2 * HD, 2 * HD), 2 * HD)]

        @pl.when(home)
        def _():
            pltpu.make_async_copy(obuf.at[t], place, orecv_sem.at[kappa]).start()

        @pl.when(jnp.logical_not(home))
        def _():
            remote(obuf.at[t], place, osend_sem.at[t], orecv_sem.at[kappa], sigma, owner).start()

        return carry

    lax.fori_loop(0, steps, step, 0)
    diagonal_in(2, 0).wait()
    pass_weight(3, 0).start()
    diagonal_in(1, 1).wait()
    pass_weight(3, 1).start()
    diagonal_in(1, 2).wait()
    diagonal_in(2, 2).wait()
    pass_weight(3, 2).start()

    def finish(t, carry):
        k, chip, mine = payload(t)

        @pl.when(jnp.logical_not(mine))
        def _():
            remote(
                pay.at[k], in_ref.at[slot], send_sem.at[k], recv_sem.at[slot], dest_core, chip
            ).wait_send()

        return carry

    lax.fori_loop(0, KV, finish, 0)

    def finish_steps(t, carry):
        forward(t).wait_send()
        for i in range(5):
            keep(i, t).wait()
        owner = 2 * t + me_s
        home = (sigma == me_s) & (owner == me_b)

        @pl.when(jnp.logical_not(home))
        def _():
            remote(
                obuf.at[t],
                o_ref.at[:, pl.ds(0, 2 * HD)],
                osend_sem.at[t],
                orecv_sem.at[0],
                sigma,
                owner,
            ).wait_send()

        return carry

    lax.fori_loop(0, steps, finish_steps, 0)

    def gather(k, carry):
        pltpu.make_async_copy(
            obuf.at[0],
            o_ref.at[:, pl.ds(pl.multiple_of(k * 2 * HD, 2 * HD), 2 * HD)],
            orecv_sem.at[k],
        ).wait()
        return carry

    lax.fori_loop(0, KV, gather, 0)
    pass_distance(3)
    for k in range(4):

        @pl.when((k <= line) & (line < 3))
        def _():
            along(k, 1, False).wait_send()

        @pl.when((k >= line) & (line > 0))
        def _():
            along(k, -1, False).wait_send()

    for n in (1, 2, 3):
        for i in range(3):
            pass_weight(n, i).wait()
    for n in (1, 2):
        for i in range(3):
            share_weight(n, i).wait_send()
        diagonal(n, n - 1).wait_send()
        diagonal(n, 2).wait_send()


def attention_forward(
    blocks, x, gain, w_query, w_key, w_value, seg, cos_all, sin_all, g, w_gate, w_up, w_down
):
    tok, d = x.shape
    steps = blocks // 2
    vm = pl.BlockSpec(memory_space=pltpu.VMEM)
    hbm = pl.BlockSpec(memory_space=pl.ANY)
    dma = pltpu.SemaphoreType.DMA
    return pl.pallas_call(
        functools.partial(attention_forward_kernel, blocks),
        out_shape=(
            jax.ShapeDtypeStruct((tok, H * HD), BF16),
            jax.ShapeDtypeStruct((tok, d), BF16),
            jax.ShapeDtypeStruct((steps, 2 * tok, 2 * HD), BF16),
            jax.ShapeDtypeStruct((steps, 2 * HD, 2 * tok), BF16),
            jax.ShapeDtypeStruct((steps, tok, 2 * HD), BF16),
            jax.ShapeDtypeStruct((steps, HD, 2 * tok), F32),
            jax.ShapeDtypeStruct((steps, 8, 2 * tok), F32),
            jax.ShapeDtypeStruct((4, *g.shape), BF16),
            jax.ShapeDtypeStruct((4, *w_gate.shape), BF16),
            jax.ShapeDtypeStruct((4, *w_up.shape), BF16),
            jax.ShapeDtypeStruct((4, *w_down.shape), BF16),
        ),
        in_specs=[vm] * 6 + [hbm] * 6,
        out_specs=(vm,) * 2 + (hbm,) * 9,
        scratch_shapes=[
            pltpu.VMEM((steps, 2 * tok, 2 * HD), BF16),
            pltpu.VMEM((steps, 2 * HD, 2 * tok), BF16),
            pltpu.VMEM((steps, tok, 2 * HD), BF16),
            pltpu.VMEM((steps, HD, 2 * tok), F32),
            pltpu.VMEM((steps, 8, 2 * tok), F32),
            dma((5, steps)),
            pltpu.VMEM((KV, tok + 16, 4 * HD), BF16),
            pltpu.VMEM((2, tok, 2 * HD), F32),
            pltpu.VMEM((steps, tok + 16, 4 * HD), BF16),
            pltpu.VMEM((steps, tok + 16, 2 * HD), BF16),
            pltpu.VMEM((steps, tok, 2 * HD), BF16),
            pltpu.VMEM((8, 128), F32),
            dma((2,)),
            dma((KV,)),
            dma((steps,)),
            dma((steps,)),
            dma((steps,)),
            dma((steps,)),
            dma((KV,)),
            dma((2, 4)),
            dma((4,)),
            dma((2, 3)),
            dma((2, 3)),
            dma((3, 3)),
            dma((3, 3)),
            dma((2, 3)),
            dma((2, 3)),
        ],
        compiler_params=pltpu.CompilerParams(
            collective_id=0, has_side_effects=True, vmem_limit_bytes=VMEM_LIMIT
        ),
        name="attention_forward",
    )(x, gain, w_query, w_key, w_value, seg, cos_all, sin_all, g, w_gate, w_up, w_down)


def attention_backward_kernel(
    blocks,
    do_ref,
    kv_any,
    kvt_any,
    q_any,
    ot_any,
    stat_any,
    cos_ref,
    sin_ref,
    mix_ref,
    dwg_ref,
    dwu_ref,
    dwd_ref,
    out_ref,
    mix_in,
    dwg_in,
    dwu_in,
    dwd_in,
    kv_ref,
    kvt_ref,
    q_ref,
    ot_ref,
    stat_ref,
    kept_sem,
    turn,
    turn_sem,
    in_ref,
    dkv,
    part,
    xch,
    done,
    send_sem,
    recv_sem,
    xsend_sem,
    xrecv_sem,
    osend_sem,
    orecv_sem,
    msend_sem,
    mrecv_sem,
    wsend_sem,
    wrecv_sem,
):
    me_s = lax.axis_index("seq")
    me_b = lax.axis_index("blk")
    tok = q_ref.shape[1]
    steps = blocks // 2
    sigma = me_b // KV
    kappa = lax.rem(me_b, KV)
    tables_in = [
        pltpu.make_async_copy(src.at[2 * t + me_s], turn.at[i, t], turn_sem.at[i, t])
        for i, src in enumerate((cos_ref, sin_ref))
        for t in range(steps)
    ]
    kept = ((q_any, q_ref), (kv_any, kv_ref), (kvt_any, kvt_ref), (ot_any, ot_ref), (stat_any, stat_ref))
    tables_in += [
        pltpu.make_async_copy(src, dst, kept_sem.at[i]) for i, (src, dst) in enumerate(kept)
    ]
    for copy in tables_in:
        copy.start()
    greet_all(2, blocks, me_s, me_b)

    dest_core = lax.rem(me_b, 2)
    slot = me_b // 2
    line, plane = me_b // 4, lax.rem(me_b, 4)
    weights = ((dwg_ref, dwg_in), (dwu_ref, dwu_in), (dwd_ref, dwd_in))

    def give_mix(n):
        return remote(
            mix_ref.at[flip(line, n)],
            mix_in.at[n - 1],
            msend_sem.at[n - 1],
            mrecv_sem.at[n - 1],
            me_s,
            flip(line, n) * 4 + plane,
        )

    def give_weight(n, i):
        src, dst = weights[i]
        return remote(
            src.at[flip(plane, n)],
            dst.at[n - 1],
            wsend_sem.at[n - 1, i],
            wrecv_sem.at[n - 1, i],
            me_s,
            line * 4 + flip(plane, n),
        )

    def outgoing(n):
        k = lax.rem(me_b + n, KV)
        chip = me_s * KV + k
        mine = (dest_core == me_s) & (chip == me_b)
        src = do_ref.at[:, pl.ds(pl.multiple_of(k * 2 * HD, 2 * HD), 2 * HD)]
        return k, chip, mine, src

    def send_grad(n, carry):
        k, chip, mine, src = outgoing(n)

        @pl.when(mine)
        def _():
            pltpu.make_async_copy(src, in_ref.at[slot], recv_sem.at[slot]).start()

        @pl.when(jnp.logical_not(mine))
        def _():
            remote(src, in_ref.at[slot], send_sem.at[k], recv_sem.at[slot], dest_core, chip).start()

        return carry

    lax.fori_loop(0, KV, send_grad, 0)
    for copy in tables_in:
        copy.wait()
    for n in (2, 1):
        give_mix(n).start()
    for i in range(3):
        for n in (1, 2):
            give_weight(n, i).start()
    give_weight(3, 2).start()
    dkv[...] = jnp.zeros_like(dkv)
    wide = 2 * tok
    lane = lax.broadcasted_iota(jnp.int32, (1, wide), 1)
    qrow = jnp.where(lane < tok, lane, lane - tok)
    low = lax.broadcasted_iota(jnp.int32, (tok, 2 * HD), 1) < HD

    def swap(t):
        return remote(part.at[t], xch.at[t], xsend_sem.at[t], xrecv_sem.at[t], 1 - me_s, me_b)

    def deliver(t, act):
        owner = 2 * t + me_s
        home = (sigma == me_s) & (owner == me_b)
        src, dst = done.at[t], out_ref.at[kappa]

        @pl.when(home)
        def _():
            if act == "start":
                pltpu.make_async_copy(src, dst, orecv_sem.at[kappa]).start()

        @pl.when(jnp.logical_not(home))
        def _():
            copy = remote(src, dst, osend_sem.at[t], orecv_sem.at[kappa], sigma, owner)
            copy.start() if act == "start" else copy.wait_send()

    def finalize(t):
        swap(t).wait_recv()
        place = pl.ds(pl.multiple_of(me_s * tok, tok), tok)
        total = dkv[t, place, :] + xch[t]
        cosine = jnp.where(low, turn[0, t], 1.0)
        sine = jnp.where(low, turn[1, t], 0.0)
        back = total * cosine - rotate_pairs(total) * sine
        done[t, :, pl.ds(2 * HD, 2 * HD)] = back.astype(BF16)
        deliver(t, "start")

    def step(n, carry):
        t = steps - 1 - n
        pltpu.make_async_copy(do_ref.at[:, pl.ds(0, 2 * HD)], in_ref.at[t], recv_sem.at[t]).wait()
        d_two = in_ref[t].astype(F32)
        q_two = q_ref[t].astype(F32)
        dt = stacked_heads(jnp.transpose(d_two))
        qt = stacked_heads(jnp.transpose(q_two))
        zero = jnp.zeros_like(dt)
        dm = jnp.concatenate([zero, dt], 0).astype(BF16)
        qm = jnp.concatenate([qt, zero], 0).astype(BF16)
        delta = jnp.sum(ot_ref[t] * dt, 0, keepdims=True)
        right = jnp.concatenate(
            [
                jnp.where(low, q_two, 0.0),
                jnp.where(low, pltpu.roll(q_two, HD, 1), 0.0),
                jnp.where(low, 0.0, pltpu.roll(d_two, HD, 1)),
                jnp.where(low, 0.0, d_two),
            ],
            0,
        ).astype(BF16)
        stat = stat_ref[t]
        lse, start = stat[0:1], stat[1:2].astype(jnp.int32)
        qpos = (2 * t + me_s) * tok + qrow

        def piece(u, dq, last):
            keys = kv_ref[u]
            score = mm(keys, qm)
            kpos = u * wide + lax.broadcasted_iota(jnp.int32, score.shape, 0)
            mask = kpos >= start
            if last:
                mask &= kpos <= qpos
            prob = jnp.where(mask, jnp.exp(score - lse), 0.0)
            dprob = mm(keys, dm)
            dscore = (prob * (dprob - delta)).astype(BF16)
            both = jnp.concatenate([dscore, prob.astype(BF16)], 1)
            dkv[u] += mm(both, right)
            return dq + mm(kvt_ref[u, :HD, :], dscore)

        dq = jnp.zeros((HD, wide), F32)
        dq = lax.fori_loop(0, t, lambda u, s: piece(u, s, False), dq)
        dq = piece(t, dq, True) * HD ** (-0.5)
        upright = jnp.transpose(jnp.concatenate([dq[:, :tok], dq[:, tok:]], 0))
        back = upright * turn[0, t] - rotate_pairs(upright) * turn[1, t]
        done[t, :, pl.ds(0, 2 * HD)] = back.astype(BF16)
        part[t] = dkv[t, pl.ds(pl.multiple_of((1 - me_s) * tok, tok), tok), :]
        swap(t).start()

        @pl.when(n > 0)
        def _():
            finalize(t + 1)

        return carry

    lax.fori_loop(0, steps, step, 0)
    finalize(0)

    def finish(n, carry):
        k, chip, mine, src = outgoing(n)

        @pl.when(jnp.logical_not(mine))
        def _():
            remote(
                src, in_ref.at[slot], send_sem.at[k], recv_sem.at[slot], dest_core, chip
            ).wait_send()

        return carry

    lax.fori_loop(0, KV, finish, 0)

    def finish_steps(t, carry):
        swap(t).wait_send()
        deliver(t, "wait")
        return carry

    lax.fori_loop(0, steps, finish_steps, 0)

    def gather(k, carry):
        pltpu.make_async_copy(done.at[0], out_ref.at[k], orecv_sem.at[k]).wait()
        return carry

    lax.fori_loop(0, KV, gather, 0)
    for n in (1, 2):
        give_mix(n).wait()
        for i in range(3):
            give_weight(n, i).wait()
    give_weight(3, 2).wait()


def attention_backward(
    blocks, vectors, mix, dwg, dwu, dwd
):
    tok = vectors[0].shape[0]
    steps = blocks // 2
    vm = pl.BlockSpec(memory_space=pltpu.VMEM)
    hbm = pl.BlockSpec(memory_space=pl.ANY)
    dma = pltpu.SemaphoreType.DMA
    return pl.pallas_call(
        functools.partial(attention_backward_kernel, blocks),
        out_shape=(
            jax.ShapeDtypeStruct((KV, tok, 4 * HD), BF16),
            jax.ShapeDtypeStruct((2, *mix.shape[1:]), BF16),
            jax.ShapeDtypeStruct((2, *dwg.shape[1:]), BF16),
            jax.ShapeDtypeStruct((2, *dwu.shape[1:]), BF16),
            jax.ShapeDtypeStruct((3, *dwd.shape[1:]), BF16),
        ),
        in_specs=[vm] + [hbm] * (len(vectors) + 3),
        out_specs=(vm,) + (hbm,) * 4,
        scratch_shapes=[
            *(pltpu.VMEM(a.shape, a.dtype) for a in vectors[1:6]),
            dma((5,)),
            pltpu.VMEM((2, steps, tok, 2 * HD), F32),
            dma((2, steps)),
            pltpu.VMEM((steps, tok, 2 * HD), BF16),
            pltpu.VMEM((steps, 2 * tok, 2 * HD), F32),
            pltpu.VMEM((steps, tok, 2 * HD), F32),
            pltpu.VMEM((steps, tok, 2 * HD), F32),
            pltpu.VMEM((steps, tok, 4 * HD), BF16),
            dma((KV,)),
            dma((steps,)),
            dma((steps,)),
            dma((steps,)),
            dma((steps,)),
            dma((KV,)),
            dma((2,)),
            dma((2,)),
            dma((3, 3)),
            dma((3, 3)),
        ],
        compiler_params=pltpu.CompilerParams(
            collective_id=1, has_side_effects=True, vmem_limit_bytes=VMEM_LIMIT
        ),
        name="attention_backward",
    )(*vectors, mix, dwg, dwu, dwd)


def mixture_kernel(
    x_ref,
    ao_ref,
    gain_ref,
    router_ref,
    routes_ref,
    weight_ref,
    wo_ref,
    g_ref,
    wg_ref,
    wu_ref,
    wd_ref,
    g_all,
    wg_all,
    wu_all,
    wd_all,
    res_any,
    mix_any,
    xl_any,
    dlog_ref,
    dh_ref,
    datt_ref,
    do_ref,
    dgain_ref,
    dwg_out,
    dwu_out,
    dwd_out,
    dwg_in,
    dwu_in,
    res_ref,
    mix_peer,
    xl_ref,
    out_sem,
    wr_ref,
    rw_ref,
    h1_ref,
    gate_ref,
    d_in,
    d_c,
    wo,
    x_in,
    c_in,
    share_ref,
    x_t,
    g_in,
    wg,
    wu,
    wd,
    hc,
    dg,
    du,
    acc_o,
    acc_d,
    acc_c,
    d_send,
    d_recv,
    c_send,
    c_recv,
    xg,
    xu,
    xd,
    load_sem,
    gload_sem,
    send_sem,
    recv_sem,
    bsend_sem,
    brecv_sem,
    psend_sem,
    precv_sem,
    store_sem,
    wsend_sem,
    wrecv_sem,
    wo_sem,
    csend_sem,
    crecv_sem,
    ksend_sem,
    krecv_sem,
):
    me_s = lax.axis_index("seq")
    me_b = lax.axis_index("blk")
    line, plane = me_b // 4, lax.rem(me_b, 4)
    tok, d = g_in.shape[1:]
    ff = wg.shape[2]
    experts = router_ref.shape[0]
    barrier = pltpu.get_barrier_semaphore()
    sibling = (1 - me_s, me_b)
    opposite = (me_s, line * 4 + flip(plane, 3))
    for place in [(me_s, flip(line, n) * 4 + plane) for n in (1, 2, 3)] + [sibling, opposite]:
        pl.semaphore_signal(barrier, inc=1, device_id=place, device_id_type=MESH)

    owns = ((wg_ref, wg_all, wg), (wu_ref, wu_all, wu), (wd_ref, wd_all, wd))

    def load_own(i):
        return pltpu.make_async_copy(owns[i][0], owns[i][2].at[plane], load_sem.at[i, plane])

    def load_other(i, e):
        return pltpu.make_async_copy(owns[i][1].at[e], owns[i][2].at[e], load_sem.at[i, e])

    load_out = pltpu.make_async_copy(wo_ref, wo, wo_sem)
    load_out.start()
    for i in (2, 0, 1):
        load_own(i).start()
        for n in (1, 2, 3):
            load_other(i, flip(plane, n)).start()

    def load_grad(k):
        return pltpu.make_async_copy(g_all.at[k], g_in.at[k], gload_sem.at[k])

    pltpu.make_async_copy(g_ref, g_in.at[line], gload_sem.at[line]).start()
    for n in (1, 2, 3):
        load_grad(flip(line, n)).start()
    lane = lax.broadcasted_iota(jnp.int32, (tok, 128), 1)
    number = lax.broadcasted_iota(jnp.int32, (128, tok), 0)
    spread = jnp.zeros((128, tok), F32)
    for j in range(TOP):
        spread += jnp.where(routes_ref[j : j + 1, :] == number, weight_ref[j : j + 1, :], 0.0)
    rw = jnp.transpose(spread)
    rw_ref[...] = rw
    row, column = (lax.broadcasted_iota(jnp.int32, (experts, 128), i) for i in range(2))
    wr_ref[...] = mm(router_ref[...], (row == column).astype(BF16), TN).astype(BF16)
    load_out.wait()
    xs = x_ref[...].astype(F32)
    h1 = xs + mm(ao_ref[...], wo[...])
    h1_ref[...] = h1
    xl = (h1 * rms_scale(h1) * gain_ref[...]).astype(BF16)
    xl_ref[...] = xl
    store_xl = pltpu.make_async_copy(xl_ref, xl_any, out_sem.at[3])
    store_xl.start()
    store_res = pltpu.make_async_copy(res_ref, res_any, out_sem.at[4])
    logits = mm(xl, wr_ref[...])
    routed = rw > 0.0
    top = jnp.max(jnp.where(routed, logits, NEG), -1, keepdims=True)
    expo = jnp.where(routed, jnp.exp(logits - top), 0.0)
    gates = expo / jnp.sum(expo, -1, keepdims=True)
    gate_ref[...] = gates
    x_in[line] = xl
    c_in[line] = jnp.transpose(rw * gates)[:experts].astype(BF16)
    pl.semaphore_wait(barrier, 5)

    def along(k, step):
        at = 0 if step < 0 else 1
        return remote(
            x_in.at[k],
            x_in.at[k],
            send_sem.at[at, k],
            recv_sem.at[k],
            me_s,
            (line + step) * 4 + plane,
        )

    def along_too(k, step):
        at = 0 if step < 0 else 1
        return remote(
            c_in.at[k],
            c_in.at[k],
            csend_sem.at[at, k],
            crecv_sem.at[k],
            me_s,
            (line + step) * 4 + plane,
        )

    def pass_on(k, step):
        @pl.when((line + step >= 0) & (line + step < 4))
        def _():
            along_too(k, step).start()
            along(k, step).start()

    for step in (-1, 1):
        pass_on(line, step)
    for k in range(4):
        load_grad(k).wait()
    g_rows = g_in.reshape(4 * tok, d)

    def grad_hidden(e, carry):
        load_other(2, e).wait()
        for part in range(2):
            rows = slice(part * 2 * tok, (part + 1) * 2 * tok)
            dg[e, rows, :] = mm(g_rows[rows, :], wd[e], NT).astype(BF16)
        return carry

    lax.fori_loop(0, 4, grad_hidden, 0)

    def load_wait(e, carry):
        for i in range(2):
            load_other(i, e).wait()
        return carry

    def apart(k):
        return lax.rem(k - line + 3, 4)

    def store_mix(n):
        return pltpu.make_async_copy(mix_peer.at[apart(n)], mix_any.at[n], out_sem.at[apart(n)])

    def place_of(j):
        return jnp.where(line < 2, lax.rem(line + j, 4), lax.rem(line + 4 - j, 4))

    def block(j, carry):
        n = place_of(j)
        filler = jnp.zeros((128 - experts, tok), F32)
        share_ref[...] = jnp.transpose(jnp.concatenate([c_in[n].astype(F32), filler], 0))
        acc_o[...] = jnp.zeros_like(acc_o)
        acc_d[...] = jnp.zeros_like(acc_d)
        acc_c[...] = jnp.zeros_like(acc_c)
        rows = pl.ds(pl.multiple_of(n * tok, tok), tok)

        def expert(e, carry):
            @pl.when(j == 0)
            def _():
                load_wait(e, 0)

            for step in (-1, 1):
                k = line - step * (j + 1)

                @pl.when((e == 3) & (j == 0) & (k >= 0) & (k < 4))
                def _():
                    pltpu.make_async_copy(c_in.at[line], c_in.at[k], crecv_sem.at[k]).wait()
                    pltpu.make_async_copy(x_in.at[line], x_in.at[k], recv_sem.at[k]).wait()
                    pass_on(k, step)

            x = x_in[n]
            here = lane == line * 4 + e
            share = jnp.sum(jnp.where(here, share_ref[...], 0.0), 1, keepdims=True)
            gate = mm(x, wg[e])
            up = mm(x, wu[e])
            dh = dg[e, rows, :].astype(F32)
            sg = jax.nn.sigmoid(gate)
            act = gate * sg
            hidden = act * up
            acc_c[...] += jnp.where(here, jnp.sum(dh * hidden, 1, keepdims=True), 0.0)
            dh = dh * share
            hcb = (hidden * share).astype(BF16)
            dgb = (dh * up * sg * (1.0 + gate * (1.0 - sg))).astype(BF16)
            dub = (dh * act).astype(BF16)
            hc[e, rows, :] = hcb
            dg[e, rows, :] = dgb
            du[e, rows, :] = dub
            acc_o[...] += mm(hcb, wd[e])
            acc_d[...] += mm(dgb, wg[e], NT) + mm(dub, wu[e], NT)
            return carry

        lax.fori_loop(0, 4, expert, 0)

        @pl.when(j == 0)
        def _():
            res_ref[...] = h1_ref[...] + acc_o[...]
            store_res.start()
            d_in[...] = acc_d[...]
            d_c[...] = acc_c[...]

        @pl.when(j > 0)
        def _():
            to = apart(n)
            mix_peer[to] = acc_o[...].astype(BF16)
            store_mix(n).start()
            d_send[to] = acc_d[...].astype(BF16)
            turned = jnp.transpose(acc_c[...])[:experts]
            high = turned.astype(BF16)
            c_send[to, :experts, :] = high
            c_send[to, experts:, :] = (turned - high.astype(F32)).astype(BF16)
            give_back_too(n).start()
            give_back(n).start()

        for step in (-1, 1):
            k = line - step * (j + 1)

            @pl.when((j > 0) & (j < 3) & (k >= 0) & (k < 4))
            def _():
                pltpu.make_async_copy(c_in.at[line], c_in.at[k], crecv_sem.at[k]).wait()
                pltpu.make_async_copy(x_in.at[line], x_in.at[k], recv_sem.at[k]).wait()
                pass_on(k, step)

        x_t[:, rows] = jnp.transpose(x_in[n].astype(F32)).astype(BF16)
        return carry

    def give_back_too(n):
        return remote(
            c_send.at[apart(n)],
            c_recv.at[lax.rem(line - n + 3, 4)],
            ksend_sem.at[n],
            krecv_sem.at[line],
            me_s,
            n * 4 + plane,
        )

    def give_back(n):
        return remote(
            d_send.at[apart(n)], d_recv.at[lax.rem(line - n + 3, 4)], bsend_sem.at[n], brecv_sem.at[line], me_s, n * 4 + plane
        )

    lax.fori_loop(0, 4, block, 0)

    half, dhalf = d // 2, ff // 2
    theirs = pl.multiple_of((1 - me_s) * half, half)
    dtheirs = pl.multiple_of((1 - me_s) * dhalf, dhalf)
    mine = pl.multiple_of(me_s * half, half)
    dmine = pl.multiple_of(me_s * dhalf, dhalf)

    def swap(i, e):
        src = (wg.at[e, pl.ds(0, half)], wu.at[e, pl.ds(0, half)], wd.at[e, pl.ds(0, dhalf)])[i]
        dst = (xg, xu, xd)[i].at[e]
        return remote(src, dst, psend_sem.at[i, e], precv_sem.at[i, e], *sibling)

    def store(i, e):
        return pltpu.make_async_copy(
            (xg, xu, xd)[i].at[e], (dwg_out, dwu_out, dwd_out)[i].at[e], store_sem.at[i, e]
        )

    def turn_of(n):
        return jnp.where(
            n == 0, flip(plane, 3), jnp.where(n == 1, flip(plane, 2), jnp.where(n == 2, flip(plane, 1), plane))
        )

    def opposed(i):
        return remote(
            (xg, xu, xd)[i].at[flip(plane, 3)],
            (dwg_in, dwu_in)[i],
            wsend_sem.at[i],
            wrecv_sem.at[i],
            *opposite,
        )

    def finished(i, n, e):
        if i == 2:
            store(i, e).start()
            return

        @pl.when(n == 0)
        def _():
            opposed(i).start()

        @pl.when(n > 0)
        def _():
            store(i, e).start()

    def give(n, carry):
        e = turn_of(n)
        left = x_t[pl.ds(theirs, half), :]
        wg[e, :half, :] = mm(left, dg[e]).astype(BF16)
        swap(0, e).start()
        wu[e, :half, :] = mm(left, du[e]).astype(BF16)
        swap(1, e).start()
        wd[e, :dhalf, :] = mm(hc[e, :, pl.ds(dtheirs, dhalf)], g_rows[...], TN).astype(BF16)
        swap(2, e).start()
        return carry

    def keep(n, carry):
        e = turn_of(n)

        left = x_t[pl.ds(mine, half), :]
        own = mm(left, dg[e])
        swap(0, e).wait_recv()
        xg[e] = (own + xg[e].astype(F32)).astype(BF16)
        finished(0, n, e)
        own = mm(left, du[e])
        swap(1, e).wait_recv()
        xu[e] = (own + xu[e].astype(F32)).astype(BF16)
        finished(1, n, e)
        own = mm(hc[e, :, pl.ds(dmine, dhalf)], g_rows[...], TN)
        swap(2, e).wait_recv()
        xd[e] = (own + xd[e].astype(F32)).astype(BF16)
        finished(2, n, e)
        return carry

    give(0, 0)

    def both(n, carry):
        give(n, 0)
        keep(n - 1, 0)
        return carry

    lax.fori_loop(1, 4, both, 0)
    keep(3, 0)

    from_line = jnp.zeros((experts, tok), F32)
    for n in (1, 2, 3):
        k = flip(line, n)
        at = apart(k)
        pltpu.make_async_copy(c_send.at[at], c_recv.at[at], krecv_sem.at[k]).wait()
        from_line += c_recv[at, :experts, :].astype(F32) + c_recv[at, experts:, :].astype(F32)
        pltpu.make_async_copy(d_send.at[at], d_recv.at[at], brecv_sem.at[k]).wait()
        d_in[...] += d_recv[at].astype(F32)
    filler = jnp.zeros((128 - experts, tok), F32)
    d_c[...] += jnp.transpose(jnp.concatenate([from_line, filler], 0))

    gates = gate_ref[...]
    d_gates = rw_ref[...] * d_c[...]
    dlog = (gates * (d_gates - jnp.sum(gates * d_gates, -1, keepdims=True))).astype(BF16)
    dlog_ref[...] = dlog
    d_xl = d_in[...] + mm(dlog, wr_ref[...], NT)
    h1 = h1_ref[...]
    scale = rms_scale(h1)
    scaled = d_xl * gain_ref[...]
    inner = jnp.mean(scaled * h1, -1, keepdims=True)
    d_h1 = g_in[line].astype(F32) + scale * scaled - h1 * scale**3 * inner
    dgain_ref[...] = jnp.sum((d_xl * h1 * scale).reshape(tok // 8, 8, d), 0)
    dh_ref[...] = d_h1
    d_att = d_h1.astype(BF16)
    datt_ref[...] = d_att
    do_ref[...] = mm(d_att, wo[...], NT).astype(BF16)
    for n in (1, 2, 3):
        give_back(flip(line, n)).wait_send()
        give_back_too(flip(line, n)).wait_send()
        store_mix(flip(line, n)).wait()
    store_xl.wait()
    store_res.wait()
    for k in range(4):

        @pl.when((k <= line) & (line < 3))
        def _():
            along(k, 1).wait_send()
            along_too(k, 1).wait_send()

        @pl.when((k >= line) & (line > 0))
        def _():
            along(k, -1).wait_send()
            along_too(k, -1).wait_send()

    def finish(n, carry):
        e = turn_of(n)
        for i in range(3):
            swap(i, e).wait_send()

            @pl.when((n > 0) | (i == 2))
            def _():
                store(i, e).wait()

        return carry

    lax.fori_loop(0, 4, finish, 0)
    for i in range(2):
        opposed(i).wait()


def mixture(vectors, w_out, g, w_gate, w_up, w_down, shared):
    tok, d = g.shape
    ff = w_gate.shape[1]
    experts = vectors[3].shape[0]
    vm = pl.BlockSpec(memory_space=pltpu.VMEM)
    hbm = pl.BlockSpec(memory_space=pl.ANY)
    dma = pltpu.SemaphoreType.DMA
    vmem = pltpu.VMEM
    return pl.pallas_call(
        mixture_kernel,
        out_shape=(
            jax.ShapeDtypeStruct((tok, d), F32),
            jax.ShapeDtypeStruct((4, tok, d), BF16),
            jax.ShapeDtypeStruct((tok, d), BF16),
            jax.ShapeDtypeStruct((tok, 128), BF16),
            jax.ShapeDtypeStruct((tok, d), F32),
            jax.ShapeDtypeStruct((tok, d), BF16),
            jax.ShapeDtypeStruct((tok, d), BF16),
            jax.ShapeDtypeStruct((8, d), F32),
            jax.ShapeDtypeStruct((4, d // 2, ff), BF16),
            jax.ShapeDtypeStruct((4, d // 2, ff), BF16),
            jax.ShapeDtypeStruct((4, ff // 2, d), BF16),
            jax.ShapeDtypeStruct((d // 2, ff), BF16),
            jax.ShapeDtypeStruct((d // 2, ff), BF16),
        ),
        in_specs=[vm] * 6 + [hbm] * 9,
        out_specs=(hbm,) * 3 + (vm,) * 5 + (hbm,) * 5,
        scratch_shapes=[
            vmem((tok, d), F32),
            vmem((3, tok, d), BF16),
            vmem((tok, d), BF16),
            dma((5,)),
            vmem((d, 128), BF16),
            vmem((tok, 128), F32),
            vmem((tok, d), F32),
            vmem((tok, 128), F32),
            vmem((tok, d), F32),
            vmem((tok, 128), F32),
            vmem((d, d), BF16),
            vmem((4, tok, d), BF16),
            vmem((4, experts, tok), BF16),
            vmem((tok, 128), F32),
            vmem((d, 4 * tok), BF16),
            vmem((4, tok, d), BF16),
            vmem((4, d, ff), BF16),
            vmem((4, d, ff), BF16),
            vmem((4, ff, d), BF16),
            vmem((4, 4 * tok, ff), BF16),
            vmem((4, 4 * tok, ff), BF16),
            vmem((4, 4 * tok, ff), BF16),
            vmem((tok, d), F32),
            vmem((tok, d), F32),
            vmem((tok, 128), F32),
            vmem((3, tok, d), BF16),
            vmem((3, tok, d), BF16),
            vmem((3, 2 * experts, tok), BF16),
            vmem((3, 2 * experts, tok), BF16),
            vmem((4, d // 2, ff), BF16),
            vmem((4, d // 2, ff), BF16),
            vmem((4, ff // 2, d), BF16),
            dma((3, 4)),
            dma((4,)),
            dma((2, 4)),
            dma((4,)),
            dma((4,)),
            dma((4,)),
            dma((3, 4)),
            dma((3, 4)),
            dma((3, 4)),
            dma((2,)),
            dma((2,)),
            dma,
            dma((2, 4)),
            dma((4,)),
            dma((4,)),
            dma((4,)),
        ],
        compiler_params=pltpu.CompilerParams(
            collective_id=2, has_side_effects=True, vmem_limit_bytes=VMEM_LIMIT
        ),
        name="mixture",
    )(*vectors, w_out, g, w_gate, w_up, w_down, *shared)


def tail_kernel(
    got,
    xa_ref,
    gain_ref,
    ao_ref,
    datt_ref,
    xl_ref,
    dlog_ref,
    dgain2_ref,
    x_any,
    dh_any,
    own_any,
    wq_any,
    wk_any,
    wv_any,
    mix_ref,
    mix_near,
    eg_ref,
    eu_ref,
    ed_ref,
    eg_in,
    eu_in,
    ed_in,
    eg_far,
    eu_far,
    res_ref,
    dx_ref,
    gsum_ref,
    o_any,
    q_any,
    kv_any,
    eg_any,
    eu_any,
    ed_any,
    fin_o,
    fin_q,
    fin_kv,
    eg_out,
    eu_out,
    ed_out,
    store_sem,
    x_ref,
    dh_ref,
    own_ref,
    late_sem,
    mix_in,
    wq_ref,
    wk_ref,
    wv_ref,
    d_all,
    ev,
    edv,
    gbuf,
    grv,
    load_sem,
    esend,
    erecv,
    gsend,
    grecv,
    msend,
    mrecv,
    *summing,
):
    me_s = lax.axis_index("seq")
    me_b = lax.axis_index("blk")
    plane = lax.rem(me_b, 4)
    tok, d = xa_ref.shape
    sums = [
        Summed(summing[8 * i : 8 * i + 6], *summing[8 * i + 6 : 8 * i + 8], fin)
        for i, fin in enumerate((fin_o, fin_q, fin_kv))
    ]
    for_out, for_q, for_kv = sums
    [sibling], planes, lines = for_q.sibling, for_q.planes, for_q.lines
    barrier = pltpu.get_barrier_semaphore()
    for place in [sibling, *planes, *lines]:
        pl.semaphore_signal(barrier, inc=1, device_id=place, device_id_type=MESH)

    experts = (
        (eg_ref, eg_in, eg_far, ev.at[0]),
        (eu_ref, eu_in, eu_far, ev.at[1]),
        (ed_ref, ed_in, None, edv),
    )

    def loads(i):
        own, arrived, far, dst = experts[i]
        near = arrived.shape[0]
        copies = [
            pltpu.make_async_copy(own.at[plane], dst.at[0], load_sem.at[i, 0]),
            pltpu.make_async_copy(arrived, dst.at[pl.ds(1, near)], load_sem.at[i, 1]),
        ]
        if far is not None:
            copies.append(pltpu.make_async_copy(far, dst.at[3], load_sem.at[i, 2]))
        return copies

    projections = [
        pltpu.make_async_copy(src, dst, load_sem.at[3, i + 1])
        for i, (src, dst) in enumerate(((wq_any, wq_ref), (wk_any, wk_ref), (wv_any, wv_ref)))
    ]
    projections += [
        pltpu.make_async_copy(src, dst, late_sem.at[i])
        for i, (src, dst) in enumerate(((x_any, x_ref), (dh_any, dh_ref), (own_any, own_ref)))
    ]
    stores = [
        pltpu.make_async_copy(src, dst, store_sem.at[i])
        for i, (src, dst) in enumerate(
            (
                (fin_o, o_any),
                (fin_q, q_any),
                (fin_kv, kv_any),
                (eg_out, eg_any),
                (eu_out, eu_any),
                (ed_out, ed_any),
            )
        )
    ]
    for copy in projections:
        copy.start()
    for i in range(3):
        for copy in loads(i):
            copy.start()
    pl.semaphore_wait(barrier, 7)
    line = me_b // 4

    far_mix = remote(mix_ref.at[flip(line, 3)], mix_in.at[2], msend, mrecv, *lines[2])
    near_mix = pltpu.make_async_copy(mix_near, mix_in.at[pl.ds(0, 2)], load_sem.at[3, 0])
    far_mix.start()
    near_mix.start()
    theirs, mine = for_q.halves()
    for_out.out[:, :d] = mm(ao_ref[:, theirs], datt_ref[...], TN).astype(BF16)
    for_out.out[:, d:] = mm(xl_ref[:, theirs], dlog_ref[...], TN).astype(BF16)
    for_out.start(0)

    low = lax.broadcasted_iota(jnp.int32, (tok, 2 * HD), 1) < HD
    for m in range(KV // 2):
        a, b = got[2 * m], got[2 * m + 1]
        d_all[:, 2 * m * 2 * HD : (2 * m + 1) * 2 * HD] = a[:, : 2 * HD]
        d_all[:, (2 * m + 1) * 2 * HD : (2 * m + 2) * 2 * HD] = b[:, : 2 * HD]
        ka, kb = a[:, 2 * HD :].astype(F32), b[:, 2 * HD :].astype(F32)
        at = H * HD + m * 2 * HD
        d_all[:, at : at + 2 * HD] = jnp.where(low, ka, pltpu.roll(kb, HD, 1)).astype(BF16)
        at += KV * HD
        d_all[:, at : at + 2 * HD] = jnp.where(low, pltpu.roll(ka, HD, 1), kb).astype(BF16)
    parts = ((for_q, slice(0, H * HD)), (for_kv, slice(H * HD, (H + 2 * KV) * HD)))
    for item, cols in parts:
        item.out[...] = mm(xa_ref[:, theirs], d_all[:, cols], TN).astype(BF16)
        item.start(0)
    for_out.acc[:, :d] = mm(ao_ref[:, mine], datt_ref[...], TN)
    for_out.acc[:, d:] = mm(xl_ref[:, mine], dlog_ref[...], TN)
    for_out.pair()
    for item, cols in parts:
        item.acc[...] = mm(xa_ref[:, mine], d_all[:, cols], TN)
        item.pair()

    for copy in projections:
        copy.wait()
    grad = (
        mm(d_all[:, : H * HD], wq_ref[...], NT)
        + mm(d_all[:, H * HD : (H + KV) * HD], wk_ref[...], NT)
        + mm(d_all[:, (H + KV) * HD :], wv_ref[...], NT)
    )
    xs = x_ref[...].astype(F32)
    scale = rms_scale(xs)
    scaled = grad * gain_ref[...]
    inner = jnp.mean(scaled * xs, -1, keepdims=True)
    dx_ref[...] = dh_ref[...] + scale * scaled - xs * scale**3 * inner
    gains = (
        jnp.sum(grad * xs * scale, 0, keepdims=True),
        jnp.sum(dgain2_ref[...], 0, keepdims=True),
    )
    part = d // 4
    gbuf[0] = jnp.concatenate(
        [gain[:, i * part : (i + 1) * part] for gain in gains for i in range(4)], 0
    )

    stages = [[sibling], planes, lines]

    def gain_copy(s, n):
        at = (0, 1, 4)[s] + n
        return remote(gbuf.at[s], grv.at[at], gsend.at[at], grecv.at[at], *stages[s][n])

    def gain_stage(s):
        for n in range(len(stages[s])):
            gain_copy(s, n).start()

    def gain_total(s):
        total = gbuf[s]
        for n in range(len(stages[s])):
            gain_copy(s, n).wait_recv()
            total = total + grv[(0, 1, 4)[s] + n]
        return total

    gain_stage(0)
    for_out.over_plane()

    outs = (eg_out, eu_out, ed_out)

    def expert_swap(i):
        rows = outs[i].shape[0] // 2
        part = outs[i].at[pl.ds(pl.multiple_of(me_s * rows, rows), rows)]
        return remote(part, part, esend.at[i], erecv.at[i], *sibling)

    for i in range(3):
        for copy in loads(i):
            copy.wait()
        terms = experts[i][3]
        rows = outs[i].shape[0] // 2
        total = terms[0].astype(F32)
        for n in (1, 2, 3):
            total = total + terms[n].astype(F32)
        outs[i][pl.ds(pl.multiple_of(me_s * rows, rows), rows), :] = total.astype(BF16)
        expert_swap(i).start()
    gbuf[1] = gain_total(0)
    gain_stage(1)
    for_q.over_plane()
    for_out.over_line()
    for_kv.over_plane()
    gbuf[2] = gain_total(1)
    gain_stage(2)
    for_q.over_line()
    for_out.back(3)
    for_kv.over_line()
    for_q.back(3)
    for_kv.back(3)
    gsum_ref[...] = gain_total(2)
    for i in range(3):
        expert_swap(i).wait()
        stores[3 + i].start()
    for item in sums:
        item.back(4)
    result = own_ref[...]
    near_mix.wait()
    far_mix.wait()
    for n in range(3):
        result = result + mix_in[n].astype(F32)
    res_ref[...] = result.astype(BF16)
    for item, store in zip(sums, stores):
        item.finish()
        store.start()
    for store in stores:
        store.wait()
    for s in range(3):
        for n in range(len(stages[s])):
            gain_copy(s, n).wait_send()


def tail(blocks_in, mix_peer, mix_near, own, arrived, far):
    tok, d = blocks_in[1].shape
    ff = own[0].shape[2]
    widths = (d + 128, H * HD, 2 * KV * HD)
    vm = pl.BlockSpec(memory_space=pltpu.VMEM)
    hbm = pl.BlockSpec(memory_space=pl.ANY)
    dma = pltpu.SemaphoreType.DMA
    vmem = pltpu.VMEM
    return pl.pallas_call(
        tail_kernel,
        out_shape=(
            jax.ShapeDtypeStruct((tok, d), BF16),
            jax.ShapeDtypeStruct((tok, d), F32),
            jax.ShapeDtypeStruct((8, d // 4), F32),
            *(jax.ShapeDtypeStruct((d, width), BF16) for width in widths),
            jax.ShapeDtypeStruct((d, ff), BF16),
            jax.ShapeDtypeStruct((d, ff), BF16),
            jax.ShapeDtypeStruct((ff, d), BF16),
        ),
        in_specs=[vm] * (len(blocks_in) - 6) + [hbm] * 16,
        out_specs=(vm,) * 3 + (hbm,) * 6,
        scratch_shapes=[
            *(vmem((d, width), BF16) for width in widths),
            vmem((d, ff), BF16),
            vmem((d, ff), BF16),
            vmem((ff, d), BF16),
            dma((6,)),
            vmem((tok, d), BF16),
            vmem((tok, d), F32),
            vmem((tok, d), F32),
            dma((3,)),
            vmem((3, tok, d), BF16),
            vmem((d, H * HD), BF16),
            vmem((d, KV * HD), BF16),
            vmem((d, KV * HD), BF16),
            vmem((tok, (H + 2 * KV) * HD), BF16),
            vmem((2, 4, d // 2, ff), BF16),
            vmem((4, ff // 2, d), BF16),
            vmem((3, 8, d // 4), F32),
            vmem((7, 8, d // 4), F32),
            dma((4, 4)),
            dma((3,)),
            dma((3,)),
            dma((7,)),
            dma((7,)),
            dma,
            dma,
            *(ref for width in widths for ref in summed_scratch(d, width)),
        ],
        compiler_params=pltpu.CompilerParams(
            collective_id=3, has_side_effects=True, vmem_limit_bytes=VMEM_LIMIT
        ),
        name="tail",
    )(*blocks_in, mix_peer, mix_near, *own, *arrived, *far)


def widen_kernel(
    gains, o, q, kv, eg, eu, ed, res, dx, n1, wq, wk, wv, wo, n2, wr, og, ou, od, res_out, dx_out
):
    d = wq.shape[1]
    half = wk.shape[1]
    wq[...] = q[...].astype(F32)
    wk[...] = kv[:, :half].astype(F32)
    wv[...] = kv[:, half:].astype(F32)
    wo[...] = o[:, :d].astype(F32)
    wr[...] = jnp.transpose(o[:, d:].astype(F32))[: wr.shape[0]]
    og[0] = eg[...].astype(F32)
    ou[0] = eu[...].astype(F32)
    od[0] = ed[...].astype(F32)
    n1[...] = jnp.concatenate([gains[i : i + 1, :] for i in range(4)], 1)
    n2[...] = jnp.concatenate([gains[i : i + 1, :] for i in range(4, 8)], 1)
    res_out[0] = res[...]
    dx_out[0] = dx[...]


def widen(gains, o, q, kv, eg, eu, ed, res, dx, experts):
    d, ff = eg.shape
    tok = res.shape[0]
    parts = 4

    def block(shape):
        return pl.BlockSpec((shape[0] // parts, shape[1]), lambda i: (i, 0))

    def deep(shape):
        return pl.BlockSpec((1, shape[0] // parts, shape[1]), lambda i: (0, i, 0))

    flat = pl.BlockSpec((1, d), lambda i: (0, 0))
    shapes = [(d, H * HD), (d, KV * HD), (d, KV * HD), (H * HD, d)]
    return pl.pallas_call(
        widen_kernel,
        grid=(parts,),
        out_shape=(
            jax.ShapeDtypeStruct((1, d), F32),
            *(jax.ShapeDtypeStruct(shape, F32) for shape in shapes),
            jax.ShapeDtypeStruct((1, d), F32),
            jax.ShapeDtypeStruct((experts, d), F32),
            jax.ShapeDtypeStruct((1, d, ff), F32),
            jax.ShapeDtypeStruct((1, d, ff), F32),
            jax.ShapeDtypeStruct((1, ff, d), F32),
            jax.ShapeDtypeStruct((1, tok, d), BF16),
            jax.ShapeDtypeStruct((1, tok, d), F32),
        ),
        in_specs=[pl.BlockSpec((8, d // 4), lambda i: (0, 0))]
        + [block(a.shape) for a in (o, q, kv, eg, eu, ed, res, dx)],
        out_specs=(
            flat,
            *(block(shape) for shape in shapes),
            flat,
            pl.BlockSpec((experts, d // parts), lambda i: (0, i)),
            deep((d, ff)),
            deep((d, ff)),
            deep((ff, d)),
            deep((tok, d)),
            deep((tok, d)),
        ),
        compiler_params=pltpu.CompilerParams(vmem_limit_bytes=VMEM_LIMIT),
        name="widen",
    )(gains, o, q, kv, eg, eu, ed, res, dx)


D = 1024
HIGH = lax.Precision.HIGHEST


def rope_tables(positions):
    half = HD // 2
    freq = jnp.exp(-math.log(10000.0) * jnp.arange(half, dtype=jnp.float32) * 2.0 / HD)
    angle = positions.astype(jnp.float32)[:, None] * freq[None, :]
    cosine = jnp.concatenate([jnp.cos(angle), jnp.cos(angle)], -1)
    sine = jnp.concatenate([jnp.sin(angle), jnp.sin(angle)], -1)
    return (cosine, sine)


def rotate_half(v):
    half = v.shape[-1] // 2
    return jnp.concatenate([-v[..., half:], v[..., :half]], -1)


def rotary(v, cosine, sine):
    return v * cosine[:, None, :] + rotate_half(v) * sine[:, None, :]


def unrotary(v, cosine, sine):
    return v * cosine[:, None, :] - rotate_half(v) * sine[:, None, :]


def rms_scale(v):
    return lax.rsqrt(jnp.mean(v * v, -1, keepdims=True) + EPS)


def rms_back(inputs, scale_rows, gain, grad):
    scaled = grad * gain
    d_inputs = scale_rows * scaled - inputs * scale_rows**3 * jnp.mean(
        scaled * inputs, -1, keepdims=True
    )
    return (d_inputs, jnp.sum(grad * inputs * scale_rows, 0))


def scores(queries, keys):
    return jnp.einsum("qkgd,skd->kgqs", queries, keys, preferred_element_type=jnp.float32) * HD ** (
        -0.5
    )


def per_device_plain(
    tokens,
    segments,
    routes,
    route_weight,
    norm1_gain,
    w_query,
    w_key,
    w_value,
    w_out,
    norm2_gain,
    w_router,
    w_gate,
    w_up,
    w_down,
    cotangent,
):
    f32 = jnp.float32
    bf16 = jnp.bfloat16
    scale = HD ** (-0.5)
    group = H // KV
    xs = tokens[0].astype(f32)
    tok = xs.shape[0]
    blocks = lax.axis_size("blk")
    length = tok * blocks
    first = lax.axis_index("blk") * tok
    last = first + tok - 1
    positions = first + jnp.arange(tok, dtype=jnp.int32)
    cosine, sine = rope_tables(positions)
    scale1 = rms_scale(xs)
    xa = (xs * scale1 * norm1_gain).astype(bf16)
    query = jnp.dot(xa, w_query, preferred_element_type=f32)
    key = jnp.dot(xa, w_key, preferred_element_type=f32)
    value = jnp.dot(xa, w_value, preferred_element_type=f32).astype(bf16)
    q_rot = rotary(query.reshape(tok, H, HD), cosine, sine).astype(bf16).reshape(tok, KV, group, HD)
    k_rot = rotary(key.reshape(tok, KV, HD), cosine, sine).astype(bf16).reshape(tok, KV * HD)
    seg_float = segments[0].astype(bf16)
    k_all, v_all, seg_all = (
        lax.all_gather(k_rot, "blk", axis=0, tiled=True),
        lax.all_gather(value, "blk", axis=0, tiled=True),
        lax.all_gather(seg_float, "blk", axis=0, tiled=True),
    )
    kblk = min(512, length)
    nblk = length // kblk
    k_blocks = k_all.reshape(nblk, kblk, KV, HD)
    v_blocks = v_all.reshape(nblk, kblk, KV, HD)
    s_blocks = seg_all.reshape(nblk, kblk)
    starts = jnp.arange(nblk, dtype=jnp.int32) * kblk

    def visible(kseg, kstart):
        kpos = kstart + jnp.arange(kblk, dtype=jnp.int32)
        return ((seg_float[:, None] == kseg[None, :]) & (kpos[None, :] <= positions[:, None]))[
            None, None
        ]

    def forward_step(carry, block):
        kb, vb, sb, start = block

        def forward_compute(state):
            running, total, acc = state
            mask = visible(sb, start)
            score = jnp.where(mask, scores(q_rot, kb), NEG)
            newmax = jnp.maximum(running, jnp.max(score, -1))
            expo = jnp.where(mask, jnp.exp(score - newmax[..., None]), 0.0)
            factor = jnp.exp(running - newmax)
            total = total * factor + jnp.sum(expo, -1)
            acc = acc * factor[..., None] + jnp.einsum(
                "kgqs,skd->kgqd", expo.astype(bf16), vb, preferred_element_type=f32
            )
            return (newmax, total, acc)

        return (lax.cond(start <= last, forward_compute, lambda state: state, carry), None)

    init = (
        jnp.full((KV, group, tok), NEG, f32),
        jnp.zeros((KV, group, tok), f32),
        jnp.zeros((KV, group, tok, HD), f32),
    )
    (running, total, acc), unused = lax.scan(
        forward_step, init, (k_blocks, v_blocks, s_blocks, starts)
    )
    lse = running + jnp.log(total)
    o_rows = (acc / total[..., None]).transpose(2, 0, 1, 3)
    att_low = o_rows.reshape(tok, H * HD).astype(bf16)
    h1 = xs + jnp.dot(att_low, w_out, preferred_element_type=f32)
    scale2 = rms_scale(h1)
    xl = (h1 * scale2 * norm2_gain).astype(bf16)
    logits = jnp.dot(xl, w_router, preferred_element_type=f32)
    experts = logits.shape[1]
    route = routes[0]
    rweight = route_weight[0]
    chooser = (route[:, :, None] == jnp.arange(experts, dtype=jnp.int32)[None, None, :]).astype(f32)
    chosen = jnp.sum(chooser * logits[:, None, :], -1)
    gates = jax.nn.softmax(chosen, -1)
    combine = (rweight * gates).astype(bf16)
    cap = min(tok, 2 * tok * TOP // experts)
    member = jnp.sum(chooser, 1)
    before = jnp.asarray(np.tril(np.ones((tok, tok), np.float32), -1))
    order = jnp.dot(before, member, precision=HIGH)
    rank = jnp.sum(chooser * order[:, None, :], -1).astype(jnp.int32)
    slots = route * cap + rank
    placed = jnp.any(
        slots[:, :, None] == jnp.arange(experts * cap, dtype=jnp.int32)[None, None, :], 1
    ).astype(bf16)
    outgoing = jnp.einsum("ts,td->sd", placed, xl, preferred_element_type=f32).astype(bf16)
    incoming = lax.all_to_all(
        outgoing.reshape(experts, cap, D), "blk", split_axis=0, concat_axis=0, tiled=True
    )
    local_exp = w_gate.shape[0]
    incoming = incoming.reshape(blocks, local_exp, cap, D)
    gate_pre = jnp.einsum("necd,edf->necf", incoming, w_gate, preferred_element_type=f32)
    up_pre = jnp.einsum("necd,edf->necf", incoming, w_up, preferred_element_type=f32)
    sigma = jax.nn.sigmoid(gate_pre)
    activated = gate_pre * sigma
    hidden = (activated * up_pre).astype(bf16)
    expert_out = jnp.einsum("necf,efd->necd", hidden, w_down, preferred_element_type=f32).astype(
        bf16
    )
    returned = lax.all_to_all(
        expert_out.reshape(experts, cap, D), "blk", split_axis=0, concat_axis=0, tiled=True
    )
    per_route = jnp.take(returned.reshape(experts * cap, D), slots.reshape(-1), axis=0).reshape(
        tok, TOP, D
    )
    mixture = jnp.einsum("tj,tjd->td", combine, per_route, preferred_element_type=f32)
    result = h1 + mixture
    grad_out = cotangent[0].astype(f32)
    grad_combine = jnp.einsum("td,tjd->tj", grad_out, per_route.astype(f32), precision=HIGH)
    route_grads = (combine.astype(f32)[:, :, None] * grad_out[:, None, :]).astype(bf16)
    grad_slots = (
        jnp.zeros((experts * cap, D), bf16)
        .at[slots.reshape(-1)]
        .set(route_grads.reshape(tok * TOP, D))
    )
    grad_incoming = lax.all_to_all(
        grad_slots.reshape(experts, cap, D), "blk", split_axis=0, concat_axis=0, tiled=True
    )
    grad_incoming = grad_incoming.reshape(blocks, local_exp, cap, D)
    grad_hidden = jnp.einsum("necd,efd->necf", grad_incoming, w_down, preferred_element_type=f32)
    grad_gate = (grad_hidden * up_pre * sigma * (1.0 + gate_pre * (1.0 - sigma))).astype(bf16)
    grad_up = (grad_hidden * activated).astype(bf16)
    d_down = jnp.einsum("necf,necd->efd", hidden, grad_incoming, preferred_element_type=f32)
    d_gate_w = jnp.einsum("necd,necf->edf", incoming, grad_gate, preferred_element_type=f32)
    d_up_w = jnp.einsum("necd,necf->edf", incoming, grad_up, preferred_element_type=f32)
    grad_in = (
        jnp.einsum("necf,edf->necd", grad_gate, w_gate, preferred_element_type=f32)
        + jnp.einsum("necf,edf->necd", grad_up, w_up, preferred_element_type=f32)
    ).astype(bf16)
    grad_back = lax.all_to_all(
        grad_in.reshape(experts, cap, D), "blk", split_axis=0, concat_axis=0, tiled=True
    )
    grad_xl = jnp.einsum(
        "ts,sd->td", placed, grad_back.reshape(experts * cap, D), preferred_element_type=f32
    )
    grad_gates = rweight * grad_combine
    grad_chosen = gates * (grad_gates - jnp.sum(gates * grad_gates, -1, keepdims=True))
    grad_logits = jnp.sum(chooser * grad_chosen[:, :, None], 1).astype(bf16)
    d_router = jnp.einsum("td,te->de", xl, grad_logits, preferred_element_type=f32)
    grad_xl = grad_xl + jnp.einsum("te,de->td", grad_logits, w_router, preferred_element_type=f32)
    grad_h1_norm, d_gain2 = rms_back(h1, scale2, norm2_gain, grad_xl)
    grad_h1 = grad_out + grad_h1_norm
    grad_att = grad_h1.astype(bf16)
    d_out_w = jnp.einsum("ti,td->id", att_low, grad_att, preferred_element_type=f32)
    grad_o = jnp.einsum("td,id->ti", grad_att, w_out, preferred_element_type=f32).astype(bf16)
    grad_o_rows = grad_o.reshape(tok, KV, group, HD)
    delta = jnp.einsum("qkgd,qkgd->kgq", grad_o_rows.astype(f32), o_rows)

    def query_terms(kb, vb, sb, start):
        mask = visible(sb, start)
        prob = jnp.where(mask, jnp.exp(scores(q_rot, kb) - lse[..., None]), 0.0)
        dprob = jnp.einsum("qkgd,skd->kgqs", grad_o_rows, vb, preferred_element_type=f32)
        dscore = (prob * (dprob - delta[..., None])).astype(bf16)
        dq_term = jnp.einsum("kgqs,skd->qkgd", dscore, kb, preferred_element_type=f32) * scale
        return (dq_term, dscore, prob)

    zero_q = jnp.zeros((tok, KV, group, HD), f32)

    def backward_step(grad_q, block):
        kb, vb, sb, start = block

        def backward_compute(acc_q):
            dq_term, dscore, prob = query_terms(kb, vb, sb, start)
            gk = jnp.einsum("kgqs,qkgd->skd", dscore, q_rot, preferred_element_type=f32) * scale
            gv = jnp.einsum(
                "kgqs,qkgd->skd", prob.astype(bf16), grad_o_rows, preferred_element_type=f32
            )
            return (acc_q + dq_term, (gk.reshape(kblk, KV * HD), gv.reshape(kblk, KV * HD)))

        def skip(acc_q):
            empty = jnp.zeros((kblk, KV * HD), f32)
            return (acc_q, (empty, empty))

        return lax.cond(start <= last, backward_compute, skip, grad_q)

    grad_q, (gk_blocks, gv_blocks) = lax.scan(
        backward_step, zero_q, (k_blocks, v_blocks, s_blocks, starts)
    )
    grad_k, grad_v = (
        lax.psum_scatter(
            gk_blocks.reshape(length, KV * HD).astype(jnp.bfloat16),
            "blk",
            scatter_dimension=0,
            tiled=True,
        ).astype(jnp.float32),
        lax.psum_scatter(
            gv_blocks.reshape(length, KV * HD).astype(jnp.bfloat16),
            "blk",
            scatter_dimension=0,
            tiled=True,
        ).astype(jnp.float32),
    )
    grad_qr = unrotary(grad_q.reshape(tok, H, HD), cosine, sine).reshape(tok, H * HD).astype(bf16)
    grad_kr = unrotary(grad_k.reshape(tok, KV, HD), cosine, sine).reshape(tok, KV * HD).astype(bf16)
    grad_vr = grad_v.astype(bf16)
    d_query = jnp.einsum("td,te->de", xa, grad_qr, preferred_element_type=f32)
    d_key = jnp.einsum("td,te->de", xa, grad_kr, preferred_element_type=f32)
    d_value = jnp.einsum("td,te->de", xa, grad_vr, preferred_element_type=f32)
    grad_xa = (
        jnp.einsum("te,de->td", grad_qr, w_query, preferred_element_type=f32)
        + jnp.einsum("te,de->td", grad_kr, w_key, preferred_element_type=f32)
        + jnp.einsum("te,de->td", grad_vr, w_value, preferred_element_type=f32)
    )
    grad_x_norm, d_gain1 = rms_back(xs, scale1, norm1_gain, grad_xa)
    grad_x = grad_h1 + grad_x_norm
    summed = lax.psum(
        (d_gain1, d_query, d_key, d_value, d_out_w, d_gain2, d_router), ("seq", "blk")
    )
    expert_summed = (
        lax.psum(d_gate_w.astype(jnp.bfloat16), "seq").astype(jnp.float32),
        lax.psum(d_up_w.astype(jnp.bfloat16), "seq").astype(jnp.float32),
        lax.psum(d_down.astype(jnp.bfloat16), "seq").astype(jnp.float32),
    )
    return (
        result.astype(bf16)[None],
        grad_x[None],
        summed[0],
        summed[1],
        summed[2],
        summed[3],
        summed[4],
        summed[5],
        summed[6],
        expert_summed[0],
        expert_summed[1],
        expert_summed[2],
    )


def tables(length):
    half = HD // 2
    freq = np.exp(-math.log(10000.0) * np.arange(half, dtype=np.float32) * 2.0 / HD).astype(np.float32)
    angle = np.arange(length, dtype=np.float32)[:, None] * freq[None, :]
    return np.tile(np.cos(angle), (1, 4)), np.tile(np.sin(angle), (1, 4))


def per_device(
    tokens,
    segments,
    routes,
    route_weight,
    norm1_gain,
    w_query,
    w_key,
    w_value,
    w_out,
    norm2_gain,
    w_router,
    w_gate,
    w_up,
    w_down,
    cotangent,
):
    tok, d = tokens[0].shape
    blocks = lax.axis_size("blk")
    experts = w_router.shape[1]
    cos_np, sin_np = tables(tok * blocks)
    cos_all = jnp.asarray(cos_np.reshape(blocks, tok, 2 * HD))
    sin_all = jnp.asarray(sin_np.reshape(blocks, tok, 2 * HD))
    seg = jnp.pad(segments[0].astype(BF16).reshape(2, tok // 2), ((0, 14), (0, 0)))
    gain1 = norm1_gain[None]
    g_low = cotangent[0]
    att_low, xa, *kept = attention_forward(
        blocks,
        tokens[0],
        gain1,
        w_query,
        w_key,
        w_value,
        seg,
        cos_all,
        sin_all,
        g_low,
        w_gate[0],
        w_up[0],
        w_down[0],
    )
    kept, shared = kept[:5], kept[5:]

    own, mix_peer, xl, grad_logits, grad_h1, grad_att, grad_o, gain2_terms, *rest = mixture(
        (tokens[0], att_low, norm2_gain[None], w_router.T, routes[0].T, route_weight[0].T),
        w_out,
        g_low,
        w_gate[0],
        w_up[0],
        w_down[0],
        shared,
    )
    (dwg, dwu, dwd), far = rest[:3], rest[3:]
    vectors = (
        grad_o,
        *kept,
        cos_all,
        sin_all,
    )
    got, mix_near, *arrived = attention_backward(
        blocks, vectors, mix_peer, dwg, dwu, dwd
    )
    blocks_in = (
        got,
        xa,
        gain1,
        att_low,
        grad_att,
        xl,
        grad_logits,
        gain2_terms,
        tokens[0],
        grad_h1,
        own,
        w_query,
        w_key,
        w_value,
    )
    result, grad_x, gains, d_out, d_query, d_kv, d_gate_w, d_up_w, d_down = tail(
        blocks_in, mix_peer, mix_near, (dwg, dwu, dwd), arrived, far
    )
    wide = widen(gains, d_out, d_query, d_kv, d_gate_w, d_up_w, d_down, result, grad_x, experts)
    d_gain1, d_query, d_key, d_value, d_out, d_gain2, d_router, *rest, result, grad_x = wide
    return (
        result,
        grad_x,
        d_gain1[0],
        d_query,
        d_key,
        d_value,
        d_out,
        d_gain2[0],
        d_router.T,
        *rest,
    )


def solution(mesh):
    fused = dict(mesh.shape) == {"seq": 2, "blk": 2 * KV}
    return jax.shard_map(
        per_device if fused else per_device_plain,
        mesh=mesh,
        in_specs=(
            P("seq", "blk", None),
            P("seq", "blk"),
            P("seq", "blk", None),
            P("seq", "blk", None),
            P(),
            P(),
            P(),
            P(),
            P(),
            P(),
            P(),
            P("blk", None, None),
            P("blk", None, None),
            P("blk", None, None),
            P("seq", "blk", None),
        ),
        out_specs=(
            P("seq", "blk", None),
            P("seq", "blk", None),
            P(),
            P(),
            P(),
            P(),
            P(),
            P(),
            P(),
            P("blk", None, None),
            P("blk", None, None),
            P("blk", None, None),
        ),
        check_vma=False,
    )
```
